128 devices in a mesh: tok: 32 (over x, z, core), head: 4 (over y).
Axes of the slice: x: 4, y: 4, z: 4, core: 2. Of those that a mesh axis runs over, the one named last changes fastest.
Arguments:
- activations: bfloat16 [8192, 2048], P('tok'), may hold values from -6 to 6
- labels: int32 [8192], P('tok'), may hold values from 0 to 2
- position: int32 [8192], P('tok'), may hold values from 0 to 8191, as said below
- norm_gains: float32 [6, 2048], replicated, may hold values from 0.1 to 1.9
- qkv_weight: bfloat16 [2048, 3, 2048], P(None, None, 'head'), may hold values from -0.125 to 0.125
- out_weight: bfloat16 [2048, 2048], P('head'), may hold values from -0.75 to 0.75
- up_weight: bfloat16 [2048, 8192], P(None, 'head'), may hold values from -0.125 to 0.125
- down_weight: bfloat16 [8192, 2048], P('head'), may hold values from -0.09375 to 0.09375
- cotangent: bfloat16 [8192, 2048], P('tok'), may hold values from -6 to 6
Outputs:
- layer_out: bfloat16 [8192, 2048], P('tok')
- grad_input: float32 [8192, 2048], P('tok')
- grad_gains: float32 [6, 2048], P(None, 'tok')
- grad_qkv: float32 [2048, 3, 2048], P('tok', None, 'head')
- grad_out: float32 [2048, 2048], P(('head', 'tok'))
- grad_up: float32 [2048, 8192], P('tok', 'head')
- grad_down: float32 [8192, 2048], P(('head', 'tok'))
The draws below stay inside these ranges and needn't reach their ends.
Inputs may be any that keep to these rules, and one draw needn't show every extreme that they name: position is a permutation of the 8192 places. Of the 256 rows of one device at most 16 have places in any one block of 256 consecutive places, and every device has exactly 16 in some block.
All inputs are finite; a program needn't handle non-finite values.
Results may differ from the reference program's by a relative error of at most 0.03.
Values may be sent and summed in bfloat16 or wider, within the bound.
A program may use at most 320 MiB of HBM per device.

```python
import math
import jax
import jax.numpy as jnp
from jax import lax

D = 2048
HEADS = 16
HD = 128
FF = 8192
MODES = 3
TOK_DEV = 256
FIRST_DEV = 192
SECOND_DEV = 64
LEN_A = 6144
LEN_B = 2048
TOKENS = 8192
N_TOK = 32


def draw_position(key, part):
    key = jax.random.fold_in(key, 7)
    key_order, key_rows, key_mix = jax.random.split(key, 3)
    base_count = TOK_DEV // N_TOK
    pair_order = jax.random.permutation(key_order, N_TOK)
    pair_other = jnp.roll(pair_order, 1)
    device_ids = jnp.arange(N_TOK, dtype=jnp.int32)
    counts = base_count + base_count * ((pair_order[:, None] == device_ids[None, :]).astype(jnp.int32) - (pair_other[:, None] == device_ids[None, :]).astype(jnp.int32))
    start_in = jnp.cumsum(counts, axis=0) - counts
    end_at = jnp.cumsum(counts, axis=1)
    begin_at = end_at - counts
    shuffle = jax.vmap(lambda sub_key: jax.random.permutation(sub_key, TOK_DEV))(jax.random.split(key_rows, N_TOK))
    slot_index = jnp.arange(TOK_DEV, dtype=jnp.int32)
    dest_dev = jnp.sum((slot_index[None, :, None] >= end_at[:, None, :]).astype(jnp.int32), axis=2)
    offset = slot_index[None, :] - jnp.take_along_axis(begin_at, dest_dev, axis=1)
    local_row = jnp.take_along_axis(start_in, dest_dev, axis=1) + offset
    target = dest_dev * TOK_DEV + shuffle[dest_dev, local_row]
    row_mix = jax.vmap(lambda sub_key: jax.random.permutation(sub_key, TOK_DEV))(jax.random.split(key_mix, N_TOK))
    target = jnp.take_along_axis(target, row_mix, axis=1)
    return target.reshape(-1).astype(jnp.int32)


def touch_ends(array, rng, low, high):
    longest = array.shape.index(max(array.shape))
    spots = []
    for shift in (0, 1):
        where = [jax.random.randint(jax.random.fold_in(rng, axis), (), 0, length) for axis, length in enumerate(array.shape)]
        where[longest] = (where[longest] + shift) % array.shape[longest]
        spots.append(tuple(where))
    return array.at[spots[0]].set(low).at[spots[1]].set(high)


def shard_levels(own_key, extent, shards, least, high):
    gain = 1.0
    for dim, parts in shards:
        heights = jax.random.uniform(jax.random.fold_in(jax.random.fold_in(own_key, 6), dim), (parts,), jnp.float32, least / len(shards), high / len(shards))
        gain = gain * jnp.repeat(jnp.exp(heights), extent[dim] // parts).reshape((-1,) + (1,) * (len(extent) - 1 - dim))
    return gain


def bell_draw(key, shape, deviation, most, shards=(), held_as=jnp.bfloat16):
    drawn = jax.random.normal(key, shape, jnp.float32) * deviation
    if len(shards) > 0:
        drawn = shard_levels(key, shape, shards, -0.22, 0.18) * drawn
    return jnp.clip(drawn, min=-most, max=most).astype(held_as)


def setup_inputs(seed: int = 0) -> dict:
    seeds = jax.random.split(jax.random.key(seed), 10)
    return {
        "activations": bell_draw(seeds[0], (TOKENS, D), 1.0, 6.0, ((0, 32),)),
        "labels": touch_ends(jax.random.randint(seeds[1], (TOKENS,), 0, MODES), jax.random.fold_in(seeds[1], 1), 0, MODES - 1).astype(jnp.int32),
        "position": draw_position(jax.random.fold_in(seeds[9], 71), 0),
        "norm_gains": jnp.clip(1.0 + 0.18 * jax.random.normal(seeds[3], (2 * MODES, D), jnp.float32), 0.1, 1.9),
        "qkv_weight": bell_draw(seeds[4], (D, 3, D), D ** -0.5, 0.125, ((2, 4),)),
        "out_weight": bell_draw(seeds[5], (D, D), (D // 32) ** -0.5, 0.75, ((0, 4),)),
        "up_weight": bell_draw(seeds[6], (D, FF), D ** -0.5, 0.125, ((1, 4),)),
        "down_weight": bell_draw(seeds[7], (FF, D), (FF // 2) ** -0.5, 0.09375, ((0, 4),)),
        "cotangent": bell_draw(seeds[8], (TOKENS, D), 1.0, 6.0, ((0, 32),)),
    }


highest = lax.Precision.HIGHEST

@jax.custom_vjp
def low(v):
    return lax.optimization_barrier(v.astype(jnp.bfloat16)).astype(jnp.float32)

@jax.custom_vjp
def low_back(v):
    return v

def low_keep(v):
    return (low(v), None)

def low_pass(kept, grad):
    return (grad,)

def back_keep(v):
    return (v, None)

def back_low(kept, grad):
    return (low(grad),)
low.defvjp(low_keep, low_pass)
low_back.defvjp(back_keep, back_low)

def layer_norm(values_in):
    row_mean = lax.optimization_barrier(jnp.mean(values_in, axis=-1, keepdims=True))
    centred = values_in - row_mean
    inverse = lax.rsqrt(lax.optimization_barrier(jnp.mean(centred * centred, axis=-1, keepdims=True)) + 1e-05)
    return centred * inverse

def tables(place_now, head_dim):
    half_dim = head_dim // 2
    frequency = jnp.exp(jnp.arange(half_dim, dtype=jnp.float32) * (-2.0 * math.log(10000.0) / head_dim))
    angles = place_now.astype(jnp.float32)[:, None] * frequency[None, :]
    angles = jnp.concatenate([angles, angles], axis=-1)
    return (jnp.cos(angles), jnp.sin(angles))

def rotate(values_in, cosine, sine):
    half_dim = values_in.shape[-1] // 2
    turned = jnp.concatenate([-values_in[..., half_dim:], values_in[..., :half_dim]], axis=-1)
    return values_in * cosine[:, None, :] + turned * sine[:, None, :]

def attend(queries, key_heads, value_heads):
    length = queries.shape[0]
    block_rows = 512 if length % 512 == 0 else length
    score_scale = HD ** (-0.5)

    def one_block(block_index):
        query_rows = lax.dynamic_slice_in_dim(queries, block_index * block_rows, block_rows, 0)
        scores = low_back(jnp.einsum('qhd,khd->hqk', query_rows, key_heads, precision=highest) * score_scale)
        query_place = block_index * block_rows + jnp.arange(block_rows, dtype=jnp.int32)
        visible = jnp.arange(length, dtype=jnp.int32)[None, :] <= query_place[:, None]
        scores = jnp.where(visible[None], scores, -1e+30)
        weights = jax.nn.softmax(scores, axis=-1)
        return jnp.einsum('hqk,khd->qhd', low(weights), value_heads, precision=highest)
    blocks = lax.map(jax.checkpoint(one_block), jnp.arange(length // block_rows, dtype=jnp.int32))
    return blocks.reshape(length, queries.shape[1], queries.shape[2])

def forward(seq_input, norm_gains, qkv_weight, out_weight, up_weight, down_weight, onehot, cosine, sine):
    mode_count = norm_gains.shape[0] // 2
    token_count = seq_input.shape[0]
    input_one = low(layer_norm(seq_input) * jnp.dot(onehot, norm_gains[:mode_count], precision=highest))
    projected = jnp.einsum('td,dkh->tkh', input_one, qkv_weight, precision=highest)

    def split_heads(values_in):
        return values_in.reshape(token_count, HEADS, HD)
    queries = low_back(low(rotate(split_heads(low_back(projected[:, 0])), cosine, sine)))
    key_heads = low_back(low(rotate(split_heads(low_back(projected[:, 1])), cosine, sine)))
    value_heads = low_back(low(split_heads(projected[:, 2])))
    first_clip = attend(queries[:LEN_A], key_heads[:LEN_A], value_heads[:LEN_A])
    second_clip = attend(queries[LEN_A:], key_heads[LEN_A:], value_heads[LEN_A:])
    attended = low_back(low(jnp.concatenate([first_clip, second_clip], axis=0).reshape(token_count, HEADS * HD)))
    middle = seq_input + low_back(jnp.dot(attended, out_weight, precision=highest))
    input_two = low(layer_norm(middle) * jnp.dot(onehot, norm_gains[mode_count:], precision=highest))
    hidden = low_back(jnp.dot(input_two, up_weight, precision=highest))
    active = low(jax.nn.gelu(hidden, approximate=True))
    return middle + low_back(jnp.dot(active, down_weight, precision=highest))

def reference(activations, labels, position, norm_gains, qkv_weight, out_weight, up_weight, down_weight, cotangent):
    dest_dev = position // TOK_DEV
    row_in = position % TOK_DEV
    seq_index = jnp.where(row_in < FIRST_DEV, dest_dev * FIRST_DEV + row_in, LEN_A + dest_dev * SECOND_DEV + row_in - FIRST_DEV).astype(jnp.int32)
    seq_input = jnp.zeros((TOKENS, D), jnp.float32).at[seq_index].set(activations.astype(jnp.float32))
    seq_cotangent = jnp.zeros((TOKENS, D), jnp.float32).at[seq_index].set(cotangent.astype(jnp.float32))
    seq_labels = jnp.zeros((TOKENS,), jnp.int32).at[seq_index].set(labels)
    onehot = (seq_labels[:, None] == jnp.arange(MODES, dtype=jnp.int32)[None, :]).astype(jnp.float32)
    place_now = jnp.concatenate([jnp.arange(LEN_A, dtype=jnp.int32), jnp.arange(LEN_B, dtype=jnp.int32)])
    cosine, sine = tables(place_now, HD)

    def run_layer(seq_in, gains_in, qkv_in, out_in, up_in, down_in):
        return forward(seq_in, gains_in, qkv_in, out_in, up_in, down_in, onehot, cosine, sine)
    result, pullback = jax.vjp(run_layer, seq_input, norm_gains, qkv_weight.astype(jnp.float32), out_weight.astype(jnp.float32), up_weight.astype(jnp.float32), down_weight.astype(jnp.float32))
    gradients = pullback(seq_cotangent)
    layer_out = result[seq_index].astype(jnp.bfloat16)
    grad_input = gradients[0][seq_index]
    return (layer_out, grad_input, gradients[1], gradients[2], gradients[3], gradients[4], gradients[5])
```

```python
import functools
import math

import jax
import jax.numpy as jnp
from jax import lax
from jax.experimental import pallas as pl
from jax.experimental.pallas import tpu as pltpu
from jax.sharding import PartitionSpec as P

HD = 128
SIDE = 4
ROWS = 256
CLIP_STEP = 8192
MESH = pl.DeviceIdType.MESH
NT = (((1,), (1,)), ((), ()))
TN = (((0,), (0,)), ((), ()))
NN = (((1,), (0,)), ((), ()))
f32 = jnp.float32
bf16 = jnp.bfloat16
highest = lax.Precision.HIGHEST
VMEM_LIMIT = 56 << 20
HOPS = (1, 3, 2)


def dot(lhs, rhs, dims=NN):
    return lax.dot_general(lhs, rhs, dims, preferred_element_type=f32)


def place():
    tok = lax.axis_index("tok")
    return (lax.div(tok, 8), lax.axis_index("head"), lax.rem(lax.div(tok, 2), 4), lax.rem(tok, 2))


def around(index, step):
    return lax.rem(index + (step % SIDE), SIDE)


def device(x, y, z, core):
    return (x * 8 + z * 2 + core, y)


def remote(src, dst, send_sem, recv_sem, target):
    return pltpu.make_async_remote_copy(
        src_ref=src,
        dst_ref=dst,
        send_sem=send_sem,
        recv_sem=recv_sem,
        device_id=target,
        device_id_type=MESH,
    )


def meet(targets):
    barrier = pltpu.get_barrier_semaphore()
    for target in targets:
        pl.semaphore_signal(barrier, inc=1, device_id=target, device_id_type=MESH)
    pl.semaphore_wait(barrier, len(targets))


class Copies:
    def __init__(self, send_sems, recv_sems):
        self.send_sems = send_sems
        self.recv_sems = recv_sems
        self.used = 0
        self.open = []

    def start(self, src, dst, target, landing):
        index = self.used
        self.used += 1
        copy = remote(src, dst, self.send_sems.at[index], self.recv_sems.at[index], target)
        copy.start()
        self.open.append(copy)
        return remote(landing, landing, self.send_sems.at[index], self.recv_sems.at[index], target)

    def finish(self):
        for copy in self.open:
            copy.wait_send()


def sum_over_y(copies, here, given, came, total):
    x, y, z, core = here
    arrivals = []
    for n, hop in enumerate(HOPS):
        other = around(y, hop)
        arrivals.append(
            copies.start(given.at[other], came.at[n], device(x, other, z, core), came.at[n])
        )
    yield
    for arrival in arrivals:
        arrival.wait_recv()
    total[y] = (
        (given[y].astype(f32) + came[0].astype(f32))
        + (came[1].astype(f32) + came[2].astype(f32))
    ).astype(bf16)
    arrivals = []
    for hop in HOPS:
        arrivals.append(
            copies.start(
                total.at[y],
                total.at[y],
                device(x, around(y, hop), z, core),
                total.at[around(y, -hop)],
            )
        )
    yield
    for arrival in arrivals:
        arrival.wait_recv()
    yield


def ring_sum(copies, own, towards, block, slots):
    up, down = towards(1), towards(-1)
    from_down = copies.start(block(2, 0), slots.at[0], up, slots.at[0])
    from_up = copies.start(block(2, 1), slots.at[1], down, slots.at[1])
    raw_down = copies.start(block(1, 1), slots.at[2], up, slots.at[2])
    raw_up = copies.start(block(-1, 0), slots.at[3], down, slots.at[3])
    yield
    from_down.wait_recv()
    onward = block(1, 0)
    onward[...] = (onward[...].astype(f32) + slots[0].astype(f32)).astype(bf16)
    sum_down = copies.start(onward, slots.at[4], up, slots.at[4])
    from_up.wait_recv()
    onward = block(-1, 1)
    onward[...] = (onward[...].astype(f32) + slots[1].astype(f32)).astype(bf16)
    sum_up = copies.start(onward, slots.at[5], down, slots.at[5])
    yield
    for arrival in (raw_down, raw_up, sum_down, sum_up):
        arrival.wait_recv()

    def finished(half):
        mine = block(0, half)[...].astype(f32)
        if half == 0:
            return mine + slots[4].astype(f32) + slots[3].astype(f32)
        return mine + slots[2].astype(f32) + slots[5].astype(f32)

    own.append(finished)


def weight_scratch(rows, cols):
    half = cols // 4
    return [
        pltpu.VMEM((16, rows, 2 * ROWS), bf16),
        pltpu.VMEM((2 * ROWS, cols), bf16),
        pltpu.VMEM((2, 4, 2, 4 * rows, half), bf16),
        pltpu.VMEM((2, 6, 4 * rows, half), bf16),
        pltpu.VMEM((2, 2, 4, rows, half), bf16),
        pltpu.VMEM((2, 6, rows, half), bf16),
        pltpu.SemaphoreType.DMA((26,)),
        pltpu.SemaphoreType.DMA((26,)),
        pltpu.SemaphoreType.DMA((2,)),
    ]


def weight_grad(here, left, right, out, scratch):
    both_left, both_right, parts, came, sums, late, send_sems, recv_sems, own_sems = scratch
    x, y, z, core = here
    rows, cols = out.shape
    half = cols // 4
    copies = Copies(send_sems, recv_sems)
    twin = device(x, y, z, 1 - core)
    own_left = pltpu.make_async_copy(
        left.at[:, core], both_left.at[:, :, pl.ds(0, ROWS)], own_sems.at[0]
    )
    own_right = pltpu.make_async_copy(right, both_right.at[pl.ds(0, ROWS)], own_sems.at[1])
    own_left.start()
    own_right.start()
    far_left = copies.start(
        left.at[:, 1 - core],
        both_left.at[:, :, pl.ds(ROWS, ROWS)],
        twin,
        both_left.at[:, :, pl.ds(ROWS, ROWS)],
    )
    far_right = copies.start(
        right,
        both_right.at[pl.ds(ROWS, ROWS)],
        twin,
        both_right.at[pl.ds(ROWS, ROWS)],
    )
    yield
    own_left.wait()
    own_right.wait()
    far_left.wait_recv()
    far_right.wait_recv()

    def spot(way, step):
        return around(x if way == 0 else z, step)

    def fill(way, step, half_index):
        at = spot(way, step)
        if way == 0:
            chosen = both_left[pl.ds(at * 4, 4)].reshape(4 * rows, 2 * ROWS)
        else:
            chosen = jnp.concatenate([both_left[k * 4 + at] for k in range(4)], axis=0)
        start = (way * 2 + half_index) * half
        parts[way, at, half_index] = dot(chosen, both_right[:, start : start + half]).astype(bf16)

    def towards(way):
        def target(step):
            if way == 0:
                return device(around(x, step), y, z, core)
            return device(x, y, around(z, step), core)

        return target

    first, first_done = [], ([], [])
    for way in (0, 1):
        for step, half_index in ((2, 0), (2, 1), (1, 1), (-1, 0)):
            fill(way, step, half_index)
        ring = ring_sum(
            copies,
            first_done[way],
            towards(way),
            lambda step, half_index, way=way: parts.at[way, spot(way, step), half_index],
            came.at[way],
        )
        next(ring)
        first.append(ring)
    for way in (0, 1):
        for step, half_index in ((1, 0), (-1, 1), (0, 0), (0, 1)):
            fill(way, step, half_index)
    yield
    for ring in first:
        next(ring)
    yield
    second, second_done = [], ([], [])
    for way in (0, 1):
        next(first[way], None)
        for half_index in (0, 1):
            sums[way, half_index] = (
                first_done[way][0](half_index).astype(bf16).reshape(4, rows, half)
            )
        ring = ring_sum(
            copies,
            second_done[way],
            towards(1 - way),
            lambda step, half_index, way=way: sums.at[way, half_index, spot(1 - way, step)],
            late.at[way],
        )
        next(ring)
        second.append(ring)
    yield
    for ring in second:
        next(ring)
    yield
    for way in (0, 1):
        next(second[way], None)
        for half_index in (0, 1):
            start = (way * 2 + half_index) * half
            out[:, start : start + half] = second_done[way][0](half_index)
    copies.finish()
    yield


def sum_kernel(shapes, *refs):
    count = len(shapes)
    given = refs[0]
    factors = refs[1 : 1 + 2 * count]
    total = refs[1 + 2 * count]
    outs = refs[2 + 2 * count : 2 + 3 * count]
    came, all_rows, y_send, y_recv = refs[2 + 3 * count : 6 + 3 * count]
    scratch = refs[6 + 3 * count :]
    here = place()
    x, y, z, core = here
    meet(
        [device(x, around(y, hop), z, core) for hop in HOPS]
        + [device(around(x, hop), y, z, core) for hop in (1, 3)]
        + [device(x, y, around(z, hop), core) for hop in (1, 3)]
        + [device(x, y, z, 1 - core)]
    )
    copies = Copies(y_send, y_recv)
    over_y = sum_over_y(copies, here, given, came, all_rows)
    grads = [
        weight_grad(here, factors[2 * n], factors[2 * n + 1], outs[n], scratch[9 * n : 9 * n + 9])
        for n in range(count)
    ]
    next(over_y)
    for grad in grads:
        next(grad)
    for grad in grads:
        next(grad)
    next(over_y)
    for grad in grads:
        next(grad)
    next(over_y)
    total[...] = all_rows[...]
    copies.finish()
    for step in range(3):
        for grad in grads:
            next(grad)


def sum_and_grads(given, factors, collective_id):
    shapes = [(left.shape[2], right.shape[1]) for left, right in factors]
    width = given.shape[1]
    quarter = ROWS // SIDE
    flat = [array for pair in factors for array in pair]
    whole = pl.BlockSpec(memory_space=pltpu.VMEM)
    outs = pl.pallas_call(
        functools.partial(sum_kernel, shapes),
        out_shape=[jax.ShapeDtypeStruct((SIDE, quarter, width), bf16)]
        + [jax.ShapeDtypeStruct(shape, f32) for shape in shapes],
        in_specs=[whole] + [pl.BlockSpec(memory_space=pl.ANY)] * len(flat),
        out_specs=[whole] * (1 + len(shapes)),
        scratch_shapes=[
            pltpu.VMEM((3, quarter, width), bf16),
            pltpu.VMEM((SIDE, quarter, width), bf16),
            pltpu.SemaphoreType.DMA((6,)),
            pltpu.SemaphoreType.DMA((6,)),
        ]
        + [entry for shape in shapes for entry in weight_scratch(*shape)],
        compiler_params=pltpu.CompilerParams(
            collective_id=collective_id, has_side_effects=True, vmem_limit_bytes=VMEM_LIMIT
        ),
        name=f"sum_and_grads_{collective_id}",
    )(given.reshape(SIDE, quarter, width), *flat)
    return [outs[0].reshape(ROWS, width)] + list(outs[1:])


def visible(key_codes, low, span):
    return (key_codes - low).astype(jnp.uint32) <= span.astype(jnp.uint32)


def key_column(codes):
    row = lax.broadcasted_iota(jnp.int32, (8, HD), 0)
    weight = jnp.where(row == 0, 128.0, jnp.where(row == 1, 1.0, 0.0)).astype(bf16)
    return dot(codes, weight, TN).astype(jnp.int32)


QUERY_TILE = 512


def forward_kernel(
    q_ref, kv_ref, codes_ref, bounds_ref, out_weight_ref,
    q_all_ref, kv_all_ref, o_ref, lse_ref, returned_ref, total_ref,
    queries, keys_values, top, norm, acc, column, o_low, back, given, came, all_rows,
    send_sems, recv_sems, y_send, y_recv, keep_sems,
):
    here = place()
    x, y, z, core = here
    twin = device(x, y, z, 1 - core)
    meet(
        [device(around(x, hop), y, z, core) for hop in HOPS]
        + [device(x, around(y, hop), z, core) for hop in HOPS]
        + [device(x, y, around(z, hop), core) for hop in (1, 3)]
        + [twin]
    )
    copies = Copies(send_sems, recv_sems)
    above, below = device(x, y, around(z, 1), core), device(x, y, around(z, -1), core)
    next_z, last_z, far_z = around(z, 1), around(z, -1), around(z, 2)
    kv_came, q_came = [], []
    for hop in HOPS:
        other = around(x, hop)
        target = device(other, y, z, core)
        kv_came.append(
            copies.start(
                kv_ref.at[other],
                keys_values.at[z, core, x],
                target,
                keys_values.at[z, core, around(x, -hop)],
            )
        )
    for hop in HOPS:
        other = around(x, hop)
        target = device(other, y, z, core)
        q_came.append(
            copies.start(q_ref.at[other], queries.at[x], target, queries.at[around(x, -hop)])
        )
    keys_values[z, core, x] = kv_ref[x]
    queries[x] = q_ref[x]
    top[...] = jnp.full_like(top, -1e30)
    norm[...] = jnp.zeros_like(norm)
    acc[...] = jnp.zeros_like(acc)
    pieces = [x] + [around(x, -hop) for hop in HOPS]
    from_last, from_next, from_twin = [], [], []
    for n, piece in enumerate(pieces):
        if n > 0:
            kv_came[n - 1].wait_recv()
        block = keys_values.at[z, core, piece]
        from_last.append(copies.start(block, block, above, keys_values.at[last_z, core, piece]))
        from_next.append(copies.start(block, block, below, keys_values.at[next_z, core, piece]))
        from_twin.append(copies.start(block, block, twin, keys_values.at[z, 1 - core, piece]))
    for arrival in q_came:
        arrival.wait_recv()

    def attend(z_at, core_at):
        column[...] = key_column(codes_ref[z_at, core_at])

        def tile(index, carry):
            at = pl.ds(pl.multiple_of(index * QUERY_TILE, QUERY_TILE), QUERY_TILE)
            query = queries[pl.ds(index * 2, 2)].reshape(QUERY_TILE, HD)
            keys = keys_values[z_at, core_at, :, :, :HD].reshape(4 * ROWS, HD)
            values = keys_values[z_at, core_at, :, :, HD:].reshape(4 * ROWS, HD)
            scores = dot(keys, query, NT)
            codes = jnp.concatenate([column[...]] * (QUERY_TILE // HD), axis=1)
            seen = visible(codes, bounds_ref[0:1, at], bounds_ref[1:2, at])
            scores = jnp.where(seen, scores, -1e30)
            top_before = top[0:1, at]
            top_now = jnp.maximum(top_before, jnp.max(scores, axis=0, keepdims=True))
            weights = jnp.exp2(scores - top_now)
            shrink = jnp.exp2(top_before - top_now)
            norm[0:1, at] = norm[0:1, at] * shrink + jnp.sum(weights, axis=0, keepdims=True)
            top[0:1, at] = top_now
            acc[:, at] = acc[:, at] * shrink + dot(values, weights.astype(bf16), TN)
            return carry

        lax.fori_loop(0, 4 * ROWS // QUERY_TILE, tile, 0)

    low_far, high_far, twin_last, twin_next = [], [], [], []

    def onward(n):
        piece = pieces[n]
        from_last[n].wait_recv()
        block = keys_values.at[last_z, core, piece]
        low = block.at[pl.ds(0, ROWS // 2)]
        low_far.append(
            copies.start(low, low, above, keys_values.at[far_z, core, piece, pl.ds(0, ROWS // 2)])
        )
        twin_last.append(
            copies.start(block, block, twin, keys_values.at[last_z, 1 - core, piece])
        )
        from_next[n].wait_recv()
        block = keys_values.at[next_z, core, piece]
        high = block.at[pl.ds(ROWS // 2, ROWS // 2)]
        high_far.append(
            copies.start(
                high,
                high,
                below,
                keys_values.at[far_z, core, piece, pl.ds(ROWS // 2, ROWS // 2)],
            )
        )
        twin_next.append(
            copies.start(block, block, twin, keys_values.at[next_z, 1 - core, piece])
        )

    def take(arrivals):
        for arrival in arrivals:
            arrival.wait_recv()

    attend(z, core)
    onward(0)
    onward(1)
    take(from_twin)
    attend(z, 1 - core)
    onward(2)
    onward(3)
    attend(last_z, core)
    attend(next_z, core)
    take(twin_last)
    attend(last_z, 1 - core)
    take(twin_next)
    attend(next_z, 1 - core)
    twin_far = []
    for n, piece in enumerate(pieces):
        low_far[n].wait_recv()
        high_far[n].wait_recv()
        block = keys_values.at[far_z, core, piece]
        twin_far.append(copies.start(block, block, twin, keys_values.at[far_z, 1 - core, piece]))
    attend(far_z, core)
    take(twin_far)
    keep = pltpu.make_async_copy(keys_values, kv_all_ref, keep_sems.at[0])
    keep.start()
    attend(far_z, 1 - core)

    total_norm = norm[0:1, :]
    attended = (acc[...] / total_norm).T
    o_ref[...] = attended
    o_low[...] = attended.astype(bf16).reshape(4, ROWS, HD)
    lse_ref[...] = jnp.broadcast_to(top[0:1, :] + jnp.log2(total_norm), lse_ref.shape)
    q_all_ref[...] = queries[...]
    came_back = []
    for hop in HOPS:
        other = around(x, hop)
        came_back.append(
            copies.start(
                o_low.at[other],
                back.at[x],
                device(other, y, z, core),
                back.at[around(x, -hop)],
            )
        )
    back[x] = o_low[x]
    take(came_back)
    returned = jnp.concatenate([back[n] for n in range(4)], axis=1)
    returned_ref[...] = returned
    given[...] = dot(returned, out_weight_ref[...]).astype(bf16).reshape(given.shape)
    y_copies = Copies(y_send, y_recv)
    for step in sum_over_y(y_copies, here, given, came, all_rows):
        pass
    total_ref[...] = all_rows[...]
    copies.finish()
    y_copies.finish()
    keep.wait()


def attention_forward(q_heads, kv_heads, codes, bounds, out_weight):
    quarter = ROWS // SIDE
    width = out_weight.shape[1]
    whole = pl.BlockSpec(memory_space=pltpu.VMEM)
    count = 3 + 3 + 12 + 16 + 4 + 3
    outs = pl.pallas_call(
        forward_kernel,
        out_shape=[
            jax.ShapeDtypeStruct((4, ROWS, HD), bf16),
            jax.ShapeDtypeStruct((4, 2, 4, ROWS, 2 * HD), bf16),
            jax.ShapeDtypeStruct((4 * ROWS, HD), f32),
            jax.ShapeDtypeStruct((8, 4 * ROWS), f32),
            jax.ShapeDtypeStruct((ROWS, 4 * HD), bf16),
            jax.ShapeDtypeStruct((SIDE, quarter, width), bf16),
        ],
        in_specs=[whole] * 5,
        out_specs=[whole, pl.BlockSpec(memory_space=pl.ANY)] + [whole] * 4,
        scratch_shapes=[
            pltpu.VMEM((4, ROWS, HD), bf16),
            pltpu.VMEM((4, 2, 4, ROWS, 2 * HD), bf16),
            pltpu.VMEM((8, 4 * ROWS), f32),
            pltpu.VMEM((8, 4 * ROWS), f32),
            pltpu.VMEM((HD, 4 * ROWS), f32),
            pltpu.VMEM((4 * ROWS, HD), jnp.int32),
            pltpu.VMEM((4, ROWS, HD), bf16),
            pltpu.VMEM((4, ROWS, HD), bf16),
            pltpu.VMEM((SIDE, quarter, width), bf16),
            pltpu.VMEM((3, quarter, width), bf16),
            pltpu.VMEM((SIDE, quarter, width), bf16),
            pltpu.SemaphoreType.DMA((count,)),
            pltpu.SemaphoreType.DMA((count,)),
            pltpu.SemaphoreType.DMA((6,)),
            pltpu.SemaphoreType.DMA((6,)),
            pltpu.SemaphoreType.DMA((1,)),
        ],
        compiler_params=pltpu.CompilerParams(
            collective_id=0, has_side_effects=True, vmem_limit_bytes=VMEM_LIMIT
        ),
        name="attention_forward",
    )(q_heads, kv_heads, codes, bounds, out_weight)
    return list(outs[:5]) + [outs[5].reshape(ROWS, width)]


BACK_TILE = 256


def backward_kernel(
    grad_ref, q_ref, kv_hbm, o_ref, lse_ref, codes_ref, bounds_ref,
    packed_ref,
    keys_values, grads, delta, grad_q, grad_k, grad_v, column, parts, met, came, sums, q_low, back_q, back_kv,
    send_sems, recv_sems, load_sems,
):
    here = place()
    x, y, z, core = here
    twin = device(x, y, z, 1 - core)
    load = pltpu.make_async_copy(kv_hbm, keys_values, load_sems.at[0])
    load.start()
    meet(
        [device(around(x, hop), y, z, core) for hop in HOPS]
        + [device(x, y, around(z, hop), core) for hop in (1, 3)]
        + [twin]
    )
    copies = Copies(send_sems, recv_sems)
    arrivals = []
    for hop in HOPS:
        other = around(x, hop)
        arrivals.append(
            copies.start(
                grad_ref.at[other],
                grads.at[x],
                device(other, y, z, core),
                grads.at[around(x, -hop)],
            )
        )
    grads[x] = grad_ref[x]
    grad_q[...] = jnp.zeros_like(grad_q)
    load.wait()
    for arrival in arrivals:
        arrival.wait_recv()
    product = grads[...].reshape(4 * ROWS, HD).astype(f32) * o_ref[...]
    delta[...] = lax.dot_general(
        jnp.ones((8, HD), f32), product, NT, preferred_element_type=f32, precision=highest
    )

    def chunk(z_at, core_at):
        column[...] = key_column(codes_ref[z_at, core_at])
        grad_k[...] = jnp.zeros_like(grad_k)
        grad_v[...] = jnp.zeros_like(grad_v)

        def tile(index, carry):
            at = pl.ds(pl.multiple_of(index * BACK_TILE, BACK_TILE), BACK_TILE)
            query = q_ref[index]
            grad = grads[index]
            keys = keys_values[z_at, core_at, :, :, :HD].reshape(4 * ROWS, HD)
            values = keys_values[z_at, core_at, :, :, HD:].reshape(4 * ROWS, HD)
            scores = dot(keys, query, NT)
            codes = jnp.concatenate([column[...]] * (BACK_TILE // HD), axis=1)
            seen = visible(codes, bounds_ref[0:1, at], bounds_ref[1:2, at])
            weights = jnp.where(seen, jnp.exp2(scores - lse_ref[0:1, at]), 0.0)
            grad_weights = dot(values, grad, NT)
            grad_scores = (weights * (grad_weights - delta[0:1, at])).astype(bf16)
            grad_v[...] += dot(weights.astype(bf16), grad)
            grad_k[...] += dot(grad_scores, query)
            grad_q[:, at] += dot(keys, grad_scores, TN)
            return carry

        lax.fori_loop(0, 4 * ROWS // BACK_TILE, tile, 0)
        parts[z_at, core_at] = jnp.concatenate(
            [grad_k[...] * math.log(2.0), grad_v[...]], axis=1
        ).astype(bf16).reshape(2, 2 * ROWS, 2 * HD)

    def hand_over(z_at):
        return copies.start(
            parts.at[z_at, 1 - core], met.at[z_at], twin, met.at[z_at]
        )

    def join(z_at):
        parts[z_at, core] = (
            parts[z_at, core].astype(f32) + met[z_at].astype(f32)
        ).astype(bf16)

    next_z, last_z, far_z = around(z, 1), around(z, -1), around(z, 2)
    above, below = device(x, y, next_z, core), device(x, y, last_z, core)
    chunk(far_z, 1 - core)
    far_met = hand_over(far_z)
    chunk(far_z, core)
    chunk(next_z, 1 - core)
    next_met = hand_over(next_z)
    far_met.wait_recv()
    join(far_z)
    from_last = copies.start(parts.at[far_z, core, 0], came.at[0], above, came.at[0])
    from_next = copies.start(parts.at[far_z, core, 1], came.at[1], below, came.at[1])
    chunk(next_z, core)
    chunk(last_z, 1 - core)
    last_met = hand_over(last_z)
    next_met.wait_recv()
    join(next_z)
    raw_last = copies.start(parts.at[next_z, core, 1], came.at[2], above, came.at[2])
    chunk(last_z, core)
    chunk(z, 1 - core)
    own_met = hand_over(z)
    last_met.wait_recv()
    join(last_z)
    raw_next = copies.start(parts.at[last_z, core, 0], came.at[3], below, came.at[3])
    from_last.wait_recv()
    parts[next_z, core, 0] = (
        parts[next_z, core, 0].astype(f32) + came[0].astype(f32)
    ).astype(bf16)
    sum_last = copies.start(parts.at[next_z, core, 0], came.at[4], above, came.at[4])
    from_next.wait_recv()
    parts[last_z, core, 1] = (
        parts[last_z, core, 1].astype(f32) + came[1].astype(f32)
    ).astype(bf16)
    sum_next = copies.start(parts.at[last_z, core, 1], came.at[5], below, came.at[5])
    chunk(z, core)
    q_low[...] = (grad_q[...] * (HD**-0.5)).T.astype(bf16).reshape(4, ROWS, HD)
    arrivals = []
    for hop in HOPS:
        other = around(x, hop)
        arrivals.append(
            copies.start(
                q_low.at[other],
                back_q.at[x],
                device(other, y, z, core),
                back_q.at[around(x, -hop)],
            )
        )
    back_q[x] = q_low[x]
    own_met.wait_recv()
    raw_last.wait_recv()
    raw_next.wait_recv()
    sum_last.wait_recv()
    sum_next.wait_recv()
    mine = parts[z, core].astype(f32) + met[z].astype(f32)
    low = mine[0] + came[4].astype(f32) + came[3].astype(f32)
    high = mine[1] + came[2].astype(f32) + came[5].astype(f32)
    sums[0:2] = low.astype(bf16).reshape(2, ROWS, 2 * HD)
    sums[2:4] = high.astype(bf16).reshape(2, ROWS, 2 * HD)
    for hop in HOPS:
        other = around(x, hop)
        arrivals.append(
            copies.start(
                sums.at[other],
                back_kv.at[x],
                device(other, y, z, core),
                back_kv.at[around(x, -hop)],
            )
        )
    back_kv[x] = sums[x]
    for arrival in arrivals:
        arrival.wait_recv()
    for n in range(4):
        packed_ref[n, :, :HD] = back_q[n]
        packed_ref[n, :, HD:] = back_kv[n]
    copies.finish()


def attention_backward(grad_heads, q_all, kv_all, o_all, lse, codes, bounds):
    whole = pl.BlockSpec(memory_space=pltpu.VMEM)
    count = 3 + 4 + 6 + 6
    return pl.pallas_call(
        backward_kernel,
        out_shape=jax.ShapeDtypeStruct((4, ROWS, 3 * HD), bf16),
        in_specs=[whole, whole, pl.BlockSpec(memory_space=pl.ANY)] + [whole] * 4,
        out_specs=whole,
        scratch_shapes=[
            pltpu.VMEM((4, 2, 4, ROWS, 2 * HD), bf16),
            pltpu.VMEM((4, ROWS, HD), bf16),
            pltpu.VMEM((8, 4 * ROWS), f32),
            pltpu.VMEM((HD, 4 * ROWS), f32),
            pltpu.VMEM((4 * ROWS, HD), f32),
            pltpu.VMEM((4 * ROWS, HD), f32),
            pltpu.VMEM((4 * ROWS, HD), jnp.int32),
            pltpu.VMEM((4, 2, 2, 2 * ROWS, 2 * HD), bf16),
            pltpu.VMEM((4, 2, 2 * ROWS, 2 * HD), bf16),
            pltpu.VMEM((6, 2 * ROWS, 2 * HD), bf16),
            pltpu.VMEM((4, ROWS, 2 * HD), bf16),
            pltpu.VMEM((4, ROWS, HD), bf16),
            pltpu.VMEM((4, ROWS, HD), bf16),
            pltpu.VMEM((4, ROWS, 2 * HD), bf16),
            pltpu.SemaphoreType.DMA((count,)),
            pltpu.SemaphoreType.DMA((count,)),
            pltpu.SemaphoreType.DMA((1,)),
        ],
        compiler_params=pltpu.CompilerParams(
            collective_id=1, has_side_effects=True, vmem_limit_bytes=VMEM_LIMIT
        ),
        name="attention_backward",
    )(grad_heads, q_all, kv_all, o_all, lse, codes, bounds)


def layer_norm(values_in):
    row_mean = jnp.mean(values_in, axis=-1, keepdims=True)
    centred = values_in - row_mean
    inverse = lax.rsqrt(jnp.mean(centred * centred, axis=-1, keepdims=True) + 1e-05)
    return (centred * inverse, inverse)


def norm_back(grad_in, normed, inverse):
    return inverse * (
        grad_in
        - jnp.mean(grad_in, axis=-1, keepdims=True)
        - normed * jnp.mean(grad_in * normed, axis=-1, keepdims=True)
    )


def tables(place_now, head_dim):
    half_dim = head_dim // 2
    frequency = jnp.exp(
        jnp.arange(half_dim, dtype=jnp.float32) * (-2.0 * math.log(10000.0) / head_dim)
    )
    angles = place_now.astype(jnp.float32)[:, None] * frequency[None, :]
    angles = jnp.concatenate([angles, angles], axis=-1)
    return (jnp.cos(angles), jnp.sin(angles))


def rotate(values_in, cosine, sine):
    half_dim = values_in.shape[-1] // 2
    turned = jnp.concatenate([-values_in[..., half_dim:], values_in[..., :half_dim]], axis=-1)
    return values_in * cosine + turned * sine


def rotate_back(grad_in, cosine, sine):
    half_dim = grad_in.shape[-1] // 2
    scaled = grad_in * sine
    return grad_in * cosine + jnp.concatenate(
        [scaled[..., half_dim:], -scaled[..., :half_dim]], axis=-1
    )


def by_owner(factor):
    return factor.T.reshape(16, 2, factor.shape[1] // 32, ROWS)


def per_device(
    activations,
    labels,
    position,
    norm_gains,
    qkv_weight,
    out_weight,
    up_weight,
    down_weight,
    cotangent,
):
    mode_count = norm_gains.shape[0] // 2
    tok = lax.axis_index("tok")
    block, row = position // 256, position % 256
    second = (row >= 192).astype(jnp.int32)
    spot = jnp.where(second == 1, block * 64 + row - 192, block * 192 + row)
    code = spot + second * CLIP_STEP
    all_codes = lax.all_gather(code, "tok", axis=0)
    all_codes = all_codes.reshape(4, 4, 2, ROWS).transpose(1, 2, 0, 3).reshape(4, 2, 4 * ROWS)
    digits = jnp.stack([all_codes // 128, all_codes % 128], axis=2)
    codes = jnp.concatenate(
        [digits, jnp.zeros((4, 2, 6, 4 * ROWS), jnp.int32)], axis=2
    ).astype(bf16)
    own_codes = all_codes.reshape(8, 4 * ROWS)[tok % 8]
    own_low = jnp.where(own_codes >= CLIP_STEP, CLIP_STEP, 0)
    bounds = jnp.concatenate(
        [own_low[None], (own_codes - own_low)[None], jnp.zeros((6, 4 * ROWS), jnp.int32)], axis=0
    )

    residual = activations.astype(f32)
    onehot = (labels[:, None] == jnp.arange(mode_count, dtype=jnp.int32)[None, :]).astype(f32)
    gain_one = jnp.dot(onehot, norm_gains[:mode_count], precision=highest)
    gain_two = jnp.dot(onehot, norm_gains[mode_count:], precision=highest)
    normed_one, inverse_one = layer_norm(residual)
    input_one = (normed_one * gain_one).astype(bf16)
    cosine, sine = tables(spot, HD)
    projected = jnp.einsum("td,dkh->kth", input_one, qkv_weight, preferred_element_type=f32)
    projected = projected.reshape(3, ROWS, 4, HD).transpose(0, 2, 1, 3)
    q_heads = (rotate(projected[0], cosine, sine) * (HD**-0.5 / math.log(2.0))).astype(bf16)
    kv_heads = jnp.concatenate([rotate(projected[1], cosine, sine), projected[2]], axis=-1).astype(
        bf16
    )
    q_all, kv_all, o_all, lse, returned, attn_sum = attention_forward(
        q_heads, kv_heads, codes, bounds, out_weight
    )

    middle = residual + attn_sum.astype(f32)
    normed_two, inverse_two = layer_norm(middle)
    input_two = (normed_two * gain_two).astype(bf16)
    hidden = jnp.dot(input_two, up_weight, preferred_element_type=f32)
    grad_active = jnp.einsum("td,fd->tf", cotangent, down_weight, preferred_element_type=f32)
    active, gelu_pull = jax.vjp(
        lambda values_in: jax.nn.gelu(values_in, approximate=True), hidden
    )
    active = active.astype(bf16)
    grad_hidden = gelu_pull(grad_active)[0].astype(bf16)
    grad_two_part = jnp.einsum(
        "tf,df->td", grad_hidden, up_weight, preferred_element_type=f32
    ).astype(bf16)
    mlp_sum = lax.psum(
        jnp.dot(active, down_weight, preferred_element_type=f32).astype(bf16), "head"
    ).astype(f32)
    layer_out = (middle + mlp_sum).astype(bf16)

    grad_in_two, grad_down, grad_up = sum_and_grads(
        grad_two_part,
        [(by_owner(active), cotangent), (by_owner(input_two), grad_hidden)],
        2,
    )
    grad_in_two = grad_in_two.astype(f32)
    gain_two_grad = jnp.einsum("tm,td->md", onehot, grad_in_two * normed_two, precision=highest)
    grad_middle = cotangent.astype(f32) + norm_back(
        grad_in_two * gain_two, normed_two, inverse_two
    )
    grad_mid_low = grad_middle.astype(bf16)
    grad_heads = (
        jnp.einsum("td,ld->tl", grad_mid_low, out_weight, preferred_element_type=f32)
        .astype(bf16)
        .reshape(ROWS, 4, HD)
        .transpose(1, 0, 2)
    )
    packed = attention_backward(grad_heads, q_all, kv_all, o_all, lse, codes, bounds)

    packed_q = rotate_back(packed[:, :, :HD].astype(f32), cosine, sine).astype(bf16)
    packed_k = rotate_back(packed[:, :, HD : 2 * HD].astype(f32), cosine, sine).astype(bf16)
    grad_proj = (
        jnp.stack([packed_q, packed_k, packed[:, :, 2 * HD :]], axis=0)
        .transpose(2, 0, 1, 3)
        .reshape(ROWS, 3, 4 * HD)
    )
    grad_one_part = jnp.einsum(
        "tkh,dkh->td", grad_proj, qkv_weight, preferred_element_type=f32
    ).astype(bf16)
    grad_in_one, grad_qkv, grad_out = sum_and_grads(
        grad_one_part,
        [
            (by_owner(input_one), grad_proj.reshape(ROWS, 12 * HD)),
            (by_owner(returned), grad_mid_low),
        ],
        3,
    )
    grad_in_one = grad_in_one.astype(f32)
    gain_one_grad = jnp.einsum("tm,td->md", onehot, grad_in_one * normed_one, precision=highest)
    grad_input = grad_middle + norm_back(grad_in_one * gain_one, normed_one, inverse_one)
    gains_grad = jnp.concatenate([gain_one_grad, gain_two_grad], axis=0)
    gains_share = lax.psum_scatter(
        gains_grad.T.astype(bf16), "tok", scatter_dimension=0, tiled=True
    ).astype(f32)
    return (
        layer_out,
        grad_input,
        gains_share.T,
        grad_qkv.reshape(-1, 3, 4 * HD),
        grad_out,
        grad_up,
        grad_down,
    )


def solution(mesh):
    return jax.shard_map(
        per_device,
        mesh=mesh,
        in_specs=(
            P("tok", None),
            P("tok"),
            P("tok"),
            P(),
            P(None, None, "head"),
            P("head", None),
            P(None, "head"),
            P("head", None),
            P("tok", None),
        ),
        out_specs=(
            P("tok", None),
            P("tok", None),
            P(None, "tok"),
            P("tok", None, "head"),
            P(("head", "tok"), None),
            P("tok", "head"),
            P(("head", "tok"), None),
        ),
        check_vma=False,
    )
```

```python
import functools
import math

import jax
import jax.numpy as jnp
from jax import lax
from jax.experimental import pallas as pl
from jax.experimental.pallas import tpu as pltpu
from jax.sharding import PartitionSpec as P

HD = 128
SIDE = 4
ROWS = 256
CODE_ROWS = 16
CLIP_STEP = 8192
MESH = pl.DeviceIdType.MESH
NT = (((1,), (1,)), ((), ()))
TN = (((0,), (0,)), ((), ()))
NN = (((1,), (0,)), ((), ()))
f32 = jnp.float32
bf16 = jnp.bfloat16
highest = lax.Precision.HIGHEST
VMEM_LIMIT = 56 << 20
HOPS = (1, 3, 2)


def dot(lhs, rhs, dims=NN):
    return lax.dot_general(lhs, rhs, dims, preferred_element_type=f32)


def place():
    tok = lax.axis_index("tok")
    return (lax.div(tok, 8), lax.axis_index("head"), lax.rem(lax.div(tok, 2), 4), lax.rem(tok, 2))


def around(index, step):
    return lax.rem(index + (step % SIDE), SIDE)


def device(x, y, z, core):
    return (x * 8 + z * 2 + core, y)


def remote(src, dst, send_sem, recv_sem, target):
    return pltpu.make_async_remote_copy(
        src_ref=src,
        dst_ref=dst,
        send_sem=send_sem,
        recv_sem=recv_sem,
        device_id=target,
        device_id_type=MESH,
    )


def meet(targets):
    barrier = pltpu.get_barrier_semaphore()
    for target in targets:
        pl.semaphore_signal(barrier, inc=1, device_id=target, device_id_type=MESH)
    pl.semaphore_wait(barrier, len(targets))


class Copies:
    def __init__(self, send_sems, recv_sems):
        self.send_sems = send_sems
        self.recv_sems = recv_sems
        self.used = 0
        self.open = []

    def start(self, src, dst, target, landing):
        index = self.used
        self.used += 1
        copy = remote(src, dst, self.send_sems.at[index], self.recv_sems.at[index], target)
        copy.start()
        self.open.append(copy)
        return remote(landing, landing, self.send_sems.at[index], self.recv_sems.at[index], target)

    def finish(self):
        for copy in self.open:
            copy.wait_send()


def sum_over_y(copies, here, given, came, total):
    x, y, z, core = here
    arrivals = []
    for n, hop in enumerate(HOPS):
        other = around(y, hop)
        arrivals.append(
            copies.start(given.at[other], came.at[n], device(x, other, z, core), came.at[n])
        )
    yield
    for arrival in arrivals:
        arrival.wait_recv()
    total[y] = (
        (given[y].astype(f32) + came[0].astype(f32))
        + (came[1].astype(f32) + came[2].astype(f32))
    ).astype(bf16)
    arrivals = []
    for hop in HOPS:
        arrivals.append(
            copies.start(
                total.at[y],
                total.at[y],
                device(x, around(y, hop), z, core),
                total.at[around(y, -hop)],
            )
        )
    yield
    for arrival in arrivals:
        arrival.wait_recv()
    yield


def sum_scratch(width):
    quarter = ROWS // SIDE
    return [
        pltpu.VMEM((3, quarter, width), bf16),
        pltpu.VMEM((SIDE, quarter, width), bf16),
        pltpu.SemaphoreType.DMA((6,)),
        pltpu.SemaphoreType.DMA((6,)),
    ]


def ring_sum(copies, own, towards, block, slots):
    up, down = towards(1), towards(-1)
    from_down = copies.start(block(2, 0), slots.at[0], up, slots.at[0])
    from_up = copies.start(block(2, 1), slots.at[1], down, slots.at[1])
    raw_down = copies.start(block(1, 1), slots.at[2], up, slots.at[2])
    raw_up = copies.start(block(-1, 0), slots.at[3], down, slots.at[3])
    yield
    from_down.wait_recv()
    onward = block(1, 0)
    onward[...] = (onward[...].astype(f32) + slots[0].astype(f32)).astype(bf16)
    sum_down = copies.start(onward, slots.at[4], up, slots.at[4])
    from_up.wait_recv()
    onward = block(-1, 1)
    onward[...] = (onward[...].astype(f32) + slots[1].astype(f32)).astype(bf16)
    sum_up = copies.start(onward, slots.at[5], down, slots.at[5])
    yield
    for arrival in (raw_down, raw_up, sum_down, sum_up):
        arrival.wait_recv()

    def finished(half):
        mine = block(0, half)[...].astype(f32)
        if half == 0:
            return mine + slots[4].astype(f32) + slots[3].astype(f32)
        return mine + slots[2].astype(f32) + slots[5].astype(f32)

    own.append(finished)


def weight_scratch(rows, cols):
    half = cols // 4
    return [
        pltpu.VMEM((16, rows, 2 * ROWS), bf16),
        pltpu.VMEM((2 * ROWS, cols), bf16),
        pltpu.VMEM((2, 4, 2, 4 * rows, half), bf16),
        pltpu.VMEM((2, 6, 4 * rows, half), bf16),
        pltpu.VMEM((2, 2, 4, rows, half), bf16),
        pltpu.VMEM((2, 6, rows, half), bf16),
        pltpu.SemaphoreType.DMA((26,)),
        pltpu.SemaphoreType.DMA((26,)),
        pltpu.SemaphoreType.DMA((2,)),
    ]


def pick(core_at, factor, rows, group):
    row = lax.broadcasted_iota(jnp.int32, (256, 512), 0)
    col = lax.broadcasted_iota(jnp.int32, (256, 512), 1)
    wanted = lax.div(row, rows) * (2 * rows) + core_at * rows + lax.rem(row, rows)
    chosen = jnp.where(col == wanted, 1.0, 0.0).astype(bf16)
    return dot(chosen, factor[:, 512 * group : 512 * (group + 1)], NT).astype(bf16)


def weight_grad(here, left, right, out, scratch, far=None):
    both_left, both_right, parts, came, sums, late, send_sems, recv_sems, own_sems = scratch
    x, y, z, core = here
    rows, cols = out.shape
    half = cols // 4
    copies = Copies(send_sems, recv_sems)
    twin = device(x, y, z, 1 - core)
    if far is None:
        far = left.at[:, 1 - core]
        own_left = pltpu.make_async_copy(
            left.at[:, core], both_left.at[:, :, pl.ds(0, ROWS)], own_sems.at[0]
        )
        own_right = pltpu.make_async_copy(right, both_right.at[pl.ds(0, ROWS)], own_sems.at[1])
        own_left.start()
        own_right.start()
    else:
        right = both_right.at[pl.ds(0, ROWS)]
        own_left = own_right = None
    far_left = copies.start(
        far,
        both_left.at[:, :, pl.ds(ROWS, ROWS)],
        twin,
        both_left.at[:, :, pl.ds(ROWS, ROWS)],
    )
    far_right = copies.start(
        right,
        both_right.at[pl.ds(ROWS, ROWS)],
        twin,
        both_right.at[pl.ds(ROWS, ROWS)],
    )
    yield
    if own_left is not None:
        own_left.wait()
        own_right.wait()
    far_left.wait_recv()
    far_right.wait_recv()

    def spot(way, step):
        return around(x if way == 0 else z, step)

    def fill(way, step, half_index):
        at = spot(way, step)
        if way == 0:
            chosen = both_left[pl.ds(at * 4, 4)].reshape(4 * rows, 2 * ROWS)
        else:
            chosen = jnp.concatenate([both_left[k * 4 + at] for k in range(4)], axis=0)
        start = (way * 2 + half_index) * half
        parts[way, at, half_index] = dot(chosen, both_right[:, start : start + half]).astype(bf16)

    def towards(way):
        def target(step):
            if way == 0:
                return device(around(x, step), y, z, core)
            return device(x, y, around(z, step), core)

        return target

    first, first_done = [], ([], [])
    for way in (0, 1):
        for step, half_index in ((2, 0), (2, 1), (1, 1), (-1, 0)):
            fill(way, step, half_index)
        ring = ring_sum(
            copies,
            first_done[way],
            towards(way),
            lambda step, half_index, way=way: parts.at[way, spot(way, step), half_index],
            came.at[way],
        )
        next(ring)
        first.append(ring)
    for way in (0, 1):
        for step, half_index in ((1, 0), (-1, 1), (0, 0), (0, 1)):
            fill(way, step, half_index)
    yield
    for ring in first:
        next(ring)
    yield
    second, second_done = [], ([], [])
    for way in (0, 1):
        next(first[way], None)
        for half_index in (0, 1):
            sums[way, half_index] = (
                first_done[way][0](half_index).astype(bf16).reshape(4, rows, half)
            )
        ring = ring_sum(
            copies,
            second_done[way],
            towards(1 - way),
            lambda step, half_index, way=way: sums.at[way, half_index, spot(1 - way, step)],
            late.at[way],
        )
        next(ring)
        second.append(ring)
    yield
    for ring in second:
        next(ring)
    yield
    for way in (0, 1):
        next(second[way], None)
        for half_index in (0, 1):
            start = (way * 2 + half_index) * half
            out[:, start : start + half] = second_done[way][0](half_index)
    copies.finish()
    yield


def sum_gains(copies, here, given, came_x, part_x, came_z, part_z, came_core, part, came_y, out):
    x, y, z, core = here
    arrivals = [
        copies.start(
            given.at[around(x, hop)], came_x.at[n], device(around(x, hop), y, z, core), came_x.at[n]
        )
        for n, hop in enumerate(HOPS)
    ]
    yield
    for arrival in arrivals:
        arrival.wait_recv()
    part_x[...] = (given[x] + came_x[0]) + (came_x[1] + came_x[2])
    arrivals = [
        copies.start(
            part_x.at[around(z, hop)], came_z.at[n], device(x, y, around(z, hop), core), came_z.at[n]
        )
        for n, hop in enumerate(HOPS)
    ]
    yield
    for arrival in arrivals:
        arrival.wait_recv()
    part_z[...] = (part_x[z] + came_z[0]) + (came_z[1] + came_z[2])
    arrival = copies.start(part_z.at[1 - core], came_core, device(x, y, z, 1 - core), came_core)
    yield
    arrival.wait_recv()
    part[...] = part_z[core] + came_core[...]
    arrivals = [
        copies.start(part, came_y.at[n], device(x, around(y, hop), z, core), came_y.at[n])
        for n, hop in enumerate(HOPS)
    ]
    yield
    for arrival in arrivals:
        arrival.wait_recv()
    out[...] = (part[...] + came_y[0]) + (came_y[1] + came_y[2])
    yield


GAIN_SCRATCH = [(3, 4, 2, 8, HD), (4, 2, 8, HD), (3, 2, 8, HD), (2, 8, HD), (8, HD), (8, HD), (3, 8, HD)]


def sum_kernel(sum_count, shapes, with_gains, *refs):
    refs = list(refs)

    def take(count):
        taken = refs[:count]
        del refs[:count]
        return taken

    count = len(shapes)
    givens, factors, gains = take(sum_count), take(2 * count), take(int(with_gains))
    totals, outs, gains_out = take(sum_count), take(count), take(int(with_gains))
    sum_scratch = [take(4) for _ in range(sum_count)]
    scratch = [take(9) for _ in range(count)]
    here = place()
    x, y, z, core = here
    hops = HOPS if with_gains else (1, 3)
    meet(
        [device(x, around(y, hop), z, core) for hop in HOPS]
        + [device(around(x, hop), y, z, core) for hop in hops]
        + [device(x, y, around(z, hop), core) for hop in hops]
        + [device(x, y, z, 1 - core)]
    )
    over_y, y_copies = [], []
    for given, (came, all_rows, y_send, y_recv) in zip(givens, sum_scratch):
        y_copies.append(Copies(y_send, y_recv))
        over_y.append(sum_over_y(y_copies[-1], here, given, came, all_rows))
    grads = [
        weight_grad(here, factors[2 * n], factors[2 * n + 1], outs[n], scratch[n])
        for n in range(count)
    ]
    over_all = iter(())
    if with_gains:
        gain_copies = Copies(refs[-2], refs[-1])
        over_all = sum_gains(gain_copies, here, gains[0], *refs[: len(GAIN_SCRATCH)], gains_out[0])
    next(over_y[0])
    for grad in grads:
        next(grad)
    next(over_all, None)
    for grad in grads:
        next(grad)
    next(over_all, None)
    next(over_y[0])
    for later in over_y[1:]:
        next(later)
    for grad in grads:
        next(grad)
    next(over_all, None)
    for later in over_y[1:]:
        next(later)
    next(over_y[0])
    totals[0][...] = sum_scratch[0][1][...]
    for grad in grads:
        next(grad)
    next(over_all, None)
    for n in range(1, sum_count):
        next(over_y[n])
        totals[n][...] = sum_scratch[n][1][...]
    for grad in grads:
        next(grad)
    next(over_all, None)
    for grad in grads:
        next(grad)
    for copies in y_copies:
        copies.finish()
    if with_gains:
        gain_copies.finish()


def sum_and_grads(givens, factors, gains, collective_id):
    shapes = [(left.shape[2], right.shape[1]) for left, right in factors]
    width = givens[0].shape[1]
    quarter = ROWS // SIDE
    flat = [array for pair in factors for array in pair]
    whole = pl.BlockSpec(memory_space=pltpu.VMEM)
    sum_count = len(givens)
    outs = pl.pallas_call(
        functools.partial(sum_kernel, sum_count, shapes, gains is not None),
        out_shape=[jax.ShapeDtypeStruct((SIDE, quarter, width), bf16)] * sum_count
        + [jax.ShapeDtypeStruct(shape, f32) for shape in shapes]
        + ([] if gains is None else [jax.ShapeDtypeStruct((8, HD), f32)]),
        in_specs=[whole] * sum_count
        + [pl.BlockSpec(memory_space=pl.ANY)] * len(flat)
        + ([] if gains is None else [whole]),
        out_specs=[whole] * (sum_count + len(shapes) + int(gains is not None)),
        scratch_shapes=[
            pltpu.VMEM((3, quarter, width), bf16),
            pltpu.VMEM((SIDE, quarter, width), bf16),
            pltpu.SemaphoreType.DMA((6,)),
            pltpu.SemaphoreType.DMA((6,)),
        ]
        * sum_count
        + [entry for shape in shapes for entry in weight_scratch(*shape)]
        + (
            []
            if gains is None
            else [pltpu.VMEM(shape, f32) for shape in GAIN_SCRATCH]
            + [pltpu.SemaphoreType.DMA((10,)), pltpu.SemaphoreType.DMA((10,))]
        ),
        compiler_params=pltpu.CompilerParams(
            collective_id=collective_id, has_side_effects=True, vmem_limit_bytes=VMEM_LIMIT
        ),
        name=f"sum_and_grads_{collective_id}",
    )(
        *[given.reshape(SIDE, quarter, width) for given in givens],
        *flat,
        *([] if gains is None else [gains]),
    )
    return [total.reshape(ROWS, width) for total in outs[:sum_count]] + list(outs[sum_count:])


def visible(key_codes, low, span):
    return (key_codes - low).astype(jnp.uint32) <= span.astype(jnp.uint32)


def key_column(keys_values, z_at, core_at):
    codes = jnp.concatenate(
        [keys_values[z_at, core_at, n, ROWS:, :] for n in range(4)], axis=1
    )
    row = lax.broadcasted_iota(jnp.int32, (CODE_ROWS, HD), 0)
    weight = jnp.where(row == 0, 128.0, jnp.where(row == 1, 1.0, 0.0)).astype(bf16)
    return dot(codes, weight, TN).astype(jnp.int32)


def query_bounds(keys_values, z, core, bounds):
    for n in range(4):
        digits = keys_values[z, core, n, ROWS:, :].astype(f32)
        code = (digits[0:1] * 128.0 + digits[1:2]).astype(jnp.int32)
        low = jnp.where(code >= CLIP_STEP, CLIP_STEP, 0)
        bounds[0:1, n * ROWS : (n + 1) * ROWS] = low
        bounds[1:2, n * ROWS : (n + 1) * ROWS] = code - low


QUERY_TILE = 512


def forward_kernel(
    q_ref, kv_ref, out_weight_ref,
    q_all_ref, kv_all_ref, o_ref, lse_ref, returned_ref, total_ref,
    queries, keys_values, top, norm, acc, column, bounds_ref, o_low, back, given, came, all_rows,
    send_sems, recv_sems, y_send, y_recv, keep_sems,
):
    here = place()
    x, y, z, core = here
    twin = device(x, y, z, 1 - core)
    meet(
        [device(around(x, hop), y, z, core) for hop in HOPS]
        + [device(x, around(y, hop), z, core) for hop in HOPS]
        + [device(x, y, around(z, hop), core) for hop in (1, 3)]
        + [twin]
    )
    copies = Copies(send_sems, recv_sems)
    above, below = device(x, y, around(z, 1), core), device(x, y, around(z, -1), core)
    next_z, last_z, far_z = around(z, 1), around(z, -1), around(z, 2)
    kv_came, q_came = [], []
    for hop in HOPS:
        other = around(x, hop)
        target = device(other, y, z, core)
        kv_came.append(
            copies.start(
                kv_ref.at[other],
                keys_values.at[z, core, x],
                target,
                keys_values.at[z, core, around(x, -hop)],
            )
        )
    for hop in HOPS:
        other = around(x, hop)
        target = device(other, y, z, core)
        q_came.append(
            copies.start(q_ref.at[other], queries.at[x], target, queries.at[around(x, -hop)])
        )
    keys_values[z, core, x] = kv_ref[x]
    queries[x] = q_ref[x]
    top[...] = jnp.full_like(top, -1e30)
    norm[...] = jnp.zeros_like(norm)
    acc[...] = jnp.zeros_like(acc)
    pieces = [x] + [around(x, -hop) for hop in HOPS]
    from_last, from_next, from_twin = [], [], []
    for n, piece in enumerate(pieces):
        if n > 0:
            kv_came[n - 1].wait_recv()
        block = keys_values.at[z, core, piece]
        from_last.append(copies.start(block, block, above, keys_values.at[last_z, core, piece]))
        from_next.append(copies.start(block, block, below, keys_values.at[next_z, core, piece]))
        from_twin.append(copies.start(block, block, twin, keys_values.at[z, 1 - core, piece]))
    for arrival in q_came:
        arrival.wait_recv()
    query_bounds(keys_values, z, core, bounds_ref)

    def attend(z_at, core_at):
        column[...] = key_column(keys_values, z_at, core_at)

        def tile(index, carry):
            at = pl.ds(pl.multiple_of(index * QUERY_TILE, QUERY_TILE), QUERY_TILE)
            query = queries[pl.ds(index * 2, 2)].reshape(QUERY_TILE, HD)
            keys = keys_values[z_at, core_at, :, :ROWS, :HD].reshape(4 * ROWS, HD)
            values = keys_values[z_at, core_at, :, :ROWS, HD:].reshape(4 * ROWS, HD)
            scores = dot(keys, query, NT)
            codes = jnp.concatenate([column[...]] * (QUERY_TILE // HD), axis=1)
            seen = visible(codes, bounds_ref[0:1, at], bounds_ref[1:2, at])
            scores = jnp.where(seen, scores, -1e30)
            top_before = top[0:1, at]
            top_now = jnp.maximum(top_before, jnp.max(scores, axis=0, keepdims=True))
            weights = jnp.exp2(scores - top_now)
            shrink = jnp.exp2(top_before - top_now)
            norm[0:1, at] = norm[0:1, at] * shrink + jnp.sum(weights, axis=0, keepdims=True)
            top[0:1, at] = top_now
            acc[:, at] = acc[:, at] * shrink + dot(values, weights.astype(bf16), TN)
            return carry

        lax.fori_loop(0, 4 * ROWS // QUERY_TILE, tile, 0)

    low_far, high_far, twin_last, twin_next = [], [], [], []

    def onward(n):
        piece = pieces[n]
        from_last[n].wait_recv()
        block = keys_values.at[last_z, core, piece]
        low = block.at[pl.ds(0, ROWS // 2)]
        low_far.append(
            copies.start(low, low, above, keys_values.at[far_z, core, piece, pl.ds(0, ROWS // 2)])
        )
        twin_last.append(
            copies.start(block, block, twin, keys_values.at[last_z, 1 - core, piece])
        )
        from_next[n].wait_recv()
        block = keys_values.at[next_z, core, piece]
        high = block.at[pl.ds(ROWS // 2, ROWS // 2 + CODE_ROWS)]
        high_far.append(
            copies.start(
                high,
                high,
                below,
                keys_values.at[far_z, core, piece, pl.ds(ROWS // 2, ROWS // 2 + CODE_ROWS)],
            )
        )
        twin_next.append(
            copies.start(block, block, twin, keys_values.at[next_z, 1 - core, piece])
        )

    def take(arrivals):
        for arrival in arrivals:
            arrival.wait_recv()

    attend(z, core)
    onward(0)
    onward(1)
    take(from_twin)
    attend(z, 1 - core)
    onward(2)
    onward(3)
    attend(last_z, core)
    attend(next_z, core)
    take(twin_last)
    attend(last_z, 1 - core)
    take(twin_next)
    attend(next_z, 1 - core)
    twin_far = []
    for n, piece in enumerate(pieces):
        low_far[n].wait_recv()
        high_far[n].wait_recv()
        block = keys_values.at[far_z, core, piece]
        twin_far.append(copies.start(block, block, twin, keys_values.at[far_z, 1 - core, piece]))
    attend(far_z, core)
    take(twin_far)
    keep = pltpu.make_async_copy(keys_values, kv_all_ref, keep_sems.at[0])
    keep.start()
    attend(far_z, 1 - core)

    total_norm = norm[0:1, :]
    attended = (acc[...] / total_norm).T
    o_ref[...] = attended
    o_low[...] = attended.astype(bf16).reshape(4, ROWS, HD)
    lse_ref[...] = jnp.broadcast_to(top[0:1, :] + jnp.log2(total_norm), lse_ref.shape)
    q_all_ref[...] = queries[...]
    came_back = []
    for hop in HOPS:
        other = around(x, hop)
        came_back.append(
            copies.start(
                o_low.at[other],
                back.at[x],
                device(other, y, z, core),
                back.at[around(x, -hop)],
            )
        )
    back[x] = o_low[x]
    take(came_back)
    returned = jnp.concatenate([back[n] for n in range(4)], axis=1)
    returned_ref[...] = returned
    given[...] = dot(returned, out_weight_ref[...]).astype(bf16).reshape(given.shape)
    y_copies = Copies(y_send, y_recv)
    for step in sum_over_y(y_copies, here, given, came, all_rows):
        pass
    total_ref[...] = all_rows[...]
    copies.finish()
    y_copies.finish()
    keep.wait()


def attention_forward(q_heads, kv_heads, out_weight):
    quarter = ROWS // SIDE
    width = out_weight.shape[1]
    whole = pl.BlockSpec(memory_space=pltpu.VMEM)
    count = 3 + 3 + 12 + 16 + 4 + 3
    outs = pl.pallas_call(
        forward_kernel,
        out_shape=[
            jax.ShapeDtypeStruct((4, ROWS, HD), bf16),
            jax.ShapeDtypeStruct((4, 2, 4, ROWS + CODE_ROWS, 2 * HD), bf16),
            jax.ShapeDtypeStruct((4 * ROWS, HD), f32),
            jax.ShapeDtypeStruct((8, 4 * ROWS), f32),
            jax.ShapeDtypeStruct((ROWS, 4 * HD), bf16),
            jax.ShapeDtypeStruct((SIDE, quarter, width), bf16),
        ],
        in_specs=[whole] * 3,
        out_specs=[whole, pl.BlockSpec(memory_space=pl.ANY)] + [whole] * 4,
        scratch_shapes=[
            pltpu.VMEM((4, ROWS, HD), bf16),
            pltpu.VMEM((4, 2, 4, ROWS + CODE_ROWS, 2 * HD), bf16),
            pltpu.VMEM((8, 4 * ROWS), f32),
            pltpu.VMEM((8, 4 * ROWS), f32),
            pltpu.VMEM((HD, 4 * ROWS), f32),
            pltpu.VMEM((4 * ROWS, HD), jnp.int32),
            pltpu.VMEM((8, 4 * ROWS), jnp.int32),
            pltpu.VMEM((4, ROWS, HD), bf16),
            pltpu.VMEM((4, ROWS, HD), bf16),
            pltpu.VMEM((SIDE, quarter, width), bf16),
            pltpu.VMEM((3, quarter, width), bf16),
            pltpu.VMEM((SIDE, quarter, width), bf16),
            pltpu.SemaphoreType.DMA((count,)),
            pltpu.SemaphoreType.DMA((count,)),
            pltpu.SemaphoreType.DMA((6,)),
            pltpu.SemaphoreType.DMA((6,)),
            pltpu.SemaphoreType.DMA((1,)),
        ],
        compiler_params=pltpu.CompilerParams(
            collective_id=0, has_side_effects=True, vmem_limit_bytes=VMEM_LIMIT
        ),
        name="attention_forward",
    )(q_heads, kv_heads, out_weight)
    return list(outs[:5]) + [outs[5].reshape(ROWS, width)]


NORM_ROWS = 32
WIDE = 512


def gain_rows(labels, gains, first):
    return jnp.where(
        labels == 0,
        gains[first : first + 1, :],
        jnp.where(labels == 1, gains[first + 1 : first + 2, :], gains[first + 2 : first + 3, :]),
    )


def gelu_and_slope(hidden):
    scale = math.sqrt(2.0 / math.pi)
    square = hidden * hidden
    bent = jnp.tanh(scale * hidden * (1.0 + 0.044715 * square))
    half = 0.5 * (1.0 + bent)
    slope = half + 0.5 * hidden * (1.0 - bent * bent) * (scale * (1.0 + 3 * 0.044715 * square))
    return hidden * half, slope


def steps(count, body):
    lax.fori_loop(0, count, lambda index, carry: (body(index), carry)[1], 0)


def slab(index, size):
    return pl.ds(pl.multiple_of(index * size, size), size)


def middle_kernel(
    x_ref, attn_ref, labels_ref, gains_ref, cotangent_ref, out_weight_ref, up_hbm, down_hbm,
    g_mid_ref, g_low_ref, heads_ref, mlp_ref, active_left_ref, gains_out_ref, weight_ref,
    up, down, xhat, inverse, normed, active, far, given, came, all_rows, y_send, y_recv, load_sems,
    *weight_scratch_refs,
):
    here = place()
    x, y, z, core = here
    load_up = pltpu.make_async_copy(up_hbm, up, load_sems.at[0])
    load_down = pltpu.make_async_copy(down_hbm, down, load_sems.at[1])
    load_up.start()
    load_down.start()
    both_left, both_right = weight_scratch_refs[:2]
    width = x_ref.shape[1]
    hidden_width = up.shape[1]

    def norm(index):
        at = slab(index, NORM_ROWS)
        middle = x_ref[at, :].astype(f32) + attn_ref[at, :].astype(f32)
        centred = middle - jnp.mean(middle, axis=-1, keepdims=True)
        scale = lax.rsqrt(jnp.mean(centred * centred, axis=-1, keepdims=True) + 1e-05)
        unit = centred * scale
        xhat[at, :] = unit
        inverse[at, :] = jnp.broadcast_to(scale, (NORM_ROWS, HD))
        normed[at, :] = (unit * gain_rows(labels_ref[at, :1], gains_ref, 3)).astype(bf16)

    steps(ROWS // NORM_ROWS, norm)
    load_up.wait()
    load_down.wait()

    def feed(index):
        at = slab(index, WIDE)
        hidden = dot(normed[...], up[:, at])
        grad_active = dot(cotangent_ref[...], down[at, :], NT)
        value, slope = gelu_and_slope(hidden)
        active[:, at] = value.astype(bf16)
        both_right[pl.ds(0, ROWS), at] = (grad_active * slope).astype(bf16)

    steps(hidden_width // WIDE, feed)

    def back_up(index):
        at = slab(index, WIDE)
        part = dot(both_right[pl.ds(0, ROWS), :], up[at, :], NT)
        given[:, :, at] = part.astype(bf16).reshape(SIDE, ROWS // SIDE, WIDE)

    steps(width // WIDE, back_up)
    meet(
        [device(x, around(y, hop), z, core) for hop in HOPS]
        + [device(around(x, hop), y, z, core) for hop in (1, 3)]
        + [device(x, y, around(z, hop), core) for hop in (1, 3)]
        + [device(x, y, z, 1 - core)]
    )
    copies = Copies(y_send, y_recv)
    over_y = sum_over_y(copies, here, given, came, all_rows)
    next(over_y)
    rows = weight_ref.shape[0]
    for group in range(4):
        at = pl.ds(4 * group, 4)
        both_left[at, :, pl.ds(0, ROWS)] = pick(core, normed, rows, group).reshape(4, rows, ROWS)
        far[at] = pick(1 - core, normed, rows, group).reshape(4, rows, ROWS)
    ring = weight_grad(here, None, None, weight_ref, weight_scratch_refs, far)
    next(ring)

    def mlp(index):
        at = slab(index, WIDE)
        mlp_ref[:, :, at] = (
            dot(active[...], down[:, at]).astype(bf16).reshape(SIDE, ROWS // SIDE, WIDE)
        )

    steps(width // WIDE, mlp)
    next(ring)
    for group in range(4):
        for core_at in range(2):
            active_left_ref[pl.ds(4 * group, 4), core_at] = pick(
                core_at, active, rows, group
            ).reshape(4, rows, ROWS)
    next(over_y)
    next(ring)
    next(over_y)
    gains_out_ref[...] = jnp.zeros_like(gains_out_ref)

    def back(index):
        at = slab(index, NORM_ROWS)
        part = lax.div(index, SIDE // 2)
        start = pl.multiple_of(lax.rem(index, SIDE // 2) * NORM_ROWS, NORM_ROWS)
        grad = all_rows[part, pl.ds(start, NORM_ROWS), :].astype(f32)
        labels = labels_ref[at, :1]
        unit = xhat[at, :]
        product = grad * unit
        for mode in range(3):
            gains_out_ref[mode : mode + 1, :] += jnp.sum(
                jnp.where(labels == mode, product, 0.0), axis=0, keepdims=True
            )
        gain = gain_rows(labels, gains_ref, 3)
        grad = grad * gain
        mean = jnp.mean(grad, axis=-1, keepdims=True)
        along = jnp.mean(product * gain, axis=-1, keepdims=True)
        g_mid = cotangent_ref[at, :].astype(f32) + inverse[at, :1] * (grad - mean - unit * along)
        g_mid_ref[at, :] = g_mid
        g_low_ref[at, :] = g_mid.astype(bf16)

    steps(ROWS // NORM_ROWS, back)
    g_heads = dot(g_low_ref[...], out_weight_ref[...], NT).astype(bf16)
    for head in range(4):
        heads_ref[head] = g_heads[:, head * HD : (head + 1) * HD]
    next(ring)
    next(ring)
    next(ring)
    copies.finish()


def middle(activations, attn_sum, labels, gains, cotangent, out_weight, up_weight, down_weight):
    width, hidden_width = up_weight.shape
    rows = width // 32
    quarter = ROWS // SIDE
    whole = pl.BlockSpec(memory_space=pltpu.VMEM)
    anywhere = pl.BlockSpec(memory_space=pl.ANY)
    return pl.pallas_call(
        middle_kernel,
        out_shape=[
            jax.ShapeDtypeStruct((ROWS, width), f32),
            jax.ShapeDtypeStruct((ROWS, width), bf16),
            jax.ShapeDtypeStruct((4, ROWS, HD), bf16),
            jax.ShapeDtypeStruct((SIDE, quarter, width), bf16),
            jax.ShapeDtypeStruct((16, 2, hidden_width // 32, ROWS), bf16),
            jax.ShapeDtypeStruct((8, width), f32),
            jax.ShapeDtypeStruct((rows, hidden_width), f32),
        ],
        in_specs=[whole] * 6 + [anywhere] * 2,
        out_specs=[whole] * 7,
        scratch_shapes=[
            pltpu.VMEM(up_weight.shape, bf16),
            pltpu.VMEM(down_weight.shape, bf16),
            pltpu.VMEM((ROWS, width), f32),
            pltpu.VMEM((ROWS, HD), f32),
            pltpu.VMEM((ROWS, width), bf16),
            pltpu.VMEM((ROWS, hidden_width), bf16),
            pltpu.VMEM((16, rows, ROWS), bf16),
            pltpu.VMEM((SIDE, quarter, width), bf16),
        ]
        + sum_scratch(width)
        + [pltpu.SemaphoreType.DMA((2,))]
        + weight_scratch(rows, hidden_width),
        compiler_params=pltpu.CompilerParams(
            collective_id=2, has_side_effects=True, vmem_limit_bytes=VMEM_LIMIT
        ),
        name="middle",
    )(activations, attn_sum, labels, gains, cotangent, out_weight, up_weight, down_weight)


BACK_TILE = 256


def backward_kernel(
    grad_ref, q_ref, kv_hbm, o_ref, lse_ref, left_ref, right_ref, given_ref,
    packed_ref, weight_ref, total_ref,
    keys_values, grads, delta, grad_q, grad_k, grad_v, column, bounds_ref, parts, met, came, sums, q_low, back_q,
    back_kv, send_sems, recv_sems, load_sems, y_came, all_rows, y_send, y_recv, *weight_scratch_refs,
):
    here = place()
    x, y, z, core = here
    twin = device(x, y, z, 1 - core)
    load = pltpu.make_async_copy(kv_hbm, keys_values, load_sems.at[0])
    load.start()
    meet(
        [device(around(x, hop), y, z, core) for hop in HOPS]
        + [device(x, around(y, hop), z, core) for hop in HOPS]
        + [device(x, y, around(z, hop), core) for hop in (1, 3)]
        + [twin]
    )
    copies = Copies(send_sems, recv_sems)
    y_copies = Copies(y_send, y_recv)
    over_y = sum_over_y(y_copies, here, given_ref, y_came, all_rows)
    arrivals = []
    for hop in HOPS:
        other = around(x, hop)
        arrivals.append(
            copies.start(
                grad_ref.at[other],
                grads.at[x],
                device(other, y, z, core),
                grads.at[around(x, -hop)],
            )
        )
    ring = weight_grad(here, left_ref, right_ref, weight_ref, weight_scratch_refs)
    next(ring)
    grads[x] = grad_ref[x]
    grad_q[...] = jnp.zeros_like(grad_q)
    load.wait()
    query_bounds(keys_values, z, core, bounds_ref)
    next(over_y)
    next(ring)
    for arrival in arrivals:
        arrival.wait_recv()
    product = grads[...].reshape(4 * ROWS, HD).astype(f32) * o_ref[...]
    delta[...] = lax.dot_general(
        jnp.ones((8, HD), f32), product, NT, preferred_element_type=f32, precision=highest
    )

    def chunk(z_at, core_at):
        column[...] = key_column(keys_values, z_at, core_at)
        grad_k[...] = jnp.zeros_like(grad_k)
        grad_v[...] = jnp.zeros_like(grad_v)

        def tile(index, carry):
            at = pl.ds(pl.multiple_of(index * BACK_TILE, BACK_TILE), BACK_TILE)
            query = q_ref[index]
            grad = grads[index]
            keys = keys_values[z_at, core_at, :, :ROWS, :HD].reshape(4 * ROWS, HD)
            values = keys_values[z_at, core_at, :, :ROWS, HD:].reshape(4 * ROWS, HD)
            scores = dot(keys, query, NT)
            codes = jnp.concatenate([column[...]] * (BACK_TILE // HD), axis=1)
            seen = visible(codes, bounds_ref[0:1, at], bounds_ref[1:2, at])
            weights = jnp.where(seen, jnp.exp2(scores - lse_ref[0:1, at]), 0.0)
            grad_weights = dot(values, grad, NT)
            grad_scores = (weights * (grad_weights - delta[0:1, at])).astype(bf16)
            grad_v[...] += dot(weights.astype(bf16), grad)
            grad_k[...] += dot(grad_scores, query)
            grad_q[:, at] += dot(keys, grad_scores, TN)
            return carry

        lax.fori_loop(0, 4 * ROWS // BACK_TILE, tile, 0)
        parts[z_at, core_at] = jnp.concatenate(
            [grad_k[...] * math.log(2.0), grad_v[...]], axis=1
        ).astype(bf16).reshape(2, 2 * ROWS, 2 * HD)

    def hand_over(z_at):
        return copies.start(
            parts.at[z_at, 1 - core], met.at[z_at], twin, met.at[z_at]
        )

    def join(z_at):
        parts[z_at, core] = (
            parts[z_at, core].astype(f32) + met[z_at].astype(f32)
        ).astype(bf16)

    next_z, last_z, far_z = around(z, 1), around(z, -1), around(z, 2)
    above, below = device(x, y, next_z, core), device(x, y, last_z, core)
    chunk(far_z, 1 - core)
    far_met = hand_over(far_z)
    chunk(far_z, core)
    chunk(next_z, 1 - core)
    next_met = hand_over(next_z)
    next(ring)
    next(over_y)
    far_met.wait_recv()
    join(far_z)
    from_last = copies.start(parts.at[far_z, core, 0], came.at[0], above, came.at[0])
    from_next = copies.start(parts.at[far_z, core, 1], came.at[1], below, came.at[1])
    chunk(next_z, core)
    chunk(last_z, 1 - core)
    last_met = hand_over(last_z)
    next(ring)
    next_met.wait_recv()
    join(next_z)
    raw_last = copies.start(parts.at[next_z, core, 1], came.at[2], above, came.at[2])
    chunk(last_z, core)
    chunk(z, 1 - core)
    own_met = hand_over(z)
    next(ring)
    next(over_y)
    total_ref[...] = all_rows[...]
    last_met.wait_recv()
    join(last_z)
    raw_next = copies.start(parts.at[last_z, core, 0], came.at[3], below, came.at[3])
    from_last.wait_recv()
    parts[next_z, core, 0] = (
        parts[next_z, core, 0].astype(f32) + came[0].astype(f32)
    ).astype(bf16)
    sum_last = copies.start(parts.at[next_z, core, 0], came.at[4], above, came.at[4])
    from_next.wait_recv()
    parts[last_z, core, 1] = (
        parts[last_z, core, 1].astype(f32) + came[1].astype(f32)
    ).astype(bf16)
    sum_next = copies.start(parts.at[last_z, core, 1], came.at[5], below, came.at[5])
    chunk(z, core)
    q_low[...] = (grad_q[...] * (HD**-0.5)).T.astype(bf16).reshape(4, ROWS, HD)
    arrivals = []
    for hop in HOPS:
        other = around(x, hop)
        arrivals.append(
            copies.start(
                q_low.at[other],
                back_q.at[x],
                device(other, y, z, core),
                back_q.at[around(x, -hop)],
            )
        )
    back_q[x] = q_low[x]
    next(ring)
    own_met.wait_recv()
    raw_last.wait_recv()
    raw_next.wait_recv()
    sum_last.wait_recv()
    sum_next.wait_recv()
    mine = parts[z, core].astype(f32) + met[z].astype(f32)
    low = mine[0] + came[4].astype(f32) + came[3].astype(f32)
    high = mine[1] + came[2].astype(f32) + came[5].astype(f32)
    sums[0:2] = low.astype(bf16).reshape(2, ROWS, 2 * HD)
    sums[2:4] = high.astype(bf16).reshape(2, ROWS, 2 * HD)
    for hop in HOPS:
        other = around(x, hop)
        arrivals.append(
            copies.start(
                sums.at[other],
                back_kv.at[x],
                device(other, y, z, core),
                back_kv.at[around(x, -hop)],
            )
        )
    back_kv[x] = sums[x]
    for arrival in arrivals:
        arrival.wait_recv()
    for n in range(4):
        packed_ref[n, :, :HD] = back_q[n]
        packed_ref[n, :, HD:] = back_kv[n]
    copies.finish()
    y_copies.finish()


def attention_backward(grad_heads, q_all, kv_all, o_all, lse, left, right, given):
    whole = pl.BlockSpec(memory_space=pltpu.VMEM)
    anywhere = pl.BlockSpec(memory_space=pl.ANY)
    count = 3 + 4 + 6 + 6
    return pl.pallas_call(
        backward_kernel,
        out_shape=[
            jax.ShapeDtypeStruct((4, ROWS, 3 * HD), bf16),
            jax.ShapeDtypeStruct((left.shape[2], right.shape[1]), f32),
            jax.ShapeDtypeStruct(given.shape, bf16),
        ],
        in_specs=[whole, whole, anywhere, whole, whole, anywhere, anywhere, whole],
        out_specs=[whole, whole, whole],
        scratch_shapes=[
            pltpu.VMEM((4, 2, 4, ROWS + CODE_ROWS, 2 * HD), bf16),
            pltpu.VMEM((4, ROWS, HD), bf16),
            pltpu.VMEM((8, 4 * ROWS), f32),
            pltpu.VMEM((HD, 4 * ROWS), f32),
            pltpu.VMEM((4 * ROWS, HD), f32),
            pltpu.VMEM((4 * ROWS, HD), f32),
            pltpu.VMEM((4 * ROWS, HD), jnp.int32),
            pltpu.VMEM((8, 4 * ROWS), jnp.int32),
            pltpu.VMEM((4, 2, 2, 2 * ROWS, 2 * HD), bf16),
            pltpu.VMEM((4, 2, 2 * ROWS, 2 * HD), bf16),
            pltpu.VMEM((6, 2 * ROWS, 2 * HD), bf16),
            pltpu.VMEM((4, ROWS, 2 * HD), bf16),
            pltpu.VMEM((4, ROWS, HD), bf16),
            pltpu.VMEM((4, ROWS, HD), bf16),
            pltpu.VMEM((4, ROWS, 2 * HD), bf16),
            pltpu.SemaphoreType.DMA((count,)),
            pltpu.SemaphoreType.DMA((count,)),
            pltpu.SemaphoreType.DMA((1,)),
        ]
        + sum_scratch(given.shape[2])
        + weight_scratch(left.shape[2], right.shape[1]),
        compiler_params=pltpu.CompilerParams(
            collective_id=1, has_side_effects=True, vmem_limit_bytes=VMEM_LIMIT
        ),
        name="attention_backward",
    )(grad_heads, q_all, kv_all, o_all, lse, left, right, given)


def layer_norm(values_in):
    row_mean = jnp.mean(values_in, axis=-1, keepdims=True)
    centred = values_in - row_mean
    inverse = lax.rsqrt(jnp.mean(centred * centred, axis=-1, keepdims=True) + 1e-05)
    return (centred * inverse, inverse)


def norm_back(grad_in, normed, inverse):
    return inverse * (
        grad_in
        - jnp.mean(grad_in, axis=-1, keepdims=True)
        - normed * jnp.mean(grad_in * normed, axis=-1, keepdims=True)
    )


def tables(place_now, head_dim):
    half_dim = head_dim // 2
    frequency = jnp.exp(
        jnp.arange(half_dim, dtype=jnp.float32) * (-2.0 * math.log(10000.0) / head_dim)
    )
    angles = place_now.astype(jnp.float32)[:, None] * frequency[None, :]
    angles = jnp.concatenate([angles, angles], axis=-1)
    return (jnp.cos(angles), jnp.sin(angles))


def rotate(values_in, cosine, sine):
    half_dim = values_in.shape[-1] // 2
    turned = jnp.concatenate([-values_in[..., half_dim:], values_in[..., :half_dim]], axis=-1)
    return values_in * cosine + turned * sine


def rotate_back(grad_in, cosine, sine):
    half_dim = grad_in.shape[-1] // 2
    scaled = grad_in * sine
    return grad_in * cosine + jnp.concatenate(
        [scaled[..., half_dim:], -scaled[..., :half_dim]], axis=-1
    )


def by_owner(factor):
    return factor.T.reshape(16, 2, factor.shape[1] // 32, ROWS)


def per_device(
    activations,
    labels,
    position,
    norm_gains,
    qkv_weight,
    out_weight,
    up_weight,
    down_weight,
    cotangent,
):
    mode_count = norm_gains.shape[0] // 2
    block, row = position // 256, position % 256
    second = (row >= 192).astype(jnp.int32)
    spot = jnp.where(second == 1, block * 64 + row - 192, block * 192 + row)
    code = spot + second * CLIP_STEP
    digits = jnp.stack([code // 128, code % 128], axis=0)
    digits = jnp.concatenate(
        [digits, jnp.zeros((CODE_ROWS - 2, ROWS), jnp.int32)], axis=0
    ).astype(bf16)

    residual = activations.astype(f32)
    onehot = (labels[:, None] == jnp.arange(mode_count, dtype=jnp.int32)[None, :]).astype(f32)
    gain_one = jnp.dot(onehot, norm_gains[:mode_count], precision=highest)
    normed_one, inverse_one = layer_norm(residual)
    input_one = (normed_one * gain_one).astype(bf16)
    cosine, sine = tables(spot, HD)
    projected = jnp.einsum("td,dkh->kth", input_one, qkv_weight, preferred_element_type=f32)
    projected = projected.reshape(3, ROWS, 4, HD).transpose(0, 2, 1, 3)
    q_heads = (rotate(projected[0], cosine, sine) * (HD**-0.5 / math.log(2.0))).astype(bf16)
    kv_heads = jnp.concatenate([rotate(projected[1], cosine, sine), projected[2]], axis=-1).astype(
        bf16
    )
    kv_heads = jnp.concatenate(
        [kv_heads, jnp.broadcast_to(digits[None], (4, CODE_ROWS, ROWS))], axis=1
    )
    q_all, kv_all, o_all, lse, returned, attn_sum = attention_forward(
        q_heads, kv_heads, out_weight
    )

    label_rows = jnp.broadcast_to(labels[:, None], (ROWS, HD))
    gain_table = jnp.pad(norm_gains, ((0, 8 - 2 * mode_count), (0, 0)))
    grad_middle, grad_mid_low, grad_heads, mlp_part, active_left, gain_two_grad, grad_up = middle(
        activations, attn_sum, label_rows, gain_table, cotangent, out_weight, up_weight, down_weight
    )
    packed, grad_down, mlp_sum = attention_backward(
        grad_heads, q_all, kv_all, o_all, lse, active_left, cotangent, mlp_part
    )
    layer_out = (
        residual + attn_sum.astype(f32) + mlp_sum.reshape(ROWS, -1).astype(f32)
    ).astype(bf16)

    packed_q = rotate_back(packed[:, :, :HD].astype(f32), cosine, sine).astype(bf16)
    packed_k = rotate_back(packed[:, :, HD : 2 * HD].astype(f32), cosine, sine).astype(bf16)
    grad_proj = (
        jnp.stack([packed_q, packed_k, packed[:, :, 2 * HD :]], axis=0)
        .transpose(2, 0, 1, 3)
        .reshape(ROWS, 3, 4 * HD)
    )
    grad_one_part = jnp.einsum("tkh,dkh->td", grad_proj, qkv_weight, preferred_element_type=f32)
    gains_part = jnp.concatenate(
        [
            jnp.einsum("tm,td->md", onehot, grad_one_part * normed_one, precision=highest),
            0.25 * gain_two_grad[:mode_count],
        ],
        axis=0,
    )
    gains_part = gains_part.reshape(2 * mode_count, 32, 64).transpose(1, 0, 2)
    gains_part = jnp.pad(gains_part, ((0, 0), (0, 8 - 2 * mode_count), (0, HD - 64)))
    grad_in_one, grad_qkv, grad_out, gains_share = sum_and_grads(
        [grad_one_part.astype(bf16)],
        [
            (by_owner(input_one), grad_proj.reshape(ROWS, 12 * HD)),
            (by_owner(returned), grad_mid_low),
        ],
        gains_part.reshape(4, 4, 2, 8, HD),
        3,
    )
    grad_in_one = grad_in_one.astype(f32)
    grad_input = grad_middle + norm_back(grad_in_one * gain_one, normed_one, inverse_one)
    return (
        layer_out,
        grad_input,
        gains_share[: 2 * mode_count, :64],
        grad_qkv.reshape(-1, 3, 4 * HD),
        grad_out,
        grad_up,
        grad_down,
    )


def solution(mesh):
    return jax.shard_map(
        per_device,
        mesh=mesh,
        in_specs=(
            P("tok", None),
            P("tok"),
            P("tok"),
            P(),
            P(None, None, "head"),
            P("head", None),
            P(None, "head"),
            P("head", None),
            P("tok", None),
        ),
        out_specs=(
            P("tok", None),
            P("tok", None),
            P(None, "tok"),
            P("tok", None, "head"),
            P(("head", "tok"), None),
            P("tok", "head"),
            P(("head", "tok"), None),
        ),
        check_vma=False,
    )
```

```python
import functools
import math

import jax
import jax.numpy as jnp
from jax import lax
from jax.experimental import pallas as pl
from jax.experimental.pallas import tpu as pltpu
from jax.sharding import PartitionSpec as P

HD = 128
SIDE = 4
ROWS = 256
CODE_ROWS = 16
CLIP_STEP = 8192
MESH = pl.DeviceIdType.MESH
NT = (((1,), (1,)), ((), ()))
TN = (((0,), (0,)), ((), ()))
NN = (((1,), (0,)), ((), ()))
f32 = jnp.float32
bf16 = jnp.bfloat16
highest = lax.Precision.HIGHEST
VMEM_LIMIT = 56 << 20
HOPS = (1, 3, 2)


def dot(lhs, rhs, dims=NN):
    return lax.dot_general(lhs, rhs, dims, preferred_element_type=f32)


def place():
    tok = lax.axis_index("tok")
    return (lax.div(tok, 8), lax.axis_index("head"), lax.rem(lax.div(tok, 2), 4), lax.rem(tok, 2))


def around(index, step):
    return lax.rem(index + (step % SIDE), SIDE)


def device(x, y, z, core):
    return (x * 8 + z * 2 + core, y)


def remote(src, dst, send_sem, recv_sem, target):
    return pltpu.make_async_remote_copy(
        src_ref=src,
        dst_ref=dst,
        send_sem=send_sem,
        recv_sem=recv_sem,
        device_id=target,
        device_id_type=MESH,
    )


def greet(targets):
    barrier = pltpu.get_barrier_semaphore()
    for target in targets:
        pl.semaphore_signal(barrier, inc=1, device_id=target, device_id_type=MESH)
    return lambda: pl.semaphore_wait(barrier, len(targets))


class Copies:
    def __init__(self, send_sems, recv_sems):
        self.send_sems = send_sems
        self.recv_sems = recv_sems
        self.used = 0
        self.open = []

    def start(self, src, dst, target, landing):
        index = self.used
        self.used += 1
        copy = remote(src, dst, self.send_sems.at[index], self.recv_sems.at[index], target)
        copy.start()
        self.open.append(copy)
        return remote(landing, landing, self.send_sems.at[index], self.recv_sems.at[index], target)

    def finish(self):
        for copy in self.open:
            copy.wait_send()


def sum_over_y(copies, here, given, came, total):
    x, y, z, core = here
    arrivals = []
    for n, hop in enumerate(HOPS):
        other = around(y, hop)
        arrivals.append(
            copies.start(given.at[other], came.at[n], device(x, other, z, core), came.at[n])
        )
    yield
    for arrival in arrivals:
        arrival.wait_recv()
    total[y] = (
        (given[y].astype(f32) + came[0].astype(f32))
        + (came[1].astype(f32) + came[2].astype(f32))
    ).astype(bf16)
    arrivals = []
    for hop in HOPS:
        arrivals.append(
            copies.start(
                total.at[y],
                total.at[y],
                device(x, around(y, hop), z, core),
                total.at[around(y, -hop)],
            )
        )
    yield
    for arrival in arrivals:
        arrival.wait_recv()
    yield


def sum_scratch(width):
    quarter = ROWS // SIDE
    return [
        pltpu.VMEM((3, quarter, width), bf16),
        pltpu.VMEM((SIDE, quarter, width), bf16),
        pltpu.SemaphoreType.DMA((6,)),
        pltpu.SemaphoreType.DMA((6,)),
    ]


def ring_sum(copies, own, towards, block, slots):
    up, down = towards(1), towards(-1)
    from_down = copies.start(block(2, 0), slots.at[0], up, slots.at[0])
    from_up = copies.start(block(2, 1), slots.at[1], down, slots.at[1])
    raw_down = copies.start(block(1, 1), slots.at[2], up, slots.at[2])
    raw_up = copies.start(block(-1, 0), slots.at[3], down, slots.at[3])
    yield
    from_down.wait_recv()
    onward = block(1, 0)
    onward[...] = (onward[...].astype(f32) + slots[0].astype(f32)).astype(bf16)
    sum_down = copies.start(onward, slots.at[4], up, slots.at[4])
    from_up.wait_recv()
    onward = block(-1, 1)
    onward[...] = (onward[...].astype(f32) + slots[1].astype(f32)).astype(bf16)
    sum_up = copies.start(onward, slots.at[5], down, slots.at[5])
    yield
    for arrival in (raw_down, raw_up, sum_down, sum_up):
        arrival.wait_recv()

    def finished(half):
        mine = block(0, half)[...].astype(f32)
        if half == 0:
            return mine + slots[4].astype(f32) + slots[3].astype(f32)
        return mine + slots[2].astype(f32) + slots[5].astype(f32)

    own.append(finished)


def weight_scratch(rows, cols):
    half = cols // 4
    return [
        pltpu.VMEM((16, rows, 2 * ROWS), bf16),
        pltpu.VMEM((2 * ROWS, cols), bf16),
        pltpu.VMEM((2, 4, 2, 4 * rows, half), bf16),
        pltpu.VMEM((2, 6, 4 * rows, half), bf16),
        pltpu.VMEM((2, 2, 4, rows, half), bf16),
        pltpu.VMEM((2, 6, rows, half), bf16),
        pltpu.SemaphoreType.DMA((26,)),
        pltpu.SemaphoreType.DMA((26,)),
        pltpu.SemaphoreType.DMA((2,)),
    ]


def store_columns(out, start, value):
    if len(out.shape) == 2:
        out[:, start : start + value.shape[1]] = value
        return
    size, done = out.shape[2], 0
    while done < value.shape[1]:
        block, offset = divmod(start + done, size)
        count = min(size - offset, value.shape[1] - done)
        out[block, :, offset : offset + count] = value[:, done : done + count]
        done += count


def pick(core_at, factor, rows, group):
    row = lax.broadcasted_iota(jnp.int32, (256, 512), 0)
    col = lax.broadcasted_iota(jnp.int32, (256, 512), 1)
    wanted = lax.div(row, rows) * (2 * rows) + core_at * rows + lax.rem(row, rows)
    chosen = jnp.where(col == wanted, 1.0, 0.0).astype(bf16)
    return dot(chosen, factor[:, 512 * group : 512 * (group + 1)], NT).astype(bf16)


def weight_grad(here, left, right, out, scratch, far=None):
    both_left, both_right, parts, came, sums, late, send_sems, recv_sems, own_sems = scratch
    x, y, z, core = here
    rows, cols = both_left.shape[1], both_right.shape[1]
    half = cols // 4
    copies = Copies(send_sems, recv_sems)
    twin = device(x, y, z, 1 - core)
    if far is None:
        far = left.at[:, 1 - core]
        own_left = pltpu.make_async_copy(
            left.at[:, core], both_left.at[:, :, pl.ds(0, ROWS)], own_sems.at[0]
        )
        own_right = pltpu.make_async_copy(right, both_right.at[pl.ds(0, ROWS)], own_sems.at[1])
        own_left.start()
        own_right.start()
    else:
        right = both_right.at[pl.ds(0, ROWS)]
        own_left = own_right = None
    far_left = copies.start(
        far,
        both_left.at[:, :, pl.ds(ROWS, ROWS)],
        twin,
        both_left.at[:, :, pl.ds(ROWS, ROWS)],
    )
    far_right = copies.start(
        right,
        both_right.at[pl.ds(ROWS, ROWS)],
        twin,
        both_right.at[pl.ds(ROWS, ROWS)],
    )
    yield
    if own_left is not None:
        own_left.wait()
        own_right.wait()
    far_left.wait_recv()
    far_right.wait_recv()

    def spot(way, step):
        return around(x if way == 0 else z, step)

    def fill(way, step, half_index):
        at = spot(way, step)
        if way == 0:
            chosen = both_left[pl.ds(at * 4, 4)].reshape(4 * rows, 2 * ROWS)
        else:
            chosen = jnp.concatenate([both_left[k * 4 + at] for k in range(4)], axis=0)
        start = (way * 2 + half_index) * half
        parts[way, at, half_index] = dot(chosen, both_right[:, start : start + half]).astype(bf16)

    def towards(way):
        def target(step):
            if way == 0:
                return device(around(x, step), y, z, core)
            return device(x, y, around(z, step), core)

        return target

    first, first_done = [], ([], [])
    for way in (0, 1):
        for step, half_index in ((2, 0), (2, 1), (1, 1), (-1, 0)):
            fill(way, step, half_index)
        ring = ring_sum(
            copies,
            first_done[way],
            towards(way),
            lambda step, half_index, way=way: parts.at[way, spot(way, step), half_index],
            came.at[way],
        )
        next(ring)
        first.append(ring)
    for way in (0, 1):
        for step, half_index in ((1, 0), (-1, 1), (0, 0), (0, 1)):
            fill(way, step, half_index)
    yield
    for ring in first:
        next(ring)
    yield
    second, second_done = [], ([], [])
    for way in (0, 1):
        next(first[way], None)
        for half_index in (0, 1):
            sums[way, half_index] = (
                first_done[way][0](half_index).astype(bf16).reshape(4, rows, half)
            )
        ring = ring_sum(
            copies,
            second_done[way],
            towards(1 - way),
            lambda step, half_index, way=way: sums.at[way, half_index, spot(1 - way, step)],
            late.at[way],
        )
        next(ring)
        second.append(ring)
    yield
    for ring in second:
        next(ring)
    yield
    for way in (0, 1):
        next(second[way], None)
        for half_index in (0, 1):
            start = (way * 2 + half_index) * half
            store_columns(out, start, second_done[way][0](half_index))
    copies.finish()
    yield


def sum_gains(copies, here, given, came_x, part_x, came_z, part_z, came_core, part, came_y, out):
    x, y, z, core = here
    arrivals = [
        copies.start(
            given.at[around(x, hop)], came_x.at[n], device(around(x, hop), y, z, core), came_x.at[n]
        )
        for n, hop in enumerate(HOPS)
    ]
    yield
    for arrival in arrivals:
        arrival.wait_recv()
    part_x[...] = (given[x] + came_x[0]) + (came_x[1] + came_x[2])
    arrivals = [
        copies.start(
            part_x.at[around(z, hop)], came_z.at[n], device(x, y, around(z, hop), core), came_z.at[n]
        )
        for n, hop in enumerate(HOPS)
    ]
    yield
    for arrival in arrivals:
        arrival.wait_recv()
    part_z[...] = (part_x[z] + came_z[0]) + (came_z[1] + came_z[2])
    arrival = copies.start(part_z.at[1 - core], came_core, device(x, y, z, 1 - core), came_core)
    yield
    arrival.wait_recv()
    part[...] = part_z[core] + came_core[...]
    arrivals = [
        copies.start(part, came_y.at[n], device(x, around(y, hop), z, core), came_y.at[n])
        for n, hop in enumerate(HOPS)
    ]
    yield
    for arrival in arrivals:
        arrival.wait_recv()
    out[...] = (part[...] + came_y[0]) + (came_y[1] + came_y[2])
    yield


GAIN_SCRATCH = [(3, 4, 2, 8, HD), (4, 2, 8, HD), (3, 2, 8, HD), (2, 8, HD), (8, HD), (8, HD), (3, 8, HD)]


NORM_ROWS = 32
WIDE = 512


def gain_rows(labels, gains, first):
    return jnp.where(
        labels == 0,
        gains[first : first + 1, :],
        jnp.where(labels == 1, gains[first + 1 : first + 2, :], gains[first + 2 : first + 3, :]),
    )


def steps(count, body):
    lax.fori_loop(0, count, lambda index, carry: (body(index), carry)[1], 0)


def slab(index, size):
    return pl.ds(pl.multiple_of(index * size, size), size)


def visible(key_codes, low, span):
    return (key_codes - low).astype(jnp.uint32) <= span.astype(jnp.uint32)


def key_column(keys_values, z_at, core_at):
    codes = jnp.concatenate(
        [keys_values[z_at, core_at, n, ROWS:, :] for n in range(4)], axis=1
    )
    row = lax.broadcasted_iota(jnp.int32, (CODE_ROWS, HD), 0)
    weight = jnp.where(row == 0, 128.0, jnp.where(row == 1, 1.0, 0.0)).astype(bf16)
    return dot(codes, weight, TN).astype(jnp.int32)


def query_bounds(keys_values, z, core, bounds):
    for n in range(4):
        digits = keys_values[z, core, n, ROWS:, :].astype(f32)
        code = (digits[0:1] * 128.0 + digits[1:2]).astype(jnp.int32)
        low = jnp.where(code >= CLIP_STEP, CLIP_STEP, 0)
        bounds[0:1, n * ROWS : (n + 1) * ROWS] = low
        bounds[1:2, n * ROWS : (n + 1) * ROWS] = code - low


def forward_kernel(
    x_ref, labels_ref, gains_ref, cos_ref, sin_ref, digits_ref, weight_hbm, out_weight_hbm,
    q_all_ref, kv_all_ref, o_ref, lse_ref, returned_ref, total_ref,
    weight, out_weight, normed, q_own, kv_own, queries, keys_values, top, norm, acc, column, bounds_ref, o_low, back,
    gathered, send_sems, recv_sems, load_sems,
):
    here = place()
    x, y, z, core = here
    twin = device(x, y, z, 1 - core)
    arrived = greet(
        [device(around(x, hop), y, z, core) for hop in HOPS]
        + [device(x, around(y, hop), z, core) for hop in HOPS]
        + [device(x, y, around(z, hop), core) for hop in (1, 3)]
        + [twin]
    )
    load_out = pltpu.make_async_copy(out_weight_hbm, out_weight.at[y], load_sems.at[0])
    load_out.start()
    load = pltpu.make_async_copy(weight_hbm, weight, load_sems.at[1])
    load.start()
    copies = Copies(send_sems, recv_sems)

    def normalise(index):
        at = slab(index, NORM_ROWS)
        rows = x_ref[at, :].astype(f32)
        centred = rows - jnp.mean(rows, axis=-1, keepdims=True)
        scale = lax.rsqrt(jnp.mean(centred * centred, axis=-1, keepdims=True) + 1e-05)
        normed[at, :] = (centred * scale * gain_rows(labels_ref[at, :1], gains_ref, 0)).astype(
            bf16
        )

    steps(ROWS // NORM_ROWS, normalise)
    arrived()
    load_out.wait()
    y_up, y_down = device(x, around(y, 1), z, core), device(x, around(y, -1), z, core)
    y_next, y_last, y_far = around(y, 1), around(y, -1), around(y, 2)
    w_last, w_next, w_far, w_twin = [], [], [None] * 4, []
    for n in range(4):
        block = out_weight.at[y, core, n]
        w_last.append(copies.start(block, block, y_up, out_weight.at[y_last, core, n]))
        w_next.append(copies.start(block, block, y_down, out_weight.at[y_next, core, n]))

    def w_onward(n):
        w_last[n].wait_recv()
        block = out_weight.at[y_last, core, n]
        if n < 2:
            w_far[n] = copies.start(block, block, y_up, out_weight.at[y_far, core, n])
        w_twin.append(copies.start(block, block, twin, out_weight.at[y_last, 1 - core, n]))
        w_next[n].wait_recv()
        block = out_weight.at[y_next, core, n]
        if n >= 2:
            w_far[n] = copies.start(block, block, y_down, out_weight.at[y_far, core, n])
        w_twin.append(copies.start(block, block, twin, out_weight.at[y_next, 1 - core, n]))

    load.wait()
    cosine, sine = cos_ref[...], sin_ref[...]

    def rotate(values, head):
        part = values[:, head * HD : (head + 1) * HD]
        turned = jnp.concatenate([-part[:, HD // 2 :], part[:, : HD // 2]], axis=1)
        return part * cosine + turned * sine

    key_part = dot(normed[...], weight[1])
    for head in range(4):
        kv_own[head, :ROWS, :HD] = rotate(key_part, head).astype(bf16)
        kv_own[head, ROWS:, :] = digits_ref[...]
    value_part = dot(normed[...], weight[2])
    for head in range(4):
        kv_own[head, :ROWS, HD:] = value_part[:, head * HD : (head + 1) * HD].astype(bf16)
    kv_came, q_came = [None] * 3, [None] * 3

    def send_kv(n):
        other = around(x, HOPS[n])
        kv_came[n] = copies.start(
            kv_own.at[other],
            keys_values.at[z, core, x],
            device(other, y, z, core),
            keys_values.at[z, core, around(x, -HOPS[n])],
        )

    send_kv(0)
    send_kv(1)
    query_part = dot(normed[...], weight[0]) * (HD**-0.5 / math.log(2.0))
    for head in range(4):
        q_own[head] = rotate(query_part, head).astype(bf16)
    for n, hop in enumerate(HOPS):
        other = around(x, hop)
        q_came[n] = copies.start(
            q_own.at[other],
            queries.at[x],
            device(other, y, z, core),
            queries.at[around(x, -hop)],
        )
    send_kv(2)
    keys_values[z, core, x] = kv_own[x]
    queries[x] = q_own[x]
    above, below = device(x, y, around(z, 1), core), device(x, y, around(z, -1), core)
    next_z, last_z, far_z = around(z, 1), around(z, -1), around(z, 2)
    pieces = [x] + [around(x, -hop) for hop in HOPS]
    from_last, from_next, from_twin = [], [], []

    def spread(n):
        block = keys_values.at[z, core, pieces[n]]
        from_last.append(copies.start(block, block, above, keys_values.at[last_z, core, pieces[n]]))
        from_next.append(copies.start(block, block, below, keys_values.at[next_z, core, pieces[n]]))
        from_twin.append(copies.start(block, block, twin, keys_values.at[z, 1 - core, pieces[n]]))

    spread(0)
    top[...] = jnp.full_like(top, -1e30)
    norm[...] = jnp.zeros_like(norm)
    acc[...] = jnp.zeros_like(acc)
    for n in range(3):
        kv_came[n].wait_recv()
        spread(n + 1)
    for arrival in q_came:
        arrival.wait_recv()
    query_bounds(keys_values, z, core, bounds_ref)

    def attend(z_at, core_at):
        column[...] = key_column(keys_values, z_at, core_at)
        query = queries[...].reshape(4 * ROWS, HD)
        keys = keys_values[z_at, core_at, :, :ROWS, :HD].reshape(4 * ROWS, HD)
        values = keys_values[z_at, core_at, :, :ROWS, HD:].reshape(4 * ROWS, HD)
        scores = dot(keys, query, NT)
        codes = jnp.concatenate([column[...]] * (4 * ROWS // HD), axis=1)
        seen = visible(codes, bounds_ref[0:1, :], bounds_ref[1:2, :])
        scores = jnp.where(seen, scores, -1e30)
        top_before = top[0:1, :]
        top_now = jnp.maximum(top_before, jnp.max(scores, axis=0, keepdims=True))
        weights = jnp.exp2(scores - top_now).astype(bf16)
        shrink = jnp.exp2(top_before - top_now)
        norm[...] = norm[...] * shrink + dot(jnp.ones((8, 4 * ROWS), bf16), weights)
        top[0:1, :] = top_now
        acc[...] = acc[...] * shrink + dot(values, weights, TN)

    low_far, high_far, twin_last, twin_next = [], [], [], []

    def onward(n):
        piece = pieces[n]
        from_last[n].wait_recv()
        block = keys_values.at[last_z, core, piece]
        low = block.at[pl.ds(0, ROWS // 2)]
        low_far.append(
            copies.start(low, low, above, keys_values.at[far_z, core, piece, pl.ds(0, ROWS // 2)])
        )
        twin_last.append(
            copies.start(block, block, twin, keys_values.at[last_z, 1 - core, piece])
        )
        from_next[n].wait_recv()
        block = keys_values.at[next_z, core, piece]
        high = block.at[pl.ds(ROWS // 2, ROWS // 2 + CODE_ROWS)]
        high_far.append(
            copies.start(
                high,
                high,
                below,
                keys_values.at[far_z, core, piece, pl.ds(ROWS // 2, ROWS // 2 + CODE_ROWS)],
            )
        )
        twin_next.append(
            copies.start(block, block, twin, keys_values.at[next_z, 1 - core, piece])
        )

    def take(arrivals):
        for arrival in arrivals:
            arrival.wait_recv()

    onward(0)
    w_onward(0)
    attend(z, core)
    onward(1)
    onward(2)
    take(from_twin)
    attend(z, 1 - core)
    onward(3)
    w_onward(1)
    attend(last_z, core)
    attend(next_z, core)
    w_onward(2)
    take(twin_last)
    attend(last_z, 1 - core)
    twin_far = []
    for n, piece in enumerate(pieces):
        low_far[n].wait_recv()
        high_far[n].wait_recv()
        block = keys_values.at[far_z, core, piece]
        twin_far.append(copies.start(block, block, twin, keys_values.at[far_z, 1 - core, piece]))
    take(twin_next)
    attend(next_z, 1 - core)
    w_onward(3)
    attend(far_z, core)
    take(twin_far)
    keep = pltpu.make_async_copy(keys_values, kv_all_ref, load_sems.at[2])
    keep.start()
    attend(far_z, 1 - core)

    total_norm = norm[0:1, :]
    attended = (acc[...] / total_norm).T
    o_low[...] = attended.astype(bf16).reshape(4, ROWS, HD)
    came_back = []
    for hop in HOPS:
        other = around(x, hop)
        came_back.append(
            copies.start(
                o_low.at[other],
                back.at[x],
                device(other, y, z, core),
                back.at[around(x, -hop)],
            )
        )
    back[x] = o_low[x]
    o_ref[...] = attended
    lse_ref[...] = jnp.broadcast_to(top[0:1, :] + jnp.log2(total_norm), lse_ref.shape)
    q_all_ref[...] = queries[...]
    for n in range(4):
        w_far[n].wait_recv()
        block = out_weight.at[y_far, core, n]
        w_twin.append(copies.start(block, block, twin, out_weight.at[y_far, 1 - core, n]))
    take(came_back)
    local = 4 * HD
    mine = pl.ds(pl.multiple_of(y * local, local), local)
    for n in range(4):
        gathered[y, :, n * HD : (n + 1) * HD] = back[n]
    spread_y = [
        copies.start(
            gathered.at[y],
            gathered.at[y],
            device(x, around(y, hop), z, core),
            gathered.at[around(y, -hop)],
        )
        for hop in HOPS
    ]
    returned_ref[...] = gathered[y]
    take(w_twin)
    take(spread_y)

    def project(index):
        at = slab(index, WIDE)
        total_ref[:, at] = sum(
            dot(gathered[n], out_weight[n, :, :, :, at].reshape(local, WIDE)) for n in range(4)
        ).astype(bf16)

    steps(total_ref.shape[1] // WIDE, project)
    copies.finish()
    keep.wait()


def attention_forward(activations, labels, gains, cosine, sine, digits, weight, out_weight):
    width = out_weight.shape[1]
    whole = pl.BlockSpec(memory_space=pltpu.VMEM)
    anywhere = pl.BlockSpec(memory_space=pl.ANY)
    count = 3 + 3 + 12 + 16 + 4 + 3 + 3 + 8 + 4 + 8 + 4
    pieces = (2, 4, out_weight.shape[0] // 8, width)
    return pl.pallas_call(
        forward_kernel,
        out_shape=[
            jax.ShapeDtypeStruct((4, ROWS, HD), bf16),
            jax.ShapeDtypeStruct((4, 2, 4, ROWS + CODE_ROWS, 2 * HD), bf16),
            jax.ShapeDtypeStruct((4 * ROWS, HD), f32),
            jax.ShapeDtypeStruct((8, 4 * ROWS), f32),
            jax.ShapeDtypeStruct((ROWS, 4 * HD), bf16),
            jax.ShapeDtypeStruct((ROWS, width), bf16),
        ],
        in_specs=[whole] * 6 + [anywhere] * 2,
        out_specs=[whole, anywhere] + [whole] * 4,
        scratch_shapes=[
            pltpu.VMEM(weight.shape, bf16),
            pltpu.VMEM((4,) + pieces, bf16),
            pltpu.VMEM(activations.shape, bf16),
            pltpu.VMEM((4, ROWS, HD), bf16),
            pltpu.VMEM((4, ROWS + CODE_ROWS, 2 * HD), bf16),
            pltpu.VMEM((4, ROWS, HD), bf16),
            pltpu.VMEM((4, 2, 4, ROWS + CODE_ROWS, 2 * HD), bf16),
            pltpu.VMEM((8, 4 * ROWS), f32),
            pltpu.VMEM((8, 4 * ROWS), f32),
            pltpu.VMEM((HD, 4 * ROWS), f32),
            pltpu.VMEM((4 * ROWS, HD), jnp.int32),
            pltpu.VMEM((8, 4 * ROWS), jnp.int32),
            pltpu.VMEM((4, ROWS, HD), bf16),
            pltpu.VMEM((4, ROWS, HD), bf16),
            pltpu.VMEM((4, ROWS, 4 * HD), bf16),
            pltpu.SemaphoreType.DMA((count,)),
            pltpu.SemaphoreType.DMA((count,)),
            pltpu.SemaphoreType.DMA((3,)),
        ],
        compiler_params=pltpu.CompilerParams(
            collective_id=0, has_side_effects=True, vmem_limit_bytes=VMEM_LIMIT
        ),
        name="attention_forward",
    )(activations, labels, gains, cosine, sine, digits, weight, out_weight.reshape(pieces))


def gelu_and_slope(hidden):
    scale = math.sqrt(2.0 / math.pi)
    square = hidden * hidden
    bent = jnp.tanh(scale * hidden * (1.0 + 0.044715 * square))
    half = 0.5 * (1.0 + bent)
    slope = half + 0.5 * hidden * (1.0 - bent * bent) * (scale * (1.0 + 3 * 0.044715 * square))
    return hidden * half, slope


def middle_kernel(
    x_ref, attn_ref, labels_ref, gains_ref, cotangent_ref, out_weight_ref, up_hbm, down_hbm,
    g_mid_ref, g_low_ref, heads_ref, mlp_ref, active_left_ref, gains_out_ref, weight_ref,
    up, down, xhat, inverse, normed, active, far, given, came, all_rows, y_send, y_recv, load_sems,
    *weight_scratch_refs,
):
    here = place()
    x, y, z, core = here
    load_up = pltpu.make_async_copy(up_hbm, up, load_sems.at[0])
    load_down = pltpu.make_async_copy(down_hbm, down, load_sems.at[1])
    load_up.start()
    load_down.start()
    arrived = greet(
        [device(x, around(y, hop), z, core) for hop in HOPS]
        + [device(around(x, hop), y, z, core) for hop in (1, 3)]
        + [device(x, y, around(z, hop), core) for hop in (1, 3)]
        + [device(x, y, z, 1 - core)]
    )
    both_left, both_right = weight_scratch_refs[:2]
    width = x_ref.shape[1]
    hidden_width = up.shape[1]

    def norm(index):
        at = slab(index, NORM_ROWS)
        middle = x_ref[at, :].astype(f32) + attn_ref[at, :].astype(f32)
        centred = middle - jnp.mean(middle, axis=-1, keepdims=True)
        scale = lax.rsqrt(jnp.mean(centred * centred, axis=-1, keepdims=True) + 1e-05)
        unit = centred * scale
        xhat[at, :] = unit
        inverse[at, :] = jnp.broadcast_to(scale, (NORM_ROWS, HD))
        normed[at, :] = (unit * gain_rows(labels_ref[at, :1], gains_ref, 3)).astype(bf16)

    steps(ROWS // NORM_ROWS, norm)
    load_up.wait()
    load_down.wait()

    def feed(index):
        at = slab(index, WIDE)
        hidden = dot(normed[...], up[:, at])
        grad_active = dot(cotangent_ref[...], down[at, :], NT)
        value, slope = gelu_and_slope(hidden)
        active[:, at] = value.astype(bf16)
        both_right[pl.ds(0, ROWS), at] = (grad_active * slope).astype(bf16)

    steps(hidden_width // WIDE, feed)

    def back_up(index):
        at = slab(index, WIDE)
        part = dot(both_right[pl.ds(0, ROWS), :], up[at, :], NT)
        given[:, :, at] = part.astype(bf16).reshape(SIDE, ROWS // SIDE, WIDE)

    steps(width // WIDE, back_up)
    arrived()
    copies = Copies(y_send, y_recv)
    over_y = sum_over_y(copies, here, given, came, all_rows)
    next(over_y)
    rows = weight_ref.shape[0]
    for group in range(4):
        at = pl.ds(4 * group, 4)
        both_left[at, :, pl.ds(0, ROWS)] = pick(core, normed, rows, group).reshape(4, rows, ROWS)
        far[at] = pick(1 - core, normed, rows, group).reshape(4, rows, ROWS)
    ring = weight_grad(here, None, None, weight_ref, weight_scratch_refs, far)
    next(ring)

    def mlp(index):
        at = slab(index, WIDE)
        mlp_ref[:, :, at] = (
            dot(active[...], down[:, at]).astype(bf16).reshape(SIDE, ROWS // SIDE, WIDE)
        )

    steps(width // WIDE, mlp)
    next(ring)
    for group in range(4):
        for core_at in range(2):
            active_left_ref[pl.ds(4 * group, 4), core_at] = pick(
                core_at, active, rows, group
            ).reshape(4, rows, ROWS)
    next(over_y)
    next(ring)
    next(over_y)
    gains_out_ref[...] = jnp.zeros_like(gains_out_ref)

    def back(index):
        at = slab(index, NORM_ROWS)
        part = lax.div(index, SIDE // 2)
        start = pl.multiple_of(lax.rem(index, SIDE // 2) * NORM_ROWS, NORM_ROWS)
        grad = all_rows[part, pl.ds(start, NORM_ROWS), :].astype(f32)
        labels = labels_ref[at, :1]
        unit = xhat[at, :]
        product = grad * unit
        for mode in range(3):
            gains_out_ref[mode + 3 : mode + 4, :] += jnp.sum(
                jnp.where(labels == mode, product, 0.0), axis=0, keepdims=True
            )
        gain = gain_rows(labels, gains_ref, 3)
        grad = grad * gain
        mean = jnp.mean(grad, axis=-1, keepdims=True)
        along = jnp.mean(product * gain, axis=-1, keepdims=True)
        g_mid = cotangent_ref[at, :].astype(f32) + inverse[at, :1] * (grad - mean - unit * along)
        g_mid_ref[at, :] = g_mid
        g_low_ref[at, :] = g_mid.astype(bf16)

    steps(ROWS // NORM_ROWS, back)
    g_heads = dot(g_low_ref[...], out_weight_ref[...], NT).astype(bf16)
    for head in range(4):
        heads_ref[head] = g_heads[:, head * HD : (head + 1) * HD]
    next(ring)
    next(ring)
    next(ring)
    copies.finish()


def middle(activations, attn_sum, labels, gains, cotangent, out_weight, up_weight, down_weight):
    width, hidden_width = up_weight.shape
    rows = width // 32
    quarter = ROWS // SIDE
    whole = pl.BlockSpec(memory_space=pltpu.VMEM)
    anywhere = pl.BlockSpec(memory_space=pl.ANY)
    return pl.pallas_call(
        middle_kernel,
        out_shape=[
            jax.ShapeDtypeStruct((ROWS, width), f32),
            jax.ShapeDtypeStruct((ROWS, width), bf16),
            jax.ShapeDtypeStruct((4, ROWS, HD), bf16),
            jax.ShapeDtypeStruct((SIDE, quarter, width), bf16),
            jax.ShapeDtypeStruct((16, 2, hidden_width // 32, ROWS), bf16),
            jax.ShapeDtypeStruct((8, width), f32),
            jax.ShapeDtypeStruct((rows, hidden_width), f32),
        ],
        in_specs=[whole] * 6 + [anywhere] * 2,
        out_specs=[whole] * 7,
        scratch_shapes=[
            pltpu.VMEM(up_weight.shape, bf16),
            pltpu.VMEM(down_weight.shape, bf16),
            pltpu.VMEM((ROWS, width), f32),
            pltpu.VMEM((ROWS, HD), f32),
            pltpu.VMEM((ROWS, width), bf16),
            pltpu.VMEM((ROWS, hidden_width), bf16),
            pltpu.VMEM((16, rows, ROWS), bf16),
            pltpu.VMEM((SIDE, quarter, width), bf16),
        ]
        + sum_scratch(width)
        + [pltpu.SemaphoreType.DMA((2,))]
        + weight_scratch(rows, hidden_width),
        compiler_params=pltpu.CompilerParams(
            collective_id=2, has_side_effects=True, vmem_limit_bytes=VMEM_LIMIT
        ),
        name="middle",
    )(activations, attn_sum, labels, gains, cotangent, out_weight, up_weight, down_weight)


BACK_TILE = 256


def backward_kernel(
    grad_ref, q_ref, kv_hbm, o_ref, lse_ref, left_ref, right_ref, given_ref,
    packed_ref, weight_ref, total_ref,
    keys_values, grads, delta, grad_q, grad_k, grad_v, column, bounds_ref, parts, met, came, sums, q_low, back_q,
    back_kv, send_sems, recv_sems, load_sems, y_came, all_rows, y_send, y_recv, *weight_scratch_refs,
):
    here = place()
    x, y, z, core = here
    twin = device(x, y, z, 1 - core)
    load = pltpu.make_async_copy(kv_hbm, keys_values, load_sems.at[0])
    load.start()
    greet(
        [device(around(x, hop), y, z, core) for hop in HOPS]
        + [device(x, around(y, hop), z, core) for hop in HOPS]
        + [device(x, y, around(z, hop), core) for hop in (1, 3)]
        + [twin]
    )()
    copies = Copies(send_sems, recv_sems)
    y_copies = Copies(y_send, y_recv)
    over_y = sum_over_y(y_copies, here, given_ref, y_came, all_rows)
    arrivals = []
    for hop in HOPS:
        other = around(x, hop)
        arrivals.append(
            copies.start(
                grad_ref.at[other],
                grads.at[x],
                device(other, y, z, core),
                grads.at[around(x, -hop)],
            )
        )
    ring = weight_grad(here, left_ref, right_ref, weight_ref, weight_scratch_refs)
    next(ring)
    grads[x] = grad_ref[x]
    grad_q[...] = jnp.zeros_like(grad_q)
    load.wait()
    query_bounds(keys_values, z, core, bounds_ref)
    next(over_y)
    next(ring)
    for arrival in arrivals:
        arrival.wait_recv()
    product = grads[...].reshape(4 * ROWS, HD).astype(f32) * o_ref[...]
    delta[...] = lax.dot_general(
        jnp.ones((8, HD), f32), product, NT, preferred_element_type=f32, precision=highest
    )

    def chunk(z_at, core_at):
        column[...] = key_column(keys_values, z_at, core_at)
        grad_k[...] = jnp.zeros_like(grad_k)
        grad_v[...] = jnp.zeros_like(grad_v)

        def tile(index, carry):
            at = pl.ds(pl.multiple_of(index * BACK_TILE, BACK_TILE), BACK_TILE)
            query = q_ref[index]
            grad = grads[index]
            keys = keys_values[z_at, core_at, :, :ROWS, :HD].reshape(4 * ROWS, HD)
            values = keys_values[z_at, core_at, :, :ROWS, HD:].reshape(4 * ROWS, HD)
            scores = dot(keys, query, NT)
            codes = jnp.concatenate([column[...]] * (BACK_TILE // HD), axis=1)
            seen = visible(codes, bounds_ref[0:1, at], bounds_ref[1:2, at])
            weights = jnp.where(seen, jnp.exp2(scores - lse_ref[0:1, at]), 0.0)
            grad_weights = dot(values, grad, NT)
            grad_scores = (weights * (grad_weights - delta[0:1, at])).astype(bf16)
            grad_v[...] += dot(weights.astype(bf16), grad)
            grad_k[...] += dot(grad_scores, query)
            grad_q[:, at] += dot(keys, grad_scores, TN)
            return carry

        lax.fori_loop(0, 4 * ROWS // BACK_TILE, tile, 0)
        parts[z_at, core_at] = jnp.concatenate(
            [grad_k[...] * math.log(2.0), grad_v[...]], axis=1
        ).astype(bf16).reshape(2, 2 * ROWS, 2 * HD)

    def hand_over(z_at):
        return copies.start(
            parts.at[z_at, 1 - core], met.at[z_at], twin, met.at[z_at]
        )

    def join(z_at):
        parts[z_at, core] = (
            parts[z_at, core].astype(f32) + met[z_at].astype(f32)
        ).astype(bf16)

    next_z, last_z, far_z = around(z, 1), around(z, -1), around(z, 2)
    above, below = device(x, y, next_z, core), device(x, y, last_z, core)
    chunk(far_z, 1 - core)
    far_met = hand_over(far_z)
    chunk(far_z, core)
    chunk(next_z, 1 - core)
    next_met = hand_over(next_z)
    next(ring)
    next(over_y)
    far_met.wait_recv()
    join(far_z)
    from_last = copies.start(parts.at[far_z, core, 0], came.at[0], above, came.at[0])
    from_next = copies.start(parts.at[far_z, core, 1], came.at[1], below, came.at[1])
    chunk(next_z, core)
    chunk(last_z, 1 - core)
    last_met = hand_over(last_z)
    next(ring)
    next_met.wait_recv()
    join(next_z)
    raw_last = copies.start(parts.at[next_z, core, 1], came.at[2], above, came.at[2])
    chunk(last_z, core)
    chunk(z, 1 - core)
    own_met = hand_over(z)
    next(ring)
    next(over_y)
    total_ref[...] = all_rows[...]
    last_met.wait_recv()
    join(last_z)
    raw_next = copies.start(parts.at[last_z, core, 0], came.at[3], below, came.at[3])
    from_last.wait_recv()
    parts[next_z, core, 0] = (
        parts[next_z, core, 0].astype(f32) + came[0].astype(f32)
    ).astype(bf16)
    sum_last = copies.start(parts.at[next_z, core, 0], came.at[4], above, came.at[4])
    from_next.wait_recv()
    parts[last_z, core, 1] = (
        parts[last_z, core, 1].astype(f32) + came[1].astype(f32)
    ).astype(bf16)
    sum_next = copies.start(parts.at[last_z, core, 1], came.at[5], below, came.at[5])
    chunk(z, core)
    q_low[...] = (grad_q[...] * (HD**-0.5)).T.astype(bf16).reshape(4, ROWS, HD)
    arrivals = []
    for hop in HOPS:
        other = around(x, hop)
        arrivals.append(
            copies.start(
                q_low.at[other],
                back_q.at[x],
                device(other, y, z, core),
                back_q.at[around(x, -hop)],
            )
        )
    back_q[x] = q_low[x]
    next(ring)
    own_met.wait_recv()
    raw_last.wait_recv()
    raw_next.wait_recv()
    sum_last.wait_recv()
    sum_next.wait_recv()
    mine = parts[z, core].astype(f32) + met[z].astype(f32)
    low = mine[0] + came[4].astype(f32) + came[3].astype(f32)
    high = mine[1] + came[2].astype(f32) + came[5].astype(f32)
    sums[0:2] = low.astype(bf16).reshape(2, ROWS, 2 * HD)
    sums[2:4] = high.astype(bf16).reshape(2, ROWS, 2 * HD)
    for hop in HOPS:
        other = around(x, hop)
        arrivals.append(
            copies.start(
                sums.at[other],
                back_kv.at[x],
                device(other, y, z, core),
                back_kv.at[around(x, -hop)],
            )
        )
    back_kv[x] = sums[x]
    for arrival in arrivals:
        arrival.wait_recv()
    for n in range(4):
        packed_ref[n, :, :HD] = back_q[n]
        packed_ref[n, :, HD:] = back_kv[n]
    copies.finish()
    y_copies.finish()


def attention_backward(grad_heads, q_all, kv_all, o_all, lse, left, right, given):
    whole = pl.BlockSpec(memory_space=pltpu.VMEM)
    anywhere = pl.BlockSpec(memory_space=pl.ANY)
    count = 3 + 4 + 6 + 6
    return pl.pallas_call(
        backward_kernel,
        out_shape=[
            jax.ShapeDtypeStruct((4, ROWS, 3 * HD), bf16),
            jax.ShapeDtypeStruct((left.shape[2], right.shape[1]), f32),
            jax.ShapeDtypeStruct(given.shape, bf16),
        ],
        in_specs=[whole, whole, anywhere, whole, whole, anywhere, anywhere, whole],
        out_specs=[whole, whole, whole],
        scratch_shapes=[
            pltpu.VMEM((4, 2, 4, ROWS + CODE_ROWS, 2 * HD), bf16),
            pltpu.VMEM((4, ROWS, HD), bf16),
            pltpu.VMEM((8, 4 * ROWS), f32),
            pltpu.VMEM((HD, 4 * ROWS), f32),
            pltpu.VMEM((4 * ROWS, HD), f32),
            pltpu.VMEM((4 * ROWS, HD), f32),
            pltpu.VMEM((4 * ROWS, HD), jnp.int32),
            pltpu.VMEM((8, 4 * ROWS), jnp.int32),
            pltpu.VMEM((4, 2, 2, 2 * ROWS, 2 * HD), bf16),
            pltpu.VMEM((4, 2, 2 * ROWS, 2 * HD), bf16),
            pltpu.VMEM((6, 2 * ROWS, 2 * HD), bf16),
            pltpu.VMEM((4, ROWS, 2 * HD), bf16),
            pltpu.VMEM((4, ROWS, HD), bf16),
            pltpu.VMEM((4, ROWS, HD), bf16),
            pltpu.VMEM((4, ROWS, 2 * HD), bf16),
            pltpu.SemaphoreType.DMA((count,)),
            pltpu.SemaphoreType.DMA((count,)),
            pltpu.SemaphoreType.DMA((1,)),
        ]
        + sum_scratch(given.shape[2])
        + weight_scratch(left.shape[2], right.shape[1]),
        compiler_params=pltpu.CompilerParams(
            collective_id=1, has_side_effects=True, vmem_limit_bytes=VMEM_LIMIT
        ),
        name="attention_backward",
    )(grad_heads, q_all, kv_all, o_all, lse, left, right, given)


def last_kernel(
    x_ref, attn_ref, mlp_ref, labels_ref, gains_ref, g_mid_ref, g_low_ref, returned_ref, packed_ref, cos_ref, sin_ref,
    gains_two_ref, weight_hbm,
    input_ref, layer_ref, gains_out_ref, grad_qkv_ref, grad_out_ref,
    weight, xhat, inverse, normed, far_qkv, far_out, given, gains_part, gains_given, came, all_rows, y_send, y_recv,
    load_sems, *more,
):
    gain_scratch = more[: len(GAIN_SCRATCH)]
    gain_send, gain_recv = more[len(GAIN_SCRATCH) : len(GAIN_SCRATCH) + 2]
    qkv_scratch = more[len(GAIN_SCRATCH) + 2 : len(GAIN_SCRATCH) + 11]
    out_scratch = more[len(GAIN_SCRATCH) + 11 :]
    here = place()
    x, y, z, core = here
    load = pltpu.make_async_copy(weight_hbm, weight, load_sems.at[0])
    load.start()
    arrived = greet(
        [device(x, around(y, hop), z, core) for hop in HOPS]
        + [device(around(x, hop), y, z, core) for hop in HOPS]
        + [device(x, y, around(z, hop), core) for hop in HOPS]
        + [device(x, y, z, 1 - core)]
    )
    width = x_ref.shape[1]
    local = returned_ref.shape[1]
    qkv_left, qkv_right = qkv_scratch[:2]
    out_left, out_right = out_scratch[:2]
    qkv_rows, out_rows = grad_qkv_ref.shape[1], grad_out_ref.shape[0]

    cosine, sine = cos_ref[...], sin_ref[...]
    for head in range(4):
        for part in range(3):
            grad = packed_ref[head, :, part * HD : (part + 1) * HD]
            if part < 2:
                grad = grad.astype(f32)
                scaled = grad * sine
                grad = (
                    grad * cosine
                    + jnp.concatenate([scaled[:, HD // 2 :], -scaled[:, : HD // 2]], axis=1)
                ).astype(bf16)
            start = part * local + head * HD
            qkv_right[0:ROWS, start : start + HD] = grad
    out_right[0:ROWS, :] = g_low_ref[...]

    def norm(index):
        at = slab(index, NORM_ROWS)
        rows = x_ref[at, :].astype(f32)
        centred = rows - jnp.mean(rows, axis=-1, keepdims=True)
        scale = lax.rsqrt(jnp.mean(centred * centred, axis=-1, keepdims=True) + 1e-05)
        unit = centred * scale
        xhat[at, :] = unit
        inverse[at, :] = jnp.broadcast_to(scale, (NORM_ROWS, HD))
        normed[at, :] = (unit * gain_rows(labels_ref[at, :1], gains_ref, 0)).astype(bf16)

    steps(ROWS // NORM_ROWS, norm)
    load.wait()
    gains_part[...] = 0.25 * gains_two_ref[...]

    def back_in(index):
        at = slab(index, WIDE)
        part = sum(
            dot(qkv_right[pl.ds(0, ROWS), k * local : (k + 1) * local], weight[k, at, :], NT)
            for k in range(3)
        )
        given[:, :, at] = part.astype(bf16).reshape(SIDE, ROWS // SIDE, WIDE)
        product = part * xhat[:, at]
        labels = labels_ref[:, :1]
        for mode in range(3):
            gains_part[mode : mode + 1, at] = jnp.sum(
                jnp.where(labels == mode, product, 0.0), axis=0, keepdims=True
            )

    steps(width // WIDE, back_in)
    arrived()
    copies = Copies(y_send, y_recv)
    over_y = sum_over_y(copies, here, given, came, all_rows)
    next(over_y)
    for group in range(4):
        at = pl.ds(4 * group, 4)
        qkv_left[at, :, pl.ds(0, ROWS)] = pick(core, normed, qkv_rows, group).reshape(
            4, qkv_rows, ROWS
        )
        far_qkv[at] = pick(1 - core, normed, qkv_rows, group).reshape(4, qkv_rows, ROWS)
    out_left[:, :, pl.ds(0, ROWS)] = pick(core, returned_ref, out_rows, 0).reshape(
        16, out_rows, ROWS
    )
    far_out[...] = pick(1 - core, returned_ref, out_rows, 0).reshape(16, out_rows, ROWS)
    rings = [
        weight_grad(here, None, None, grad_qkv_ref, qkv_scratch, far_qkv),
        weight_grad(here, None, None, grad_out_ref, out_scratch, far_out),
    ]
    for ring in rings:
        next(ring)
    for owner in range(32):
        gains_given[owner // 8, (owner // 2) % 4, owner % 2] = jnp.zeros((8, HD), f32)
        gains_given[owner // 8, (owner // 2) % 4, owner % 2, :, :64] = gains_part[
            :, owner * 64 : (owner + 1) * 64
        ]
    gain_copies = Copies(gain_send, gain_recv)
    over_all = sum_gains(gain_copies, here, gains_given, *gain_scratch, gains_out_ref)
    next(over_all)

    def finish_layer(index):
        at = slab(index, NORM_ROWS)
        part = lax.div(index, SIDE // 2)
        start = pl.multiple_of(lax.rem(index, SIDE // 2) * NORM_ROWS, NORM_ROWS)
        mlp = mlp_ref[part, pl.ds(start, NORM_ROWS), :].astype(f32)
        layer_ref[at, :] = (x_ref[at, :].astype(f32) + attn_ref[at, :].astype(f32) + mlp).astype(
            bf16
        )

    steps(ROWS // NORM_ROWS, finish_layer)
    for ring in rings:
        next(ring)
    next(over_all)
    next(over_y)
    for ring in rings:
        next(ring)
    next(over_all)
    next(over_y)

    def finish_input(index):
        at = slab(index, NORM_ROWS)
        part = lax.div(index, SIDE // 2)
        start = pl.multiple_of(lax.rem(index, SIDE // 2) * NORM_ROWS, NORM_ROWS)
        grad = all_rows[part, pl.ds(start, NORM_ROWS), :].astype(f32)
        unit = xhat[at, :]
        grad = grad * gain_rows(labels_ref[at, :1], gains_ref, 0)
        mean = jnp.mean(grad, axis=-1, keepdims=True)
        along = jnp.mean(grad * unit, axis=-1, keepdims=True)
        input_ref[at, :] = g_mid_ref[at, :] + inverse[at, :1] * (grad - mean - unit * along)

    steps(ROWS // NORM_ROWS, finish_input)
    for ring in rings:
        next(ring)
    next(over_all)
    for ring in rings:
        next(ring)
    next(over_all)
    for ring in rings:
        next(ring)
    copies.finish()
    gain_copies.finish()


def last(
    activations, attn_sum, mlp_sum, labels, gains, g_mid, g_low, returned, packed, cosine, sine, gains_two, weight
):
    width = activations.shape[1]
    local = returned.shape[1]
    cols = 3 * local
    rows = width // 32
    quarter = ROWS // SIDE
    whole = pl.BlockSpec(memory_space=pltpu.VMEM)
    return pl.pallas_call(
        last_kernel,
        out_shape=[
            jax.ShapeDtypeStruct((ROWS, width), f32),
            jax.ShapeDtypeStruct((ROWS, width), bf16),
            jax.ShapeDtypeStruct((8, HD), f32),
            jax.ShapeDtypeStruct((3, rows, local), f32),
            jax.ShapeDtypeStruct((local // 32, width), f32),
        ],
        in_specs=[whole] * 12 + [pl.BlockSpec(memory_space=pl.ANY)],
        out_specs=[whole] * 5,
        scratch_shapes=[
            pltpu.VMEM(weight.shape, bf16),
            pltpu.VMEM((ROWS, width), f32),
            pltpu.VMEM((ROWS, HD), f32),
            pltpu.VMEM((ROWS, width), bf16),
            pltpu.VMEM((16, rows, ROWS), bf16),
            pltpu.VMEM((16, local // 32, ROWS), bf16),
            pltpu.VMEM((SIDE, quarter, width), bf16),
            pltpu.VMEM((8, width), f32),
            pltpu.VMEM((4, 4, 2, 8, HD), f32),
        ]
        + sum_scratch(width)
        + [pltpu.SemaphoreType.DMA((1,))]
        + [pltpu.VMEM(shape, f32) for shape in GAIN_SCRATCH]
        + [pltpu.SemaphoreType.DMA((10,)), pltpu.SemaphoreType.DMA((10,))]
        + weight_scratch(rows, cols)
        + weight_scratch(local // 32, width),
        compiler_params=pltpu.CompilerParams(
            collective_id=3, has_side_effects=True, vmem_limit_bytes=VMEM_LIMIT
        ),
        name="last",
    )(activations, attn_sum, mlp_sum, labels, gains, g_mid, g_low, returned, packed, cosine, sine, gains_two, weight)


def tables(place_now, head_dim):
    half_dim = head_dim // 2
    frequency = jnp.exp(
        jnp.arange(half_dim, dtype=jnp.float32) * (-2.0 * math.log(10000.0) / head_dim)
    )
    angles = place_now.astype(jnp.float32)[:, None] * frequency[None, :]
    angles = jnp.concatenate([angles, angles], axis=-1)
    return (jnp.cos(angles), jnp.sin(angles))


def per_device(
    activations,
    labels,
    position,
    norm_gains,
    qkv_weight,
    out_weight,
    up_weight,
    down_weight,
    cotangent,
):
    mode_count = norm_gains.shape[0] // 2
    block, row = position // 256, position % 256
    second = (row >= 192).astype(jnp.int32)
    spot = jnp.where(second == 1, block * 64 + row - 192, block * 192 + row)
    code = spot + second * CLIP_STEP
    digits = jnp.stack([code // 128, code % 128], axis=0)
    digits = jnp.concatenate(
        [digits, jnp.zeros((CODE_ROWS - 2, ROWS), jnp.int32)], axis=0
    ).astype(bf16)

    cosine, sine = tables(spot, HD)
    label_rows = jnp.broadcast_to(labels[:, None], (ROWS, HD))
    gain_table = jnp.pad(norm_gains, ((0, 8 - 2 * mode_count), (0, 0)))
    projections = qkv_weight.transpose(1, 0, 2)
    q_all, kv_all, o_all, lse, returned, attn_sum = attention_forward(
        activations, label_rows, gain_table, cosine, sine, digits, projections, out_weight
    )
    grad_middle, grad_mid_low, grad_heads, mlp_part, active_left, gain_two_grad, grad_up = middle(
        activations, attn_sum, label_rows, gain_table, cotangent, out_weight, up_weight, down_weight
    )
    packed, grad_down, mlp_sum = attention_backward(
        grad_heads, q_all, kv_all, o_all, lse, active_left, cotangent, mlp_part
    )
    grad_input, layer_out, gains_share, grad_qkv, grad_out = last(
        activations,
        attn_sum,
        mlp_sum,
        label_rows,
        gain_table,
        grad_middle,
        grad_mid_low,
        returned,
        packed,
        cosine,
        sine,
        gain_two_grad,
        projections,
    )
    return (
        layer_out,
        grad_input,
        gains_share[: 2 * mode_count, :64],
        grad_qkv.transpose(1, 0, 2),
        grad_out,
        grad_up,
        grad_down,
    )


def solution(mesh):
    return jax.shard_map(
        per_device,
        mesh=mesh,
        in_specs=(
            P("tok", None),
            P("tok"),
            P("tok"),
            P(),
            P(None, None, "head"),
            P("head", None),
            P(None, "head"),
            P("head", None),
            P("tok", None),
        ),
        out_specs=(
            P("tok", None),
            P("tok", None),
            P(None, "tok"),
            P("tok", None, "head"),
            P(("head", "tok"), None),
            P("tok", "head"),
            P(("head", "tok"), None),
        ),
        check_vma=False,
    )
```

```python
import functools
import math

import jax
import jax.numpy as jnp
from jax import lax
from jax.experimental import pallas as pl
from jax.experimental.pallas import tpu as pltpu
from jax.sharding import PartitionSpec as P

HD = 128
SIDE = 4
ROWS = 256
CODE_ROWS = 16
CLIP_STEP = 8192
MESH = pl.DeviceIdType.MESH
NT = (((1,), (1,)), ((), ()))
TN = (((0,), (0,)), ((), ()))
NN = (((1,), (0,)), ((), ()))
f32 = jnp.float32
bf16 = jnp.bfloat16
highest = lax.Precision.HIGHEST
VMEM_LIMIT = 60 << 20
HOPS = (1, 3, 2)


def dot(lhs, rhs, dims=NN):
    return lax.dot_general(lhs, rhs, dims, preferred_element_type=f32)


def place():
    tok = lax.axis_index("tok")
    return (lax.div(tok, 8), lax.axis_index("head"), lax.rem(lax.div(tok, 2), 4), lax.rem(tok, 2))


def around(index, step):
    return lax.rem(index + (step % SIDE), SIDE)


def device(x, y, z, core):
    return (x * 8 + z * 2 + core, y)


def remote(src, dst, send_sem, recv_sem, target):
    return pltpu.make_async_remote_copy(
        src_ref=src,
        dst_ref=dst,
        send_sem=send_sem,
        recv_sem=recv_sem,
        device_id=target,
        device_id_type=MESH,
    )


def greet(targets):
    barrier = pltpu.get_barrier_semaphore()
    for target in targets:
        pl.semaphore_signal(barrier, inc=1, device_id=target, device_id_type=MESH)
    return lambda: pl.semaphore_wait(barrier, len(targets))


class Copies:
    def __init__(self, send_sems, recv_sems):
        self.send_sems = send_sems
        self.recv_sems = recv_sems
        self.used = 0
        self.open = []

    def start(self, src, dst, target, landing):
        index = self.used
        self.used += 1
        copy = remote(src, dst, self.send_sems.at[index], self.recv_sems.at[index], target)
        copy.start()
        self.open.append(copy)
        return remote(landing, landing, self.send_sems.at[index], self.recv_sems.at[index], target)

    def finish(self):
        for copy in self.open:
            copy.wait_send()


def sum_over_y(copies, here, given, came, total):
    x, y, z, core = here
    arrivals = []
    for n, hop in enumerate(HOPS):
        other = around(y, hop)
        arrivals.append(
            copies.start(given.at[other], came.at[n], device(x, other, z, core), came.at[n])
        )
    yield
    for arrival in arrivals:
        arrival.wait_recv()
    total[y] = (
        (given[y].astype(f32) + came[0].astype(f32))
        + (came[1].astype(f32) + came[2].astype(f32))
    ).astype(bf16)
    arrivals = []
    for hop in HOPS:
        arrivals.append(
            copies.start(
                total.at[y],
                total.at[y],
                device(x, around(y, hop), z, core),
                total.at[around(y, -hop)],
            )
        )
    yield
    for arrival in arrivals:
        arrival.wait_recv()
    yield


def sum_scratch(width):
    quarter = ROWS // SIDE
    return [
        pltpu.VMEM((2, 3, quarter, width // 2), bf16),
        pltpu.VMEM((2, SIDE, quarter, width // 2), bf16),
        pltpu.SemaphoreType.DMA((12,)),
        pltpu.SemaphoreType.DMA((12,)),
    ]


def summed_rows(all_rows, index):
    part = lax.div(index, SIDE // 2)
    start = pl.multiple_of(lax.rem(index, SIDE // 2) * NORM_ROWS, NORM_ROWS)
    halves = [all_rows[half, part, pl.ds(start, NORM_ROWS), :] for half in range(2)]
    return jnp.concatenate(halves, axis=1).astype(f32)


def ring_sum(copies, own, towards, block, slots):
    up, down = towards(1), towards(-1)
    from_down = copies.start(block(2, 0), slots.at[0], up, slots.at[0])
    from_up = copies.start(block(2, 1), slots.at[1], down, slots.at[1])
    raw_down = copies.start(block(1, 1), slots.at[2], up, slots.at[2])
    raw_up = copies.start(block(-1, 0), slots.at[3], down, slots.at[3])
    yield
    from_down.wait_recv()
    onward = block(1, 0)
    onward[...] = (onward[...].astype(f32) + slots[0].astype(f32)).astype(bf16)
    sum_down = copies.start(onward, slots.at[4], up, slots.at[4])
    from_up.wait_recv()
    onward = block(-1, 1)
    onward[...] = (onward[...].astype(f32) + slots[1].astype(f32)).astype(bf16)
    sum_up = copies.start(onward, slots.at[5], down, slots.at[5])
    yield
    for arrival in (raw_down, raw_up, sum_down, sum_up):
        arrival.wait_recv()

    def finished(half):
        mine = block(0, half)[...].astype(f32)
        if half == 0:
            return mine + slots[4].astype(f32) + slots[3].astype(f32)
        return mine + slots[2].astype(f32) + slots[5].astype(f32)

    own.append(finished)


def ring_shapes(rows, cols):
    if rows >= 32:
        width = cols // 4
        return 2, (2 * rows, width), (rows // 2, width)
    return 1, (4 * rows, cols // 4), (rows, cols // 4)


def weight_scratch(rows, cols):
    chunks, first, late = ring_shapes(rows, cols)
    return [
        pltpu.VMEM((16, rows, 2 * ROWS), bf16),
        pltpu.VMEM((2 * ROWS, cols), bf16),
        pltpu.VMEM((2, chunks, 4, 2) + first, bf16),
        pltpu.VMEM((2, chunks, 6) + first, bf16),
        pltpu.VMEM((2, chunks, 4, 2) + late, bf16),
        pltpu.VMEM((2, chunks, 6) + late, bf16),
        pltpu.SemaphoreType.DMA((2 + 24 * chunks,)),
        pltpu.SemaphoreType.DMA((2 + 24 * chunks,)),
        pltpu.SemaphoreType.DMA((2,)),
    ]


def store_part(out, row, start, value):
    rows = slice(row, row + value.shape[0])
    if len(out.shape) == 2:
        out[rows, start : start + value.shape[1]] = value
        return
    size, done = out.shape[2], 0
    while done < value.shape[1]:
        block, offset = divmod(start + done, size)
        count = min(size - offset, value.shape[1] - done)
        out[block, rows, offset : offset + count] = value[:, done : done + count]
        done += count


def pick(core_at, factor, rows, group):
    row = lax.broadcasted_iota(jnp.int32, (256, 512), 0)
    col = lax.broadcasted_iota(jnp.int32, (256, 512), 1)
    wanted = lax.div(row, rows) * (2 * rows) + core_at * rows + lax.rem(row, rows)
    chosen = jnp.where(col == wanted, 1.0, 0.0).astype(bf16)
    return dot(chosen, factor[:, 512 * group : 512 * (group + 1)], NT).astype(bf16)


def weight_grad(here, left, right, out, scratch, far=None):
    both_left, both_right, parts, came, sums, late, send_sems, recv_sems, own_sems = scratch
    x, y, z, core = here
    rows, cols = both_left.shape[1], both_right.shape[1]
    copies = Copies(send_sems, recv_sems)
    twin = device(x, y, z, 1 - core)
    if far is None:
        far = left.at[:, 1 - core]
        own_left = pltpu.make_async_copy(
            left.at[:, core], both_left.at[:, :, pl.ds(0, ROWS)], own_sems.at[0]
        )
        own_right = pltpu.make_async_copy(right, both_right.at[pl.ds(0, ROWS)], own_sems.at[1])
        own_left.start()
        own_right.start()
    else:
        right = both_right.at[pl.ds(0, ROWS)]
        own_left = own_right = None
    far_left = copies.start(
        far,
        both_left.at[:, :, pl.ds(ROWS, ROWS)],
        twin,
        both_left.at[:, :, pl.ds(ROWS, ROWS)],
    )
    far_right = copies.start(
        right,
        both_right.at[pl.ds(ROWS, ROWS)],
        twin,
        both_right.at[pl.ds(ROWS, ROWS)],
    )
    yield
    if own_left is not None:
        own_left.wait()
        own_right.wait()
    far_left.wait_recv()
    far_right.wait_recv()

    chunks, first_shape, late_shape = ring_shapes(rows, cols)
    by_rows = chunks == 2
    width = cols // 2 // chunks

    def spot(way, step):
        return around(x if way == 0 else z, step)

    def fill(way, chunk, step):
        at = spot(way, step)
        if way == 0:
            chosen = both_left[pl.ds(at * 4, 4)].reshape(4 * rows, 2 * ROWS)
        else:
            chosen = jnp.concatenate([both_left[k * 4 + at] for k in range(4)], axis=0)
        start = (way * chunks + chunk) * width
        value = dot(chosen, both_right[:, start : start + width]).astype(bf16)
        if by_rows:
            parts[way, chunk, at] = value.reshape((2,) + first_shape)
        else:
            for half_index in range(2):
                parts[way, chunk, at, half_index] = value[
                    :, half_index * first_shape[1] : (half_index + 1) * first_shape[1]
                ]

    def towards(way):
        def target(step):
            if way == 0:
                return device(around(x, step), y, z, core)
            return device(x, y, around(z, step), core)

        return target

    every = [(way, chunk) for chunk in range(chunks) for way in (0, 1)]
    first, first_done = {}, {}
    for way, chunk in every:
        for step in (2, 1, -1):
            fill(way, chunk, step)
        first_done[way, chunk] = []
        first[way, chunk] = ring_sum(
            copies,
            first_done[way, chunk],
            towards(way),
            lambda step, half_index, way=way, chunk=chunk: parts.at[
                way, chunk, spot(way, step), half_index
            ],
            came.at[way, chunk],
        )
        next(first[way, chunk])
    for way, chunk in every:
        fill(way, chunk, 0)
    yield
    for chunk in range(2):
        for way in (0, 1):
            if chunk < chunks:
                next(first[way, chunk])
        yield
    second, second_done = {}, {}
    for chunk in range(2):
        for way in (0, 1):
            if chunk >= chunks:
                continue
            next(first[way, chunk], None)
            finished = first_done[way, chunk][0]
            for half_index in (0, 1):
                value = finished(half_index).astype(bf16)
                if by_rows:
                    sums[way, chunk, 2 * half_index : 2 * half_index + 2] = value.reshape(
                        (2, 2) + late_shape
                    )
                else:
                    sums[way, chunk, :, half_index] = value.reshape((4,) + late_shape)
            second_done[way, chunk] = []
            second[way, chunk] = ring_sum(
                copies,
                second_done[way, chunk],
                towards(1 - way),
                lambda step, half_index, way=way, chunk=chunk: sums.at[
                    way, chunk, spot(1 - way, step), half_index
                ],
                late.at[way, chunk],
            )
            next(second[way, chunk])
        yield
    for at in every:
        next(second[at])
    yield
    for way, chunk in every:
        next(second[way, chunk], None)
        start = (way * chunks + chunk) * width
        for half_index in (0, 1):
            value = second_done[way, chunk][0](half_index)
            if by_rows:
                store_part(out, half_index * late_shape[0], start, value)
            else:
                store_part(out, 0, start + half_index * late_shape[1], value)
    copies.finish()
    yield


def sum_gains(copies, here, given, came_x, part_x, came_z, part_z, came_core, part, came_y, out):
    x, y, z, core = here
    arrivals = [
        copies.start(
            given.at[around(x, hop)], came_x.at[n], device(around(x, hop), y, z, core), came_x.at[n]
        )
        for n, hop in enumerate(HOPS)
    ]
    yield
    for arrival in arrivals:
        arrival.wait_recv()
    part_x[...] = (given[x] + came_x[0]) + (came_x[1] + came_x[2])
    arrivals = [
        copies.start(
            part_x.at[around(z, hop)], came_z.at[n], device(x, y, around(z, hop), core), came_z.at[n]
        )
        for n, hop in enumerate(HOPS)
    ]
    yield
    for arrival in arrivals:
        arrival.wait_recv()
    part_z[...] = (part_x[z] + came_z[0]) + (came_z[1] + came_z[2])
    arrival = copies.start(part_z.at[1 - core], came_core, device(x, y, z, 1 - core), came_core)
    yield
    arrival.wait_recv()
    part[...] = part_z[core] + came_core[...]
    arrivals = [
        copies.start(part, came_y.at[n], device(x, around(y, hop), z, core), came_y.at[n])
        for n, hop in enumerate(HOPS)
    ]
    yield
    for arrival in arrivals:
        arrival.wait_recv()
    out[...] = (part[...] + came_y[0]) + (came_y[1] + came_y[2])
    yield


GAIN_SCRATCH = [(3, 4, 2, 8, HD), (4, 2, 8, HD), (3, 2, 8, HD), (2, 8, HD), (8, HD), (8, HD), (3, 8, HD)]


NORM_ROWS = 32
WIDE = 512


def gain_rows(labels, gains, first):
    return jnp.where(
        labels == 0,
        gains[first : first + 1, :],
        jnp.where(labels == 1, gains[first + 1 : first + 2, :], gains[first + 2 : first + 3, :]),
    )


def steps(count, body):
    lax.fori_loop(0, count, lambda index, carry: (body(index), carry)[1], 0)


def slab(index, size):
    return pl.ds(pl.multiple_of(index * size, size), size)


def visible(key_codes, low, span):
    return (key_codes - low).astype(jnp.uint32) <= span.astype(jnp.uint32)


def key_column(keys_values, z_at, core_at):
    codes = jnp.concatenate(
        [keys_values[z_at, core_at, n, ROWS:, :] for n in range(4)], axis=1
    )
    row = lax.broadcasted_iota(jnp.int32, (CODE_ROWS, HD), 0)
    weight = jnp.where(row == 0, 128.0, jnp.where(row == 1, 1.0, 0.0)).astype(bf16)
    return dot(codes, weight, TN).astype(jnp.int32)


def query_bounds(keys_values, z, core, bounds):
    for n in range(4):
        digits = keys_values[z, core, n, ROWS:, :].astype(f32)
        code = (digits[0:1] * 128.0 + digits[1:2]).astype(jnp.int32)
        low = jnp.where(code >= CLIP_STEP, CLIP_STEP, 0)
        bounds[0:1, n * ROWS : (n + 1) * ROWS] = low
        bounds[1:2, n * ROWS : (n + 1) * ROWS] = code - low


def forward_kernel(
    x_ref, label_ref, position_ref, gains_ref, cotangent_ref, weight_hbm, out_weight_hbm, down_hbm,
    q_all_ref, kv_all_ref, o_ref, lse_ref, returned_ref, total_ref, grad_active_hbm, weights_ref, tops_ref, labels_ref,
    cos_ref, sin_ref,
    grad_active_ref, weight, out_weight, down, weights, normed, q_own, kv_own, queries, keys_values, top, norm, acc, column, bounds_ref, o_low, back,
    gathered, send_sems, recv_sems, load_sems, weight_sems,
):
    here = place()
    x, y, z, core = here
    twin = device(x, y, z, 1 - core)
    arrived = greet(
        [device(around(x, hop), y, z, core) for hop in HOPS]
        + [device(x, around(y, hop), z, core) for hop in HOPS]
        + [device(x, y, around(z, hop), core) for hop in (1, 3)]
        + [twin]
    )
    load_out = pltpu.make_async_copy(out_weight_hbm, out_weight.at[y], load_sems.at[0])
    load_out.start()
    load = pltpu.make_async_copy(weight_hbm, weight, load_sems.at[1])
    load.start()
    load_down = pltpu.make_async_copy(down_hbm, down, load_sems.at[3])
    load_down.start()
    copies = Copies(send_sems, recv_sems)

    position = position_ref[...]
    block, row = lax.shift_right_logical(position, 8), lax.bitwise_and(position, 255)
    second = row >= 192
    spot = jnp.where(second, block * 64 + row - 192, block * 192 + row)
    code = spot + jnp.where(second, CLIP_STEP, 0)
    kind = lax.broadcasted_iota(jnp.int32, (CODE_ROWS, ROWS), 0)
    digits = jnp.where(
        kind == 0,
        lax.shift_right_logical(code, 7),
        jnp.where(kind == 1, lax.bitwise_and(code, 127), 0),
    )
    digits = digits.astype(f32).astype(bf16)
    kind = lax.broadcasted_iota(jnp.int32, (8, ROWS), 0)
    small = jnp.where(
        kind == 0,
        lax.shift_right_logical(spot, 7),
        jnp.where(kind == 1, lax.bitwise_and(spot, 127), jnp.where(kind == 2, label_ref[...], 0)),
    )
    small = small.astype(f32).astype(bf16)
    kind = lax.broadcasted_iota(jnp.int32, (8, HD), 0)
    spot_weight = jnp.where(kind == 0, 128.0, jnp.where(kind == 1, 1.0, 0.0)).astype(bf16)
    label_weight = jnp.where(kind == 2, 1.0, 0.0).astype(bf16)
    labels_ref[...] = dot(small, label_weight, TN).astype(jnp.int32)
    feature = lax.rem(lax.broadcasted_iota(jnp.int32, (1, HD), 1), HD // 2).astype(f32)
    angle = dot(small, spot_weight, TN) * jnp.exp(feature * (-2.0 * math.log(10000.0) / HD))
    cos_ref[...] = jnp.cos(angle)
    sin_ref[...] = jnp.sin(angle)

    def normalise(index):
        at = slab(index, NORM_ROWS)
        rows = x_ref[at, :].astype(f32)
        centred = rows - jnp.mean(rows, axis=-1, keepdims=True)
        scale = lax.rsqrt(jnp.mean(centred * centred, axis=-1, keepdims=True) + 1e-05)
        normed[at, :] = (centred * scale * gain_rows(labels_ref[at, :1], gains_ref, 0)).astype(
            bf16
        )

    steps(ROWS // NORM_ROWS, normalise)
    arrived()
    load_out.wait()
    y_up, y_down = device(x, around(y, 1), z, core), device(x, around(y, -1), z, core)
    y_next, y_last, y_far = around(y, 1), around(y, -1), around(y, 2)
    w_last, w_next, w_far, w_twin = [], [], [None] * 4, []
    for n in range(4):
        block = out_weight.at[y, core, n]
        w_last.append(copies.start(block, block, y_up, out_weight.at[y_last, core, n]))
        w_next.append(copies.start(block, block, y_down, out_weight.at[y_next, core, n]))

    def w_onward(n):
        w_last[n].wait_recv()
        block = out_weight.at[y_last, core, n]
        if n < 2:
            w_far[n] = copies.start(block, block, y_up, out_weight.at[y_far, core, n])
        w_twin.append(copies.start(block, block, twin, out_weight.at[y_last, 1 - core, n]))
        w_next[n].wait_recv()
        block = out_weight.at[y_next, core, n]
        if n >= 2:
            w_far[n] = copies.start(block, block, y_down, out_weight.at[y_far, core, n])
        w_twin.append(copies.start(block, block, twin, out_weight.at[y_next, 1 - core, n]))

    load.wait()
    cosine, sine = cos_ref[...], sin_ref[...]

    def rotate(values, head):
        part = values[:, head * HD : (head + 1) * HD]
        turned = jnp.concatenate([-part[:, HD // 2 :], part[:, : HD // 2]], axis=1)
        return part * cosine + turned * sine

    key_part = dot(normed[...], weight[1])
    for head in range(4):
        kv_own[head, :ROWS, :HD] = rotate(key_part, head).astype(bf16)
        kv_own[head, ROWS:, :] = digits
    value_part = dot(normed[...], weight[2])
    for head in range(4):
        kv_own[head, :ROWS, HD:] = value_part[:, head * HD : (head + 1) * HD].astype(bf16)
    kv_came, q_came = [None] * 3, [None] * 3

    def send_kv(n):
        other = around(x, HOPS[n])
        kv_came[n] = copies.start(
            kv_own.at[other],
            keys_values.at[z, core, x],
            device(other, y, z, core),
            keys_values.at[z, core, around(x, -HOPS[n])],
        )

    send_kv(0)
    send_kv(1)
    query_part = dot(normed[...], weight[0]) * (HD**-0.5 / math.log(2.0))
    for head in range(4):
        q_own[head] = rotate(query_part, head).astype(bf16)
    for n, hop in enumerate(HOPS):
        other = around(x, hop)
        q_came[n] = copies.start(
            q_own.at[other],
            queries.at[x],
            device(other, y, z, core),
            queries.at[around(x, -hop)],
        )
    send_kv(2)
    keys_values[z, core, x] = kv_own[x]
    queries[x] = q_own[x]
    above, below = device(x, y, around(z, 1), core), device(x, y, around(z, -1), core)
    next_z, last_z, far_z = around(z, 1), around(z, -1), around(z, 2)
    pieces = [x] + [around(x, -hop) for hop in HOPS]
    from_last, from_next, from_twin = [], [], []

    def spread(n):
        block = keys_values.at[z, core, pieces[n]]
        from_last.append(copies.start(block, block, above, keys_values.at[last_z, core, pieces[n]]))
        from_next.append(copies.start(block, block, below, keys_values.at[next_z, core, pieces[n]]))
        from_twin.append(copies.start(block, block, twin, keys_values.at[z, 1 - core, pieces[n]]))

    spread(0)
    top[...] = jnp.full_like(top, -1e30)
    norm[...] = jnp.zeros_like(norm)
    acc[...] = jnp.zeros_like(acc)
    load_down.wait()

    def grad_active(index):
        at = slab(index, WIDE)
        grad_active_ref[:, at] = dot(cotangent_ref[...], down[at, :], NT)

    half_steps = grad_active_ref.shape[1] // WIDE // 2
    keep_grad = pltpu.make_async_copy(grad_active_ref, grad_active_hbm, load_sems.at[4])
    steps(half_steps, grad_active)
    for n in range(3):
        kv_came[n].wait_recv()
        spread(n + 1)
        if n == 1:
            steps(half_steps, lambda index: grad_active(index + half_steps))
            keep_grad.start()
    for arrival in q_came:
        arrival.wait_recv()
    query_bounds(keys_values, z, core, bounds_ref)

    stored = []

    def attend(z_at, core_at):
        count = len(stored)
        column[...] = key_column(keys_values, z_at, core_at)
        query = queries[...].reshape(4 * ROWS, HD)
        keys = keys_values[z_at, core_at, :, :ROWS, :HD].reshape(4 * ROWS, HD)
        values = keys_values[z_at, core_at, :, :ROWS, HD:].reshape(4 * ROWS, HD)
        scores = dot(keys, query, NT)
        codes = jnp.concatenate([column[...]] * (4 * ROWS // HD), axis=1)
        seen = visible(codes, bounds_ref[0:1, :], bounds_ref[1:2, :])
        scores = jnp.where(seen, scores, -1e30)
        top_before = top[0:1, :]
        top_now = jnp.maximum(top_before, jnp.max(scores, axis=0, keepdims=True))
        if count >= 2:
            stored[count - 2].wait()
        slot = weights.at[count % 2]
        slot[...] = jnp.exp2(scores - top_now).astype(bf16)
        shrink = jnp.exp2(top_before - top_now)
        norm[...] = norm[...] * shrink + dot(jnp.ones((8, 4 * ROWS), bf16), slot[...])
        top[0:1, :] = top_now
        acc[...] = acc[...] * shrink + dot(values, slot[...], TN)
        tops_ref[z_at, core_at] = jnp.broadcast_to(top_now, tops_ref.shape[2:])
        copy = pltpu.make_async_copy(
            slot, weights_ref.at[z_at, core_at], weight_sems.at[count % 2]
        )
        copy.start()
        stored.append(copy)

    low_far, high_far, twin_last, twin_next = [], [], [], []

    def onward(n):
        piece = pieces[n]
        from_last[n].wait_recv()
        block = keys_values.at[last_z, core, piece]
        low = block.at[pl.ds(0, ROWS // 2)]
        low_far.append(
            copies.start(low, low, above, keys_values.at[far_z, core, piece, pl.ds(0, ROWS // 2)])
        )
        twin_last.append(
            copies.start(block, block, twin, keys_values.at[last_z, 1 - core, piece])
        )
        from_next[n].wait_recv()
        block = keys_values.at[next_z, core, piece]
        high = block.at[pl.ds(ROWS // 2, ROWS // 2 + CODE_ROWS)]
        high_far.append(
            copies.start(
                high,
                high,
                below,
                keys_values.at[far_z, core, piece, pl.ds(ROWS // 2, ROWS // 2 + CODE_ROWS)],
            )
        )
        twin_next.append(
            copies.start(block, block, twin, keys_values.at[next_z, 1 - core, piece])
        )

    def take(arrivals):
        for arrival in arrivals:
            arrival.wait_recv()

    onward(0)
    w_onward(0)
    attend(z, core)
    onward(1)
    onward(2)
    take(from_twin)
    attend(z, 1 - core)
    onward(3)
    w_onward(1)
    attend(last_z, core)
    attend(next_z, core)
    w_onward(2)
    take(twin_last)
    attend(last_z, 1 - core)
    twin_far = []
    for n, piece in enumerate(pieces):
        low_far[n].wait_recv()
        high_far[n].wait_recv()
        block = keys_values.at[far_z, core, piece]
        twin_far.append(copies.start(block, block, twin, keys_values.at[far_z, 1 - core, piece]))
    take(twin_next)
    attend(next_z, 1 - core)
    w_onward(3)
    attend(far_z, core)
    take(twin_far)
    keep = pltpu.make_async_copy(keys_values, kv_all_ref, load_sems.at[2])
    keep.start()
    attend(far_z, 1 - core)

    total_norm = norm[0:1, :]
    attended = (acc[...] / total_norm).T
    o_low[...] = attended.astype(bf16).reshape(4, ROWS, HD)
    came_back = []
    for hop in HOPS:
        other = around(x, hop)
        came_back.append(
            copies.start(
                o_low.at[other],
                back.at[x],
                device(other, y, z, core),
                back.at[around(x, -hop)],
            )
        )
    back[x] = o_low[x]
    o_ref[...] = attended
    lse_ref[...] = jnp.broadcast_to(top[0:1, :] + jnp.log2(total_norm), lse_ref.shape)
    q_all_ref[...] = queries[...]
    for n in range(4):
        w_far[n].wait_recv()
        block = out_weight.at[y_far, core, n]
        w_twin.append(copies.start(block, block, twin, out_weight.at[y_far, 1 - core, n]))
    take(came_back)
    local = 4 * HD
    mine = pl.ds(pl.multiple_of(y * local, local), local)
    for n in range(4):
        gathered[y, :, n * HD : (n + 1) * HD] = back[n]
    spread_y = [
        copies.start(
            gathered.at[y],
            gathered.at[y],
            device(x, around(y, hop), z, core),
            gathered.at[around(y, -hop)],
        )
        for hop in HOPS
    ]
    returned_ref[...] = gathered[y]
    take(w_twin)
    take(spread_y)

    def project(index):
        at = slab(index, WIDE)
        total_ref[:, at] = sum(
            dot(gathered[n], out_weight[n, :, :, :, at].reshape(local, WIDE)) for n in range(4)
        ).astype(bf16)

    steps(total_ref.shape[1] // WIDE, project)
    copies.finish()
    keep.wait()
    keep_grad.wait()
    for copy in stored[-2:]:
        copy.wait()


def attention_forward(
    activations, labels, position, gains, cotangent, weight, out_weight, down_weight
):
    width = out_weight.shape[1]
    whole = pl.BlockSpec(memory_space=pltpu.VMEM)
    anywhere = pl.BlockSpec(memory_space=pl.ANY)
    count = 3 + 3 + 12 + 16 + 4 + 3 + 3 + 8 + 4 + 8 + 4
    pieces = (2, 4, out_weight.shape[0] // 8, width)
    return pl.pallas_call(
        forward_kernel,
        out_shape=[
            jax.ShapeDtypeStruct((4, ROWS, HD), bf16),
            jax.ShapeDtypeStruct((4, 2, 4, ROWS + CODE_ROWS, 2 * HD), bf16),
            jax.ShapeDtypeStruct((4 * ROWS, HD), f32),
            jax.ShapeDtypeStruct((8, 4 * ROWS), f32),
            jax.ShapeDtypeStruct((ROWS, 4 * HD), bf16),
            jax.ShapeDtypeStruct((ROWS, width), bf16),
            jax.ShapeDtypeStruct((ROWS, down_weight.shape[0]), f32),
            jax.ShapeDtypeStruct((4, 2, 4 * ROWS, 4 * ROWS), bf16),
            jax.ShapeDtypeStruct((4, 2, 8, 4 * ROWS), f32),
            jax.ShapeDtypeStruct((ROWS, HD), jnp.int32),
            jax.ShapeDtypeStruct((ROWS, HD), f32),
            jax.ShapeDtypeStruct((ROWS, HD), f32),
        ],
        in_specs=[whole] * 5 + [anywhere] * 3,
        out_specs=[whole, anywhere] + [whole] * 4 + [anywhere, anywhere] + [whole] * 4,
        scratch_shapes=[
            pltpu.VMEM((ROWS, down_weight.shape[0]), f32),
            pltpu.VMEM(weight.shape, bf16),
            pltpu.VMEM((4,) + pieces, bf16),
            pltpu.VMEM(down_weight.shape, bf16),
            pltpu.VMEM((2, 4 * ROWS, 4 * ROWS), bf16),
            pltpu.VMEM(activations.shape, bf16),
            pltpu.VMEM((4, ROWS, HD), bf16),
            pltpu.VMEM((4, ROWS + CODE_ROWS, 2 * HD), bf16),
            pltpu.VMEM((4, ROWS, HD), bf16),
            pltpu.VMEM((4, 2, 4, ROWS + CODE_ROWS, 2 * HD), bf16),
            pltpu.VMEM((8, 4 * ROWS), f32),
            pltpu.VMEM((8, 4 * ROWS), f32),
            pltpu.VMEM((HD, 4 * ROWS), f32),
            pltpu.VMEM((4 * ROWS, HD), jnp.int32),
            pltpu.VMEM((8, 4 * ROWS), jnp.int32),
            pltpu.VMEM((4, ROWS, HD), bf16),
            pltpu.VMEM((4, ROWS, HD), bf16),
            pltpu.VMEM((4, ROWS, 4 * HD), bf16),
            pltpu.SemaphoreType.DMA((count,)),
            pltpu.SemaphoreType.DMA((count,)),
            pltpu.SemaphoreType.DMA((5,)),
            pltpu.SemaphoreType.DMA((2,)),
        ],
        compiler_params=pltpu.CompilerParams(
            collective_id=0, has_side_effects=True, vmem_limit_bytes=VMEM_LIMIT
        ),
        name="attention_forward",
    )(
        activations,
        labels,
        position,
        gains,
        cotangent,
        weight,
        out_weight.reshape(pieces),
        down_weight,
    )


def gelu_and_slope(hidden):
    scale = math.sqrt(2.0 / math.pi)
    square = hidden * hidden
    bent = jnp.tanh(scale * hidden * (1.0 + 0.044715 * square))
    half = 0.5 * (1.0 + bent)
    slope = half + 0.5 * hidden * (1.0 - bent * bent) * (scale * (1.0 + 3 * 0.044715 * square))
    return hidden * half, slope


def middle_kernel(
    x_ref, attn_ref, labels_ref, gains_ref, cotangent_hbm, out_weight_hbm, grad_active_hbm, up_hbm, down_hbm,
    g_mid_hbm, g_low_hbm, heads_ref, mlp_hbm, active_left_hbm, gains_out_ref, grad_up_ref, grad_down_ref,
    up, down, cotangent, out_weight, grad_active, g_mid, g_low, mlp, active_left, xhat, inverse, normed, active,
    far, far_down, given, g_heads, came, all_rows, y_send, y_recv, load_sems, x_send, x_recv, *more,
):
    here = place()
    x, y, z, core = here
    arrived = greet(
        [device(x, around(y, hop), z, core) for hop in HOPS]
        + [device(around(x, hop), y, z, core) for hop in HOPS]
        + [device(x, y, around(z, hop), core) for hop in (1, 3)]
        + [device(x, y, z, 1 - core)]
    )
    up_scratch, down_scratch = more[:9], more[9:]
    both_left, both_right = up_scratch[:2]
    down_left, down_right = down_scratch[:2]
    used = [0]

    def move(src, dst):
        copy = pltpu.make_async_copy(src, dst, load_sems.at[used[0]])
        used[0] += 1
        copy.start()
        return copy

    load_up = move(up_hbm, up)
    load_active = move(grad_active_hbm, grad_active)
    load_part = move(
        cotangent_hbm.at[:, pl.ds(0, down_right.shape[1])], down_right.at[pl.ds(0, ROWS)]
    )
    load_down = move(down_hbm, down)
    load_cotangent = move(cotangent_hbm, cotangent)
    load_out = move(out_weight_hbm, out_weight)
    width = x_ref.shape[1]
    hidden_width = up.shape[1]

    def norm(index):
        at = slab(index, NORM_ROWS)
        middle = x_ref[at, :].astype(f32) + attn_ref[at, :].astype(f32)
        centred = middle - jnp.mean(middle, axis=-1, keepdims=True)
        scale = lax.rsqrt(jnp.mean(centred * centred, axis=-1, keepdims=True) + 1e-05)
        unit = centred * scale
        xhat[at, :] = unit
        inverse[at, :] = jnp.broadcast_to(scale, (NORM_ROWS, HD))
        normed[at, :] = (unit * gain_rows(labels_ref[at, :1], gains_ref, 3)).astype(bf16)

    steps(ROWS // NORM_ROWS, norm)
    rows = grad_up_ref.shape[0]
    for group in range(4):
        at = pl.ds(4 * group, 4)
        both_left[at, :, pl.ds(0, ROWS)] = pick(core, normed, rows, group).reshape(4, rows, ROWS)
        far[at] = pick(1 - core, normed, rows, group).reshape(4, rows, ROWS)
    load_up.wait()
    load_active.wait()

    def feed(index):
        at = slab(index, WIDE)
        hidden = dot(normed[...], up[:, at])
        value, slope = gelu_and_slope(hidden)
        active[:, at] = value.astype(bf16)
        both_right[pl.ds(0, ROWS), at] = (grad_active[:, at] * slope).astype(bf16)

    steps(hidden_width // WIDE, feed)
    arrived()
    ring = weight_grad(here, None, None, grad_up_ref, up_scratch, far)
    next(ring)

    copies = Copies(y_send, y_recv)
    half_steps = width // WIDE // 2
    over_y = []
    for half in range(2):

        def back_up(index, half=half):
            at = slab(index + half * half_steps, WIDE)
            part = dot(both_right[pl.ds(0, ROWS), :], up[at, :], NT)
            given[half, :, :, slab(index, WIDE)] = part.astype(bf16).reshape(
                SIDE, ROWS // SIDE, WIDE
            )

        steps(half_steps, back_up)
        over_y.append(
            sum_over_y(copies, here, given.at[half], came.at[half], all_rows.at[half])
        )
        next(over_y[half])
    next(ring)
    for group in range(4):
        at = pl.ds(4 * group, 4)
        for core_at in range(2):
            active_left[at, core_at] = pick(core_at, active, rows, group).reshape(4, rows, ROWS)
        down_left[at, :, pl.ds(0, ROWS)] = active_left[at, core]
        far_down[at] = active_left[at, 1 - core]
    load_part.wait()
    keep = [move(active_left, active_left_hbm)]
    ring_down = weight_grad(here, None, None, grad_down_ref, down_scratch, far_down)
    next(ring_down)
    load_down.wait()

    def feed_out(index, half):
        at = slab(index + half * half_steps, WIDE)
        mlp[half, :, :, slab(index, WIDE)] = (
            dot(active[...], down[:, at]).astype(bf16).reshape(SIDE, ROWS // SIDE, WIDE)
        )

    steps(half_steps, lambda index: feed_out(index, 0))
    next(over_y[0])
    next(ring_down)
    steps(half_steps, lambda index: feed_out(index, 1))
    keep.append(move(mlp, mlp_hbm))
    next(over_y[1])
    next(ring)
    next(ring)
    load_cotangent.wait()
    load_out.wait()
    gains_out_ref[...] = jnp.zeros_like(gains_out_ref)
    next(over_y[0])
    next(ring_down)
    next(ring)
    next(over_y[1])

    def back(index):
        at = slab(index, NORM_ROWS)
        grad = summed_rows(all_rows, index)
        labels = labels_ref[at, :1]
        unit = xhat[at, :]
        product = grad * unit
        for mode in range(3):
            gains_out_ref[mode + 3 : mode + 4, :] += jnp.sum(
                jnp.where(labels == mode, product, 0.0), axis=0, keepdims=True
            )
        gain = gain_rows(labels, gains_ref, 3)
        grad = grad * gain
        mean = jnp.mean(grad, axis=-1, keepdims=True)
        along = jnp.mean(product * gain, axis=-1, keepdims=True)
        total = cotangent[at, :].astype(f32) + inverse[at, :1] * (grad - mean - unit * along)
        g_mid[at, :] = total
        g_low[at, :] = total.astype(bf16)

    steps(ROWS // NORM_ROWS, back)
    by_head = dot(g_low[...], out_weight[...], NT).astype(bf16)
    for head in range(4):
        g_heads[head] = by_head[:, head * HD : (head + 1) * HD]
    x_copies = Copies(x_send, x_recv)
    arrivals = [
        x_copies.start(
            g_heads.at[around(x, hop)],
            heads_ref.at[x],
            device(around(x, hop), y, z, core),
            heads_ref.at[around(x, -hop)],
        )
        for hop in HOPS
    ]
    heads_ref[x] = g_heads[x]
    keep += [move(g_mid, g_mid_hbm), move(g_low, g_low_hbm)]
    next(ring_down)
    next(ring)
    next(ring_down)
    next(ring)
    next(ring_down)
    for arrival in arrivals:
        arrival.wait_recv()
    next(ring)
    next(ring_down)
    next(ring_down)
    copies.finish()
    x_copies.finish()
    for copy in keep:
        copy.wait()


def middle(
    activations, attn_sum, labels, gains, cotangent, out_weight, grad_active, up_weight, down_weight
):
    width, hidden_width = up_weight.shape
    rows = width // 32
    down_rows = hidden_width // 32
    whole = pl.BlockSpec(memory_space=pltpu.VMEM)
    anywhere = pl.BlockSpec(memory_space=pl.ANY)
    summed = (2, SIDE, ROWS // SIDE, width // 2)
    left = (16, 2, down_rows, ROWS)
    return pl.pallas_call(
        middle_kernel,
        out_shape=[
            jax.ShapeDtypeStruct((ROWS, width), f32),
            jax.ShapeDtypeStruct((ROWS, width), bf16),
            jax.ShapeDtypeStruct((4, ROWS, HD), bf16),
            jax.ShapeDtypeStruct(summed, bf16),
            jax.ShapeDtypeStruct(left, bf16),
            jax.ShapeDtypeStruct((8, width), f32),
            jax.ShapeDtypeStruct((rows, hidden_width), f32),
            jax.ShapeDtypeStruct((down_rows, width // 2), f32),
        ],
        in_specs=[whole] * 4 + [anywhere] * 5,
        out_specs=[anywhere] * 2 + [whole] + [anywhere] * 2 + [whole] * 3,
        scratch_shapes=[
            pltpu.VMEM(up_weight.shape, bf16),
            pltpu.VMEM(down_weight.shape, bf16),
            pltpu.VMEM((ROWS, width), bf16),
            pltpu.VMEM(out_weight.shape, bf16),
            pltpu.VMEM((ROWS, hidden_width), f32),
            pltpu.VMEM((ROWS, width), f32),
            pltpu.VMEM((ROWS, width), bf16),
            pltpu.VMEM(summed, bf16),
            pltpu.VMEM(left, bf16),
            pltpu.VMEM((ROWS, width), f32),
            pltpu.VMEM((ROWS, HD), f32),
            pltpu.VMEM((ROWS, width), bf16),
            pltpu.VMEM((ROWS, hidden_width), bf16),
            pltpu.VMEM((16, rows, ROWS), bf16),
            pltpu.VMEM((16, down_rows, ROWS), bf16),
            pltpu.VMEM(summed, bf16),
            pltpu.VMEM((4, ROWS, HD), bf16),
        ]
        + sum_scratch(width)
        + [pltpu.SemaphoreType.DMA((10,))]
        + [pltpu.SemaphoreType.DMA((3,)), pltpu.SemaphoreType.DMA((3,))]
        + weight_scratch(rows, hidden_width)
        + weight_scratch(down_rows, width // 2),
        compiler_params=pltpu.CompilerParams(
            collective_id=2, has_side_effects=True, vmem_limit_bytes=VMEM_LIMIT
        ),
        name="middle",
    )(
        activations,
        attn_sum,
        labels,
        gains,
        cotangent,
        out_weight,
        grad_active,
        up_weight,
        down_weight,
    )


def backward_kernel(
    grads, q_ref, kv_hbm, o_ref, lse_ref, tops_ref, weights_hbm, left_ref, right_ref, given_ref,
    packed_ref, weight_ref, total_ref,
    keys_values, weights, delta, grad_q, parts, met, came, sums, q_low, back_q,
    back_kv, send_sems, recv_sems, load_sems, weight_sems, y_came, all_rows, y_send, y_recv, *weight_scratch_refs,
):
    here = place()
    x, y, z, core = here
    twin = device(x, y, z, 1 - core)
    arrived = greet(
        [device(around(x, hop), y, z, core) for hop in HOPS]
        + [device(x, around(y, hop), z, core) for hop in HOPS]
        + [device(x, y, around(z, hop), core) for hop in (1, 3)]
        + [twin]
    )
    next_z, last_z, far_z = around(z, 1), around(z, -1), around(z, 2)
    order = [
        (at, core_at)
        for at in (far_z, next_z, last_z, z)
        for core_at in (1 - core, core)
    ]
    load = pltpu.make_async_copy(kv_hbm, keys_values, load_sems.at[0])
    load.start()

    def fetch(index):
        copy = pltpu.make_async_copy(
            weights_hbm.at[order[index][0], order[index][1]],
            weights.at[index % 3],
            weight_sems.at[index % 3],
        )
        copy.start()
        return copy

    fetched = [fetch(0), fetch(1)]
    copies = Copies(send_sems, recv_sems)
    y_copies = Copies(y_send, y_recv)
    over_y = [
        sum_over_y(y_copies, here, given_ref.at[half], y_came.at[half], all_rows.at[half])
        for half in range(2)
    ]
    half = weight_ref.shape[1]
    ring = weight_grad(
        here, left_ref, right_ref.at[:, pl.ds(half, half)], weight_ref, weight_scratch_refs
    )
    grad_q[...] = jnp.zeros_like(grad_q)
    product = grads[...].reshape(4 * ROWS, HD).astype(f32) * o_ref[...]
    delta[...] = lax.dot_general(
        jnp.ones((8, HD), f32), product, NT, preferred_element_type=f32, precision=highest
    )
    load.wait()
    arrived()
    next(ring)
    for half in over_y:
        next(half)
    done = []

    def chunk(z_at, core_at):
        index = len(done)
        done.append(index)
        if index + 2 < len(order):
            fetched.append(fetch(index + 2))
        fetched[index].wait()
        slot = weights.at[index % 3]
        query = q_ref[...].reshape(4 * ROWS, HD)
        grad = grads[...].reshape(4 * ROWS, HD)
        keys = keys_values[z_at, core_at, :, :ROWS, :HD].reshape(4 * ROWS, HD)
        values = keys_values[z_at, core_at, :, :ROWS, HD:].reshape(4 * ROWS, HD)
        rescale = jnp.exp2(tops_ref[z_at, core_at, 0:1, :] - lse_ref[0:1, :])
        grad_weights = dot(values, grad, NT)
        taken = slot[...].astype(f32) * rescale
        slot[...] = taken.astype(bf16)
        grad_v = dot(slot[...], grad)
        slot[...] = (taken * (grad_weights - delta[0:1, :])).astype(bf16)
        grad_k = dot(slot[...], query)
        grad_q[...] += dot(keys, slot[...], TN)
        parts[z_at, core_at] = (
            jnp.concatenate([grad_k * math.log(2.0), grad_v], axis=1)
            .astype(bf16)
            .reshape(2, 2 * ROWS, 2 * HD)
        )

    def hand_over(z_at):
        return copies.start(
            parts.at[z_at, 1 - core], met.at[z_at], twin, met.at[z_at]
        )

    def join(z_at):
        parts[z_at, core] = (
            parts[z_at, core].astype(f32) + met[z_at].astype(f32)
        ).astype(bf16)

    above, below = device(x, y, next_z, core), device(x, y, last_z, core)
    chunk(far_z, 1 - core)
    far_met = hand_over(far_z)
    next(ring)
    chunk(far_z, core)
    chunk(next_z, 1 - core)
    next_met = hand_over(next_z)
    far_met.wait_recv()
    join(far_z)
    from_last = copies.start(parts.at[far_z, core, 0], came.at[0], above, came.at[0])
    from_next = copies.start(parts.at[far_z, core, 1], came.at[1], below, came.at[1])
    chunk(next_z, core)
    next(ring)
    chunk(last_z, 1 - core)
    last_met = hand_over(last_z)
    next_met.wait_recv()
    join(next_z)
    raw_last = copies.start(parts.at[next_z, core, 1], came.at[2], above, came.at[2])
    for half in over_y:
        next(half)
    next(ring)
    chunk(last_z, core)
    chunk(z, 1 - core)
    own_met = hand_over(z)
    last_met.wait_recv()
    join(last_z)
    raw_next = copies.start(parts.at[last_z, core, 0], came.at[3], below, came.at[3])
    from_last.wait_recv()
    parts[next_z, core, 0] = (
        parts[next_z, core, 0].astype(f32) + came[0].astype(f32)
    ).astype(bf16)
    sum_last = copies.start(parts.at[next_z, core, 0], came.at[4], above, came.at[4])
    from_next.wait_recv()
    parts[last_z, core, 1] = (
        parts[last_z, core, 1].astype(f32) + came[1].astype(f32)
    ).astype(bf16)
    sum_next = copies.start(parts.at[last_z, core, 1], came.at[5], below, came.at[5])
    chunk(z, core)
    q_low[...] = (grad_q[...] * (HD**-0.5)).T.astype(bf16).reshape(4, ROWS, HD)
    arrivals = []
    for hop in HOPS:
        other = around(x, hop)
        arrivals.append(
            copies.start(
                q_low.at[other],
                back_q.at[x],
                device(other, y, z, core),
                back_q.at[around(x, -hop)],
            )
        )
    back_q[x] = q_low[x]
    next(ring)
    own_met.wait_recv()
    raw_last.wait_recv()
    raw_next.wait_recv()
    sum_last.wait_recv()
    sum_next.wait_recv()
    mine = parts[z, core].astype(f32) + met[z].astype(f32)
    low = mine[0] + came[4].astype(f32) + came[3].astype(f32)
    high = mine[1] + came[2].astype(f32) + came[5].astype(f32)
    sums[0:2] = low.astype(bf16).reshape(2, ROWS, 2 * HD)
    sums[2:4] = high.astype(bf16).reshape(2, ROWS, 2 * HD)
    for hop in HOPS:
        other = around(x, hop)
        arrivals.append(
            copies.start(
                sums.at[other],
                back_kv.at[x],
                device(other, y, z, core),
                back_kv.at[around(x, -hop)],
            )
        )
    back_kv[x] = sums[x]
    for half in over_y:
        next(half)
    total_ref[...] = all_rows[...]
    next(ring)
    next(ring)
    next(ring)
    for arrival in arrivals:
        arrival.wait_recv()
    for n in range(4):
        packed_ref[n, :, :HD] = back_q[n]
        packed_ref[n, :, HD:] = back_kv[n]
    copies.finish()
    y_copies.finish()


def attention_backward(grad_heads, q_all, kv_all, o_all, lse, tops, weights, left, right, given):
    whole = pl.BlockSpec(memory_space=pltpu.VMEM)
    anywhere = pl.BlockSpec(memory_space=pl.ANY)
    count = 4 + 6 + 6
    return pl.pallas_call(
        backward_kernel,
        out_shape=[
            jax.ShapeDtypeStruct((4, ROWS, 3 * HD), bf16),
            jax.ShapeDtypeStruct((left.shape[2], right.shape[1] // 2), f32),
            jax.ShapeDtypeStruct(given.shape, bf16),
        ],
        in_specs=[whole, whole, anywhere] + [whole] * 3 + [anywhere] * 3 + [whole],
        out_specs=[whole, whole, whole],
        scratch_shapes=[
            pltpu.VMEM((4, 2, 4, ROWS + CODE_ROWS, 2 * HD), bf16),
            pltpu.VMEM((3, 4 * ROWS, 4 * ROWS), bf16),
            pltpu.VMEM((8, 4 * ROWS), f32),
            pltpu.VMEM((HD, 4 * ROWS), f32),
            pltpu.VMEM((4, 2, 2, 2 * ROWS, 2 * HD), bf16),
            pltpu.VMEM((4, 2, 2 * ROWS, 2 * HD), bf16),
            pltpu.VMEM((6, 2 * ROWS, 2 * HD), bf16),
            pltpu.VMEM((4, ROWS, 2 * HD), bf16),
            pltpu.VMEM((4, ROWS, HD), bf16),
            pltpu.VMEM((4, ROWS, HD), bf16),
            pltpu.VMEM((4, ROWS, 2 * HD), bf16),
            pltpu.SemaphoreType.DMA((count,)),
            pltpu.SemaphoreType.DMA((count,)),
            pltpu.SemaphoreType.DMA((1,)),
            pltpu.SemaphoreType.DMA((3,)),
        ]
        + sum_scratch(2 * given.shape[3])
        + weight_scratch(left.shape[2], right.shape[1] // 2),
        compiler_params=pltpu.CompilerParams(
            collective_id=1, has_side_effects=True, vmem_limit_bytes=VMEM_LIMIT
        ),
        name="attention_backward",
    )(grad_heads, q_all, kv_all, o_all, lse, tops, weights, left, right, given)


def last_kernel(
    x_ref, labels_ref, gains_ref, returned_ref, packed_ref, cos_ref, sin_ref, gains_two_ref, g_low_hbm, attn_hbm,
    mlp_hbm, g_mid_hbm, weight_hbm,
    input_ref, layer_ref, gains_out_ref, grad_qkv_ref, grad_out_ref,
    attn, mlp, g_mid, weight, xhat, inverse, normed, far_qkv, far_out, given, gains_part, gains_given, came, all_rows, y_send, y_recv,
    load_sems, *more,
):
    gain_scratch = more[: len(GAIN_SCRATCH)]
    gain_send, gain_recv = more[len(GAIN_SCRATCH) : len(GAIN_SCRATCH) + 2]
    qkv_scratch = more[len(GAIN_SCRATCH) + 2 : len(GAIN_SCRATCH) + 11]
    out_scratch = more[len(GAIN_SCRATCH) + 11 :]
    here = place()
    x, y, z, core = here
    out_left, out_right = out_scratch[:2]
    loads = []
    for n, (src, dst) in enumerate(
        (
            (weight_hbm, weight),
            (g_low_hbm, out_right.at[pl.ds(0, ROWS)]),
            (attn_hbm, attn),
            (mlp_hbm, mlp),
            (g_mid_hbm, g_mid),
        )
    ):
        loads.append(pltpu.make_async_copy(src, dst, load_sems.at[n]))
        loads[n].start()
    arrived = greet(
        [device(x, around(y, hop), z, core) for hop in HOPS]
        + [device(around(x, hop), y, z, core) for hop in HOPS]
        + [device(x, y, around(z, hop), core) for hop in HOPS]
        + [device(x, y, z, 1 - core)]
    )
    width = x_ref.shape[1]
    local = returned_ref.shape[1]
    qkv_left, qkv_right = qkv_scratch[:2]
    qkv_rows, out_rows = grad_qkv_ref.shape[1], grad_out_ref.shape[0]

    cosine, sine = cos_ref[...], sin_ref[...]
    for head in range(4):
        for part in range(3):
            grad = packed_ref[head, :, part * HD : (part + 1) * HD]
            if part < 2:
                grad = grad.astype(f32)
                scaled = grad * sine
                grad = (
                    grad * cosine
                    + jnp.concatenate([scaled[:, HD // 2 :], -scaled[:, : HD // 2]], axis=1)
                ).astype(bf16)
            start = part * local + head * HD
            qkv_right[0:ROWS, start : start + HD] = grad

    def norm(index):
        at = slab(index, NORM_ROWS)
        rows = x_ref[at, :].astype(f32)
        centred = rows - jnp.mean(rows, axis=-1, keepdims=True)
        scale = lax.rsqrt(jnp.mean(centred * centred, axis=-1, keepdims=True) + 1e-05)
        unit = centred * scale
        xhat[at, :] = unit
        inverse[at, :] = jnp.broadcast_to(scale, (NORM_ROWS, HD))
        normed[at, :] = (unit * gain_rows(labels_ref[at, :1], gains_ref, 0)).astype(bf16)

    steps(ROWS // NORM_ROWS, norm)
    for group in range(4):
        at = pl.ds(4 * group, 4)
        qkv_left[at, :, pl.ds(0, ROWS)] = pick(core, normed, qkv_rows, group).reshape(
            4, qkv_rows, ROWS
        )
        far_qkv[at] = pick(1 - core, normed, qkv_rows, group).reshape(4, qkv_rows, ROWS)
    out_left[:, :, pl.ds(0, ROWS)] = pick(core, returned_ref, out_rows, 0).reshape(
        16, out_rows, ROWS
    )
    far_out[...] = pick(1 - core, returned_ref, out_rows, 0).reshape(16, out_rows, ROWS)
    arrived()
    rings = [
        weight_grad(here, None, None, grad_qkv_ref, qkv_scratch, far_qkv),
        weight_grad(here, None, None, grad_out_ref, out_scratch, far_out),
    ]
    loads[1].wait()
    for ring in rings:
        next(ring)
    loads[0].wait()
    gains_part[...] = 0.25 * gains_two_ref[...]
    copies = Copies(y_send, y_recv)
    half_steps = width // WIDE // 2
    over_y = []
    for half in range(2):

        def back_in(index, half=half):
            at = slab(index + half * half_steps, WIDE)
            part = sum(
                dot(qkv_right[pl.ds(0, ROWS), k * local : (k + 1) * local], weight[k, at, :], NT)
                for k in range(3)
            )
            given[half, :, :, slab(index, WIDE)] = part.astype(bf16).reshape(
                SIDE, ROWS // SIDE, WIDE
            )
            product = part * xhat[:, at]
            labels = labels_ref[:, :1]
            for mode in range(3):
                gains_part[mode : mode + 1, at] = jnp.sum(
                    jnp.where(labels == mode, product, 0.0), axis=0, keepdims=True
                )

        steps(half_steps, back_in)
        over_y.append(
            sum_over_y(copies, here, given.at[half], came.at[half], all_rows.at[half])
        )
        next(over_y[half])
    for owner in range(32):
        gains_given[owner // 8, (owner // 2) % 4, owner % 2] = jnp.zeros((8, HD), f32)
        gains_given[owner // 8, (owner // 2) % 4, owner % 2, :, :64] = gains_part[
            :, owner * 64 : (owner + 1) * 64
        ]
    gain_copies = Copies(gain_send, gain_recv)
    over_all = sum_gains(gain_copies, here, gains_given, *gain_scratch, gains_out_ref)
    next(over_all)
    for ring in rings:
        next(ring)
    for load in loads[2:]:
        load.wait()

    def finish_layer(index):
        at = slab(index, NORM_ROWS)
        total = x_ref[at, :].astype(f32) + attn[at, :].astype(f32) + summed_rows(mlp, index)
        layer_ref[at, :] = total.astype(bf16)

    steps(ROWS // NORM_ROWS, finish_layer)
    next(over_y[0])
    for ring in rings:
        next(ring)
    next(over_all)
    next(over_y[1])
    for step in range(2):
        for ring in rings:
            next(ring)
    next(over_y[0])
    for ring in rings:
        next(ring)
    next(over_all)
    next(over_y[1])

    def finish_input(index):
        at = slab(index, NORM_ROWS)
        unit = xhat[at, :]
        grad = summed_rows(all_rows, index) * gain_rows(labels_ref[at, :1], gains_ref, 0)
        mean = jnp.mean(grad, axis=-1, keepdims=True)
        along = jnp.mean(grad * unit, axis=-1, keepdims=True)
        input_ref[at, :] = g_mid[at, :] + inverse[at, :1] * (grad - mean - unit * along)

    steps(ROWS // NORM_ROWS, finish_input)
    for ring in rings:
        next(ring)
    next(over_all)
    for ring in rings:
        next(ring)
    next(over_all)
    copies.finish()
    gain_copies.finish()


def last(
    activations, labels, gains, returned, packed, cosine, sine, gains_two, g_low, attn_sum, mlp_sum, g_mid, weight
):
    width = activations.shape[1]
    local = returned.shape[1]
    cols = 3 * local
    rows = width // 32
    whole = pl.BlockSpec(memory_space=pltpu.VMEM)
    anywhere = pl.BlockSpec(memory_space=pl.ANY)
    return pl.pallas_call(
        last_kernel,
        out_shape=[
            jax.ShapeDtypeStruct((ROWS, width), f32),
            jax.ShapeDtypeStruct((ROWS, width), bf16),
            jax.ShapeDtypeStruct((8, HD), f32),
            jax.ShapeDtypeStruct((3, rows, local), f32),
            jax.ShapeDtypeStruct((local // 32, width), f32),
        ],
        in_specs=[whole] * 8 + [anywhere] * 5,
        out_specs=[whole] * 5,
        scratch_shapes=[
            pltpu.VMEM(attn_sum.shape, bf16),
            pltpu.VMEM(mlp_sum.shape, bf16),
            pltpu.VMEM(g_mid.shape, f32),
            pltpu.VMEM(weight.shape, bf16),
            pltpu.VMEM((ROWS, width), f32),
            pltpu.VMEM((ROWS, HD), f32),
            pltpu.VMEM((ROWS, width), bf16),
            pltpu.VMEM((16, rows, ROWS), bf16),
            pltpu.VMEM((16, local // 32, ROWS), bf16),
            pltpu.VMEM(mlp_sum.shape, bf16),
            pltpu.VMEM((8, width), f32),
            pltpu.VMEM((4, 4, 2, 8, HD), f32),
        ]
        + sum_scratch(width)
        + [pltpu.SemaphoreType.DMA((5,))]
        + [pltpu.VMEM(shape, f32) for shape in GAIN_SCRATCH]
        + [pltpu.SemaphoreType.DMA((10,)), pltpu.SemaphoreType.DMA((10,))]
        + weight_scratch(rows, cols)
        + weight_scratch(local // 32, width),
        compiler_params=pltpu.CompilerParams(
            collective_id=3, has_side_effects=True, vmem_limit_bytes=VMEM_LIMIT
        ),
        name="last",
    )(
        activations,
        labels,
        gains,
        returned,
        packed,
        cosine,
        sine,
        gains_two,
        g_low,
        attn_sum,
        mlp_sum,
        g_mid,
        weight,
    )


def finish_kernel(
    share_ref, layer_in, input_in, qkv_in, out_in, up_in, low_in, high_in,
    gains_ref, layer_out, input_out, qkv_out, out_out, up_out, down_out,
    layer, grad_input, qkv, out, up, low, high, load_sems, store_sems,
):
    half = low_in.shape[1]
    ways = (
        (layer_in, layer, layer_out),
        (up_in, up, up_out),
        (qkv_in, qkv, qkv_out),
        (low_in, low, down_out.at[:, pl.ds(0, half)]),
        (high_in, high, down_out.at[:, pl.ds(half, half)]),
        (out_in, out, out_out),
        (input_in, grad_input, input_out),
    )
    loads = [
        pltpu.make_async_copy(src, held, load_sems.at[n]) for n, (src, held, dst) in enumerate(ways)
    ]
    stores = [
        pltpu.make_async_copy(held, dst, store_sems.at[n]) for n, (src, held, dst) in enumerate(ways)
    ]
    for load in loads:
        load.start()
    gains_ref[...] = share_ref[: gains_ref.shape[0], : gains_ref.shape[1]]
    for load, store in zip(loads, stores):
        load.wait()
        store.start()
    for store in stores:
        store.wait()


def finish(modes, share, layer, grad_input, qkv, out, up, low, high):
    whole = pl.BlockSpec(memory_space=pltpu.VMEM)
    anywhere = pl.BlockSpec(memory_space=pl.ANY)
    results = [
        jax.ShapeDtypeStruct(array.shape, array.dtype) for array in (layer, grad_input, qkv, out, up)
    ]
    results.append(jax.ShapeDtypeStruct((low.shape[0], 2 * low.shape[1]), f32))
    return pl.pallas_call(
        finish_kernel,
        out_shape=[jax.ShapeDtypeStruct((2 * modes, layer.shape[1] // 32), f32)] + results,
        in_specs=[whole] + [anywhere] * 7,
        out_specs=[whole] + [anywhere] * 6,
        scratch_shapes=[
            pltpu.VMEM(array.shape, array.dtype)
            for array in (layer, grad_input, qkv, out, up, low, high)
        ]
        + [pltpu.SemaphoreType.DMA((7,)), pltpu.SemaphoreType.DMA((7,))],
        name="finish",
    )(share, layer, grad_input, qkv, out, up, low, high)


def per_device(
    activations,
    labels,
    position,
    norm_gains,
    qkv_weight,
    out_weight,
    up_weight,
    down_weight,
    cotangent,
):
    projections = qkv_weight.transpose(1, 0, 2)
    (
        q_all,
        kv_all,
        o_all,
        lse,
        returned,
        attn_sum,
        grad_active,
        weights,
        tops,
        label_rows,
        cosine,
        sine,
    ) = attention_forward(
        activations,
        labels.reshape(1, ROWS),
        position.reshape(1, ROWS),
        norm_gains,
        cotangent,
        projections,
        out_weight,
        down_weight,
    )
    g_mid, g_low, grad_heads, mlp_part, active_left, gains_two, grad_up, down_low = middle(
        activations,
        attn_sum,
        label_rows,
        norm_gains,
        cotangent,
        out_weight,
        grad_active,
        up_weight,
        down_weight,
    )
    packed, down_high, mlp_sum = attention_backward(
        grad_heads, q_all, kv_all, o_all, lse, tops, weights, active_left, cotangent, mlp_part
    )
    grad_input, layer_out, share, grad_qkv, grad_out = last(
        activations,
        label_rows,
        norm_gains,
        returned,
        packed,
        cosine,
        sine,
        gains_two,
        g_low,
        attn_sum,
        mlp_sum,
        g_mid,
        projections,
    )
    grad_gains, layer_out, grad_input, grad_qkv, grad_out, grad_up, grad_down = finish(
        norm_gains.shape[0] // 2,
        share,
        layer_out,
        grad_input,
        grad_qkv,
        grad_out,
        grad_up,
        down_low,
        down_high,
    )
    return (
        layer_out,
        grad_input,
        grad_gains,
        grad_qkv.transpose(1, 0, 2),
        grad_out,
        grad_up,
        grad_down,
    )


def solution(mesh):
    return jax.shard_map(
        per_device,
        mesh=mesh,
        in_specs=(
            P("tok", None),
            P("tok"),
            P("tok"),
            P(),
            P(None, None, "head"),
            P("head", None),
            P(None, "head"),
            P("head", None),
            P("tok", None),
        ),
        out_specs=(
            P("tok", None),
            P("tok", None),
            P(None, "tok"),
            P("tok", None, "head"),
            P(("head", "tok"), None),
            P("tok", "head"),
            P(("head", "tok"), None),
        ),
        check_vma=False,
    )
```

```python
import functools
import math

import jax
import jax.numpy as jnp
from jax import lax
from jax.experimental import pallas as pl
from jax.experimental.pallas import tpu as pltpu
from jax.sharding import PartitionSpec as P

HD = 128
SIDE = 4
ROWS = 256
CODE_ROWS = 16
CLIP_STEP = 8192
MESH = pl.DeviceIdType.MESH
NT = (((1,), (1,)), ((), ()))
TN = (((0,), (0,)), ((), ()))
NN = (((1,), (0,)), ((), ()))
f32 = jnp.float32
bf16 = jnp.bfloat16
highest = lax.Precision.HIGHEST
VMEM_LIMIT = 60 << 20
HOPS = (1, 3, 2)


def dot(lhs, rhs, dims=NN):
    return lax.dot_general(lhs, rhs, dims, preferred_element_type=f32)


def place():
    tok = lax.axis_index("tok")
    return (lax.div(tok, 8), lax.axis_index("head"), lax.rem(lax.div(tok, 2), 4), lax.rem(tok, 2))


def around(index, step):
    return lax.rem(index + (step % SIDE), SIDE)


def device(x, y, z, core):
    return (x * 8 + z * 2 + core, y)


def remote(src, dst, send_sem, recv_sem, target):
    return pltpu.make_async_remote_copy(
        src_ref=src,
        dst_ref=dst,
        send_sem=send_sem,
        recv_sem=recv_sem,
        device_id=target,
        device_id_type=MESH,
    )


def greet(targets):
    barrier = pltpu.get_barrier_semaphore()
    for target in targets:
        pl.semaphore_signal(barrier, inc=1, device_id=target, device_id_type=MESH)
    return lambda: pl.semaphore_wait(barrier, len(targets))


class Copies:
    def __init__(self, send_sems, recv_sems):
        self.send_sems = send_sems
        self.recv_sems = recv_sems
        self.used = 0
        self.open = []

    def start(self, src, dst, target, landing):
        index = self.used
        self.used += 1
        copy = remote(src, dst, self.send_sems.at[index], self.recv_sems.at[index], target)
        copy.start()
        self.open.append(copy)
        return remote(landing, landing, self.send_sems.at[index], self.recv_sems.at[index], target)

    def finish(self):
        for copy in self.open:
            copy.wait_send()


def advance(steps_left, count=1):
    for _ in range(count):
        next(steps_left)


def ring_sum(copies, own, towards, source, block, slots):
    up, down = towards(1), towards(-1)
    from_down = copies.start(source(2, 0), slots.at[0], up, slots.at[0])
    from_up = copies.start(source(2, 1), slots.at[1], down, slots.at[1])
    raw_down = copies.start(source(1, 1), slots.at[2], up, slots.at[2])
    raw_up = copies.start(source(-1, 0), slots.at[3], down, slots.at[3])
    yield
    from_down.wait_recv()
    slots[0] = (block(1, 0)[...].astype(f32) + slots[0].astype(f32)).astype(bf16)
    sum_down = copies.start(slots.at[0], slots.at[4], up, slots.at[4])
    from_up.wait_recv()
    slots[1] = (block(-1, 1)[...].astype(f32) + slots[1].astype(f32)).astype(bf16)
    sum_up = copies.start(slots.at[1], slots.at[5], down, slots.at[5])
    yield
    for arrival in (raw_down, raw_up, sum_down, sum_up):
        arrival.wait_recv()

    def finished(half):
        mine = block(0, half)[...].astype(f32)
        if half == 0:
            return mine + slots[4].astype(f32) + slots[3].astype(f32)
        return mine + slots[2].astype(f32) + slots[5].astype(f32)

    own.append(finished)


def sum_over_y(copies, here, given, came, total):
    x, y, z, core = here
    rows = given.shape[1] // 2
    halves = (pl.ds(0, rows), pl.ds(rows, rows))

    def towards(step):
        return device(x, around(y, step), z, core)

    def block(step, half):
        return given.at[around(y, step), halves[half]]

    done = []
    ring = ring_sum(copies, done, towards, block, block, came)
    next(ring)
    yield
    next(ring)
    yield
    next(ring, None)
    for half in range(2):
        total[y, halves[half]] = done[0](half).astype(bf16)
    last_y, next_y, far_y = around(y, -1), around(y, 1), around(y, 2)
    mine = total.at[y]
    from_last = copies.start(mine, mine, towards(1), total.at[last_y])
    from_next = copies.start(mine, mine, towards(-1), total.at[next_y])
    yield
    from_last.wait_recv()
    part = total.at[last_y, halves[0]]
    far_low = copies.start(part, part, towards(1), total.at[far_y, halves[0]])
    from_next.wait_recv()
    part = total.at[next_y, halves[1]]
    far_high = copies.start(part, part, towards(-1), total.at[far_y, halves[1]])
    yield
    far_low.wait_recv()
    far_high.wait_recv()
    yield


def sum_scratch(width):
    quarter = ROWS // SIDE
    return [
        pltpu.VMEM((2, 6, quarter // 2, width // 2), bf16),
        pltpu.VMEM((2, SIDE, quarter, width // 2), bf16),
        pltpu.SemaphoreType.DMA((20,)),
        pltpu.SemaphoreType.DMA((20,)),
    ]


def summed_rows(all_rows, index):
    part = lax.div(index, SIDE // 2)
    start = pl.multiple_of(lax.rem(index, SIDE // 2) * NORM_ROWS, NORM_ROWS)
    halves = [all_rows[half, part, pl.ds(start, NORM_ROWS), :] for half in range(2)]
    return jnp.concatenate(halves, axis=1).astype(f32)


WAYS = (0, 1, 0, 1)
DOWN_WAYS = (0, 1, 0, 0)


def ring_shapes(rows, cols):
    if rows >= 32:
        width = cols // 4
        return 4, (2 * rows, width), (rows // 2, width)
    return 2, (4 * rows, cols // 4), (rows, cols // 4)


def factor_scratch(rows, cols):
    return [pltpu.VMEM((16, rows, 2 * ROWS), bf16), pltpu.VMEM((2 * ROWS, cols), bf16)]


def weight_scratch(rows, cols):
    groups, first, late = ring_shapes(rows, cols)
    return [
        pltpu.VMEM((groups, 4, 2) + first, bf16),
        pltpu.VMEM((groups, 6) + first, bf16),
        pltpu.VMEM((groups, 4, 2) + late, bf16),
        pltpu.VMEM((groups, 6) + late, bf16),
        pltpu.SemaphoreType.DMA((2 + 12 * groups,)),
        pltpu.SemaphoreType.DMA((2 + 12 * groups,)),
        pltpu.SemaphoreType.DMA((2 + 4 * groups,)),
    ]


def store_part(out, row, start, value):
    rows = slice(row, row + value.shape[0])
    if len(out.shape) == 2:
        out[rows, start : start + value.shape[1]] = value
        return
    size, done = out.shape[2], 0
    while done < value.shape[1]:
        block, offset = divmod(start + done, size)
        count = min(size - offset, value.shape[1] - done)
        out[block, rows, offset : offset + count] = value[:, done : done + count]
        done += count


def pick(core_at, factor, rows, group):
    row = lax.broadcasted_iota(jnp.int32, (256, 512), 0)
    col = lax.broadcasted_iota(jnp.int32, (256, 512), 1)
    wanted = lax.div(row, rows) * (2 * rows) + core_at * rows + lax.rem(row, rows)
    chosen = jnp.where(col == wanted, 1.0, 0.0).astype(bf16)
    return dot(chosen, factor[:, 512 * group : 512 * (group + 1)], NT).astype(bf16)


def partial_block(both_left, both_right, way, at, group, width):
    rows = both_left.shape[1]
    if way == 0:
        chosen = both_left[pl.ds(at * 4, 4)].reshape(4 * rows, 2 * ROWS)
    else:
        chosen = jnp.concatenate([both_left[k * 4 + at] for k in range(4)], axis=0)
    return dot(chosen, both_right[:, group * width : (group + 1) * width]).astype(bf16)


def weight_grad(here, out, scratch, factors=None, far=None, left=None, right=None, parts_hbm=None, ways=WAYS,
                ready=None):
    parts, came, sums, late, send_sems, recv_sems, own_sems = scratch
    x, y, z, core = here
    copies = Copies(send_sems, recv_sems)
    twin = device(x, y, z, 1 - core)
    groups = parts.shape[0]
    rows = out.shape[-2]
    by_rows = groups == 4
    first_shape, late_shape = parts.shape[3:], late.shape[2:]
    width = first_shape[1] if by_rows else 2 * first_shape[1]

    def spot(way, step):
        return around(x if way == 0 else z, step)

    def towards(way):
        def target(step):
            if way == 0:
                return device(around(x, step), y, z, core)
            return device(x, y, around(z, step), core)

        return target

    waits = []
    if parts_hbm is None:
        both_left, both_right = factors
    if parts_hbm is None and ready is None:
        if left is not None:
            far = left.at[:, 1 - core]
            own = pltpu.make_async_copy(
                left.at[:, core], both_left.at[:, :, pl.ds(0, ROWS)], own_sems.at[0]
            )
            own.start()
            waits.append(own.wait)
        if right is not None:
            own = pltpu.make_async_copy(right, both_right.at[pl.ds(0, ROWS)], own_sems.at[1])
            own.start()
            waits.append(own.wait)
        else:
            right = both_right.at[pl.ds(0, ROWS)]
        if far is not None:
            theirs = both_left.at[:, :, pl.ds(ROWS, ROWS)]
            waits.append(copies.start(far, theirs, twin, theirs).wait_recv)
        theirs = both_right.at[pl.ds(ROWS, ROWS)]
        waits.append(copies.start(right, theirs, twin, theirs).wait_recv)
    elif ready is None:
        for group in range(groups):
            for n, (step, half_index) in enumerate(((1, 0), (-1, 1), (0, 0), (0, 1))):
                at = spot(ways[group], step)
                own = pltpu.make_async_copy(
                    parts_hbm.at[group, at, half_index],
                    parts.at[group, at, half_index],
                    own_sems.at[2 + 4 * group + n],
                )
                own.start()
                waits.append(own.wait)
    yield

    def fill(group, step):
        at = spot(ways[group], step)
        value = partial_block(both_left, both_right, ways[group], at, group, width)
        if by_rows:
            parts[group, at] = value.reshape((2,) + first_shape)
        else:
            for half_index in range(2):
                parts[group, at, half_index] = value[
                    :, half_index * first_shape[1] : (half_index + 1) * first_shape[1]
                ]

    if parts_hbm is None:
        for wait in waits:
            wait()
        waits = []
    source = parts if parts_hbm is None else parts_hbm
    first, first_done, second, second_done = {}, {}, {}, {}
    for group in range(4):
        if group >= groups:
            yield
            continue
        if ready is not None:
            ready(group)
        if parts_hbm is None:
            for step in (2, 1, -1):
                fill(group, step)
        first_done[group] = []
        first[group] = ring_sum(
            copies,
            first_done[group],
            towards(ways[group]),
            lambda step, half, group=group: source.at[group, spot(ways[group], step), half],
            lambda step, half, group=group: parts.at[group, spot(ways[group], step), half],
            came.at[group],
        )
        next(first[group])
        yield
    if parts_hbm is None:
        for group in range(groups):
            fill(group, 0)
    for wait in waits:
        wait()
    yield
    stages = [range(groups // 2), range(groups // 2, groups)] if by_rows else [range(groups), ()]
    for stage in stages:
        for group in stage:
            next(first[group])
        yield
    for stage in stages:
        for group in stage:
            next(first[group], None)
            for half_index in (0, 1):
                value = first_done[group][0](half_index).astype(bf16)
                if by_rows:
                    sums[group, 2 * half_index : 2 * half_index + 2] = value.reshape(
                        (2, 2) + late_shape
                    )
                else:
                    sums[group, :, half_index] = value.reshape((4,) + late_shape)
            second_done[group] = []

            def block(step, half, group=group):
                return sums.at[group, spot(1 - ways[group], step), half]

            second[group] = ring_sum(
                copies,
                second_done[group],
                towards(1 - ways[group]),
                block,
                block,
                late.at[group],
            )
            next(second[group])
        yield
    for group in range(groups):
        next(second[group])
    yield
    for group in range(groups):
        next(second[group], None)
        for half_index in (0, 1):
            value = second_done[group][0](half_index)
            if by_rows:
                store_part(out, half_index * late_shape[0], group * width, value)
            else:
                store_part(out, 0, group * width + half_index * late_shape[1], value)
    copies.finish()
    yield


def sum_gains(copies, here, given, came_x, part_x, came_z, part_z, came_core, part, came_y, out):
    x, y, z, core = here
    arrivals = [
        copies.start(
            given.at[around(x, hop)], came_x.at[n], device(around(x, hop), y, z, core), came_x.at[n]
        )
        for n, hop in enumerate(HOPS)
    ]
    yield
    for arrival in arrivals:
        arrival.wait_recv()
    part_x[...] = (given[x] + came_x[0]) + (came_x[1] + came_x[2])
    arrivals = [
        copies.start(
            part_x.at[around(z, hop)], came_z.at[n], device(x, y, around(z, hop), core), came_z.at[n]
        )
        for n, hop in enumerate(HOPS)
    ]
    yield
    for arrival in arrivals:
        arrival.wait_recv()
    part_z[...] = (part_x[z] + came_z[0]) + (came_z[1] + came_z[2])
    arrival = copies.start(part_z.at[1 - core], came_core, device(x, y, z, 1 - core), came_core)
    yield
    arrival.wait_recv()
    part[...] = part_z[core] + came_core[...]
    arrivals = [
        copies.start(part, came_y.at[n], device(x, around(y, hop), z, core), came_y.at[n])
        for n, hop in enumerate(HOPS)
    ]
    yield
    for arrival in arrivals:
        arrival.wait_recv()
    out[...] = (part[...] + came_y[0]) + (came_y[1] + came_y[2])
    yield


GAIN_SCRATCH = [(3, 4, 2, 8, HD), (4, 2, 8, HD), (3, 2, 8, HD), (2, 8, HD), (8, HD), (8, HD), (3, 8, HD)]


NORM_ROWS = 32
WIDE = 512


def gain_rows(labels, gains, first):
    return jnp.where(
        labels == 0,
        gains[first : first + 1, :],
        jnp.where(labels == 1, gains[first + 1 : first + 2, :], gains[first + 2 : first + 3, :]),
    )


def steps(count, body):
    lax.fori_loop(0, count, lambda index, carry: (body(index), carry)[1], 0)


def slab(index, size):
    return pl.ds(pl.multiple_of(index * size, size), size)


def visible(key_codes, low, span):
    return (key_codes - low).astype(jnp.uint32) <= span.astype(jnp.uint32)


def key_column(keys_values, z_at, core_at):
    codes = jnp.concatenate(
        [keys_values[z_at, core_at, n, ROWS:, :] for n in range(4)], axis=1
    )
    row = lax.broadcasted_iota(jnp.int32, (CODE_ROWS, HD), 0)
    weight = jnp.where(row == 0, 128.0, jnp.where(row == 1, 1.0, 0.0)).astype(bf16)
    return dot(codes, weight, TN).astype(jnp.int32)


def query_bounds(keys_values, z, core, bounds):
    for n in range(4):
        digits = keys_values[z, core, n, ROWS:, :].astype(f32)
        code = (digits[0:1] * 128.0 + digits[1:2]).astype(jnp.int32)
        low = jnp.where(code >= CLIP_STEP, CLIP_STEP, 0)
        bounds[0:1, n * ROWS : (n + 1) * ROWS] = low
        bounds[1:2, n * ROWS : (n + 1) * ROWS] = code - low


def forward_kernel(
    x_ref, label_ref, position_ref, gains_ref, cotangent_ref, weight_hbm, out_weight_hbm, down_hbm,
    q_all_ref, kv_all_ref, o_ref, lse_ref, out_left_ref, total_ref, grad_active_hbm, weights_ref, tops_ref, labels_ref,
    cos_ref, sin_ref, qkv_left_hbm, cotangent_both,
    own_left, far_left, grad_active_ref, weight, out_weight, down, weights, normed, q_own, kv_own, queries, keys_values, top, norm, acc, column, bounds_ref, o_low, back,
    gathered, send_sems, recv_sems, load_sems, weight_sems,
):
    here = place()
    x, y, z, core = here
    twin = device(x, y, z, 1 - core)
    arrived = greet(
        [device(around(x, hop), y, z, core) for hop in HOPS]
        + [device(x, around(y, hop), z, core) for hop in HOPS]
        + [device(x, y, around(z, hop), core) for hop in (1, 3)]
        + [twin]
    )
    load_out = pltpu.make_async_copy(out_weight_hbm, out_weight.at[y], load_sems.at[0])
    load_out.start()
    load = pltpu.make_async_copy(weight_hbm, weight, load_sems.at[1])
    load.start()
    load_down = pltpu.make_async_copy(down_hbm, down, load_sems.at[3])
    copies = Copies(send_sems, recv_sems)

    position = position_ref[...]
    block, row = lax.shift_right_logical(position, 8), lax.bitwise_and(position, 255)
    second = row >= 192
    spot = jnp.where(second, block * 64 + row - 192, block * 192 + row)
    code = spot + jnp.where(second, CLIP_STEP, 0)
    kind = lax.broadcasted_iota(jnp.int32, (CODE_ROWS, ROWS), 0)
    digits = jnp.where(
        kind == 0,
        lax.shift_right_logical(code, 7),
        jnp.where(kind == 1, lax.bitwise_and(code, 127), 0),
    )
    digits = digits.astype(f32).astype(bf16)
    kind = lax.broadcasted_iota(jnp.int32, (8, ROWS), 0)
    small = jnp.where(
        kind == 0,
        lax.shift_right_logical(spot, 7),
        jnp.where(kind == 1, lax.bitwise_and(spot, 127), jnp.where(kind == 2, label_ref[...], 0)),
    )
    small = small.astype(f32).astype(bf16)
    kind = lax.broadcasted_iota(jnp.int32, (8, HD), 0)
    spot_weight = jnp.where(kind == 0, 128.0, jnp.where(kind == 1, 1.0, 0.0)).astype(bf16)
    label_weight = jnp.where(kind == 2, 1.0, 0.0).astype(bf16)
    labels_ref[...] = dot(small, label_weight, TN).astype(jnp.int32)
    feature = lax.rem(lax.broadcasted_iota(jnp.int32, (1, HD), 1), HD // 2).astype(f32)
    angle = dot(small, spot_weight, TN) * jnp.exp(feature * (-2.0 * math.log(10000.0) / HD))
    cos_ref[...] = jnp.cos(angle)
    sin_ref[...] = jnp.sin(angle)

    def normalise(index):
        at = slab(index, NORM_ROWS)
        rows = x_ref[at, :].astype(f32)
        centred = rows - jnp.mean(rows, axis=-1, keepdims=True)
        scale = lax.rsqrt(jnp.mean(centred * centred, axis=-1, keepdims=True) + 1e-05)
        normed[at, :] = (centred * scale * gain_rows(labels_ref[at, :1], gains_ref, 0)).astype(
            bf16
        )

    steps(ROWS // NORM_ROWS, normalise)
    arrived()
    load_out.wait()
    y_up, y_down = device(x, around(y, 1), z, core), device(x, around(y, -1), z, core)
    y_next, y_last, y_far = around(y, 1), around(y, -1), around(y, 2)
    w_last, w_next, w_far, w_twin = [], [], [None] * 4, []
    for n in range(4):
        block = out_weight.at[y, core, n]
        w_last.append(copies.start(block, block, y_up, out_weight.at[y_last, core, n]))
        w_next.append(copies.start(block, block, y_down, out_weight.at[y_next, core, n]))

    def w_onward(n):
        w_last[n].wait_recv()
        block = out_weight.at[y_last, core, n]
        if n < 2:
            w_far[n] = copies.start(block, block, y_up, out_weight.at[y_far, core, n])
        w_twin.append(copies.start(block, block, twin, out_weight.at[y_last, 1 - core, n]))
        w_next[n].wait_recv()
        block = out_weight.at[y_next, core, n]
        if n >= 2:
            w_far[n] = copies.start(block, block, y_down, out_weight.at[y_far, core, n])
        w_twin.append(copies.start(block, block, twin, out_weight.at[y_next, 1 - core, n]))

    load.wait()
    load_down.start()
    cosine, sine = cos_ref[...], sin_ref[...]

    def rotate(values, head):
        part = values[:, head * HD : (head + 1) * HD]
        turned = jnp.concatenate([-part[:, HD // 2 :], part[:, : HD // 2]], axis=1)
        return part * cosine + turned * sine

    key_part = dot(normed[...], weight[1])
    for head in range(4):
        kv_own[head, :ROWS, :HD] = rotate(key_part, head).astype(bf16)
        kv_own[head, ROWS:, :] = digits
    value_part = dot(normed[...], weight[2])
    for head in range(4):
        kv_own[head, :ROWS, HD:] = value_part[:, head * HD : (head + 1) * HD].astype(bf16)
    kv_came, q_came = [None] * 3, [None] * 3

    def send_kv(n):
        other = around(x, HOPS[n])
        kv_came[n] = copies.start(
            kv_own.at[other],
            keys_values.at[z, core, x],
            device(other, y, z, core),
            keys_values.at[z, core, around(x, -HOPS[n])],
        )

    send_kv(0)
    send_kv(1)
    query_part = dot(normed[...], weight[0]) * (HD**-0.5 / math.log(2.0))
    for head in range(4):
        q_own[head] = rotate(query_part, head).astype(bf16)
    for n, hop in enumerate(HOPS):
        other = around(x, hop)
        q_came[n] = copies.start(
            q_own.at[other],
            queries.at[x],
            device(other, y, z, core),
            queries.at[around(x, -hop)],
        )
    send_kv(2)
    keys_values[z, core, x] = kv_own[x]
    queries[x] = q_own[x]
    above, below = device(x, y, around(z, 1), core), device(x, y, around(z, -1), core)
    next_z, last_z, far_z = around(z, 1), around(z, -1), around(z, 2)
    pieces = [x] + [around(x, -hop) for hop in HOPS]
    from_last, from_next, from_twin = [], [], []

    def spread(n):
        block = keys_values.at[z, core, pieces[n]]
        from_last.append(copies.start(block, block, above, keys_values.at[last_z, core, pieces[n]]))
        from_next.append(copies.start(block, block, below, keys_values.at[next_z, core, pieces[n]]))
        from_twin.append(copies.start(block, block, twin, keys_values.at[z, 1 - core, pieces[n]]))

    spread(0)
    top[...] = jnp.full_like(top, -1e30)
    norm[...] = jnp.zeros_like(norm)
    acc[...] = jnp.zeros_like(acc)
    load_down.wait()

    def grad_active(index):
        at = slab(index, WIDE)
        grad_active_ref[:, at] = dot(cotangent_ref[...], down[at, :], NT)

    keep_more = [
        pltpu.make_async_copy(
            cotangent_ref, cotangent_both.at[pl.ds(0, ROWS)], load_sems.at[5]
        )
    ]
    theirs = cotangent_both.at[pl.ds(ROWS, ROWS)]
    for_twin = [copies.start(cotangent_ref, theirs, twin, theirs)]
    rows = far_left.shape[1]
    for group in range(4):
        at = pl.ds(4 * group, 4)
        own_left[at] = pick(core, normed, rows, group).reshape(4, rows, ROWS)
        far_left[at] = pick(1 - core, normed, rows, group).reshape(4, rows, ROWS)
    keep_more.append(
        pltpu.make_async_copy(
            own_left, qkv_left_hbm.at[:, :, pl.ds(0, ROWS)], load_sems.at[6]
        )
    )
    theirs = qkv_left_hbm.at[:, :, pl.ds(ROWS, ROWS)]
    for_twin.append(copies.start(far_left, theirs, twin, theirs))
    for copy in keep_more:
        copy.start()
    half_steps = grad_active_ref.shape[1] // WIDE // 2
    keep_grad = pltpu.make_async_copy(grad_active_ref, grad_active_hbm, load_sems.at[4])
    steps(half_steps, grad_active)
    for n in range(3):
        kv_came[n].wait_recv()
        spread(n + 1)
        if n == 1:
            steps(half_steps, lambda index: grad_active(index + half_steps))
            keep_grad.start()
    for arrival in q_came:
        arrival.wait_recv()
    query_bounds(keys_values, z, core, bounds_ref)

    stored = []

    def attend(z_at, core_at):
        count = len(stored)
        column[...] = key_column(keys_values, z_at, core_at)
        query = queries[...].reshape(4 * ROWS, HD)
        keys = keys_values[z_at, core_at, :, :ROWS, :HD].reshape(4 * ROWS, HD)
        values = keys_values[z_at, core_at, :, :ROWS, HD:].reshape(4 * ROWS, HD)
        scores = dot(keys, query, NT)
        codes = jnp.concatenate([column[...]] * (4 * ROWS // HD), axis=1)
        seen = visible(codes, bounds_ref[0:1, :], bounds_ref[1:2, :])
        scores = jnp.where(seen, scores, -1e30)
        top_before = top[0:1, :]
        top_now = jnp.maximum(top_before, jnp.max(scores, axis=0, keepdims=True))
        if count >= 2:
            stored[count - 2].wait()
        slot = weights.at[count % 2]
        slot[...] = jnp.exp2(scores - top_now).astype(bf16)
        shrink = jnp.exp2(top_before - top_now)
        norm[...] = norm[...] * shrink + dot(jnp.ones((8, 4 * ROWS), bf16), slot[...])
        top[0:1, :] = top_now
        acc[...] = acc[...] * shrink + dot(values, slot[...], TN)
        tops_ref[z_at, core_at] = jnp.broadcast_to(top_now, tops_ref.shape[2:])
        copy = pltpu.make_async_copy(
            slot, weights_ref.at[z_at, core_at], weight_sems.at[count % 2]
        )
        copy.start()
        stored.append(copy)

    low_far, high_far, twin_last, twin_next = [], [], [], []

    def onward(n):
        piece = pieces[n]
        from_last[n].wait_recv()
        block = keys_values.at[last_z, core, piece]
        low = block.at[pl.ds(0, ROWS // 2)]
        low_far.append(
            copies.start(low, low, above, keys_values.at[far_z, core, piece, pl.ds(0, ROWS // 2)])
        )
        twin_last.append(
            copies.start(block, block, twin, keys_values.at[last_z, 1 - core, piece])
        )
        from_next[n].wait_recv()
        block = keys_values.at[next_z, core, piece]
        high = block.at[pl.ds(ROWS // 2, ROWS // 2 + CODE_ROWS)]
        high_far.append(
            copies.start(
                high,
                high,
                below,
                keys_values.at[far_z, core, piece, pl.ds(ROWS // 2, ROWS // 2 + CODE_ROWS)],
            )
        )
        twin_next.append(
            copies.start(block, block, twin, keys_values.at[next_z, 1 - core, piece])
        )

    def take(arrivals):
        for arrival in arrivals:
            arrival.wait_recv()

    onward(0)
    w_onward(0)
    attend(z, core)
    onward(1)
    onward(2)
    take(from_twin)
    attend(z, 1 - core)
    onward(3)
    w_onward(1)
    attend(last_z, core)
    attend(next_z, core)
    w_onward(2)
    take(twin_last)
    attend(last_z, 1 - core)
    twin_far = []
    for n, piece in enumerate(pieces):
        low_far[n].wait_recv()
        high_far[n].wait_recv()
        block = keys_values.at[far_z, core, piece]
        twin_far.append(copies.start(block, block, twin, keys_values.at[far_z, 1 - core, piece]))
    take(twin_next)
    attend(next_z, 1 - core)
    w_onward(3)
    attend(far_z, core)
    take(twin_far)
    keep = pltpu.make_async_copy(keys_values, kv_all_ref, load_sems.at[2])
    keep.start()
    attend(far_z, 1 - core)

    total_norm = norm[0:1, :]
    attended = (acc[...] / total_norm).T
    o_low[...] = attended.astype(bf16).reshape(4, ROWS, HD)
    came_back = []
    for hop in HOPS:
        other = around(x, hop)
        came_back.append(
            copies.start(
                o_low.at[other],
                back.at[x],
                device(other, y, z, core),
                back.at[around(x, -hop)],
            )
        )
    back[x] = o_low[x]
    o_ref[...] = attended
    lse_ref[...] = jnp.broadcast_to(top[0:1, :] + jnp.log2(total_norm), lse_ref.shape)
    q_all_ref[...] = queries[...]
    for n in range(4):
        w_far[n].wait_recv()
        block = out_weight.at[y_far, core, n]
        w_twin.append(copies.start(block, block, twin, out_weight.at[y_far, 1 - core, n]))
    take(came_back)
    local = 4 * HD
    for n in range(4):
        gathered[y, :, n * HD : (n + 1) * HD] = back[n]
    half = ROWS // 2
    block = gathered.at[y]
    ring_last = copies.start(block, block, y_up, gathered.at[y_last])
    ring_next = copies.start(block, block, y_down, gathered.at[y_next])
    out_rows = out_left_ref.shape[2]
    for core_at in range(2):
        out_left_ref[:, core_at] = pick(core_at, gathered[y], out_rows, 0).reshape(
            16, out_rows, ROWS
        )
    keep_grad.wait()
    summed = grad_active_ref

    def project(index, owners, first, final):
        at = slab(index, WIDE)
        part = sum(
            dot(gathered[n], out_weight[n, :, :, :, at].reshape(local, WIDE)) for n in owners
        )
        if not first:
            part = part + summed[:, at]
        if final:
            total_ref[:, at] = part.astype(bf16)
        else:
            summed[:, at] = part

    count = total_ref.shape[1] // WIDE
    steps(count, lambda index: project(index, (y,), True, False))
    take(w_twin)
    ring_last.wait_recv()
    block = gathered.at[y_last, pl.ds(0, half)]
    ring_low = copies.start(block, block, y_up, gathered.at[y_far, pl.ds(0, half)])
    ring_next.wait_recv()
    block = gathered.at[y_next, pl.ds(half, half)]
    ring_high = copies.start(block, block, y_down, gathered.at[y_far, pl.ds(half, half)])
    steps(count, lambda index: project(index, (y_last, y_next), False, False))
    ring_low.wait_recv()
    ring_high.wait_recv()
    steps(count, lambda index: project(index, (y_far,), False, True))
    copies.finish()
    keep.wait()
    for copy in keep_more:
        copy.wait()
    take(for_twin)
    for copy in stored[-2:]:
        copy.wait()


def attention_forward(
    activations, labels, position, gains, cotangent, weight, out_weight, down_weight
):
    width = out_weight.shape[1]
    whole = pl.BlockSpec(memory_space=pltpu.VMEM)
    anywhere = pl.BlockSpec(memory_space=pl.ANY)
    count = 3 + 3 + 12 + 16 + 4 + 3 + 4 + 8 + 4 + 8 + 4 + 2
    local = out_weight.shape[0]
    pieces = (2, 4, out_weight.shape[0] // 8, width)
    return pl.pallas_call(
        forward_kernel,
        out_shape=[
            jax.ShapeDtypeStruct((4, ROWS, HD), bf16),
            jax.ShapeDtypeStruct((4, 2, 4, ROWS + CODE_ROWS, 2 * HD), bf16),
            jax.ShapeDtypeStruct((4 * ROWS, HD), f32),
            jax.ShapeDtypeStruct((8, 4 * ROWS), f32),
            jax.ShapeDtypeStruct((16, 2, local // 32, ROWS), bf16),
            jax.ShapeDtypeStruct((ROWS, width), bf16),
            jax.ShapeDtypeStruct((ROWS, down_weight.shape[0]), f32),
            jax.ShapeDtypeStruct((4, 2, 4 * ROWS, 4 * ROWS), bf16),
            jax.ShapeDtypeStruct((4, 2, 8, 4 * ROWS), f32),
            jax.ShapeDtypeStruct((ROWS, HD), jnp.int32),
            jax.ShapeDtypeStruct((ROWS, HD), f32),
            jax.ShapeDtypeStruct((ROWS, HD), f32),
            jax.ShapeDtypeStruct((16, width // 32, 2 * ROWS), bf16),
            jax.ShapeDtypeStruct((2 * ROWS, width), bf16),
        ],
        in_specs=[whole] * 5 + [anywhere] * 3,
        out_specs=[whole, anywhere]
        + [whole] * 4
        + [anywhere, anywhere]
        + [whole] * 4
        + [anywhere] * 2,
        scratch_shapes=[
            pltpu.VMEM((16, width // 32, ROWS), bf16),
            pltpu.VMEM((16, width // 32, ROWS), bf16),
            pltpu.VMEM((ROWS, down_weight.shape[0]), f32),
            pltpu.VMEM(weight.shape, bf16),
            pltpu.VMEM((4,) + pieces, bf16),
            pltpu.VMEM(down_weight.shape, bf16),
            pltpu.VMEM((2, 4 * ROWS, 4 * ROWS), bf16),
            pltpu.VMEM(activations.shape, bf16),
            pltpu.VMEM((4, ROWS, HD), bf16),
            pltpu.VMEM((4, ROWS + CODE_ROWS, 2 * HD), bf16),
            pltpu.VMEM((4, ROWS, HD), bf16),
            pltpu.VMEM((4, 2, 4, ROWS + CODE_ROWS, 2 * HD), bf16),
            pltpu.VMEM((8, 4 * ROWS), f32),
            pltpu.VMEM((8, 4 * ROWS), f32),
            pltpu.VMEM((HD, 4 * ROWS), f32),
            pltpu.VMEM((4 * ROWS, HD), jnp.int32),
            pltpu.VMEM((8, 4 * ROWS), jnp.int32),
            pltpu.VMEM((4, ROWS, HD), bf16),
            pltpu.VMEM((4, ROWS, HD), bf16),
            pltpu.VMEM((4, ROWS, 4 * HD), bf16),
            pltpu.SemaphoreType.DMA((count,)),
            pltpu.SemaphoreType.DMA((count,)),
            pltpu.SemaphoreType.DMA((7,)),
            pltpu.SemaphoreType.DMA((2,)),
        ],
        compiler_params=pltpu.CompilerParams(
            collective_id=0, has_side_effects=True, vmem_limit_bytes=VMEM_LIMIT
        ),
        name="attention_forward",
    )(
        activations,
        labels,
        position,
        gains,
        cotangent,
        weight,
        out_weight.reshape(pieces),
        down_weight,
    )


def gelu_and_slope(hidden):
    scale = math.sqrt(2.0 / math.pi)
    square = hidden * hidden
    bent = jnp.tanh(scale * hidden * (1.0 + 0.044715 * square))
    half = 0.5 * (1.0 + bent)
    slope = half + 0.5 * hidden * (1.0 - bent * bent) * (scale * (1.0 + 3 * 0.044715 * square))
    return hidden * half, slope


def middle_kernel(
    x_ref, attn_ref, labels_ref, gains_ref, cotangent_hbm, out_weight_hbm, grad_active_hbm, up_hbm, down_hbm,
    g_mid_hbm, g_low_hbm, heads_ref, mlp_hbm, down_parts_hbm, gains_out_ref, grad_up_ref,
    up, down, out_weight, grad_active, g_mid, g_low, mlp, xhat, inverse, normed, active, far, far_down, down_left,
    down_right, down_parts, given, g_heads, came, all_rows, y_send, y_recv, load_sems, x_send, x_recv,
    exchange_send, exchange_recv, both_left, both_right, *up_scratch,
):
    here = place()
    x, y, z, core = here
    arrived = greet(
        [device(x, around(y, hop), z, core) for hop in HOPS]
        + [device(around(x, hop), y, z, core) for hop in HOPS]
        + [device(x, y, around(z, hop), core) for hop in (1, 3)]
        + [device(x, y, z, 1 - core)]
    )
    used = [0]

    def move(src, dst):
        copy = pltpu.make_async_copy(src, dst, load_sems.at[used[0]])
        used[0] += 1
        copy.start()
        return copy

    load_up = move(up_hbm, up)
    load_active = move(grad_active_hbm, grad_active)
    width = x_ref.shape[1]
    hidden_width = up.shape[1]

    def norm(index):
        at = slab(index, NORM_ROWS)
        middle = x_ref[at, :].astype(f32) + attn_ref[at, :].astype(f32)
        centred = middle - jnp.mean(middle, axis=-1, keepdims=True)
        scale = lax.rsqrt(jnp.mean(centred * centred, axis=-1, keepdims=True) + 1e-05)
        unit = centred * scale
        xhat[at, :] = unit
        inverse[at, :] = jnp.broadcast_to(scale, (NORM_ROWS, HD))
        normed[at, :] = (unit * gain_rows(labels_ref[at, :1], gains_ref, 3)).astype(bf16)

    steps(ROWS // NORM_ROWS, norm)
    rows = grad_up_ref.shape[0]
    for group in range(4):
        at = pl.ds(4 * group, 4)
        both_left[at, :, pl.ds(0, ROWS)] = pick(core, normed, rows, group).reshape(4, rows, ROWS)
        far[at] = pick(1 - core, normed, rows, group).reshape(4, rows, ROWS)
    load_up.wait()
    load_active.wait()
    load_down = move(down_hbm, down)
    load_cotangent = move(cotangent_hbm, down_right)
    load_out = move(out_weight_hbm, out_weight)
    arrived()
    twin = device(x, y, z, 1 - core)
    exchange = Copies(exchange_send, exchange_recv)
    theirs = both_left.at[:, :, pl.ds(ROWS, ROWS)]
    left_came = exchange.start(far, theirs, twin, theirs)
    right_came = []
    for index in range(hidden_width // WIDE):
        at = pl.ds(index * WIDE, WIDE)
        hidden = dot(normed[...], up[:, at])
        value, slope = gelu_and_slope(hidden)
        active[:, at] = value.astype(bf16)
        both_right[pl.ds(0, ROWS), at] = (grad_active[:, at] * slope).astype(bf16)
        theirs = both_right.at[pl.ds(ROWS, ROWS), at]
        right_came.append(
            exchange.start(both_right.at[pl.ds(0, ROWS), at], theirs, twin, theirs)
        )

    def ready(group):
        if group == 0:
            left_came.wait_recv()
        right_came[group].wait_recv()

    ring = weight_grad(here, grad_up_ref, up_scratch, (both_left, both_right), ready=ready)
    advance(ring)
    copies = Copies(y_send, y_recv)
    half_steps = width // WIDE // 2
    over_y = [
        sum_over_y(copies, here, given.at[half], came.at[half], all_rows.at[half])
        for half in range(2)
    ]

    def back_up(index, half):
        at = slab(index + half * half_steps, WIDE)
        part = dot(both_right[pl.ds(0, ROWS), :], up[at, :], NT)
        given[half, :, :, slab(index, WIDE)] = part.astype(bf16).reshape(
            SIDE, ROWS // SIDE, WIDE
        )

    def feed_out(index, half):
        at = slab(index + half * half_steps, WIDE)
        mlp[half, :, :, slab(index, WIDE)] = (
            dot(active[...], down[:, at]).astype(bf16).reshape(SIDE, ROWS // SIDE, WIDE)
        )

    groups, first_shape = down_parts.shape[0], down_parts.shape[3:]
    keep = []

    def fill_down(group):
        for at in range(4):
            down_parts[group, at] = partial_block(
                down_left, down_right, DOWN_WAYS[group], at, group, first_shape[1]
            ).reshape((2,) + first_shape)
        keep.append(move(down_parts.at[group], down_parts_hbm.at[group]))

    steps(half_steps, lambda index: back_up(index, 0))
    advance(over_y[0])
    advance(ring)
    steps(half_steps, lambda index: back_up(index, 1))
    advance(over_y[1])
    advance(ring, 2)
    advance(over_y[0])
    advance(ring, 2)
    load_down.wait()
    feed_out(0, 0)
    advance(over_y[1])
    feed_out(1, 0)
    advance(over_y[0])
    feed_out(0, 1)
    advance(over_y[1])
    feed_out(1, 1)
    keep.append(move(mlp, mlp_hbm))
    for group in range(4):
        at = pl.ds(4 * group, 4)
        down_left[at, :, pl.ds(0, ROWS)] = pick(core, active, rows, group).reshape(4, rows, ROWS)
        far_down[at] = pick(1 - core, active, rows, group).reshape(4, rows, ROWS)
    theirs = down_left.at[:, :, pl.ds(ROWS, ROWS)]
    down_came = exchange.start(far_down, theirs, twin, theirs)
    advance(over_y[0])
    advance(ring)
    advance(over_y[1])
    load_cotangent.wait()
    down_came.wait_recv()
    fill_down(0)
    advance(ring)
    fill_down(1)
    advance(ring)
    load_out.wait()
    gains_out_ref[...] = jnp.zeros_like(gains_out_ref)
    advance(over_y[0])
    advance(over_y[1])

    def back(index):
        at = slab(index, NORM_ROWS)
        grad = summed_rows(all_rows, index)
        labels = labels_ref[at, :1]
        unit = xhat[at, :]
        product = grad * unit
        for mode in range(3):
            gains_out_ref[mode + 3 : mode + 4, :] += jnp.sum(
                jnp.where(labels == mode, product, 0.0), axis=0, keepdims=True
            )
        gain = gain_rows(labels, gains_ref, 3)
        grad = grad * gain
        mean = jnp.mean(grad, axis=-1, keepdims=True)
        along = jnp.mean(product * gain, axis=-1, keepdims=True)
        total = down_right[at, :].astype(f32) + inverse[at, :1] * (grad - mean - unit * along)
        g_mid[at, :] = total
        g_low[at, :] = total.astype(bf16)

    steps(ROWS // NORM_ROWS, back)
    by_head = dot(g_low[...], out_weight[...], NT).astype(bf16)
    for head in range(4):
        g_heads[head] = by_head[:, head * HD : (head + 1) * HD]
    x_copies = Copies(x_send, x_recv)
    arrivals = [
        x_copies.start(
            g_heads.at[around(x, hop)],
            heads_ref.at[x],
            device(around(x, hop), y, z, core),
            heads_ref.at[around(x, -hop)],
        )
        for hop in HOPS
    ]
    heads_ref[x] = g_heads[x]
    keep += [move(g_mid, g_mid_hbm), move(g_low, g_low_hbm)]
    advance(ring)
    fill_down(2)
    advance(ring)
    fill_down(3)
    advance(ring)
    for arrival in arrivals:
        arrival.wait_recv()
    copies.finish()
    x_copies.finish()
    exchange.finish()
    for copy in keep:
        copy.wait()


def middle(
    activations, attn_sum, labels, gains, cotangent, out_weight, grad_active, up_weight, down_weight
):
    width, hidden_width = up_weight.shape
    rows = width // 32
    down_rows = hidden_width // 32
    whole = pl.BlockSpec(memory_space=pltpu.VMEM)
    anywhere = pl.BlockSpec(memory_space=pl.ANY)
    summed = (2, SIDE, ROWS // SIDE, width // 2)
    groups, first_shape, late_shape = ring_shapes(down_rows, width)
    down_parts = (groups, 4, 2) + first_shape
    return pl.pallas_call(
        middle_kernel,
        out_shape=[
            jax.ShapeDtypeStruct((ROWS, width), f32),
            jax.ShapeDtypeStruct((ROWS, width), bf16),
            jax.ShapeDtypeStruct((4, ROWS, HD), bf16),
            jax.ShapeDtypeStruct(summed, bf16),
            jax.ShapeDtypeStruct(down_parts, bf16),
            jax.ShapeDtypeStruct((8, width), f32),
            jax.ShapeDtypeStruct((rows, hidden_width), f32),
        ],
        in_specs=[whole] * 4 + [anywhere] * 5,
        out_specs=[anywhere] * 2 + [whole] + [anywhere] * 2 + [whole] * 2,
        scratch_shapes=[
            pltpu.VMEM(up_weight.shape, bf16),
            pltpu.VMEM(down_weight.shape, bf16),
            pltpu.VMEM(out_weight.shape, bf16),
            pltpu.VMEM((ROWS, hidden_width), f32),
            pltpu.VMEM((ROWS, width), f32),
            pltpu.VMEM((ROWS, width), bf16),
            pltpu.VMEM(summed, bf16),
            pltpu.VMEM((ROWS, width), f32),
            pltpu.VMEM((ROWS, HD), f32),
            pltpu.VMEM((ROWS, width), bf16),
            pltpu.VMEM((ROWS, hidden_width), bf16),
            pltpu.VMEM((16, rows, ROWS), bf16),
            pltpu.VMEM((16, down_rows, ROWS), bf16),
        ]
        + factor_scratch(down_rows, width)
        + [
            pltpu.VMEM(down_parts, bf16),
            pltpu.VMEM(summed, bf16),
            pltpu.VMEM((4, ROWS, HD), bf16),
        ]
        + sum_scratch(width)
        + [pltpu.SemaphoreType.DMA((12,))]
        + [pltpu.SemaphoreType.DMA((3,)), pltpu.SemaphoreType.DMA((3,))]
        + [pltpu.SemaphoreType.DMA((6,)), pltpu.SemaphoreType.DMA((6,))]
        + factor_scratch(rows, hidden_width)
        + weight_scratch(rows, hidden_width),
        compiler_params=pltpu.CompilerParams(
            collective_id=2, has_side_effects=True, vmem_limit_bytes=VMEM_LIMIT
        ),
        name="middle",
    )(
        activations,
        attn_sum,
        labels,
        gains,
        cotangent,
        out_weight,
        grad_active,
        up_weight,
        down_weight,
    )


def backward_kernel(
    grads, q_ref, kv_hbm, o_ref, lse_ref, tops_ref, weights_hbm, down_parts_hbm, out_left_hbm, g_low_hbm, given_ref,
    packed_ref, grad_down_ref, grad_out_ref, total_ref,
    keys_values, weights, delta, grad_q, parts, met, came, sums, q_low, back_q,
    back_kv, send_sems, recv_sems, load_sems, weight_sems, y_came, all_rows, y_send, y_recv, *more,
):
    here = place()
    x, y, z, core = here
    twin = device(x, y, z, 1 - core)
    arrived = greet(
        [device(around(x, hop), y, z, core) for hop in HOPS]
        + [device(x, around(y, hop), z, core) for hop in HOPS]
        + [device(x, y, around(z, hop), core) for hop in (1, 3)]
        + [twin]
    )
    next_z, last_z, far_z = around(z, 1), around(z, -1), around(z, 2)
    order = [
        (at, core_at)
        for at in (far_z, next_z, last_z, z)
        for core_at in (1 - core, core)
    ]
    load = pltpu.make_async_copy(kv_hbm, keys_values, load_sems.at[0])
    load.start()

    def fetch(index):
        copy = pltpu.make_async_copy(
            weights_hbm.at[order[index][0], order[index][1]],
            weights.at[index % 3],
            weight_sems.at[index % 3],
        )
        copy.start()
        return copy

    fetched = [fetch(0), fetch(1)]
    copies = Copies(send_sems, recv_sems)
    y_copies = Copies(y_send, y_recv)
    over_y = [
        sum_over_y(y_copies, here, given_ref.at[half], y_came.at[half], all_rows.at[half])
        for half in range(2)
    ]
    ring = weight_grad(here, grad_down_ref, more[:7], parts_hbm=down_parts_hbm, ways=DOWN_WAYS)
    ring_out = weight_grad(
        here, grad_out_ref, more[9:], more[7:9], left=out_left_hbm, right=g_low_hbm
    )
    arrived()
    advance(ring, 5)
    for half in over_y:
        advance(half)
    advance(ring_out)
    grad_q[...] = jnp.zeros_like(grad_q)
    product = grads[...].reshape(4 * ROWS, HD).astype(f32) * o_ref[...]
    delta[...] = lax.dot_general(
        jnp.ones((8, HD), f32), product, NT, preferred_element_type=f32, precision=highest
    )
    load.wait()
    done = []

    def chunk(z_at, core_at):
        index = len(done)
        done.append(index)
        if index + 2 < len(order):
            fetched.append(fetch(index + 2))
        fetched[index].wait()
        slot = weights.at[index % 3]
        query = q_ref[...].reshape(4 * ROWS, HD)
        grad = grads[...].reshape(4 * ROWS, HD)
        keys = keys_values[z_at, core_at, :, :ROWS, :HD].reshape(4 * ROWS, HD)
        values = keys_values[z_at, core_at, :, :ROWS, HD:].reshape(4 * ROWS, HD)
        rescale = jnp.exp2(tops_ref[z_at, core_at, 0:1, :] - lse_ref[0:1, :])
        grad_weights = dot(values, grad, NT)
        taken = slot[...].astype(f32) * rescale
        slot[...] = taken.astype(bf16)
        grad_v = dot(slot[...], grad)
        slot[...] = (taken * (grad_weights - delta[0:1, :])).astype(bf16)
        grad_k = dot(slot[...], query)
        grad_q[...] += dot(keys, slot[...], TN)
        parts[z_at, core_at] = (
            jnp.concatenate([grad_k * math.log(2.0), grad_v], axis=1)
            .astype(bf16)
            .reshape(2, 2 * ROWS, 2 * HD)
        )

    def hand_over(z_at):
        return copies.start(
            parts.at[z_at, 1 - core], met.at[z_at], twin, met.at[z_at]
        )

    def join(z_at):
        parts[z_at, core] = (
            parts[z_at, core].astype(f32) + met[z_at].astype(f32)
        ).astype(bf16)

    above, below = device(x, y, next_z, core), device(x, y, last_z, core)
    chunk(far_z, 1 - core)
    far_met = hand_over(far_z)
    advance(ring_out, 5)
    chunk(far_z, core)
    chunk(next_z, 1 - core)
    next_met = hand_over(next_z)
    far_met.wait_recv()
    join(far_z)
    from_last = copies.start(parts.at[far_z, core, 0], came.at[0], above, came.at[0])
    from_next = copies.start(parts.at[far_z, core, 1], came.at[1], below, came.at[1])
    for half in over_y:
        advance(half)
    advance(ring, 2)
    chunk(next_z, core)
    chunk(last_z, 1 - core)
    last_met = hand_over(last_z)
    next_met.wait_recv()
    join(next_z)
    raw_last = copies.start(parts.at[next_z, core, 1], came.at[2], above, came.at[2])
    for half in over_y:
        advance(half)
    chunk(last_z, core)
    chunk(z, 1 - core)
    own_met = hand_over(z)
    last_met.wait_recv()
    join(last_z)
    raw_next = copies.start(parts.at[last_z, core, 0], came.at[3], below, came.at[3])
    from_last.wait_recv()
    parts[next_z, core, 0] = (
        parts[next_z, core, 0].astype(f32) + came[0].astype(f32)
    ).astype(bf16)
    sum_last = copies.start(parts.at[next_z, core, 0], came.at[4], above, came.at[4])
    from_next.wait_recv()
    parts[last_z, core, 1] = (
        parts[last_z, core, 1].astype(f32) + came[1].astype(f32)
    ).astype(bf16)
    sum_next = copies.start(parts.at[last_z, core, 1], came.at[5], below, came.at[5])
    for half in over_y:
        advance(half)
    advance(ring)
    advance(ring_out)
    chunk(z, core)
    q_low[...] = (grad_q[...] * (HD**-0.5)).T.astype(bf16).reshape(4, ROWS, HD)
    arrivals = []
    for hop in HOPS:
        other = around(x, hop)
        arrivals.append(
            copies.start(
                q_low.at[other],
                back_q.at[x],
                device(other, y, z, core),
                back_q.at[around(x, -hop)],
            )
        )
    back_q[x] = q_low[x]
    advance(ring)
    advance(ring_out, 2)
    own_met.wait_recv()
    raw_last.wait_recv()
    raw_next.wait_recv()
    sum_last.wait_recv()
    sum_next.wait_recv()
    mine = parts[z, core].astype(f32) + met[z].astype(f32)
    low = mine[0] + came[4].astype(f32) + came[3].astype(f32)
    high = mine[1] + came[2].astype(f32) + came[5].astype(f32)
    sums[0:2] = low.astype(bf16).reshape(2, ROWS, 2 * HD)
    sums[2:4] = high.astype(bf16).reshape(2, ROWS, 2 * HD)
    for hop in HOPS:
        other = around(x, hop)
        arrivals.append(
            copies.start(
                sums.at[other],
                back_kv.at[x],
                device(other, y, z, core),
                back_kv.at[around(x, -hop)],
            )
        )
    back_kv[x] = sums[x]
    for half in over_y:
        advance(half)
    total_ref[...] = all_rows[...]
    advance(ring)
    advance(ring_out, 2)
    advance(ring)
    advance(ring_out)
    advance(ring)
    for arrival in arrivals:
        arrival.wait_recv()
    for n in range(4):
        packed_ref[n, :, :HD] = back_q[n]
        packed_ref[n, :, HD:] = back_kv[n]
    copies.finish()
    y_copies.finish()


def attention_backward(
    grad_heads, q_all, kv_all, o_all, lse, tops, weights, down_parts, out_left, g_low, given
):
    whole = pl.BlockSpec(memory_space=pltpu.VMEM)
    anywhere = pl.BlockSpec(memory_space=pl.ANY)
    count = 4 + 6 + 6
    width = g_low.shape[1]
    down_rows, out_rows = down_parts.shape[3] // 2, out_left.shape[2]
    return pl.pallas_call(
        backward_kernel,
        out_shape=[
            jax.ShapeDtypeStruct((4, ROWS, 3 * HD), bf16),
            jax.ShapeDtypeStruct((down_rows, width), f32),
            jax.ShapeDtypeStruct((out_rows, width), f32),
            jax.ShapeDtypeStruct(given.shape, bf16),
        ],
        in_specs=[whole, whole, anywhere] + [whole] * 3 + [anywhere] * 4 + [whole],
        out_specs=[whole] * 4,
        scratch_shapes=[
            pltpu.VMEM((4, 2, 4, ROWS + CODE_ROWS, 2 * HD), bf16),
            pltpu.VMEM((3, 4 * ROWS, 4 * ROWS), bf16),
            pltpu.VMEM((8, 4 * ROWS), f32),
            pltpu.VMEM((HD, 4 * ROWS), f32),
            pltpu.VMEM((4, 2, 2, 2 * ROWS, 2 * HD), bf16),
            pltpu.VMEM((4, 2, 2 * ROWS, 2 * HD), bf16),
            pltpu.VMEM((6, 2 * ROWS, 2 * HD), bf16),
            pltpu.VMEM((4, ROWS, 2 * HD), bf16),
            pltpu.VMEM((4, ROWS, HD), bf16),
            pltpu.VMEM((4, ROWS, HD), bf16),
            pltpu.VMEM((4, ROWS, 2 * HD), bf16),
            pltpu.SemaphoreType.DMA((count,)),
            pltpu.SemaphoreType.DMA((count,)),
            pltpu.SemaphoreType.DMA((1,)),
            pltpu.SemaphoreType.DMA((3,)),
        ]
        + sum_scratch(2 * given.shape[3])
        + weight_scratch(down_rows, width)
        + factor_scratch(out_rows, width)
        + weight_scratch(out_rows, width),
        compiler_params=pltpu.CompilerParams(
            collective_id=1, has_side_effects=True, vmem_limit_bytes=VMEM_LIMIT
        ),
        name="attention_backward",
    )(
        grad_heads, q_all, kv_all, o_all, lse, tops, weights, down_parts, out_left, g_low, given
    )


def last_kernel(
    x_ref, labels_ref, gains_ref, packed_ref, cos_ref, sin_ref, gains_two_ref, left_hbm, attn_hbm, mlp_hbm, g_mid_hbm,
    weight_hbm,
    input_ref, layer_ref, gains_out_ref, grad_qkv_ref,
    attn, mlp, g_mid, weight, xhat, inverse, given, gains_part, gains_given, came, all_rows, y_send, y_recv, load_sems,
    qkv_left, qkv_right, *more,
):
    gain_scratch = more[: len(GAIN_SCRATCH)]
    gain_send, gain_recv = more[len(GAIN_SCRATCH) : len(GAIN_SCRATCH) + 2]
    qkv_scratch = more[len(GAIN_SCRATCH) + 2 :]
    here = place()
    x, y, z, core = here
    loads = []
    for n, (src, dst) in enumerate(
        (
            (weight_hbm, weight),
            (left_hbm, qkv_left),
            (attn_hbm, attn),
            (mlp_hbm, mlp),
            (g_mid_hbm, g_mid),
        )
    ):
        loads.append(pltpu.make_async_copy(src, dst, load_sems.at[n]))
    loads[0].start()
    arrived = greet(
        [device(x, around(y, hop), z, core) for hop in HOPS]
        + [device(around(x, hop), y, z, core) for hop in HOPS]
        + [device(x, y, around(z, hop), core) for hop in HOPS]
        + [device(x, y, z, 1 - core)]
    )
    width = x_ref.shape[1]
    local = qkv_right.shape[1] // 3

    cosine, sine = cos_ref[...], sin_ref[...]
    for head in range(4):
        for part in range(3):
            grad = packed_ref[head, :, part * HD : (part + 1) * HD]
            if part < 2:
                grad = grad.astype(f32)
                scaled = grad * sine
                grad = (
                    grad * cosine
                    + jnp.concatenate([scaled[:, HD // 2 :], -scaled[:, : HD // 2]], axis=1)
                ).astype(bf16)
            start = part * local + head * HD
            qkv_right[0:ROWS, start : start + HD] = grad
    arrived()
    ring = weight_grad(here, grad_qkv_ref, qkv_scratch, (qkv_left, qkv_right))
    advance(ring)
    loads[0].wait()
    for load in loads[1:]:
        load.start()
    copies = Copies(y_send, y_recv)
    half_steps = width // WIDE // 2
    over_y = [
        sum_over_y(copies, here, given.at[half], came.at[half], all_rows.at[half])
        for half in range(2)
    ]

    def back_in(index, half):
        at = slab(index + half * half_steps, WIDE)
        part = sum(
            dot(qkv_right[pl.ds(0, ROWS), k * local : (k + 1) * local], weight[k, at, :], NT)
            for k in range(3)
        )
        given[half, :, :, slab(index, WIDE)] = part.astype(bf16).reshape(
            SIDE, ROWS // SIDE, WIDE
        )

    steps(half_steps, lambda index: back_in(index, 0))
    advance(over_y[0])
    loads[1].wait()
    advance(ring)
    steps(half_steps, lambda index: back_in(index, 1))
    advance(over_y[1])
    advance(ring, 2)
    advance(over_y[0])
    advance(ring, 2)
    gains_part[...] = 0.25 * gains_two_ref[...]

    def norm(index):
        at = slab(index, NORM_ROWS)
        rows = x_ref[at, :].astype(f32)
        centred = rows - jnp.mean(rows, axis=-1, keepdims=True)
        scale = lax.rsqrt(jnp.mean(centred * centred, axis=-1, keepdims=True) + 1e-05)
        unit = centred * scale
        xhat[at, :] = unit
        inverse[at, :] = jnp.broadcast_to(scale, (NORM_ROWS, HD))
        labels = labels_ref[at, :1]
        product = summed_rows(given, index) * unit
        for mode in range(3):
            gains_part[mode : mode + 1, :] += jnp.sum(
                jnp.where(labels == mode, product, 0.0), axis=0, keepdims=True
            )

    norm_steps = ROWS // NORM_ROWS // 2
    steps(norm_steps, norm)
    advance(over_y[1])
    advance(over_y[0])
    steps(norm_steps, lambda index: norm(index + norm_steps))
    advance(over_y[1])
    for owner in range(32):
        gains_given[owner // 8, (owner // 2) % 4, owner % 2] = jnp.zeros((8, HD), f32)
        gains_given[owner // 8, (owner // 2) % 4, owner % 2, :, :64] = gains_part[
            :, owner * 64 : (owner + 1) * 64
        ]
    gain_copies = Copies(gain_send, gain_recv)
    over_all = sum_gains(gain_copies, here, gains_given, *gain_scratch, gains_out_ref)
    advance(over_all)
    advance(ring)
    for load in loads[2:]:
        load.wait()

    def finish_layer(index):
        at = slab(index, NORM_ROWS)
        total = x_ref[at, :].astype(f32) + attn[at, :].astype(f32) + summed_rows(mlp, index)
        layer_ref[at, :] = total.astype(bf16)

    steps(ROWS // NORM_ROWS, finish_layer)
    advance(over_y[0])
    advance(over_all)
    advance(ring)
    advance(over_y[1])
    advance(over_y[0])
    advance(ring)
    advance(over_all)
    advance(over_y[1])

    def finish_input(index):
        at = slab(index, NORM_ROWS)
        unit = xhat[at, :]
        grad = summed_rows(all_rows, index) * gain_rows(labels_ref[at, :1], gains_ref, 0)
        mean = jnp.mean(grad, axis=-1, keepdims=True)
        along = jnp.mean(grad * unit, axis=-1, keepdims=True)
        input_ref[at, :] = g_mid[at, :] + inverse[at, :1] * (grad - mean - unit * along)

    steps(ROWS // NORM_ROWS, finish_input)
    advance(ring)
    advance(over_all)
    advance(ring)
    advance(over_all)
    advance(ring)
    copies.finish()
    gain_copies.finish()


def last(
    activations, labels, gains, packed, cosine, sine, gains_two, left, attn_sum, mlp_sum, g_mid, weight
):
    width = activations.shape[1]
    local = weight.shape[2]
    cols = 3 * local
    rows = width // 32
    whole = pl.BlockSpec(memory_space=pltpu.VMEM)
    anywhere = pl.BlockSpec(memory_space=pl.ANY)
    return pl.pallas_call(
        last_kernel,
        out_shape=[
            jax.ShapeDtypeStruct((ROWS, width), f32),
            jax.ShapeDtypeStruct((ROWS, width), bf16),
            jax.ShapeDtypeStruct((8, HD), f32),
            jax.ShapeDtypeStruct((3, rows, local), f32),
        ],
        in_specs=[whole] * 7 + [anywhere] * 5,
        out_specs=[whole] * 4,
        scratch_shapes=[
            pltpu.VMEM(attn_sum.shape, bf16),
            pltpu.VMEM(mlp_sum.shape, bf16),
            pltpu.VMEM(g_mid.shape, f32),
            pltpu.VMEM(weight.shape, bf16),
            pltpu.VMEM((ROWS, width), f32),
            pltpu.VMEM((ROWS, HD), f32),
            pltpu.VMEM(mlp_sum.shape, bf16),
            pltpu.VMEM((8, width), f32),
            pltpu.VMEM((4, 4, 2, 8, HD), f32),
        ]
        + sum_scratch(width)
        + [pltpu.SemaphoreType.DMA((5,))]
        + factor_scratch(rows, cols)
        + [pltpu.VMEM(shape, f32) for shape in GAIN_SCRATCH]
        + [pltpu.SemaphoreType.DMA((10,)), pltpu.SemaphoreType.DMA((10,))]
        + weight_scratch(rows, cols),
        compiler_params=pltpu.CompilerParams(
            collective_id=3, has_side_effects=True, vmem_limit_bytes=VMEM_LIMIT
        ),
        name="last",
    )(
        activations,
        labels,
        gains,
        packed,
        cosine,
        sine,
        gains_two,
        left,
        attn_sum,
        mlp_sum,
        g_mid,
        weight,
    )


def finish_kernel(
    share_ref, layer_in, input_in, qkv_in, out_in, up_in, down_in,
    gains_ref, layer_out, input_out, qkv_out, out_out, up_out, down_out,
    layer, grad_input, qkv, out, up, down, load_sems, store_sems,
):
    ways = (
        (layer_in, layer, layer_out),
        (up_in, up, up_out),
        (qkv_in, qkv, qkv_out),
        (down_in, down, down_out),
        (out_in, out, out_out),
        (input_in, grad_input, input_out),
    )
    loads = [
        pltpu.make_async_copy(src, held, load_sems.at[n]) for n, (src, held, dst) in enumerate(ways)
    ]
    stores = [
        pltpu.make_async_copy(held, dst, store_sems.at[n]) for n, (src, held, dst) in enumerate(ways)
    ]
    for load in loads:
        load.start()
    gains_ref[...] = share_ref[: gains_ref.shape[0], : gains_ref.shape[1]]
    for load, store in zip(loads, stores):
        load.wait()
        store.start()
    for store in stores:
        store.wait()


def finish(modes, share, *arrays):
    whole = pl.BlockSpec(memory_space=pltpu.VMEM)
    anywhere = pl.BlockSpec(memory_space=pl.ANY)
    count = len(arrays)
    return pl.pallas_call(
        finish_kernel,
        out_shape=[jax.ShapeDtypeStruct((2 * modes, arrays[0].shape[1] // 32), f32)]
        + [jax.ShapeDtypeStruct(array.shape, array.dtype) for array in arrays],
        in_specs=[whole] + [anywhere] * count,
        out_specs=[whole] + [anywhere] * count,
        scratch_shapes=[pltpu.VMEM(array.shape, array.dtype) for array in arrays]
        + [pltpu.SemaphoreType.DMA((count,)), pltpu.SemaphoreType.DMA((count,))],
        name="finish",
    )(share, *arrays)


def per_device(
    activations,
    labels,
    position,
    norm_gains,
    qkv_weight,
    out_weight,
    up_weight,
    down_weight,
    cotangent,
):
    projections = qkv_weight.transpose(1, 0, 2)
    (
        q_all,
        kv_all,
        o_all,
        lse,
        out_left,
        attn_sum,
        grad_active,
        weights,
        tops,
        label_rows,
        cosine,
        sine,
        qkv_left,
        both_cotangents,
    ) = attention_forward(
        activations,
        labels.reshape(1, ROWS),
        position.reshape(1, ROWS),
        norm_gains,
        cotangent,
        projections,
        out_weight,
        down_weight,
    )
    g_mid, g_low, grad_heads, mlp_part, down_parts, gains_two, grad_up = middle(
        activations,
        attn_sum,
        label_rows,
        norm_gains,
        both_cotangents,
        out_weight,
        grad_active,
        up_weight,
        down_weight,
    )
    packed, grad_down, grad_out, mlp_sum = attention_backward(
        grad_heads,
        q_all,
        kv_all,
        o_all,
        lse,
        tops,
        weights,
        down_parts,
        out_left,
        g_low,
        mlp_part,
    )
    grad_input, layer_out, share, grad_qkv = last(
        activations,
        label_rows,
        norm_gains,
        packed,
        cosine,
        sine,
        gains_two,
        qkv_left,
        attn_sum,
        mlp_sum,
        g_mid,
        projections,
    )
    grad_gains, layer_out, grad_input, grad_qkv, grad_out, grad_up, grad_down = finish(
        norm_gains.shape[0] // 2,
        share,
        layer_out,
        grad_input,
        grad_qkv,
        grad_out,
        grad_up,
        grad_down,
    )
    return (
        layer_out,
        grad_input,
        grad_gains,
        grad_qkv.transpose(1, 0, 2),
        grad_out,
        grad_up,
        grad_down,
    )


def solution(mesh):
    return jax.shard_map(
        per_device,
        mesh=mesh,
        in_specs=(
            P("tok", None),
            P("tok"),
            P("tok"),
            P(),
            P(None, None, "head"),
            P("head", None),
            P(None, "head"),
            P("head", None),
            P("tok", None),
        ),
        out_specs=(
            P("tok", None),
            P("tok", None),
            P(None, "tok"),
            P("tok", None, "head"),
            P(("head", "tok"), None),
            P("tok", "head"),
            P(("head", "tok"), None),
        ),
        check_vma=False,
    )
```

```python
import functools
import math

import jax
import jax.numpy as jnp
from jax import lax
from jax.experimental import pallas as pl
from jax.experimental.pallas import tpu as pltpu
from jax.sharding import PartitionSpec as P

HD = 128
SIDE = 4
ROWS = 256
CODE_ROWS = 16
CLIP_STEP = 8192
MESH = pl.DeviceIdType.MESH
NT = (((1,), (1,)), ((), ()))
TN = (((0,), (0,)), ((), ()))
NN = (((1,), (0,)), ((), ()))
f32 = jnp.float32
bf16 = jnp.bfloat16
highest = lax.Precision.HIGHEST
VMEM_LIMIT = 60 << 20
HOPS = (1, 3, 2)


def dot(lhs, rhs, dims=NN):
    return lax.dot_general(lhs, rhs, dims, preferred_element_type=f32)


def place():
    tok = lax.axis_index("tok")
    return (lax.div(tok, 8), lax.axis_index("head"), lax.rem(lax.div(tok, 2), 4), lax.rem(tok, 2))


def around(index, step):
    return lax.rem(index + (step % SIDE), SIDE)


def device(x, y, z, core):
    return (x * 8 + z * 2 + core, y)


def remote(src, dst, send_sem, recv_sem, target):
    return pltpu.make_async_remote_copy(
        src_ref=src,
        dst_ref=dst,
        send_sem=send_sem,
        recv_sem=recv_sem,
        device_id=target,
        device_id_type=MESH,
    )


def greet(targets):
    barrier = pltpu.get_barrier_semaphore()
    for target in targets:
        pl.semaphore_signal(barrier, inc=1, device_id=target, device_id_type=MESH)
    return lambda: pl.semaphore_wait(barrier, len(targets))


class Copies:
    def __init__(self, send_sems, recv_sems):
        self.send_sems = send_sems
        self.recv_sems = recv_sems
        self.used = 0
        self.open = []

    def start(self, src, dst, target, landing):
        index = self.used
        self.used += 1
        copy = remote(src, dst, self.send_sems.at[index], self.recv_sems.at[index], target)
        copy.start()
        self.open.append(copy)
        return remote(landing, landing, self.send_sems.at[index], self.recv_sems.at[index], target)

    def finish(self):
        for copy in self.open:
            copy.wait_send()


def advance(steps_left, count=1):
    for _ in range(count):
        next(steps_left)


def ring_sum(copies, own, towards, source, block, slots):
    up, down = towards(1), towards(-1)
    from_down = copies.start(source(2, 0), slots.at[0], up, slots.at[0])
    from_up = copies.start(source(2, 1), slots.at[1], down, slots.at[1])
    raw_down = copies.start(source(1, 1), slots.at[2], up, slots.at[2])
    raw_up = copies.start(source(-1, 0), slots.at[3], down, slots.at[3])
    yield
    from_down.wait_recv()
    slots[0] = (block(1, 0)[...].astype(f32) + slots[0].astype(f32)).astype(bf16)
    sum_down = copies.start(slots.at[0], slots.at[4], up, slots.at[4])
    from_up.wait_recv()
    slots[1] = (block(-1, 1)[...].astype(f32) + slots[1].astype(f32)).astype(bf16)
    sum_up = copies.start(slots.at[1], slots.at[5], down, slots.at[5])
    yield
    for arrival in (raw_down, raw_up, sum_down, sum_up):
        arrival.wait_recv()

    def finished(half):
        mine = block(0, half)[...].astype(f32)
        if half == 0:
            return mine + slots[4].astype(f32) + slots[3].astype(f32)
        return mine + slots[2].astype(f32) + slots[5].astype(f32)

    own.append(finished)


def sum_over_y(copies, here, given, came, total):
    x, y, z, core = here
    rows = given.shape[1] // 2
    halves = (pl.ds(0, rows), pl.ds(rows, rows))

    def towards(step):
        return device(x, around(y, step), z, core)

    def block(step, half):
        return given.at[around(y, step), halves[half]]

    done = []
    ring = ring_sum(copies, done, towards, block, block, came)
    next(ring)
    yield
    next(ring)
    yield
    next(ring, None)
    for half in range(2):
        total[y, halves[half]] = done[0](half).astype(bf16)
    last_y, next_y, far_y = around(y, -1), around(y, 1), around(y, 2)
    mine = total.at[y]
    from_last = copies.start(mine, mine, towards(1), total.at[last_y])
    from_next = copies.start(mine, mine, towards(-1), total.at[next_y])
    yield
    from_last.wait_recv()
    part = total.at[last_y, halves[0]]
    far_low = copies.start(part, part, towards(1), total.at[far_y, halves[0]])
    from_next.wait_recv()
    part = total.at[next_y, halves[1]]
    far_high = copies.start(part, part, towards(-1), total.at[far_y, halves[1]])
    yield
    far_low.wait_recv()
    far_high.wait_recv()
    yield


def sum_scratch(width):
    quarter = ROWS // SIDE
    return [
        pltpu.VMEM((2, 6, quarter // 2, width // 2), bf16),
        pltpu.VMEM((2, SIDE, quarter, width // 2), bf16),
        pltpu.SemaphoreType.DMA((20,)),
        pltpu.SemaphoreType.DMA((20,)),
    ]


def summed_rows(all_rows, index):
    part = lax.div(index, SIDE // 2)
    start = pl.multiple_of(lax.rem(index, SIDE // 2) * NORM_ROWS, NORM_ROWS)
    halves = [all_rows[half, part, pl.ds(start, NORM_ROWS), :] for half in range(2)]
    return jnp.concatenate(halves, axis=1).astype(f32)


WAYS = (0, 1, 0, 1)
DOWN_WAYS = (0, 1, 0, 0)


def ring_shapes(rows, cols):
    if rows >= 32:
        width = cols // 4
        return 4, (2 * rows, width), (rows // 2, width)
    return 2, (4 * rows, cols // 4), (rows, cols // 4)


def factor_scratch(rows, cols):
    return [pltpu.VMEM((16, rows, 2 * ROWS), bf16), pltpu.VMEM((2 * ROWS, cols), bf16)]


def weight_scratch(rows, cols):
    groups, first, late = ring_shapes(rows, cols)
    return [
        pltpu.VMEM((groups, 4, 2) + first, bf16),
        pltpu.VMEM((groups, 6) + first, bf16),
        pltpu.VMEM((groups, 4, 2) + late, bf16),
        pltpu.VMEM((groups, 6) + late, bf16),
        pltpu.SemaphoreType.DMA((2 + 12 * groups,)),
        pltpu.SemaphoreType.DMA((2 + 12 * groups,)),
        pltpu.SemaphoreType.DMA((2 + 4 * groups,)),
    ]


def store_part(out, row, start, value):
    rows = slice(row, row + value.shape[0])
    if len(out.shape) == 2:
        out[rows, start : start + value.shape[1]] = value
        return
    size, done = out.shape[2], 0
    while done < value.shape[1]:
        block, offset = divmod(start + done, size)
        count = min(size - offset, value.shape[1] - done)
        out[block, rows, offset : offset + count] = value[:, done : done + count]
        done += count


def pick(core_at, factor, rows, group):
    row = lax.broadcasted_iota(jnp.int32, (256, 512), 0)
    col = lax.broadcasted_iota(jnp.int32, (256, 512), 1)
    wanted = lax.div(row, rows) * (2 * rows) + core_at * rows + lax.rem(row, rows)
    chosen = jnp.where(col == wanted, 1.0, 0.0).astype(bf16)
    return dot(chosen, factor[:, 512 * group : 512 * (group + 1)], NT).astype(bf16)


def partial_block(both_left, both_right, way, at, group, width):
    rows = both_left.shape[1]
    if way == 0:
        chosen = both_left[pl.ds(at * 4, 4)].reshape(4 * rows, 2 * ROWS)
    else:
        chosen = jnp.concatenate([both_left[k * 4 + at] for k in range(4)], axis=0)
    return dot(chosen, both_right[:, group * width : (group + 1) * width]).astype(bf16)


def weight_grad(here, out, scratch, factors=None, far=None, left=None, right=None, parts_hbm=None, ways=WAYS,
                ready=None):
    parts, came, sums, late, send_sems, recv_sems, own_sems = scratch
    x, y, z, core = here
    copies = Copies(send_sems, recv_sems)
    twin = device(x, y, z, 1 - core)
    groups = parts.shape[0]
    rows = out.shape[-2]
    by_rows = groups == 4
    first_shape, late_shape = parts.shape[3:], late.shape[2:]
    width = first_shape[1] if by_rows else 2 * first_shape[1]

    def spot(way, step):
        return around(x if way == 0 else z, step)

    def towards(way):
        def target(step):
            if way == 0:
                return device(around(x, step), y, z, core)
            return device(x, y, around(z, step), core)

        return target

    waits = []
    if parts_hbm is None:
        both_left, both_right = factors
    if parts_hbm is None and ready is None:
        if left is not None:
            far = left.at[:, 1 - core]
            own = pltpu.make_async_copy(
                left.at[:, core], both_left.at[:, :, pl.ds(0, ROWS)], own_sems.at[0]
            )
            own.start()
            waits.append(own.wait)
        if right is not None:
            own = pltpu.make_async_copy(right, both_right.at[pl.ds(0, ROWS)], own_sems.at[1])
            own.start()
            waits.append(own.wait)
        else:
            right = both_right.at[pl.ds(0, ROWS)]
        if far is not None:
            theirs = both_left.at[:, :, pl.ds(ROWS, ROWS)]
            waits.append(copies.start(far, theirs, twin, theirs).wait_recv)
        theirs = both_right.at[pl.ds(ROWS, ROWS)]
        waits.append(copies.start(right, theirs, twin, theirs).wait_recv)
    elif ready is None:
        for group in range(groups):
            for n, (step, half_index) in enumerate(((1, 0), (-1, 1), (0, 0), (0, 1))):
                at = spot(ways[group], step)
                own = pltpu.make_async_copy(
                    parts_hbm.at[group, at, half_index],
                    parts.at[group, at, half_index],
                    own_sems.at[2 + 4 * group + n],
                )
                own.start()
                waits.append(own.wait)
    yield

    def fill(group, step):
        at = spot(ways[group], step)
        value = partial_block(both_left, both_right, ways[group], at, group, width)
        parts[group, at] = value.reshape((2,) + first_shape)

    def fill_all(group):
        tall = both_left[...].reshape(16 * rows, 2 * ROWS)
        value = dot(tall, both_right[:, group * width : (group + 1) * width]).astype(bf16)
        for at in range(4):
            if ways[group] == 0:
                block = value[at * 4 * rows : (at + 1) * 4 * rows]
            else:
                block = jnp.concatenate(
                    [value[(k * 4 + at) * rows : (k * 4 + at + 1) * rows] for k in range(4)],
                    axis=0,
                )
            for half_index in range(2):
                parts[group, at, half_index] = block[
                    :, half_index * first_shape[1] : (half_index + 1) * first_shape[1]
                ]

    if parts_hbm is None:
        for wait in waits:
            wait()
        waits = []
    source = parts if parts_hbm is None else parts_hbm
    first, first_done, second, second_done = {}, {}, {}, {}
    for group in range(4):
        if group >= groups:
            yield
            continue
        if ready is not None:
            ready(group)
        if parts_hbm is None and by_rows:
            for step in (2, 1, -1):
                fill(group, step)
        elif parts_hbm is None:
            fill_all(group)
        first_done[group] = []
        first[group] = ring_sum(
            copies,
            first_done[group],
            towards(ways[group]),
            lambda step, half, group=group: source.at[group, spot(ways[group], step), half],
            lambda step, half, group=group: parts.at[group, spot(ways[group], step), half],
            came.at[group],
        )
        next(first[group])
        yield
    if parts_hbm is None and by_rows:
        for group in range(groups):
            fill(group, 0)
    for wait in waits:
        wait()
    yield
    stages = [range(groups // 2), range(groups // 2, groups)] if by_rows else [range(groups), ()]
    for stage in stages:
        for group in stage:
            next(first[group])
        yield
    for stage in stages:
        for group in stage:
            next(first[group], None)
            for half_index in (0, 1):
                value = first_done[group][0](half_index).astype(bf16)
                if by_rows:
                    sums[group, 2 * half_index : 2 * half_index + 2] = value.reshape(
                        (2, 2) + late_shape
                    )
                else:
                    sums[group, :, half_index] = value.reshape((4,) + late_shape)
            second_done[group] = []

            def block(step, half, group=group):
                return sums.at[group, spot(1 - ways[group], step), half]

            second[group] = ring_sum(
                copies,
                second_done[group],
                towards(1 - ways[group]),
                block,
                block,
                late.at[group],
            )
            next(second[group])
        yield
    for group in range(groups):
        next(second[group])
    yield
    for group in range(groups):
        next(second[group], None)
        for half_index in (0, 1):
            value = second_done[group][0](half_index)
            if by_rows:
                store_part(out, half_index * late_shape[0], group * width, value)
            else:
                store_part(out, 0, group * width + half_index * late_shape[1], value)
    copies.finish()
    yield


def sum_gains(copies, here, given, came_x, part_x, came_z, part_z, came_core, part, came_y, out):
    x, y, z, core = here
    arrivals = [
        copies.start(
            given.at[around(x, hop)], came_x.at[n], device(around(x, hop), y, z, core), came_x.at[n]
        )
        for n, hop in enumerate(HOPS)
    ]
    yield
    for arrival in arrivals:
        arrival.wait_recv()
    part_x[...] = (given[x] + came_x[0]) + (came_x[1] + came_x[2])
    arrivals = [
        copies.start(
            part_x.at[around(z, hop)], came_z.at[n], device(x, y, around(z, hop), core), came_z.at[n]
        )
        for n, hop in enumerate(HOPS)
    ]
    yield
    for arrival in arrivals:
        arrival.wait_recv()
    part_z[...] = (part_x[z] + came_z[0]) + (came_z[1] + came_z[2])
    arrival = copies.start(part_z.at[1 - core], came_core, device(x, y, z, 1 - core), came_core)
    yield
    arrival.wait_recv()
    part[...] = part_z[core] + came_core[...]
    arrivals = [
        copies.start(part, came_y.at[n], device(x, around(y, hop), z, core), came_y.at[n])
        for n, hop in enumerate(HOPS)
    ]
    yield
    for arrival in arrivals:
        arrival.wait_recv()
    out[...] = (part[...] + came_y[0]) + (came_y[1] + came_y[2])
    yield


GAIN_SCRATCH = [(3, 4, 2, 8, HD), (4, 2, 8, HD), (3, 2, 8, HD), (2, 8, HD), (8, HD), (8, HD), (3, 8, HD)]


NORM_ROWS = 32
WIDE = 512


def gain_rows(labels, gains, first):
    return jnp.where(
        labels == 0,
        gains[first : first + 1, :],
        jnp.where(labels == 1, gains[first + 1 : first + 2, :], gains[first + 2 : first + 3, :]),
    )


def steps(count, body):
    lax.fori_loop(0, count, lambda index, carry: (body(index), carry)[1], 0)


def slab(index, size):
    return pl.ds(pl.multiple_of(index * size, size), size)


def visible(key_codes, low, span):
    return (key_codes - low).astype(jnp.uint32) <= span.astype(jnp.uint32)


def key_column(keys_values, z_at, core_at):
    codes = jnp.concatenate(
        [keys_values[z_at, core_at, n, ROWS:, :] for n in range(4)], axis=1
    )
    row = lax.broadcasted_iota(jnp.int32, (CODE_ROWS, HD), 0)
    weight = jnp.where(row == 0, 128.0, jnp.where(row == 1, 1.0, 0.0)).astype(bf16)
    return dot(codes, weight, TN).astype(jnp.int32)


def query_bounds(keys_values, z, core, bounds):
    size = ROWS // 2
    for n in range(4):
        digits = keys_values[z, core, n, ROWS:, :].astype(f32)
        code = (digits[0:1] * 128.0 + digits[1:2]).astype(jnp.int32)
        low = jnp.where(code >= CLIP_STEP, CLIP_STEP, 0)
        for half in range(2):
            at = slice((half * 4 + n) * size, (half * 4 + n + 1) * size)
            bounds[0:1, at] = low[:, half * size : (half + 1) * size]
            bounds[1:2, at] = (code - low)[:, half * size : (half + 1) * size]


def forward_kernel(
    x_ref, label_ref, position_ref, gains_ref, cotangent_ref, weight_hbm, out_weight_hbm, down_hbm,
    q_all_ref, kv_all_ref, o_ref, lse_ref, out_left_ref, total_ref, grad_active_hbm, weights_ref, tops_ref, labels_ref,
    cos_ref, sin_ref, qkv_left_hbm, cotangent_both,
    own_left, far_left, grad_active_ref, weight, out_weight, down, weights, normed, q_own, kv_own, queries, keys_values, top, norm, acc, column, bounds_ref, o_low, back,
    gathered, send_sems, recv_sems, load_sems, weight_sems,
):
    here = place()
    x, y, z, core = here
    twin = device(x, y, z, 1 - core)
    arrived = greet(
        [device(around(x, hop), y, z, core) for hop in HOPS]
        + [device(x, around(y, hop), z, core) for hop in HOPS]
        + [device(x, y, around(z, hop), core) for hop in (1, 3)]
        + [twin]
    )
    load_out = pltpu.make_async_copy(out_weight_hbm, out_weight.at[y], load_sems.at[0])
    load_out.start()
    load = pltpu.make_async_copy(weight_hbm, weight, load_sems.at[1])
    load.start()
    load_down = pltpu.make_async_copy(down_hbm, down, load_sems.at[3])
    copies = Copies(send_sems, recv_sems)

    position = position_ref[...]
    block, row = lax.shift_right_logical(position, 8), lax.bitwise_and(position, 255)
    second = row >= 192
    spot = jnp.where(second, block * 64 + row - 192, block * 192 + row)
    code = spot + jnp.where(second, CLIP_STEP, 0)
    kind = lax.broadcasted_iota(jnp.int32, (CODE_ROWS, ROWS), 0)
    digits = jnp.where(
        kind == 0,
        lax.shift_right_logical(code, 7),
        jnp.where(kind == 1, lax.bitwise_and(code, 127), 0),
    )
    digits = digits.astype(f32).astype(bf16)
    kind = lax.broadcasted_iota(jnp.int32, (8, ROWS), 0)
    small = jnp.where(
        kind == 0,
        lax.shift_right_logical(spot, 7),
        jnp.where(kind == 1, lax.bitwise_and(spot, 127), jnp.where(kind == 2, label_ref[...], 0)),
    )
    small = small.astype(f32).astype(bf16)
    kind = lax.broadcasted_iota(jnp.int32, (8, HD), 0)
    spot_weight = jnp.where(kind == 0, 128.0, jnp.where(kind == 1, 1.0, 0.0)).astype(bf16)
    label_weight = jnp.where(kind == 2, 1.0, 0.0).astype(bf16)
    labels_ref[...] = dot(small, label_weight, TN).astype(jnp.int32)
    feature = lax.rem(lax.broadcasted_iota(jnp.int32, (1, HD), 1), HD // 2).astype(f32)
    angle = dot(small, spot_weight, TN) * jnp.exp(feature * (-2.0 * math.log(10000.0) / HD))
    cos_ref[...] = jnp.cos(angle)
    sin_ref[...] = jnp.sin(angle)

    def normalise(index):
        at = slab(index, NORM_ROWS)
        rows = x_ref[at, :].astype(f32)
        centred = rows - jnp.mean(rows, axis=-1, keepdims=True)
        scale = lax.rsqrt(jnp.mean(centred * centred, axis=-1, keepdims=True) + 1e-05)
        normed[at, :] = (centred * scale * gain_rows(labels_ref[at, :1], gains_ref, 0)).astype(
            bf16
        )

    steps(ROWS // NORM_ROWS, normalise)
    arrived()
    load_out.wait()
    y_up, y_down = device(x, around(y, 1), z, core), device(x, around(y, -1), z, core)
    y_next, y_last, y_far = around(y, 1), around(y, -1), around(y, 2)
    w_last, w_next, w_far, w_twin = [], [], [None] * 4, []
    for n in range(4):
        block = out_weight.at[y, core, n]
        w_last.append(copies.start(block, block, y_up, out_weight.at[y_last, core, n]))
        w_next.append(copies.start(block, block, y_down, out_weight.at[y_next, core, n]))

    def w_onward(n):
        w_last[n].wait_recv()
        block = out_weight.at[y_last, core, n]
        if n < 2:
            w_far[n] = copies.start(block, block, y_up, out_weight.at[y_far, core, n])
        w_twin.append(copies.start(block, block, twin, out_weight.at[y_last, 1 - core, n]))
        w_next[n].wait_recv()
        block = out_weight.at[y_next, core, n]
        if n >= 2:
            w_far[n] = copies.start(block, block, y_down, out_weight.at[y_far, core, n])
        w_twin.append(copies.start(block, block, twin, out_weight.at[y_next, 1 - core, n]))

    load.wait()
    load_down.start()
    cosine, sine = cos_ref[...], sin_ref[...]

    def rotate(values, head):
        part = values[:, head * HD : (head + 1) * HD]
        turned = jnp.concatenate([-part[:, HD // 2 :], part[:, : HD // 2]], axis=1)
        return part * cosine + turned * sine

    key_part = dot(normed[...], weight[1])
    for head in range(4):
        kv_own[head, :ROWS, :HD] = rotate(key_part, head).astype(bf16)
        kv_own[head, ROWS:, :] = digits
    value_part = dot(normed[...], weight[2])
    for head in range(4):
        kv_own[head, :ROWS, HD:] = value_part[:, head * HD : (head + 1) * HD].astype(bf16)
    kv_came, q_came = [None] * 3, [None] * 3

    def send_kv(n):
        other = around(x, HOPS[n])
        kv_came[n] = copies.start(
            kv_own.at[other],
            keys_values.at[z, core, x],
            device(other, y, z, core),
            keys_values.at[z, core, around(x, -HOPS[n])],
        )

    send_kv(0)
    send_kv(1)
    query_part = dot(normed[...], weight[0]) * (HD**-0.5 / math.log(2.0))
    for head in range(4):
        q_own[head] = rotate(query_part, head).astype(bf16).reshape(2, ROWS // 2, HD)
    for n, hop in enumerate(HOPS):
        other = around(x, hop)
        q_came[n] = copies.start(
            q_own.at[other],
            queries.at[:, x],
            device(other, y, z, core),
            queries.at[:, around(x, -hop)],
        )
    send_kv(2)
    keys_values[z, core, x] = kv_own[x]
    queries[:, x] = q_own[x]
    above, below = device(x, y, around(z, 1), core), device(x, y, around(z, -1), core)
    next_z, last_z, far_z = around(z, 1), around(z, -1), around(z, 2)
    pieces = [x] + [around(x, -hop) for hop in HOPS]
    from_last, from_next, from_twin = [], [], []

    def spread(n):
        block = keys_values.at[z, core, pieces[n]]
        from_last.append(copies.start(block, block, above, keys_values.at[last_z, core, pieces[n]]))
        from_next.append(copies.start(block, block, below, keys_values.at[next_z, core, pieces[n]]))
        from_twin.append(copies.start(block, block, twin, keys_values.at[z, 1 - core, pieces[n]]))

    spread(0)
    top[...] = jnp.full_like(top, -1e30)
    norm[...] = jnp.zeros_like(norm)
    acc[...] = jnp.zeros_like(acc)
    load_down.wait()

    def grad_active(index):
        at = slab(index, WIDE)
        grad_active_ref[:, at] = dot(cotangent_ref[...], down[at, :], NT)

    keep_more = [
        pltpu.make_async_copy(
            cotangent_ref, cotangent_both.at[pl.ds(0, ROWS)], load_sems.at[5]
        )
    ]
    theirs = cotangent_both.at[pl.ds(ROWS, ROWS)]
    for_twin = [copies.start(cotangent_ref, theirs, twin, theirs)]
    rows = far_left.shape[1]
    for group in range(4):
        at = pl.ds(4 * group, 4)
        own_left[at] = pick(core, normed, rows, group).reshape(4, rows, ROWS)
        far_left[at] = pick(1 - core, normed, rows, group).reshape(4, rows, ROWS)
    keep_more.append(
        pltpu.make_async_copy(
            own_left, qkv_left_hbm.at[:, :, pl.ds(0, ROWS)], load_sems.at[6]
        )
    )
    theirs = qkv_left_hbm.at[:, :, pl.ds(ROWS, ROWS)]
    for_twin.append(copies.start(far_left, theirs, twin, theirs))
    for copy in keep_more:
        copy.start()
    half_steps = grad_active_ref.shape[1] // WIDE // 2
    keep_grad = pltpu.make_async_copy(grad_active_ref, grad_active_hbm, load_sems.at[4])
    steps(half_steps, grad_active)
    for n in range(3):
        kv_came[n].wait_recv()
        spread(n + 1)
        if n == 1:
            steps(half_steps, lambda index: grad_active(index + half_steps))
            keep_grad.start()
    for arrival in q_came:
        arrival.wait_recv()
    query_bounds(keys_values, z, core, bounds_ref)

    stored, chunks = {}, []

    def attend_half(count, half):
        z_at, core_at = chunks[count]
        at = slice(half * 2 * ROWS, (half + 1) * 2 * ROWS)
        if half == 0:
            column[count % 2] = key_column(keys_values, z_at, core_at)
        query = queries[half].reshape(2 * ROWS, HD)
        keys = keys_values[z_at, core_at, :, :ROWS, :HD].reshape(4 * ROWS, HD)
        values = keys_values[z_at, core_at, :, :ROWS, HD:].reshape(4 * ROWS, HD)
        scores = dot(keys, query, NT)
        codes = jnp.concatenate([column[count % 2]] * (2 * ROWS // HD), axis=1)
        seen = visible(codes, bounds_ref[0:1, at], bounds_ref[1:2, at])
        scores = jnp.where(seen, scores, -1e30)
        top_before = top[0:1, at]
        top_now = jnp.maximum(top_before, jnp.max(scores, axis=0, keepdims=True))
        if count >= 2:
            stored[count - 2, half].wait()
        slot = weights.at[count % 2, half]
        slot[...] = jnp.exp2(scores - top_now).astype(bf16)
        shrink = jnp.exp2(top_before - top_now)
        norm[:, at] = norm[:, at] * shrink + dot(jnp.ones((8, 4 * ROWS), bf16), slot[...])
        top[0:1, at] = top_now
        acc[:, at] = acc[:, at] * shrink + dot(values, slot[...], TN)
        tops_ref[z_at, core_at, :, at] = jnp.broadcast_to(top_now, (8, 2 * ROWS))
        copy = pltpu.make_async_copy(
            slot, weights_ref.at[z_at, core_at, half], weight_sems.at[count % 2, half]
        )
        copy.start()
        stored[count, half] = copy

    def attend(z_at, core_at):
        chunks.append((z_at, core_at))
        for half in range(2):
            attend_half(len(chunks) - 1, half)

    low_far, high_far, twin_last, twin_next = [], [], [], []

    def onward(n):
        piece = pieces[n]
        from_last[n].wait_recv()
        block = keys_values.at[last_z, core, piece]
        low = block.at[pl.ds(0, ROWS // 2)]
        low_far.append(
            copies.start(low, low, above, keys_values.at[far_z, core, piece, pl.ds(0, ROWS // 2)])
        )
        twin_last.append(
            copies.start(block, block, twin, keys_values.at[last_z, 1 - core, piece])
        )
        from_next[n].wait_recv()
        block = keys_values.at[next_z, core, piece]
        high = block.at[pl.ds(ROWS // 2, ROWS // 2 + CODE_ROWS)]
        high_far.append(
            copies.start(
                high,
                high,
                below,
                keys_values.at[far_z, core, piece, pl.ds(ROWS // 2, ROWS // 2 + CODE_ROWS)],
            )
        )
        twin_next.append(
            copies.start(block, block, twin, keys_values.at[next_z, 1 - core, piece])
        )

    def take(arrivals):
        for arrival in arrivals:
            arrival.wait_recv()

    onward(0)
    w_onward(0)
    attend(z, core)
    onward(1)
    onward(2)
    take(from_twin)
    attend(z, 1 - core)
    onward(3)
    w_onward(1)
    attend(last_z, core)
    attend(next_z, core)
    w_onward(2)
    take(twin_last)
    attend(last_z, 1 - core)
    twin_far = []
    for n, piece in enumerate(pieces):
        low_far[n].wait_recv()
        high_far[n].wait_recv()
        block = keys_values.at[far_z, core, piece]
        twin_far.append(copies.start(block, block, twin, keys_values.at[far_z, 1 - core, piece]))
    take(twin_next)
    attend(next_z, 1 - core)
    w_onward(3)
    size = ROWS // 2
    came_back = {}

    def give_back(half):
        at = slice(half * 2 * ROWS, (half + 1) * 2 * ROWS)
        total_norm = norm[0:1, at]
        attended = (acc[:, at] / total_norm).T
        o_low[half] = attended.astype(bf16).reshape(4, size, HD)
        came_back[half] = [
            copies.start(
                o_low.at[half, around(x, hop)],
                back.at[half, x],
                device(around(x, hop), y, z, core),
                back.at[half, around(x, -hop)],
            )
            for hop in HOPS
        ]
        back[half, x] = o_low[half, x]
        o_ref[at, :] = attended
        lse_ref[:, at] = jnp.broadcast_to(top[0:1, at] + jnp.log2(total_norm), (8, 2 * ROWS))

    ring_last, ring_next, ring_low, ring_high = [], [], [], []

    def spread_y(half):
        take(came_back[half])
        for n in range(4):
            gathered[y, half, :, n * HD : (n + 1) * HD] = back[half, n]
        block = gathered.at[y, half]
        ring_last.append(copies.start(block, block, y_up, gathered.at[y_last, half]))
        ring_next.append(copies.start(block, block, y_down, gathered.at[y_next, half]))

    def onward_y(half):
        low, high = pl.ds(0, size // 2), pl.ds(size // 2, size // 2)
        ring_last[half].wait_recv()
        block = gathered.at[y_last, half, low]
        ring_low.append(copies.start(block, block, y_up, gathered.at[y_far, half, low]))
        ring_next[half].wait_recv()
        block = gathered.at[y_next, half, high]
        ring_high.append(copies.start(block, block, y_down, gathered.at[y_far, half, high]))

    chunks += [(far_z, core), (far_z, 1 - core)]
    attend_half(6, 0)
    take(twin_far)
    attend_half(7, 0)
    give_back(0)
    attend_half(6, 1)
    spread_y(0)
    attend_half(7, 1)
    give_back(1)
    keep = pltpu.make_async_copy(keys_values, kv_all_ref, load_sems.at[2])
    keep.start()
    q_all_ref[...] = queries[...]
    for n in range(4):
        w_far[n].wait_recv()
        block = out_weight.at[y_far, core, n]
        w_twin.append(copies.start(block, block, twin, out_weight.at[y_far, 1 - core, n]))
    local = 4 * HD
    spread_y(1)
    out_rows = out_left_ref.shape[2]
    for core_at in range(2):
        out_left_ref[:, core_at] = pick(
            core_at, gathered[y].reshape(ROWS, local), out_rows, 0
        ).reshape(16, out_rows, ROWS)
    keep_grad.wait()
    summed = grad_active_ref

    def project(index, owners, first, final):
        at = slab(index, WIDE)
        part = sum(
            dot(
                gathered[n].reshape(ROWS, local),
                out_weight[n, :, :, :, at].reshape(local, WIDE),
            )
            for n in owners
        )
        if not first:
            part = part + summed[:, at]
        if final:
            total_ref[:, at] = part.astype(bf16)
        else:
            summed[:, at] = part

    count = total_ref.shape[1] // WIDE
    steps(count, lambda index: project(index, (y,), True, False))
    take(w_twin)
    onward_y(0)
    onward_y(1)
    steps(count, lambda index: project(index, (y_last, y_next), False, False))
    take(ring_low + ring_high)
    steps(count, lambda index: project(index, (y_far,), False, True))
    copies.finish()
    keep.wait()
    for copy in keep_more:
        copy.wait()
    take(for_twin)
    for count in (6, 7):
        for half in range(2):
            stored[count, half].wait()


def attention_forward(
    activations, labels, position, gains, cotangent, weight, out_weight, down_weight
):
    width = out_weight.shape[1]
    whole = pl.BlockSpec(memory_space=pltpu.VMEM)
    anywhere = pl.BlockSpec(memory_space=pl.ANY)
    count = 3 + 3 + 12 + 16 + 4 + 6 + 8 + 8 + 4 + 8 + 4 + 2
    local = out_weight.shape[0]
    pieces = (2, 4, out_weight.shape[0] // 8, width)
    return pl.pallas_call(
        forward_kernel,
        out_shape=[
            jax.ShapeDtypeStruct((2, 4, ROWS // 2, HD), bf16),
            jax.ShapeDtypeStruct((4, 2, 4, ROWS + CODE_ROWS, 2 * HD), bf16),
            jax.ShapeDtypeStruct((4 * ROWS, HD), f32),
            jax.ShapeDtypeStruct((8, 4 * ROWS), f32),
            jax.ShapeDtypeStruct((16, 2, local // 32, ROWS), bf16),
            jax.ShapeDtypeStruct((ROWS, width), bf16),
            jax.ShapeDtypeStruct((ROWS, down_weight.shape[0]), f32),
            jax.ShapeDtypeStruct((4, 2, 2, 4 * ROWS, 2 * ROWS), bf16),
            jax.ShapeDtypeStruct((4, 2, 8, 4 * ROWS), f32),
            jax.ShapeDtypeStruct((ROWS, HD), jnp.int32),
            jax.ShapeDtypeStruct((ROWS, HD), f32),
            jax.ShapeDtypeStruct((ROWS, HD), f32),
            jax.ShapeDtypeStruct((16, width // 32, 2 * ROWS), bf16),
            jax.ShapeDtypeStruct((2 * ROWS, width), bf16),
        ],
        in_specs=[whole] * 5 + [anywhere] * 3,
        out_specs=[whole, anywhere]
        + [whole] * 4
        + [anywhere, anywhere]
        + [whole] * 4
        + [anywhere] * 2,
        scratch_shapes=[
            pltpu.VMEM((16, width // 32, ROWS), bf16),
            pltpu.VMEM((16, width // 32, ROWS), bf16),
            pltpu.VMEM((ROWS, down_weight.shape[0]), f32),
            pltpu.VMEM(weight.shape, bf16),
            pltpu.VMEM((4,) + pieces, bf16),
            pltpu.VMEM(down_weight.shape, bf16),
            pltpu.VMEM((2, 2, 4 * ROWS, 2 * ROWS), bf16),
            pltpu.VMEM(activations.shape, bf16),
            pltpu.VMEM((4, 2, ROWS // 2, HD), bf16),
            pltpu.VMEM((4, ROWS + CODE_ROWS, 2 * HD), bf16),
            pltpu.VMEM((2, 4, ROWS // 2, HD), bf16),
            pltpu.VMEM((4, 2, 4, ROWS + CODE_ROWS, 2 * HD), bf16),
            pltpu.VMEM((8, 4 * ROWS), f32),
            pltpu.VMEM((8, 4 * ROWS), f32),
            pltpu.VMEM((HD, 4 * ROWS), f32),
            pltpu.VMEM((2, 4 * ROWS, HD), jnp.int32),
            pltpu.VMEM((8, 4 * ROWS), jnp.int32),
            pltpu.VMEM((2, 4, ROWS // 2, HD), bf16),
            pltpu.VMEM((2, 4, ROWS // 2, HD), bf16),
            pltpu.VMEM((4, 2, ROWS // 2, 4 * HD), bf16),
            pltpu.SemaphoreType.DMA((count,)),
            pltpu.SemaphoreType.DMA((count,)),
            pltpu.SemaphoreType.DMA((7,)),
            pltpu.SemaphoreType.DMA((2, 2)),
        ],
        compiler_params=pltpu.CompilerParams(
            collective_id=0, has_side_effects=True, vmem_limit_bytes=VMEM_LIMIT
        ),
        name="attention_forward",
    )(
        activations,
        labels,
        position,
        gains,
        cotangent,
        weight,
        out_weight.reshape(pieces),
        down_weight,
    )


def gelu_and_slope(hidden):
    scale = math.sqrt(2.0 / math.pi)
    square = hidden * hidden
    bent = jnp.tanh(scale * hidden * (1.0 + 0.044715 * square))
    half = 0.5 * (1.0 + bent)
    slope = half + 0.5 * hidden * (1.0 - bent * bent) * (scale * (1.0 + 3 * 0.044715 * square))
    return hidden * half, slope


def middle_kernel(
    x_ref, attn_ref, labels_ref, gains_ref, cotangent_hbm, out_weight_hbm, grad_active_hbm, up_hbm, down_hbm,
    g_mid_hbm, g_low_hbm, heads_ref, mlp_hbm, down_parts_hbm, gains_out_ref, grad_up_ref,
    up, down, out_weight, grad_active, g_mid, g_low, mlp, xhat, inverse, normed, active, far, far_down, down_left,
    down_right, down_parts, given, g_heads, came, all_rows, y_send, y_recv, load_sems, x_send, x_recv,
    exchange_send, exchange_recv, both_left, both_right, *up_scratch,
):
    here = place()
    x, y, z, core = here
    arrived = greet(
        [device(x, around(y, hop), z, core) for hop in HOPS]
        + [device(around(x, hop), y, z, core) for hop in HOPS]
        + [device(x, y, around(z, hop), core) for hop in (1, 3)]
        + [device(x, y, z, 1 - core)]
    )
    used = [0]

    def move(src, dst):
        copy = pltpu.make_async_copy(src, dst, load_sems.at[used[0]])
        used[0] += 1
        copy.start()
        return copy

    load_up = move(up_hbm, up)
    load_active = move(grad_active_hbm, grad_active)
    width = x_ref.shape[1]
    hidden_width = up.shape[1]

    def norm(index):
        at = slab(index, NORM_ROWS)
        middle = x_ref[at, :].astype(f32) + attn_ref[at, :].astype(f32)
        centred = middle - jnp.mean(middle, axis=-1, keepdims=True)
        scale = lax.rsqrt(jnp.mean(centred * centred, axis=-1, keepdims=True) + 1e-05)
        unit = centred * scale
        xhat[at, :] = unit
        inverse[at, :] = jnp.broadcast_to(scale, (NORM_ROWS, HD))
        normed[at, :] = (unit * gain_rows(labels_ref[at, :1], gains_ref, 3)).astype(bf16)

    steps(ROWS // NORM_ROWS, norm)
    rows = grad_up_ref.shape[0]
    for group in range(4):
        at = pl.ds(4 * group, 4)
        both_left[at, :, pl.ds(0, ROWS)] = pick(core, normed, rows, group).reshape(4, rows, ROWS)
        far[at] = pick(1 - core, normed, rows, group).reshape(4, rows, ROWS)
    load_up.wait()
    load_active.wait()
    load_down = move(down_hbm, down)
    load_cotangent = move(cotangent_hbm, down_right)
    load_out = move(out_weight_hbm, out_weight)
    arrived()
    twin = device(x, y, z, 1 - core)
    exchange = Copies(exchange_send, exchange_recv)
    theirs = both_left.at[:, :, pl.ds(ROWS, ROWS)]
    left_came = exchange.start(far, theirs, twin, theirs)
    right_came = []
    for index in range(hidden_width // WIDE):
        at = pl.ds(index * WIDE, WIDE)
        hidden = dot(normed[...], up[:, at])
        value, slope = gelu_and_slope(hidden)
        active[:, at] = value.astype(bf16)
        both_right[pl.ds(0, ROWS), at] = (grad_active[:, at] * slope).astype(bf16)
        theirs = both_right.at[pl.ds(ROWS, ROWS), at]
        right_came.append(
            exchange.start(both_right.at[pl.ds(0, ROWS), at], theirs, twin, theirs)
        )

    def ready(group):
        if group == 0:
            left_came.wait_recv()
        right_came[group].wait_recv()

    ring = weight_grad(here, grad_up_ref, up_scratch, (both_left, both_right), ready=ready)
    advance(ring)
    copies = Copies(y_send, y_recv)
    half_steps = width // WIDE // 2
    over_y = [
        sum_over_y(copies, here, given.at[half], came.at[half], all_rows.at[half])
        for half in range(2)
    ]

    def back_up(index, half):
        at = slab(index + half * half_steps, WIDE)
        part = dot(both_right[pl.ds(0, ROWS), :], up[at, :], NT)
        given[half, :, :, slab(index, WIDE)] = part.astype(bf16).reshape(
            SIDE, ROWS // SIDE, WIDE
        )

    def feed_out(index, half):
        at = slab(index + half * half_steps, WIDE)
        mlp[half, :, :, slab(index, WIDE)] = (
            dot(active[...], down[:, at]).astype(bf16).reshape(SIDE, ROWS // SIDE, WIDE)
        )

    groups, first_shape = down_parts.shape[0], down_parts.shape[3:]
    keep = []

    def fill_down(group):
        for at in range(4):
            down_parts[group, at] = partial_block(
                down_left, down_right, DOWN_WAYS[group], at, group, first_shape[1]
            ).reshape((2,) + first_shape)
        keep.append(move(down_parts.at[group], down_parts_hbm.at[group]))

    steps(half_steps, lambda index: back_up(index, 0))
    advance(over_y[0])
    advance(ring)
    steps(half_steps, lambda index: back_up(index, 1))
    advance(over_y[1])
    advance(ring, 2)
    advance(over_y[0])
    advance(ring, 2)
    load_down.wait()
    feed_out(0, 0)
    advance(over_y[1])
    feed_out(1, 0)
    advance(over_y[0])
    feed_out(0, 1)
    advance(over_y[1])
    feed_out(1, 1)
    keep.append(move(mlp, mlp_hbm))
    for group in range(4):
        at = pl.ds(4 * group, 4)
        down_left[at, :, pl.ds(0, ROWS)] = pick(core, active, rows, group).reshape(4, rows, ROWS)
        far_down[at] = pick(1 - core, active, rows, group).reshape(4, rows, ROWS)
    theirs = down_left.at[:, :, pl.ds(ROWS, ROWS)]
    down_came = exchange.start(far_down, theirs, twin, theirs)
    advance(over_y[0])
    advance(ring)
    advance(over_y[1])
    load_cotangent.wait()
    down_came.wait_recv()
    fill_down(0)
    advance(ring)
    fill_down(1)
    advance(ring)
    load_out.wait()
    gains_out_ref[...] = jnp.zeros_like(gains_out_ref)
    advance(over_y[0])
    advance(over_y[1])

    def back(index):
        at = slab(index, NORM_ROWS)
        grad = summed_rows(all_rows, index)
        labels = labels_ref[at, :1]
        unit = xhat[at, :]
        product = grad * unit
        for mode in range(3):
            gains_out_ref[mode + 3 : mode + 4, :] += jnp.sum(
                jnp.where(labels == mode, product, 0.0), axis=0, keepdims=True
            )
        gain = gain_rows(labels, gains_ref, 3)
        grad = grad * gain
        mean = jnp.mean(grad, axis=-1, keepdims=True)
        along = jnp.mean(product * gain, axis=-1, keepdims=True)
        total = down_right[at, :].astype(f32) + inverse[at, :1] * (grad - mean - unit * along)
        g_mid[at, :] = total
        g_low[at, :] = total.astype(bf16)

    steps(ROWS // NORM_ROWS, back)
    by_head = dot(g_low[...], out_weight[...], NT).astype(bf16)
    for head in range(4):
        g_heads[head] = by_head[:, head * HD : (head + 1) * HD].reshape(2, ROWS // 2, HD)
    x_copies = Copies(x_send, x_recv)
    arrivals = [
        x_copies.start(
            g_heads.at[around(x, hop)],
            heads_ref.at[:, x],
            device(around(x, hop), y, z, core),
            heads_ref.at[:, around(x, -hop)],
        )
        for hop in HOPS
    ]
    heads_ref[:, x] = g_heads[x]
    keep += [move(g_mid, g_mid_hbm), move(g_low, g_low_hbm)]
    advance(ring)
    fill_down(2)
    advance(ring)
    fill_down(3)
    advance(ring)
    for arrival in arrivals:
        arrival.wait_recv()
    copies.finish()
    x_copies.finish()
    exchange.finish()
    for copy in keep:
        copy.wait()


def middle(
    activations, attn_sum, labels, gains, cotangent, out_weight, grad_active, up_weight, down_weight
):
    width, hidden_width = up_weight.shape
    rows = width // 32
    down_rows = hidden_width // 32
    whole = pl.BlockSpec(memory_space=pltpu.VMEM)
    anywhere = pl.BlockSpec(memory_space=pl.ANY)
    summed = (2, SIDE, ROWS // SIDE, width // 2)
    groups, first_shape, late_shape = ring_shapes(down_rows, width)
    down_parts = (groups, 4, 2) + first_shape
    return pl.pallas_call(
        middle_kernel,
        out_shape=[
            jax.ShapeDtypeStruct((ROWS, width), f32),
            jax.ShapeDtypeStruct((ROWS, width), bf16),
            jax.ShapeDtypeStruct((2, 4, ROWS // 2, HD), bf16),
            jax.ShapeDtypeStruct(summed, bf16),
            jax.ShapeDtypeStruct(down_parts, bf16),
            jax.ShapeDtypeStruct((8, width), f32),
            jax.ShapeDtypeStruct((rows, hidden_width), f32),
        ],
        in_specs=[whole] * 4 + [anywhere] * 5,
        out_specs=[anywhere] * 2 + [whole] + [anywhere] * 2 + [whole] * 2,
        scratch_shapes=[
            pltpu.VMEM(up_weight.shape, bf16),
            pltpu.VMEM(down_weight.shape, bf16),
            pltpu.VMEM(out_weight.shape, bf16),
            pltpu.VMEM((ROWS, hidden_width), f32),
            pltpu.VMEM((ROWS, width), f32),
            pltpu.VMEM((ROWS, width), bf16),
            pltpu.VMEM(summed, bf16),
            pltpu.VMEM((ROWS, width), f32),
            pltpu.VMEM((ROWS, HD), f32),
            pltpu.VMEM((ROWS, width), bf16),
            pltpu.VMEM((ROWS, hidden_width), bf16),
            pltpu.VMEM((16, rows, ROWS), bf16),
            pltpu.VMEM((16, down_rows, ROWS), bf16),
        ]
        + factor_scratch(down_rows, width)
        + [
            pltpu.VMEM(down_parts, bf16),
            pltpu.VMEM(summed, bf16),
            pltpu.VMEM((4, 2, ROWS // 2, HD), bf16),
        ]
        + sum_scratch(width)
        + [pltpu.SemaphoreType.DMA((12,))]
        + [pltpu.SemaphoreType.DMA((3,)), pltpu.SemaphoreType.DMA((3,))]
        + [pltpu.SemaphoreType.DMA((6,)), pltpu.SemaphoreType.DMA((6,))]
        + factor_scratch(rows, hidden_width)
        + weight_scratch(rows, hidden_width),
        compiler_params=pltpu.CompilerParams(
            collective_id=2, has_side_effects=True, vmem_limit_bytes=VMEM_LIMIT
        ),
        name="middle",
    )(
        activations,
        attn_sum,
        labels,
        gains,
        cotangent,
        out_weight,
        grad_active,
        up_weight,
        down_weight,
    )


def backward_kernel(
    grads, q_ref, kv_hbm, o_ref, lse_ref, tops_ref, weights_hbm, down_parts_hbm, out_left_hbm, g_low_hbm, given_hbm,
    packed_ref, grad_down_ref, grad_out_ref, total_hbm,
    given_ref, keys_values, weights, delta, grad_q, parts, met, came, sums, q_low, back_q,
    back_kv, send_sems, recv_sems, load_sems, weight_sems, y_came, all_rows, y_send, y_recv, *more,
):
    here = place()
    x, y, z, core = here
    twin = device(x, y, z, 1 - core)
    arrived = greet(
        [device(around(x, hop), y, z, core) for hop in HOPS]
        + [device(x, around(y, hop), z, core) for hop in HOPS]
        + [device(x, y, around(z, hop), core) for hop in (1, 3)]
        + [twin]
    )
    next_z, last_z, far_z = around(z, 1), around(z, -1), around(z, 2)
    order = [
        (at, core_at)
        for at in (far_z, next_z, last_z, z)
        for core_at in (1 - core, core)
    ]

    def fetch(index):
        copy = pltpu.make_async_copy(
            weights_hbm.at[order[index][0], order[index][1]],
            weights.at[index % 3],
            weight_sems.at[index % 3],
        )
        copy.start()
        return copy

    load_given = pltpu.make_async_copy(given_hbm, given_ref, load_sems.at[8])
    load_given.start()
    fetched = [fetch(0)]
    loads = []
    for n, (z_at, core_at) in enumerate(order):
        loads.append(
            pltpu.make_async_copy(
                kv_hbm.at[z_at, core_at], keys_values.at[z_at, core_at], load_sems.at[n]
            )
        )
        loads[n].start()
        if n == 0:
            fetched.append(fetch(1))
    copies = Copies(send_sems, recv_sems)
    y_copies = Copies(y_send, y_recv)
    over_y = [
        sum_over_y(y_copies, here, given_ref.at[half], y_came.at[half], all_rows.at[half])
        for half in range(2)
    ]
    ring = weight_grad(here, grad_down_ref, more[:7], parts_hbm=down_parts_hbm, ways=DOWN_WAYS)
    ring_out = weight_grad(
        here, grad_out_ref, more[9:], more[7:9], left=out_left_hbm, right=g_low_hbm
    )
    arrived()
    advance(ring, 5)
    load_given.wait()
    for half in over_y:
        advance(half)
    advance(ring_out)
    grad_q[...] = jnp.zeros_like(grad_q)
    product = grads[...].reshape(4 * ROWS, HD).astype(f32) * o_ref[...]
    delta[...] = lax.dot_general(
        jnp.ones((8, HD), f32), product, NT, preferred_element_type=f32, precision=highest
    )
    done = []

    def chunk(z_at, core_at):
        index = len(done)
        done.append(index)
        if index + 2 < len(order):
            fetched.append(fetch(index + 2))
        loads[index].wait()
        fetched[index].wait()
        keys = keys_values[z_at, core_at, :, :ROWS, :HD].reshape(4 * ROWS, HD)
        values = keys_values[z_at, core_at, :, :ROWS, HD:].reshape(4 * ROWS, HD)
        grad_k = grad_v = 0.0
        for half in range(2):
            at = slice(half * 2 * ROWS, (half + 1) * 2 * ROWS)
            slot = weights.at[index % 3, half]
            query = q_ref[half].reshape(2 * ROWS, HD)
            grad = grads[half].reshape(2 * ROWS, HD)
            rescale = jnp.exp2(tops_ref[z_at, core_at, 0:1, at] - lse_ref[0:1, at])
            grad_weights = dot(values, grad, NT)
            taken = slot[...].astype(f32) * rescale
            slot[...] = taken.astype(bf16)
            grad_v += dot(slot[...], grad)
            slot[...] = (taken * (grad_weights - delta[0:1, at])).astype(bf16)
            grad_k += dot(slot[...], query)
            grad_q[:, at] += dot(keys, slot[...], TN)
        parts[z_at, core_at] = (
            jnp.concatenate([grad_k * math.log(2.0), grad_v], axis=1)
            .astype(bf16)
            .reshape(2, 2 * ROWS, 2 * HD)
        )

    def hand_over(z_at):
        return copies.start(
            parts.at[z_at, 1 - core], met.at[z_at], twin, met.at[z_at]
        )

    def join(z_at):
        parts[z_at, core] = (
            parts[z_at, core].astype(f32) + met[z_at].astype(f32)
        ).astype(bf16)

    above, below = device(x, y, next_z, core), device(x, y, last_z, core)
    chunk(far_z, 1 - core)
    far_met = hand_over(far_z)
    advance(ring_out, 5)
    chunk(far_z, core)
    chunk(next_z, 1 - core)
    next_met = hand_over(next_z)
    far_met.wait_recv()
    join(far_z)
    from_last = copies.start(parts.at[far_z, core, 0], came.at[0], above, came.at[0])
    from_next = copies.start(parts.at[far_z, core, 1], came.at[1], below, came.at[1])
    for half in over_y:
        advance(half)
    advance(ring, 2)
    chunk(next_z, core)
    chunk(last_z, 1 - core)
    last_met = hand_over(last_z)
    next_met.wait_recv()
    join(next_z)
    raw_last = copies.start(parts.at[next_z, core, 1], came.at[2], above, came.at[2])
    for half in over_y:
        advance(half)
    chunk(last_z, core)
    chunk(z, 1 - core)
    own_met = hand_over(z)
    last_met.wait_recv()
    join(last_z)
    raw_next = copies.start(parts.at[last_z, core, 0], came.at[3], below, came.at[3])
    from_last.wait_recv()
    parts[next_z, core, 0] = (
        parts[next_z, core, 0].astype(f32) + came[0].astype(f32)
    ).astype(bf16)
    sum_last = copies.start(parts.at[next_z, core, 0], came.at[4], above, came.at[4])
    from_next.wait_recv()
    parts[last_z, core, 1] = (
        parts[last_z, core, 1].astype(f32) + came[1].astype(f32)
    ).astype(bf16)
    sum_next = copies.start(parts.at[last_z, core, 1], came.at[5], below, came.at[5])
    for half in over_y:
        advance(half)
    advance(ring)
    advance(ring_out)
    chunk(z, core)
    q_low[...] = (grad_q[...] * (HD**-0.5)).T.astype(bf16).reshape(2, 4, ROWS // 2, HD)
    arrivals = []
    for hop in HOPS:
        other = around(x, hop)
        arrivals.append(
            copies.start(
                q_low.at[:, other],
                back_q.at[x],
                device(other, y, z, core),
                back_q.at[around(x, -hop)],
            )
        )
    back_q[x] = q_low[:, x]
    advance(ring)
    advance(ring_out, 2)
    own_met.wait_recv()
    raw_last.wait_recv()
    raw_next.wait_recv()
    sum_last.wait_recv()
    sum_next.wait_recv()
    mine = parts[z, core].astype(f32) + met[z].astype(f32)
    low = mine[0] + came[4].astype(f32) + came[3].astype(f32)
    high = mine[1] + came[2].astype(f32) + came[5].astype(f32)
    sums[0:2] = low.astype(bf16).reshape(2, ROWS, 2 * HD)
    sums[2:4] = high.astype(bf16).reshape(2, ROWS, 2 * HD)
    for hop in HOPS:
        other = around(x, hop)
        arrivals.append(
            copies.start(
                sums.at[other],
                back_kv.at[x],
                device(other, y, z, core),
                back_kv.at[around(x, -hop)],
            )
        )
    back_kv[x] = sums[x]
    for half in over_y:
        advance(half)
    keep = pltpu.make_async_copy(all_rows, total_hbm, load_sems.at[9])
    keep.start()
    advance(ring)
    advance(ring_out, 2)
    advance(ring)
    advance(ring_out)
    advance(ring)
    for arrival in arrivals:
        arrival.wait_recv()
    for n in range(4):
        packed_ref[n, :, :HD] = back_q[n].reshape(ROWS, HD)
        packed_ref[n, :, HD:] = back_kv[n]
    keep.wait()
    copies.finish()
    y_copies.finish()


def attention_backward(
    grad_heads, q_all, kv_all, o_all, lse, tops, weights, down_parts, out_left, g_low, given
):
    whole = pl.BlockSpec(memory_space=pltpu.VMEM)
    anywhere = pl.BlockSpec(memory_space=pl.ANY)
    count = 4 + 6 + 6
    width = g_low.shape[1]
    down_rows, out_rows = down_parts.shape[3] // 2, out_left.shape[2]
    return pl.pallas_call(
        backward_kernel,
        out_shape=[
            jax.ShapeDtypeStruct((4, ROWS, 3 * HD), bf16),
            jax.ShapeDtypeStruct((down_rows, width), f32),
            jax.ShapeDtypeStruct((out_rows, width), f32),
            jax.ShapeDtypeStruct(given.shape, bf16),
        ],
        in_specs=[whole, whole, anywhere] + [whole] * 3 + [anywhere] * 5,
        out_specs=[whole] * 3 + [anywhere],
        scratch_shapes=[
            pltpu.VMEM(given.shape, bf16),
            pltpu.VMEM((4, 2, 4, ROWS + CODE_ROWS, 2 * HD), bf16),
            pltpu.VMEM((3, 2, 4 * ROWS, 2 * ROWS), bf16),
            pltpu.VMEM((8, 4 * ROWS), f32),
            pltpu.VMEM((HD, 4 * ROWS), f32),
            pltpu.VMEM((4, 2, 2, 2 * ROWS, 2 * HD), bf16),
            pltpu.VMEM((4, 2, 2 * ROWS, 2 * HD), bf16),
            pltpu.VMEM((6, 2 * ROWS, 2 * HD), bf16),
            pltpu.VMEM((4, ROWS, 2 * HD), bf16),
            pltpu.VMEM((2, 4, ROWS // 2, HD), bf16),
            pltpu.VMEM((4, 2, ROWS // 2, HD), bf16),
            pltpu.VMEM((4, ROWS, 2 * HD), bf16),
            pltpu.SemaphoreType.DMA((count,)),
            pltpu.SemaphoreType.DMA((count,)),
            pltpu.SemaphoreType.DMA((10,)),
            pltpu.SemaphoreType.DMA((3,)),
        ]
        + sum_scratch(2 * given.shape[3])
        + weight_scratch(down_rows, width)
        + factor_scratch(out_rows, width)
        + weight_scratch(out_rows, width),
        compiler_params=pltpu.CompilerParams(
            collective_id=1, has_side_effects=True, vmem_limit_bytes=VMEM_LIMIT
        ),
        name="attention_backward",
    )(
        grad_heads, q_all, kv_all, o_all, lse, tops, weights, down_parts, out_left, g_low, given
    )


def last_kernel(
    x_ref, labels_ref, gains_ref, packed_ref, cos_ref, sin_ref, gains_two_ref, left_hbm, attn_hbm, mlp_hbm, g_mid_hbm,
    weight_hbm,
    input_hbm, layer_hbm, gains_out_ref, grad_qkv_ref,
    input_ref, layer_ref, attn, mlp, g_mid, weight, xhat, inverse, given, gains_part, gains_given, came, all_rows, y_send, y_recv, load_sems,
    qkv_left, qkv_right, *more,
):
    gain_scratch = more[: len(GAIN_SCRATCH)]
    gain_send, gain_recv = more[len(GAIN_SCRATCH) : len(GAIN_SCRATCH) + 2]
    qkv_scratch = more[len(GAIN_SCRATCH) + 2 :]
    here = place()
    x, y, z, core = here
    loads = []
    for n, (src, dst) in enumerate(
        (
            (weight_hbm, weight),
            (left_hbm, qkv_left),
            (attn_hbm, attn),
            (mlp_hbm, mlp),
            (g_mid_hbm, g_mid),
        )
    ):
        loads.append(pltpu.make_async_copy(src, dst, load_sems.at[n]))
    loads[0].start()
    arrived = greet(
        [device(x, around(y, hop), z, core) for hop in HOPS]
        + [device(around(x, hop), y, z, core) for hop in HOPS]
        + [device(x, y, around(z, hop), core) for hop in HOPS]
        + [device(x, y, z, 1 - core)]
    )
    width = x_ref.shape[1]
    local = qkv_right.shape[1] // 3

    cosine, sine = cos_ref[...], sin_ref[...]
    for head in range(4):
        for part in range(3):
            grad = packed_ref[head, :, part * HD : (part + 1) * HD]
            if part < 2:
                grad = grad.astype(f32)
                scaled = grad * sine
                grad = (
                    grad * cosine
                    + jnp.concatenate([scaled[:, HD // 2 :], -scaled[:, : HD // 2]], axis=1)
                ).astype(bf16)
            start = part * local + head * HD
            qkv_right[0:ROWS, start : start + HD] = grad
    arrived()
    ring = weight_grad(here, grad_qkv_ref, qkv_scratch, (qkv_left, qkv_right))
    advance(ring)
    loads[0].wait()
    for load in loads[1:]:
        load.start()
    copies = Copies(y_send, y_recv)
    half_steps = width // WIDE // 2
    over_y = [
        sum_over_y(copies, here, given.at[half], came.at[half], all_rows.at[half])
        for half in range(2)
    ]

    def back_in(index, half):
        at = slab(index + half * half_steps, WIDE)
        part = sum(
            dot(qkv_right[pl.ds(0, ROWS), k * local : (k + 1) * local], weight[k, at, :], NT)
            for k in range(3)
        )
        given[half, :, :, slab(index, WIDE)] = part.astype(bf16).reshape(
            SIDE, ROWS // SIDE, WIDE
        )

    steps(half_steps, lambda index: back_in(index, 0))
    advance(over_y[0])
    loads[1].wait()
    advance(ring)
    steps(half_steps, lambda index: back_in(index, 1))
    advance(over_y[1])
    advance(ring, 2)
    advance(over_y[0])
    advance(ring, 2)
    gains_part[...] = 0.25 * gains_two_ref[...]

    def norm(index):
        at = slab(index, NORM_ROWS)
        rows = x_ref[at, :].astype(f32)
        centred = rows - jnp.mean(rows, axis=-1, keepdims=True)
        scale = lax.rsqrt(jnp.mean(centred * centred, axis=-1, keepdims=True) + 1e-05)
        unit = centred * scale
        xhat[at, :] = unit
        inverse[at, :] = jnp.broadcast_to(scale, (NORM_ROWS, HD))
        labels = labels_ref[at, :1]
        product = summed_rows(given, index) * unit
        for mode in range(3):
            gains_part[mode : mode + 1, :] += jnp.sum(
                jnp.where(labels == mode, product, 0.0), axis=0, keepdims=True
            )

    norm_steps = ROWS // NORM_ROWS // 2
    steps(norm_steps, norm)
    advance(over_y[1])
    advance(over_y[0])
    steps(norm_steps, lambda index: norm(index + norm_steps))
    advance(over_y[1])
    for owner in range(32):
        gains_given[owner // 8, (owner // 2) % 4, owner % 2] = jnp.zeros((8, HD), f32)
        gains_given[owner // 8, (owner // 2) % 4, owner % 2, :, :64] = gains_part[
            :, owner * 64 : (owner + 1) * 64
        ]
    gain_copies = Copies(gain_send, gain_recv)
    over_all = sum_gains(gain_copies, here, gains_given, *gain_scratch, gains_out_ref)
    advance(over_all)
    advance(ring)
    for load in loads[2:]:
        load.wait()

    def finish_layer(index):
        at = slab(index, NORM_ROWS)
        total = x_ref[at, :].astype(f32) + attn[at, :].astype(f32) + summed_rows(mlp, index)
        layer_ref[at, :] = total.astype(bf16)

    steps(ROWS // NORM_ROWS, finish_layer)
    keep = [pltpu.make_async_copy(layer_ref, layer_hbm, load_sems.at[5])]
    keep[0].start()
    advance(over_y[0])
    advance(over_all)
    advance(ring)
    advance(over_y[1])
    advance(over_all)
    advance(ring)
    advance(over_all)
    advance(ring)
    advance(over_y[0])
    advance(over_y[1])

    def finish_input(index):
        at = slab(index, NORM_ROWS)
        unit = xhat[at, :]
        grad = summed_rows(all_rows, index) * gain_rows(labels_ref[at, :1], gains_ref, 0)
        mean = jnp.mean(grad, axis=-1, keepdims=True)
        along = jnp.mean(grad * unit, axis=-1, keepdims=True)
        input_ref[at, :] = g_mid[at, :] + inverse[at, :1] * (grad - mean - unit * along)

    for half in range(2):
        steps(norm_steps, lambda index: finish_input(index + half * norm_steps))
        at = pl.ds(half * (ROWS // 2), ROWS // 2)
        keep.append(
            pltpu.make_async_copy(input_ref.at[at], input_hbm.at[at], load_sems.at[6 + half])
        )
        keep[-1].start()
        advance(ring)
    advance(over_all)
    for copy in keep:
        copy.wait()
    copies.finish()
    gain_copies.finish()


def last(
    activations, labels, gains, packed, cosine, sine, gains_two, left, attn_sum, mlp_sum, g_mid, weight
):
    width = activations.shape[1]
    local = weight.shape[2]
    cols = 3 * local
    rows = width // 32
    whole = pl.BlockSpec(memory_space=pltpu.VMEM)
    anywhere = pl.BlockSpec(memory_space=pl.ANY)
    return pl.pallas_call(
        last_kernel,
        out_shape=[
            jax.ShapeDtypeStruct((ROWS, width), f32),
            jax.ShapeDtypeStruct((ROWS, width), bf16),
            jax.ShapeDtypeStruct((8, HD), f32),
            jax.ShapeDtypeStruct((3, rows, local), f32),
        ],
        in_specs=[whole] * 7 + [anywhere] * 5,
        out_specs=[anywhere] * 2 + [whole] * 2,
        scratch_shapes=[
            pltpu.VMEM((ROWS, width), f32),
            pltpu.VMEM((ROWS, width), bf16),
            pltpu.VMEM(attn_sum.shape, bf16),
            pltpu.VMEM(mlp_sum.shape, bf16),
            pltpu.VMEM(g_mid.shape, f32),
            pltpu.VMEM(weight.shape, bf16),
            pltpu.VMEM((ROWS, width), f32),
            pltpu.VMEM((ROWS, HD), f32),
            pltpu.VMEM(mlp_sum.shape, bf16),
            pltpu.VMEM((8, width), f32),
            pltpu.VMEM((4, 4, 2, 8, HD), f32),
        ]
        + sum_scratch(width)
        + [pltpu.SemaphoreType.DMA((8,))]
        + factor_scratch(rows, cols)
        + [pltpu.VMEM(shape, f32) for shape in GAIN_SCRATCH]
        + [pltpu.SemaphoreType.DMA((10,)), pltpu.SemaphoreType.DMA((10,))]
        + weight_scratch(rows, cols),
        compiler_params=pltpu.CompilerParams(
            collective_id=3, has_side_effects=True, vmem_limit_bytes=VMEM_LIMIT
        ),
        name="last",
    )(
        activations,
        labels,
        gains,
        packed,
        cosine,
        sine,
        gains_two,
        left,
        attn_sum,
        mlp_sum,
        g_mid,
        weight,
    )


def finish_kernel(
    share_ref, layer_in, input_in, qkv_in, out_in, up_in, down_in,
    gains_ref, layer_out, input_out, qkv_out, out_out, up_out, down_out,
    layer, grad_input, qkv, out, up, down, load_sems, store_sems,
):
    ways = (
        (layer_in, layer, layer_out),
        (up_in, up, up_out),
        (qkv_in, qkv, qkv_out),
        (down_in, down, down_out),
        (out_in, out, out_out),
        (input_in, grad_input, input_out),
    )
    loads = [
        pltpu.make_async_copy(src, held, load_sems.at[n]) for n, (src, held, dst) in enumerate(ways)
    ]
    stores = [
        pltpu.make_async_copy(held, dst, store_sems.at[n]) for n, (src, held, dst) in enumerate(ways)
    ]
    for load in loads:
        load.start()
    gains_ref[...] = share_ref[: gains_ref.shape[0], : gains_ref.shape[1]]
    for load, store in zip(loads, stores):
        load.wait()
        store.start()
    for store in stores:
        store.wait()


def finish(modes, share, *arrays):
    whole = pl.BlockSpec(memory_space=pltpu.VMEM)
    anywhere = pl.BlockSpec(memory_space=pl.ANY)
    count = len(arrays)
    return pl.pallas_call(
        finish_kernel,
        out_shape=[jax.ShapeDtypeStruct((2 * modes, arrays[0].shape[1] // 32), f32)]
        + [jax.ShapeDtypeStruct(array.shape, array.dtype) for array in arrays],
        in_specs=[whole] + [anywhere] * count,
        out_specs=[whole] + [anywhere] * count,
        scratch_shapes=[pltpu.VMEM(array.shape, array.dtype) for array in arrays]
        + [pltpu.SemaphoreType.DMA((count,)), pltpu.SemaphoreType.DMA((count,))],
        name="finish",
    )(share, *arrays)


def per_device(
    activations,
    labels,
    position,
    norm_gains,
    qkv_weight,
    out_weight,
    up_weight,
    down_weight,
    cotangent,
):
    projections = qkv_weight.transpose(1, 0, 2)
    (
        q_all,
        kv_all,
        o_all,
        lse,
        out_left,
        attn_sum,
        grad_active,
        weights,
        tops,
        label_rows,
        cosine,
        sine,
        qkv_left,
        both_cotangents,
    ) = attention_forward(
        activations,
        labels.reshape(1, ROWS),
        position.reshape(1, ROWS),
        norm_gains,
        cotangent,
        projections,
        out_weight,
        down_weight,
    )
    g_mid, g_low, grad_heads, mlp_part, down_parts, gains_two, grad_up = middle(
        activations,
        attn_sum,
        label_rows,
        norm_gains,
        both_cotangents,
        out_weight,
        grad_active,
        up_weight,
        down_weight,
    )
    packed, grad_down, grad_out, mlp_sum = attention_backward(
        grad_heads,
        q_all,
        kv_all,
        o_all,
        lse,
        tops,
        weights,
        down_parts,
        out_left,
        g_low,
        mlp_part,
    )
    grad_input, layer_out, share, grad_qkv = last(
        activations,
        label_rows,
        norm_gains,
        packed,
        cosine,
        sine,
        gains_two,
        qkv_left,
        attn_sum,
        mlp_sum,
        g_mid,
        projections,
    )
    grad_gains, layer_out, grad_input, grad_qkv, grad_out, grad_up, grad_down = finish(
        norm_gains.shape[0] // 2,
        share,
        layer_out,
        grad_input,
        grad_qkv,
        grad_out,
        grad_up,
        grad_down,
    )
    return (
        layer_out,
        grad_input,
        grad_gains,
        grad_qkv.transpose(1, 0, 2),
        grad_out,
        grad_up,
        grad_down,
    )


def solution(mesh):
    return jax.shard_map(
        per_device,
        mesh=mesh,
        in_specs=(
            P("tok", None),
            P("tok"),
            P("tok"),
            P(),
            P(None, None, "head"),
            P("head", None),
            P(None, "head"),
            P("head", None),
            P("tok", None),
        ),
        out_specs=(
            P("tok", None),
            P("tok", None),
            P(None, "tok"),
            P("tok", None, "head"),
            P(("head", "tok"), None),
            P("tok", "head"),
            P(("head", "tok"), None),
        ),
        check_vma=False,
    )
```

```python
import functools
import math

import jax
import jax.numpy as jnp
from jax import lax
from jax.experimental import pallas as pl
from jax.experimental.pallas import tpu as pltpu
from jax.sharding import PartitionSpec as P

HD = 128
SIDE = 4
ROWS = 256
CODE_ROWS = 16
CLIP_STEP = 8192
MESH = pl.DeviceIdType.MESH
NT = (((1,), (1,)), ((), ()))
TN = (((0,), (0,)), ((), ()))
NN = (((1,), (0,)), ((), ()))
f32 = jnp.float32
bf16 = jnp.bfloat16
highest = lax.Precision.HIGHEST
VMEM_LIMIT = 60 << 20
HOPS = (1, 3, 2)


def dot(lhs, rhs, dims=NN):
    return lax.dot_general(lhs, rhs, dims, preferred_element_type=f32)


def place():
    tok = lax.axis_index("tok")
    return (lax.div(tok, 8), lax.axis_index("head"), lax.rem(lax.div(tok, 2), 4), lax.rem(tok, 2))


def around(index, step):
    return lax.rem(index + (step % SIDE), SIDE)


def device(x, y, z, core):
    return (x * 8 + z * 2 + core, y)


def remote(src, dst, send_sem, recv_sem, target):
    return pltpu.make_async_remote_copy(
        src_ref=src,
        dst_ref=dst,
        send_sem=send_sem,
        recv_sem=recv_sem,
        device_id=target,
        device_id_type=MESH,
    )


def greet(targets):
    barrier = pltpu.get_barrier_semaphore()
    for target in targets:
        pl.semaphore_signal(barrier, inc=1, device_id=target, device_id_type=MESH)
    return lambda: pl.semaphore_wait(barrier, len(targets))


class Copies:
    def __init__(self, send_sems, recv_sems):
        self.send_sems = send_sems
        self.recv_sems = recv_sems
        self.used = 0
        self.open = []

    def start(self, src, dst, target, landing):
        index = self.used
        self.used += 1
        copy = remote(src, dst, self.send_sems.at[index], self.recv_sems.at[index], target)
        copy.start()
        self.open.append(copy)
        return remote(landing, landing, self.send_sems.at[index], self.recv_sems.at[index], target)

    def finish(self):
        for copy in self.open:
            copy.wait_send()


def advance(steps_left, count=1):
    for _ in range(count):
        next(steps_left)


def ring_sum(copies, own, towards, source, block, slots):
    up, down = towards(1), towards(-1)
    from_down = copies.start(source(2, 0), slots.at[0], up, slots.at[0])
    from_up = copies.start(source(2, 1), slots.at[1], down, slots.at[1])
    raw_down = copies.start(source(1, 1), slots.at[2], up, slots.at[2])
    raw_up = copies.start(source(-1, 0), slots.at[3], down, slots.at[3])
    yield
    from_down.wait_recv()
    slots[0] = (block(1, 0)[...].astype(f32) + slots[0].astype(f32)).astype(bf16)
    sum_down = copies.start(slots.at[0], slots.at[4], up, slots.at[4])
    from_up.wait_recv()
    slots[1] = (block(-1, 1)[...].astype(f32) + slots[1].astype(f32)).astype(bf16)
    sum_up = copies.start(slots.at[1], slots.at[5], down, slots.at[5])
    yield
    for arrival in (raw_down, raw_up, sum_down, sum_up):
        arrival.wait_recv()

    def finished(half):
        mine = block(0, half)[...].astype(f32)
        if half == 0:
            return mine + slots[4].astype(f32) + slots[3].astype(f32)
        return mine + slots[2].astype(f32) + slots[5].astype(f32)

    own.append(finished)


def sum_over_y(copies, here, given, came, total):
    x, y, z, core = here
    rows = given.shape[1] // 2
    halves = (pl.ds(0, rows), pl.ds(rows, rows))

    def towards(step):
        return device(x, around(y, step), z, core)

    def block(step, half):
        return given.at[around(y, step), halves[half]]

    done = []
    ring = ring_sum(copies, done, towards, block, block, came)
    next(ring)
    yield
    next(ring)
    yield
    next(ring, None)
    for half in range(2):
        total[y, halves[half]] = done[0](half).astype(bf16)
    last_y, next_y, far_y = around(y, -1), around(y, 1), around(y, 2)
    mine = total.at[y]
    from_last = copies.start(mine, mine, towards(1), total.at[last_y])
    from_next = copies.start(mine, mine, towards(-1), total.at[next_y])
    yield
    from_last.wait_recv()
    part = total.at[last_y, halves[0]]
    far_low = copies.start(part, part, towards(1), total.at[far_y, halves[0]])
    from_next.wait_recv()
    part = total.at[next_y, halves[1]]
    far_high = copies.start(part, part, towards(-1), total.at[far_y, halves[1]])
    yield
    far_low.wait_recv()
    far_high.wait_recv()
    yield


def sum_scratch(width):
    quarter = ROWS // SIDE
    return [
        pltpu.VMEM((2, 6, quarter // 2, width // 2), bf16),
        pltpu.VMEM((2, SIDE, quarter, width // 2), bf16),
        pltpu.SemaphoreType.DMA((20,)),
        pltpu.SemaphoreType.DMA((20,)),
    ]


def summed_rows(all_rows, index):
    part = lax.div(index, SIDE // 2)
    start = pl.multiple_of(lax.rem(index, SIDE // 2) * NORM_ROWS, NORM_ROWS)
    halves = [all_rows[half, part, pl.ds(start, NORM_ROWS), :] for half in range(2)]
    return jnp.concatenate(halves, axis=1).astype(f32)


WAYS = (0, 1, 0, 1)
DOWN_WAYS = (0, 1, 0, 0)


def ring_shapes(rows, cols):
    if rows >= 32:
        width = cols // 4
        return 4, (2 * rows, width), (rows // 2, width)
    return 2, (4 * rows, cols // 4), (rows, cols // 4)


def factor_scratch(rows, cols):
    return [pltpu.VMEM((16, rows, 2 * ROWS), bf16), pltpu.VMEM((2 * ROWS, cols), bf16)]


def weight_scratch(rows, cols):
    groups, first, late = ring_shapes(rows, cols)
    return [
        pltpu.VMEM((groups, 4, 2) + first, bf16),
        pltpu.VMEM((groups, 6) + first, bf16),
        pltpu.VMEM((groups, 4, 2) + late, bf16),
        pltpu.VMEM((groups, 6) + late, bf16),
        pltpu.SemaphoreType.DMA((2 + 12 * groups,)),
        pltpu.SemaphoreType.DMA((2 + 12 * groups,)),
        pltpu.SemaphoreType.DMA((2 + 4 * groups,)),
    ]


def store_part(out, row, start, value):
    rows = slice(row, row + value.shape[0])
    if len(out.shape) == 2:
        out[rows, start : start + value.shape[1]] = value
        return
    size, done = out.shape[2], 0
    while done < value.shape[1]:
        block, offset = divmod(start + done, size)
        count = min(size - offset, value.shape[1] - done)
        out[block, rows, offset : offset + count] = value[:, done : done + count]
        done += count


def pick(core_at, factor, rows, group):
    row = lax.broadcasted_iota(jnp.int32, (256, 512), 0)
    col = lax.broadcasted_iota(jnp.int32, (256, 512), 1)
    wanted = lax.div(row, rows) * (2 * rows) + core_at * rows + lax.rem(row, rows)
    chosen = jnp.where(col == wanted, 1.0, 0.0).astype(bf16)
    return dot(chosen, factor[:, 512 * group : 512 * (group + 1)], NT).astype(bf16)


def partial_block(both_left, both_right, way, at, group, width):
    rows = both_left.shape[1]
    if way == 0:
        chosen = both_left[pl.ds(at * 4, 4)].reshape(4 * rows, 2 * ROWS)
    else:
        chosen = jnp.concatenate([both_left[k * 4 + at] for k in range(4)], axis=0)
    return dot(chosen, both_right[:, group * width : (group + 1) * width]).astype(bf16)


def weight_grad(here, out, scratch, factors=None, far=None, left=None, right=None, parts_hbm=None, ways=WAYS,
                ready=None):
    parts, came, sums, late, send_sems, recv_sems, own_sems = scratch
    x, y, z, core = here
    copies = Copies(send_sems, recv_sems)
    twin = device(x, y, z, 1 - core)
    groups = parts.shape[0]
    rows = out.shape[-2]
    by_rows = groups == 4
    first_shape, late_shape = parts.shape[3:], late.shape[2:]
    width = first_shape[1] if by_rows else 2 * first_shape[1]

    def spot(way, step):
        return around(x if way == 0 else z, step)

    def towards(way):
        def target(step):
            if way == 0:
                return device(around(x, step), y, z, core)
            return device(x, y, around(z, step), core)

        return target

    waits = []
    if parts_hbm is None:
        both_left, both_right = factors
    if parts_hbm is None and ready is None:
        if left is not None:
            far = left.at[:, 1 - core]
            own = pltpu.make_async_copy(
                left.at[:, core], both_left.at[:, :, pl.ds(0, ROWS)], own_sems.at[0]
            )
            own.start()
            waits.append(own.wait)
        if right is not None:
            own = pltpu.make_async_copy(right, both_right.at[pl.ds(0, ROWS)], own_sems.at[1])
            own.start()
            waits.append(own.wait)
        else:
            right = both_right.at[pl.ds(0, ROWS)]
        if far is not None:
            theirs = both_left.at[:, :, pl.ds(ROWS, ROWS)]
            waits.append(copies.start(far, theirs, twin, theirs).wait_recv)
        theirs = both_right.at[pl.ds(ROWS, ROWS)]
        waits.append(copies.start(right, theirs, twin, theirs).wait_recv)
    elif ready is None:
        for group in range(groups):
            for n, (step, half_index) in enumerate(((1, 0), (-1, 1), (0, 0), (0, 1))):
                at = spot(ways[group], step)
                own = pltpu.make_async_copy(
                    parts_hbm.at[group, at, half_index],
                    parts.at[group, at, half_index],
                    own_sems.at[2 + 4 * group + n],
                )
                own.start()
                waits.append(own.wait)
    yield

    def fill(group, step):
        at = spot(ways[group], step)
        value = partial_block(both_left, both_right, ways[group], at, group, width)
        parts[group, at] = value.reshape((2,) + first_shape)

    def fill_all(group):
        tall = both_left[...].reshape(16 * rows, 2 * ROWS)
        value = dot(tall, both_right[:, group * width : (group + 1) * width]).astype(bf16)
        for at in range(4):
            if ways[group] == 0:
                block = value[at * 4 * rows : (at + 1) * 4 * rows]
            else:
                block = jnp.concatenate(
                    [value[(k * 4 + at) * rows : (k * 4 + at + 1) * rows] for k in range(4)],
                    axis=0,
                )
            for half_index in range(2):
                parts[group, at, half_index] = block[
                    :, half_index * first_shape[1] : (half_index + 1) * first_shape[1]
                ]

    if parts_hbm is None:
        for wait in waits:
            wait()
        waits = []
    source = parts if parts_hbm is None else parts_hbm
    first, first_done, second, second_done = {}, {}, {}, {}
    for group in range(4):
        if group >= groups:
            yield
            continue
        if ready is not None:
            ready(group)
        if parts_hbm is None and by_rows:
            for step in (2, 1, -1):
                fill(group, step)
        elif parts_hbm is None:
            fill_all(group)
        first_done[group] = []
        first[group] = ring_sum(
            copies,
            first_done[group],
            towards(ways[group]),
            lambda step, half, group=group: source.at[group, spot(ways[group], step), half],
            lambda step, half, group=group: parts.at[group, spot(ways[group], step), half],
            came.at[group],
        )
        next(first[group])
        yield
    if parts_hbm is None and by_rows:
        for group in range(groups):
            fill(group, 0)
    for wait in waits:
        wait()
    yield
    stages = [range(groups // 2), range(groups // 2, groups)] if by_rows else [range(groups), ()]
    for stage in stages:
        for group in stage:
            next(first[group])
        yield
    for stage in stages:
        for group in stage:
            next(first[group], None)
            for half_index in (0, 1):
                value = first_done[group][0](half_index).astype(bf16)
                if by_rows:
                    sums[group, 2 * half_index : 2 * half_index + 2] = value.reshape(
                        (2, 2) + late_shape
                    )
                else:
                    sums[group, :, half_index] = value.reshape((4,) + late_shape)
            second_done[group] = []

            def block(step, half, group=group):
                return sums.at[group, spot(1 - ways[group], step), half]

            second[group] = ring_sum(
                copies,
                second_done[group],
                towards(1 - ways[group]),
                block,
                block,
                late.at[group],
            )
            next(second[group])
        yield
    for group in range(groups):
        next(second[group])
    yield
    for group in range(groups):
        next(second[group], None)
        for half_index in (0, 1):
            value = second_done[group][0](half_index)
            if by_rows:
                store_part(out, half_index * late_shape[0], group * width, value)
            else:
                store_part(out, 0, group * width + half_index * late_shape[1], value)
    copies.finish()
    yield


def sum_gains(copies, here, given, came_x, part_x, came_z, part_z, came_core, part, came_y, out):
    x, y, z, core = here
    arrivals = [
        copies.start(
            given.at[around(x, hop)], came_x.at[n], device(around(x, hop), y, z, core), came_x.at[n]
        )
        for n, hop in enumerate(HOPS)
    ]
    yield
    for arrival in arrivals:
        arrival.wait_recv()
    part_x[...] = (given[x] + came_x[0]) + (came_x[1] + came_x[2])
    arrivals = [
        copies.start(
            part_x.at[around(z, hop)], came_z.at[n], device(x, y, around(z, hop), core), came_z.at[n]
        )
        for n, hop in enumerate(HOPS)
    ]
    yield
    for arrival in arrivals:
        arrival.wait_recv()
    part_z[...] = (part_x[z] + came_z[0]) + (came_z[1] + came_z[2])
    arrival = copies.start(part_z.at[1 - core], came_core, device(x, y, z, 1 - core), came_core)
    yield
    arrival.wait_recv()
    part[...] = part_z[core] + came_core[...]
    arrivals = [
        copies.start(part, came_y.at[n], device(x, around(y, hop), z, core), came_y.at[n])
        for n, hop in enumerate(HOPS)
    ]
    yield
    for arrival in arrivals:
        arrival.wait_recv()
    out[...] = (part[...] + came_y[0]) + (came_y[1] + came_y[2])
    yield


GAIN_SCRATCH = [(3, 4, 2, 8, HD), (4, 2, 8, HD), (3, 2, 8, HD), (2, 8, HD), (8, HD), (8, HD), (3, 8, HD)]


NORM_ROWS = 32
WIDE = 512


def gain_rows(labels, gains, first):
    return jnp.where(
        labels == 0,
        gains[first : first + 1, :],
        jnp.where(labels == 1, gains[first + 1 : first + 2, :], gains[first + 2 : first + 3, :]),
    )


def steps(count, body):
    lax.fori_loop(0, count, lambda index, carry: (body(index), carry)[1], 0)


def slab(index, size):
    return pl.ds(pl.multiple_of(index * size, size), size)


def visible(key_codes, low, span):
    return (key_codes - low).astype(jnp.uint32) <= span.astype(jnp.uint32)


def key_column(keys_values, z_at, core_at):
    codes = jnp.concatenate(
        [keys_values[z_at, core_at, n, ROWS:, :] for n in range(4)], axis=1
    )
    row = lax.broadcasted_iota(jnp.int32, (CODE_ROWS, HD), 0)
    weight = jnp.where(row == 0, 128.0, jnp.where(row == 1, 1.0, 0.0)).astype(bf16)
    return dot(codes, weight, TN).astype(jnp.int32)


def query_bounds(keys_values, z, core, bounds):
    size = ROWS // 2
    for n in range(4):
        digits = keys_values[z, core, n, ROWS:, :].astype(f32)
        code = (digits[0:1] * 128.0 + digits[1:2]).astype(jnp.int32)
        low = jnp.where(code >= CLIP_STEP, CLIP_STEP, 0)
        for half in range(2):
            at = slice((half * 4 + n) * size, (half * 4 + n + 1) * size)
            bounds[0:1, at] = low[:, half * size : (half + 1) * size]
            bounds[1:2, at] = (code - low)[:, half * size : (half + 1) * size]


def forward_kernel(
    x_ref, label_ref, position_ref, gains_ref, cotangent_ref, weight_hbm, out_weight_hbm, down_hbm,
    q_all_ref, kv_all_ref, o_ref, lse_ref, out_left_ref, total_ref, grad_active_hbm, weights_ref, tops_ref, labels_ref,
    cos_ref, sin_ref, qkv_left_hbm, cotangent_both,
    own_left, far_left, grad_active_ref, weight, out_weight, down, weights, normed, q_own, kv_own, queries, keys_values, top, norm, acc, column, bounds_ref, o_low, back,
    gathered, send_sems, recv_sems, load_sems, weight_sems,
):
    here = place()
    x, y, z, core = here
    twin = device(x, y, z, 1 - core)
    arrived = greet(
        [device(around(x, hop), y, z, core) for hop in HOPS]
        + [device(x, around(y, hop), z, core) for hop in HOPS]
        + [device(x, y, around(z, hop), core) for hop in (1, 3)]
        + [twin]
    )
    load_out = pltpu.make_async_copy(out_weight_hbm, out_weight.at[y], load_sems.at[0])
    load_out.start()
    load = pltpu.make_async_copy(weight_hbm, weight, load_sems.at[1])
    load.start()
    load_down = pltpu.make_async_copy(down_hbm, down, load_sems.at[3])
    copies = Copies(send_sems, recv_sems)

    position = position_ref[...]
    block, row = lax.shift_right_logical(position, 8), lax.bitwise_and(position, 255)
    second = row >= 192
    spot = jnp.where(second, block * 64 + row - 192, block * 192 + row)
    code = spot + jnp.where(second, CLIP_STEP, 0)
    kind = lax.broadcasted_iota(jnp.int32, (CODE_ROWS, ROWS), 0)
    digits = jnp.where(
        kind == 0,
        lax.shift_right_logical(code, 7),
        jnp.where(kind == 1, lax.bitwise_and(code, 127), 0),
    )
    digits = digits.astype(f32).astype(bf16)
    kind = lax.broadcasted_iota(jnp.int32, (8, ROWS), 0)
    small = jnp.where(
        kind == 0,
        lax.shift_right_logical(spot, 7),
        jnp.where(kind == 1, lax.bitwise_and(spot, 127), jnp.where(kind == 2, label_ref[...], 0)),
    )
    small = small.astype(f32).astype(bf16)
    kind = lax.broadcasted_iota(jnp.int32, (8, HD), 0)
    spot_weight = jnp.where(kind == 0, 128.0, jnp.where(kind == 1, 1.0, 0.0)).astype(bf16)
    label_weight = jnp.where(kind == 2, 1.0, 0.0).astype(bf16)
    labels_ref[...] = dot(small, label_weight, TN).astype(jnp.int32)
    feature = lax.rem(lax.broadcasted_iota(jnp.int32, (1, HD), 1), HD // 2).astype(f32)
    angle = dot(small, spot_weight, TN) * jnp.exp(feature * (-2.0 * math.log(10000.0) / HD))
    cos_ref[...] = jnp.cos(angle)
    sin_ref[...] = jnp.sin(angle)

    def normalise(index):
        at = slab(index, NORM_ROWS)
        rows = x_ref[at, :].astype(f32)
        centred = rows - jnp.mean(rows, axis=-1, keepdims=True)
        scale = lax.rsqrt(jnp.mean(centred * centred, axis=-1, keepdims=True) + 1e-05)
        normed[at, :] = (centred * scale * gain_rows(labels_ref[at, :1], gains_ref, 0)).astype(
            bf16
        )

    steps(ROWS // NORM_ROWS, normalise)
    arrived()
    load_out.wait()
    y_up, y_down = device(x, around(y, 1), z, core), device(x, around(y, -1), z, core)
    y_next, y_last, y_far = around(y, 1), around(y, -1), around(y, 2)
    w_last, w_next, w_far, w_twin = [], [], [None] * 4, []
    for n in range(4):
        block = out_weight.at[y, core, n]
        w_last.append(copies.start(block, block, y_up, out_weight.at[y_last, core, n]))
        w_next.append(copies.start(block, block, y_down, out_weight.at[y_next, core, n]))

    def w_onward(n):
        w_last[n].wait_recv()
        block = out_weight.at[y_last, core, n]
        if n < 2:
            w_far[n] = copies.start(block, block, y_up, out_weight.at[y_far, core, n])
        w_twin.append(copies.start(block, block, twin, out_weight.at[y_last, 1 - core, n]))
        w_next[n].wait_recv()
        block = out_weight.at[y_next, core, n]
        if n >= 2:
            w_far[n] = copies.start(block, block, y_down, out_weight.at[y_far, core, n])
        w_twin.append(copies.start(block, block, twin, out_weight.at[y_next, 1 - core, n]))

    load.wait()
    load_down.start()
    cosine, sine = cos_ref[...], sin_ref[...]

    def rotate(values, head):
        part = values[:, head * HD : (head + 1) * HD]
        turned = jnp.concatenate([-part[:, HD // 2 :], part[:, : HD // 2]], axis=1)
        return part * cosine + turned * sine

    key_part = dot(normed[...], weight[1])
    for head in range(4):
        kv_own[head, :ROWS, :HD] = rotate(key_part, head).astype(bf16)
        kv_own[head, ROWS:, :] = digits
    value_part = dot(normed[...], weight[2])
    for head in range(4):
        kv_own[head, :ROWS, HD:] = value_part[:, head * HD : (head + 1) * HD].astype(bf16)
    kv_came, q_came = [None] * 3, [None] * 3

    def send_kv(n):
        other = around(x, HOPS[n])
        kv_came[n] = copies.start(
            kv_own.at[other],
            keys_values.at[z, core, x],
            device(other, y, z, core),
            keys_values.at[z, core, around(x, -HOPS[n])],
        )

    send_kv(0)
    send_kv(1)
    query_part = dot(normed[...], weight[0]) * (HD**-0.5 / math.log(2.0))
    for head in range(4):
        q_own[head] = rotate(query_part, head).astype(bf16).reshape(2, ROWS // 2, HD)
    for n, hop in enumerate(HOPS):
        other = around(x, hop)
        q_came[n] = copies.start(
            q_own.at[other],
            queries.at[:, x],
            device(other, y, z, core),
            queries.at[:, around(x, -hop)],
        )
    send_kv(2)
    keys_values[z, core, x] = kv_own[x]
    queries[:, x] = q_own[x]
    above, below = device(x, y, around(z, 1), core), device(x, y, around(z, -1), core)
    next_z, last_z, far_z = around(z, 1), around(z, -1), around(z, 2)
    pieces = [x] + [around(x, -hop) for hop in HOPS]
    from_last, from_next, from_twin = [], [], []

    def spread(n):
        block = keys_values.at[z, core, pieces[n]]
        from_last.append(copies.start(block, block, above, keys_values.at[last_z, core, pieces[n]]))
        from_next.append(copies.start(block, block, below, keys_values.at[next_z, core, pieces[n]]))
        from_twin.append(copies.start(block, block, twin, keys_values.at[z, 1 - core, pieces[n]]))

    spread(0)
    top[...] = jnp.full_like(top, -1e30)
    norm[...] = jnp.zeros_like(norm)
    acc[...] = jnp.zeros_like(acc)
    load_down.wait()

    def grad_active(index):
        at = slab(index, WIDE)
        grad_active_ref[:, at] = dot(cotangent_ref[...], down[at, :], NT)

    keep_more = [
        pltpu.make_async_copy(
            cotangent_ref, cotangent_both.at[pl.ds(0, ROWS)], load_sems.at[5]
        )
    ]
    theirs = cotangent_both.at[pl.ds(ROWS, ROWS)]
    for_twin = [copies.start(cotangent_ref, theirs, twin, theirs)]
    rows = far_left.shape[1]
    for group in range(4):
        at = pl.ds(4 * group, 4)
        own_left[at] = pick(core, normed, rows, group).reshape(4, rows, ROWS)
        far_left[at] = pick(1 - core, normed, rows, group).reshape(4, rows, ROWS)
    keep_more.append(
        pltpu.make_async_copy(
            own_left, qkv_left_hbm.at[:, :, pl.ds(0, ROWS)], load_sems.at[6]
        )
    )
    theirs = qkv_left_hbm.at[:, :, pl.ds(ROWS, ROWS)]
    for_twin.append(copies.start(far_left, theirs, twin, theirs))
    for copy in keep_more:
        copy.start()
    half_steps = grad_active_ref.shape[1] // WIDE // 2
    keep_grad = pltpu.make_async_copy(grad_active_ref, grad_active_hbm, load_sems.at[4])
    steps(half_steps, grad_active)
    for n in range(3):
        kv_came[n].wait_recv()
        spread(n + 1)
        if n == 1:
            steps(half_steps, lambda index: grad_active(index + half_steps))
            keep_grad.start()
    for arrival in q_came:
        arrival.wait_recv()
    query_bounds(keys_values, z, core, bounds_ref)

    stored, chunks = {}, []

    def attend_half(count, half):
        z_at, core_at = chunks[count]
        at = slice(half * 2 * ROWS, (half + 1) * 2 * ROWS)
        if half == 0:
            column[count % 2] = key_column(keys_values, z_at, core_at)
        query = queries[half].reshape(2 * ROWS, HD)
        keys = keys_values[z_at, core_at, :, :ROWS, :HD].reshape(4 * ROWS, HD)
        values = keys_values[z_at, core_at, :, :ROWS, HD:].reshape(4 * ROWS, HD)
        scores = dot(keys, query, NT)
        codes = jnp.concatenate([column[count % 2]] * (2 * ROWS // HD), axis=1)
        seen = visible(codes, bounds_ref[0:1, at], bounds_ref[1:2, at])
        scores = jnp.where(seen, scores, -1e30)
        top_before = top[0:1, at]
        top_now = jnp.maximum(top_before, jnp.max(scores, axis=0, keepdims=True))
        if count >= 2:
            stored[count - 2, half].wait()
        slot = weights.at[count % 2, half]
        slot[...] = jnp.exp2(scores - top_now).astype(bf16)
        shrink = jnp.exp2(top_before - top_now)
        norm[:, at] = norm[:, at] * shrink + dot(jnp.ones((8, 4 * ROWS), bf16), slot[...])
        top[0:1, at] = top_now
        acc[:, at] = acc[:, at] * shrink + dot(values, slot[...], TN)
        tops_ref[z_at, core_at, :, at] = jnp.broadcast_to(top_now, (8, 2 * ROWS))
        copy = pltpu.make_async_copy(
            slot, weights_ref.at[z_at, core_at, half], weight_sems.at[count % 2, half]
        )
        copy.start()
        stored[count, half] = copy

    def attend(z_at, core_at):
        chunks.append((z_at, core_at))
        for half in range(2):
            attend_half(len(chunks) - 1, half)

    low_far, high_far, twin_last, twin_next = [], [], [], []

    def onward(n):
        piece = pieces[n]
        from_last[n].wait_recv()
        block = keys_values.at[last_z, core, piece]
        low = block.at[pl.ds(0, ROWS // 2)]
        low_far.append(
            copies.start(low, low, above, keys_values.at[far_z, core, piece, pl.ds(0, ROWS // 2)])
        )
        twin_last.append(
            copies.start(block, block, twin, keys_values.at[last_z, 1 - core, piece])
        )
        from_next[n].wait_recv()
        block = keys_values.at[next_z, core, piece]
        high = block.at[pl.ds(ROWS // 2, ROWS // 2 + CODE_ROWS)]
        high_far.append(
            copies.start(
                high,
                high,
                below,
                keys_values.at[far_z, core, piece, pl.ds(ROWS // 2, ROWS // 2 + CODE_ROWS)],
            )
        )
        twin_next.append(
            copies.start(block, block, twin, keys_values.at[next_z, 1 - core, piece])
        )

    def take(arrivals):
        for arrival in arrivals:
            arrival.wait_recv()

    onward(0)
    w_onward(0)
    attend(z, core)
    onward(1)
    onward(2)
    take(from_twin)
    attend(z, 1 - core)
    onward(3)
    w_onward(1)
    attend(last_z, core)
    attend(next_z, core)
    w_onward(2)
    take(twin_last)
    attend(last_z, 1 - core)
    twin_far = []
    for n, piece in enumerate(pieces):
        low_far[n].wait_recv()
        high_far[n].wait_recv()
        block = keys_values.at[far_z, core, piece]
        twin_far.append(copies.start(block, block, twin, keys_values.at[far_z, 1 - core, piece]))
    take(twin_next)
    attend(next_z, 1 - core)
    w_onward(3)
    size = ROWS // 2
    came_back = {}

    def give_back(half):
        at = slice(half * 2 * ROWS, (half + 1) * 2 * ROWS)
        total_norm = norm[0:1, at]
        attended = (acc[:, at] / total_norm).T
        o_low[half] = attended.astype(bf16).reshape(4, size, HD)
        came_back[half] = [
            copies.start(
                o_low.at[half, around(x, hop)],
                back.at[half, x],
                device(around(x, hop), y, z, core),
                back.at[half, around(x, -hop)],
            )
            for hop in HOPS
        ]
        back[half, x] = o_low[half, x]
        o_ref[at, :] = attended
        lse_ref[:, at] = jnp.broadcast_to(top[0:1, at] + jnp.log2(total_norm), (8, 2 * ROWS))

    ring_last, ring_next, ring_low, ring_high = [], [], [], []

    def spread_y(half):
        take(came_back[half])
        for n in range(4):
            gathered[y, half, :, n * HD : (n + 1) * HD] = back[half, n]
        block = gathered.at[y, half]
        ring_last.append(copies.start(block, block, y_up, gathered.at[y_last, half]))
        ring_next.append(copies.start(block, block, y_down, gathered.at[y_next, half]))

    def onward_y(half):
        low, high = pl.ds(0, size // 2), pl.ds(size // 2, size // 2)
        ring_last[half].wait_recv()
        block = gathered.at[y_last, half, low]
        ring_low.append(copies.start(block, block, y_up, gathered.at[y_far, half, low]))
        ring_next[half].wait_recv()
        block = gathered.at[y_next, half, high]
        ring_high.append(copies.start(block, block, y_down, gathered.at[y_far, half, high]))

    chunks += [(far_z, core), (far_z, 1 - core)]
    attend_half(6, 0)
    take(twin_far)
    attend_half(7, 0)
    give_back(0)
    attend_half(6, 1)
    spread_y(0)
    attend_half(7, 1)
    give_back(1)
    keep = pltpu.make_async_copy(keys_values, kv_all_ref, load_sems.at[2])
    keep.start()
    q_all_ref[...] = queries[...]
    for n in range(4):
        w_far[n].wait_recv()
        block = out_weight.at[y_far, core, n]
        w_twin.append(copies.start(block, block, twin, out_weight.at[y_far, 1 - core, n]))
    local = 4 * HD
    spread_y(1)
    out_rows = out_left_ref.shape[2]
    for core_at in range(2):
        out_left_ref[:, core_at] = pick(
            core_at, gathered[y].reshape(ROWS, local), out_rows, 0
        ).reshape(16, out_rows, ROWS)
    keep_grad.wait()
    summed = grad_active_ref

    def project(index, owners, first, final):
        at = slab(index, WIDE)
        part = sum(
            dot(
                gathered[n].reshape(ROWS, local),
                out_weight[n, :, :, :, at].reshape(local, WIDE),
            )
            for n in owners
        )
        if not first:
            part = part + summed[:, at]
        if final:
            total_ref[:, at] = part.astype(bf16)
        else:
            summed[:, at] = part

    count = total_ref.shape[1] // WIDE
    steps(count, lambda index: project(index, (y,), True, False))
    take(w_twin)
    onward_y(0)
    onward_y(1)
    steps(count, lambda index: project(index, (y_last, y_next), False, False))
    take(ring_low + ring_high)
    steps(count, lambda index: project(index, (y_far,), False, True))
    copies.finish()
    keep.wait()
    for copy in keep_more:
        copy.wait()
    take(for_twin)
    for count in (6, 7):
        for half in range(2):
            stored[count, half].wait()


def attention_forward(
    activations, labels, position, gains, cotangent, weight, out_weight, down_weight
):
    width = out_weight.shape[1]
    whole = pl.BlockSpec(memory_space=pltpu.VMEM)
    anywhere = pl.BlockSpec(memory_space=pl.ANY)
    count = 3 + 3 + 12 + 16 + 4 + 6 + 8 + 8 + 4 + 8 + 4 + 2
    local = out_weight.shape[0]
    pieces = (2, 4, out_weight.shape[0] // 8, width)
    return pl.pallas_call(
        forward_kernel,
        out_shape=[
            jax.ShapeDtypeStruct((2, 4, ROWS // 2, HD), bf16),
            jax.ShapeDtypeStruct((4, 2, 4, ROWS + CODE_ROWS, 2 * HD), bf16),
            jax.ShapeDtypeStruct((4 * ROWS, HD), f32),
            jax.ShapeDtypeStruct((8, 4 * ROWS), f32),
            jax.ShapeDtypeStruct((16, 2, local // 32, ROWS), bf16),
            jax.ShapeDtypeStruct((ROWS, width), bf16),
            jax.ShapeDtypeStruct((ROWS, down_weight.shape[0]), f32),
            jax.ShapeDtypeStruct((4, 2, 2, 4 * ROWS, 2 * ROWS), bf16),
            jax.ShapeDtypeStruct((4, 2, 8, 4 * ROWS), f32),
            jax.ShapeDtypeStruct((ROWS, HD), jnp.int32),
            jax.ShapeDtypeStruct((ROWS, HD), f32),
            jax.ShapeDtypeStruct((ROWS, HD), f32),
            jax.ShapeDtypeStruct((16, width // 32, 2 * ROWS), bf16),
            jax.ShapeDtypeStruct((2 * ROWS, width), bf16),
        ],
        in_specs=[whole] * 5 + [anywhere] * 3,
        out_specs=[whole, anywhere]
        + [whole] * 4
        + [anywhere, anywhere]
        + [whole] * 4
        + [anywhere] * 2,
        scratch_shapes=[
            pltpu.VMEM((16, width // 32, ROWS), bf16),
            pltpu.VMEM((16, width // 32, ROWS), bf16),
            pltpu.VMEM((ROWS, down_weight.shape[0]), f32),
            pltpu.VMEM(weight.shape, bf16),
            pltpu.VMEM((4,) + pieces, bf16),
            pltpu.VMEM(down_weight.shape, bf16),
            pltpu.VMEM((2, 2, 4 * ROWS, 2 * ROWS), bf16),
            pltpu.VMEM(activations.shape, bf16),
            pltpu.VMEM((4, 2, ROWS // 2, HD), bf16),
            pltpu.VMEM((4, ROWS + CODE_ROWS, 2 * HD), bf16),
            pltpu.VMEM((2, 4, ROWS // 2, HD), bf16),
            pltpu.VMEM((4, 2, 4, ROWS + CODE_ROWS, 2 * HD), bf16),
            pltpu.VMEM((8, 4 * ROWS), f32),
            pltpu.VMEM((8, 4 * ROWS), f32),
            pltpu.VMEM((HD, 4 * ROWS), f32),
            pltpu.VMEM((2, 4 * ROWS, HD), jnp.int32),
            pltpu.VMEM((8, 4 * ROWS), jnp.int32),
            pltpu.VMEM((2, 4, ROWS // 2, HD), bf16),
            pltpu.VMEM((2, 4, ROWS // 2, HD), bf16),
            pltpu.VMEM((4, 2, ROWS // 2, 4 * HD), bf16),
            pltpu.SemaphoreType.DMA((count,)),
            pltpu.SemaphoreType.DMA((count,)),
            pltpu.SemaphoreType.DMA((7,)),
            pltpu.SemaphoreType.DMA((2, 2)),
        ],
        compiler_params=pltpu.CompilerParams(
            collective_id=0, has_side_effects=True, vmem_limit_bytes=VMEM_LIMIT
        ),
        name="attention_forward",
    )(
        activations,
        labels,
        position,
        gains,
        cotangent,
        weight,
        out_weight.reshape(pieces),
        down_weight,
    )


def gelu_and_slope(hidden):
    scale = math.sqrt(2.0 / math.pi)
    square = hidden * hidden
    bent = jnp.tanh(scale * hidden * (1.0 + 0.044715 * square))
    half = 0.5 * (1.0 + bent)
    slope = half + 0.5 * hidden * (1.0 - bent * bent) * (scale * (1.0 + 3 * 0.044715 * square))
    return hidden * half, slope


def middle_kernel(
    x_ref, attn_ref, labels_ref, gains_ref, cotangent_hbm, out_weight_hbm, grad_active_hbm, up_hbm, down_hbm,
    g_mid_hbm, g_low_hbm, heads_ref, mlp_hbm, down_parts_hbm, gains_out_ref, grad_up_ref,
    up, down, out_weight, grad_active, g_mid, g_low, mlp, xhat, inverse, normed, active, far, far_down, down_left,
    down_right, down_parts, given, g_heads, came, all_rows, y_send, y_recv, load_sems, x_send, x_recv,
    exchange_send, exchange_recv, both_left, both_right, *up_scratch,
):
    here = place()
    x, y, z, core = here
    arrived = greet(
        [device(x, around(y, hop), z, core) for hop in HOPS]
        + [device(around(x, hop), y, z, core) for hop in HOPS]
        + [device(x, y, around(z, hop), core) for hop in (1, 3)]
        + [device(x, y, z, 1 - core)]
    )
    used = [0]

    def move(src, dst):
        copy = pltpu.make_async_copy(src, dst, load_sems.at[used[0]])
        used[0] += 1
        copy.start()
        return copy

    load_up = move(up_hbm, up)
    load_active = move(grad_active_hbm, grad_active)
    width = x_ref.shape[1]
    hidden_width = up.shape[1]

    def norm(index):
        at = slab(index, NORM_ROWS)
        middle = x_ref[at, :].astype(f32) + attn_ref[at, :].astype(f32)
        centred = middle - jnp.mean(middle, axis=-1, keepdims=True)
        scale = lax.rsqrt(jnp.mean(centred * centred, axis=-1, keepdims=True) + 1e-05)
        unit = centred * scale
        xhat[at, :] = unit
        inverse[at, :] = jnp.broadcast_to(scale, (NORM_ROWS, HD))
        normed[at, :] = (unit * gain_rows(labels_ref[at, :1], gains_ref, 3)).astype(bf16)

    steps(ROWS // NORM_ROWS, norm)
    rows = grad_up_ref.shape[0]
    for group in range(4):
        at = pl.ds(4 * group, 4)
        both_left[at, :, pl.ds(0, ROWS)] = pick(core, normed, rows, group).reshape(4, rows, ROWS)
        far[at] = pick(1 - core, normed, rows, group).reshape(4, rows, ROWS)
    load_up.wait()
    load_active.wait()
    load_down = move(down_hbm, down)
    load_cotangent = move(cotangent_hbm, down_right)
    load_out = move(out_weight_hbm, out_weight)
    arrived()
    twin = device(x, y, z, 1 - core)
    exchange = Copies(exchange_send, exchange_recv)
    theirs = both_left.at[:, :, pl.ds(ROWS, ROWS)]
    left_came = exchange.start(far, theirs, twin, theirs)
    right_came = []
    for index in range(hidden_width // WIDE):
        at = pl.ds(index * WIDE, WIDE)
        hidden = dot(normed[...], up[:, at])
        value, slope = gelu_and_slope(hidden)
        active[:, at] = value.astype(bf16)
        both_right[pl.ds(0, ROWS), at] = (grad_active[:, at] * slope).astype(bf16)
        theirs = both_right.at[pl.ds(ROWS, ROWS), at]
        right_came.append(
            exchange.start(both_right.at[pl.ds(0, ROWS), at], theirs, twin, theirs)
        )

    def ready(group):
        if group == 0:
            left_came.wait_recv()
        right_came[group].wait_recv()

    ring = weight_grad(here, grad_up_ref, up_scratch, (both_left, both_right), ready=ready)
    advance(ring)
    copies = Copies(y_send, y_recv)
    half_steps = width // WIDE // 2
    over_y = [
        sum_over_y(copies, here, given.at[half], came.at[half], all_rows.at[half])
        for half in range(2)
    ]

    def back_up(index, half):
        at = slab(index + half * half_steps, WIDE)
        part = dot(both_right[pl.ds(0, ROWS), :], up[at, :], NT)
        given[half, :, :, slab(index, WIDE)] = part.astype(bf16).reshape(
            SIDE, ROWS // SIDE, WIDE
        )

    def feed_out(index, half):
        at = slab(index + half * half_steps, WIDE)
        mlp[half, :, :, slab(index, WIDE)] = (
            dot(active[...], down[:, at]).astype(bf16).reshape(SIDE, ROWS // SIDE, WIDE)
        )

    groups, first_shape = down_parts.shape[0], down_parts.shape[3:]
    keep = []

    def fill_down(group):
        for at in range(4):
            down_parts[group, at] = partial_block(
                down_left, down_right, DOWN_WAYS[group], at, group, first_shape[1]
            ).reshape((2,) + first_shape)
        keep.append(move(down_parts.at[group], down_parts_hbm.at[group]))

    steps(half_steps, lambda index: back_up(index, 0))
    advance(over_y[0])
    advance(ring)
    steps(half_steps, lambda index: back_up(index, 1))
    advance(over_y[1])
    advance(ring, 2)
    advance(over_y[0])
    advance(ring, 2)
    load_down.wait()
    feed_out(0, 0)
    advance(over_y[1])
    feed_out(1, 0)
    advance(over_y[0])
    feed_out(0, 1)
    advance(over_y[1])
    feed_out(1, 1)
    keep.append(move(mlp, mlp_hbm))
    for group in range(4):
        at = pl.ds(4 * group, 4)
        down_left[at, :, pl.ds(0, ROWS)] = pick(core, active, rows, group).reshape(4, rows, ROWS)
        far_down[at] = pick(1 - core, active, rows, group).reshape(4, rows, ROWS)
    theirs = down_left.at[:, :, pl.ds(ROWS, ROWS)]
    down_came = exchange.start(far_down, theirs, twin, theirs)
    advance(over_y[0])
    advance(ring)
    advance(over_y[1])
    load_cotangent.wait()
    down_came.wait_recv()
    fill_down(0)
    advance(ring)
    fill_down(1)
    advance(ring)
    load_out.wait()
    gains_out_ref[...] = jnp.zeros_like(gains_out_ref)
    advance(over_y[0])
    advance(over_y[1])

    def back(index):
        at = slab(index, NORM_ROWS)
        grad = summed_rows(all_rows, index)
        labels = labels_ref[at, :1]
        unit = xhat[at, :]
        product = grad * unit
        for mode in range(3):
            gains_out_ref[mode + 3 : mode + 4, :] += jnp.sum(
                jnp.where(labels == mode, product, 0.0), axis=0, keepdims=True
            )
        gain = gain_rows(labels, gains_ref, 3)
        grad = grad * gain
        mean = jnp.mean(grad, axis=-1, keepdims=True)
        along = jnp.mean(product * gain, axis=-1, keepdims=True)
        total = down_right[at, :].astype(f32) + inverse[at, :1] * (grad - mean - unit * along)
        g_mid[at, :] = total
        g_low[at, :] = total.astype(bf16)

    steps(ROWS // NORM_ROWS, back)
    by_head = dot(g_low[...], out_weight[...], NT).astype(bf16)
    for head in range(4):
        g_heads[head] = by_head[:, head * HD : (head + 1) * HD].reshape(2, ROWS // 2, HD)
    x_copies = Copies(x_send, x_recv)
    arrivals = [
        x_copies.start(
            g_heads.at[around(x, hop)],
            heads_ref.at[:, x],
            device(around(x, hop), y, z, core),
            heads_ref.at[:, around(x, -hop)],
        )
        for hop in HOPS
    ]
    heads_ref[:, x] = g_heads[x]
    keep += [move(g_mid, g_mid_hbm), move(g_low, g_low_hbm)]
    advance(ring)
    fill_down(2)
    advance(ring)
    fill_down(3)
    advance(ring)
    for arrival in arrivals:
        arrival.wait_recv()
    copies.finish()
    x_copies.finish()
    exchange.finish()
    for copy in keep:
        copy.wait()


def middle(
    activations, attn_sum, labels, gains, cotangent, out_weight, grad_active, up_weight, down_weight
):
    width, hidden_width = up_weight.shape
    rows = width // 32
    down_rows = hidden_width // 32
    whole = pl.BlockSpec(memory_space=pltpu.VMEM)
    anywhere = pl.BlockSpec(memory_space=pl.ANY)
    summed = (2, SIDE, ROWS // SIDE, width // 2)
    groups, first_shape, late_shape = ring_shapes(down_rows, width)
    down_parts = (groups, 4, 2) + first_shape
    return pl.pallas_call(
        middle_kernel,
        out_shape=[
            jax.ShapeDtypeStruct((ROWS, width), f32),
            jax.ShapeDtypeStruct((ROWS, width), bf16),
            jax.ShapeDtypeStruct((2, 4, ROWS // 2, HD), bf16),
            jax.ShapeDtypeStruct(summed, bf16),
            jax.ShapeDtypeStruct(down_parts, bf16),
            jax.ShapeDtypeStruct((8, width), f32),
            jax.ShapeDtypeStruct((rows, hidden_width), f32),
        ],
        in_specs=[whole] * 4 + [anywhere] * 5,
        out_specs=[anywhere] * 2 + [whole] + [anywhere] * 2 + [whole] * 2,
        scratch_shapes=[
            pltpu.VMEM(up_weight.shape, bf16),
            pltpu.VMEM(down_weight.shape, bf16),
            pltpu.VMEM(out_weight.shape, bf16),
            pltpu.VMEM((ROWS, hidden_width), f32),
            pltpu.VMEM((ROWS, width), f32),
            pltpu.VMEM((ROWS, width), bf16),
            pltpu.VMEM(summed, bf16),
            pltpu.VMEM((ROWS, width), f32),
            pltpu.VMEM((ROWS, HD), f32),
            pltpu.VMEM((ROWS, width), bf16),
            pltpu.VMEM((ROWS, hidden_width), bf16),
            pltpu.VMEM((16, rows, ROWS), bf16),
            pltpu.VMEM((16, down_rows, ROWS), bf16),
        ]
        + factor_scratch(down_rows, width)
        + [
            pltpu.VMEM(down_parts, bf16),
            pltpu.VMEM(summed, bf16),
            pltpu.VMEM((4, 2, ROWS // 2, HD), bf16),
        ]
        + sum_scratch(width)
        + [pltpu.SemaphoreType.DMA((12,))]
        + [pltpu.SemaphoreType.DMA((3,)), pltpu.SemaphoreType.DMA((3,))]
        + [pltpu.SemaphoreType.DMA((6,)), pltpu.SemaphoreType.DMA((6,))]
        + factor_scratch(rows, hidden_width)
        + weight_scratch(rows, hidden_width),
        compiler_params=pltpu.CompilerParams(
            collective_id=2, has_side_effects=True, vmem_limit_bytes=VMEM_LIMIT
        ),
        name="middle",
    )(
        activations,
        attn_sum,
        labels,
        gains,
        cotangent,
        out_weight,
        grad_active,
        up_weight,
        down_weight,
    )


def backward_kernel(
    grads, q_ref, kv_hbm, o_ref, lse_ref, tops_ref, weights_hbm, down_parts_hbm, given_hbm,
    packed_ref, grad_down_ref, total_hbm,
    given_ref, keys_values, weights, delta, grad_q, parts, met, came, sums, q_low, back_q,
    back_kv, send_sems, recv_sems, load_sems, weight_sems, y_came, all_rows, y_send, y_recv, *more,
):
    here = place()
    x, y, z, core = here
    twin = device(x, y, z, 1 - core)
    arrived = greet(
        [device(around(x, hop), y, z, core) for hop in HOPS]
        + [device(x, around(y, hop), z, core) for hop in HOPS]
        + [device(x, y, around(z, hop), core) for hop in (1, 3)]
        + [twin]
    )
    next_z, last_z, far_z = around(z, 1), around(z, -1), around(z, 2)
    order = [
        (at, core_at)
        for at in (far_z, next_z, last_z, z)
        for core_at in (1 - core, core)
    ]

    def fetch(index):
        copy = pltpu.make_async_copy(
            weights_hbm.at[order[index][0], order[index][1]],
            weights.at[index % 3],
            weight_sems.at[index % 3],
        )
        copy.start()
        return copy

    load_given = pltpu.make_async_copy(given_hbm, given_ref, load_sems.at[8])
    load_given.start()
    fetched = [fetch(0)]
    loads = []
    for n, (z_at, core_at) in enumerate(order):
        loads.append(
            pltpu.make_async_copy(
                kv_hbm.at[z_at, core_at], keys_values.at[z_at, core_at], load_sems.at[n]
            )
        )
        loads[n].start()
        if n == 0:
            fetched.append(fetch(1))
    copies = Copies(send_sems, recv_sems)
    y_copies = Copies(y_send, y_recv)
    over_y = [
        sum_over_y(y_copies, here, given_ref.at[half], y_came.at[half], all_rows.at[half])
        for half in range(2)
    ]
    ring = weight_grad(here, grad_down_ref, more[:7], parts_hbm=down_parts_hbm, ways=DOWN_WAYS)
    arrived()
    advance(ring, 5)
    load_given.wait()
    for half in over_y:
        advance(half)
    grad_q[...] = jnp.zeros_like(grad_q)
    product = grads[...].reshape(4 * ROWS, HD).astype(f32) * o_ref[...]
    delta[...] = lax.dot_general(
        jnp.ones((8, HD), f32), product, NT, preferred_element_type=f32, precision=highest
    )
    done = []

    def chunk(z_at, core_at):
        index = len(done)
        done.append(index)
        if index + 2 < len(order):
            fetched.append(fetch(index + 2))
        loads[index].wait()
        fetched[index].wait()
        keys = keys_values[z_at, core_at, :, :ROWS, :HD].reshape(4 * ROWS, HD)
        values = keys_values[z_at, core_at, :, :ROWS, HD:].reshape(4 * ROWS, HD)
        grad_k = grad_v = 0.0
        for half in range(2):
            at = slice(half * 2 * ROWS, (half + 1) * 2 * ROWS)
            slot = weights.at[index % 3, half]
            query = q_ref[half].reshape(2 * ROWS, HD)
            grad = grads[half].reshape(2 * ROWS, HD)
            rescale = jnp.exp2(tops_ref[z_at, core_at, 0:1, at] - lse_ref[0:1, at])
            grad_weights = dot(values, grad, NT)
            taken = slot[...].astype(f32) * rescale
            slot[...] = taken.astype(bf16)
            grad_v += dot(slot[...], grad)
            slot[...] = (taken * (grad_weights - delta[0:1, at])).astype(bf16)
            grad_k += dot(slot[...], query)
            grad_q[:, at] += dot(keys, slot[...], TN)
        parts[z_at, core_at] = (
            jnp.concatenate([grad_k * math.log(2.0), grad_v], axis=1)
            .astype(bf16)
            .reshape(2, 2 * ROWS, 2 * HD)
        )

    def hand_over(z_at):
        return copies.start(
            parts.at[z_at, 1 - core], met.at[z_at], twin, met.at[z_at]
        )

    def join(z_at):
        parts[z_at, core] = (
            parts[z_at, core].astype(f32) + met[z_at].astype(f32)
        ).astype(bf16)

    above, below = device(x, y, next_z, core), device(x, y, last_z, core)
    chunk(far_z, 1 - core)
    far_met = hand_over(far_z)
    chunk(far_z, core)
    chunk(next_z, 1 - core)
    next_met = hand_over(next_z)
    far_met.wait_recv()
    join(far_z)
    from_last = copies.start(parts.at[far_z, core, 0], came.at[0], above, came.at[0])
    from_next = copies.start(parts.at[far_z, core, 1], came.at[1], below, came.at[1])
    for half in over_y:
        advance(half)
    advance(ring, 2)
    chunk(next_z, core)
    chunk(last_z, 1 - core)
    last_met = hand_over(last_z)
    next_met.wait_recv()
    join(next_z)
    raw_last = copies.start(parts.at[next_z, core, 1], came.at[2], above, came.at[2])
    for half in over_y:
        advance(half)
    chunk(last_z, core)
    chunk(z, 1 - core)
    own_met = hand_over(z)
    last_met.wait_recv()
    join(last_z)
    raw_next = copies.start(parts.at[last_z, core, 0], came.at[3], below, came.at[3])
    from_last.wait_recv()
    parts[next_z, core, 0] = (
        parts[next_z, core, 0].astype(f32) + came[0].astype(f32)
    ).astype(bf16)
    sum_last = copies.start(parts.at[next_z, core, 0], came.at[4], above, came.at[4])
    from_next.wait_recv()
    parts[last_z, core, 1] = (
        parts[last_z, core, 1].astype(f32) + came[1].astype(f32)
    ).astype(bf16)
    sum_next = copies.start(parts.at[last_z, core, 1], came.at[5], below, came.at[5])
    for half in over_y:
        advance(half)
    advance(ring)
    chunk(z, core)
    q_low[...] = (grad_q[...] * (HD**-0.5)).T.astype(bf16).reshape(2, 4, ROWS // 2, HD)
    arrivals = []
    for hop in HOPS:
        other = around(x, hop)
        arrivals.append(
            copies.start(
                q_low.at[:, other],
                back_q.at[x],
                device(other, y, z, core),
                back_q.at[around(x, -hop)],
            )
        )
    back_q[x] = q_low[:, x]
    advance(ring)
    own_met.wait_recv()
    raw_last.wait_recv()
    raw_next.wait_recv()
    sum_last.wait_recv()
    sum_next.wait_recv()
    mine = parts[z, core].astype(f32) + met[z].astype(f32)
    low = mine[0] + came[4].astype(f32) + came[3].astype(f32)
    high = mine[1] + came[2].astype(f32) + came[5].astype(f32)
    sums[0:2] = low.astype(bf16).reshape(2, ROWS, 2 * HD)
    sums[2:4] = high.astype(bf16).reshape(2, ROWS, 2 * HD)
    for hop in HOPS:
        other = around(x, hop)
        arrivals.append(
            copies.start(
                sums.at[other],
                back_kv.at[x],
                device(other, y, z, core),
                back_kv.at[around(x, -hop)],
            )
        )
    back_kv[x] = sums[x]
    for half in over_y:
        advance(half)
    keep = pltpu.make_async_copy(all_rows, total_hbm, load_sems.at[9])
    keep.start()
    advance(ring)
    advance(ring)
    advance(ring)
    for arrival in arrivals:
        arrival.wait_recv()
    for n in range(4):
        packed_ref[n, :, :HD] = back_q[n].reshape(ROWS, HD)
        packed_ref[n, :, HD:] = back_kv[n]
    keep.wait()
    copies.finish()
    y_copies.finish()


def attention_backward(grad_heads, q_all, kv_all, o_all, lse, tops, weights, down_parts, given):
    whole = pl.BlockSpec(memory_space=pltpu.VMEM)
    anywhere = pl.BlockSpec(memory_space=pl.ANY)
    count = 4 + 6 + 6
    width = 2 * given.shape[3]
    down_rows = down_parts.shape[3] // 2
    return pl.pallas_call(
        backward_kernel,
        out_shape=[
            jax.ShapeDtypeStruct((4, ROWS, 3 * HD), bf16),
            jax.ShapeDtypeStruct((down_rows, width), f32),
            jax.ShapeDtypeStruct(given.shape, bf16),
        ],
        in_specs=[whole, whole, anywhere] + [whole] * 3 + [anywhere] * 3,
        out_specs=[whole] * 2 + [anywhere],
        scratch_shapes=[
            pltpu.VMEM(given.shape, bf16),
            pltpu.VMEM((4, 2, 4, ROWS + CODE_ROWS, 2 * HD), bf16),
            pltpu.VMEM((3, 2, 4 * ROWS, 2 * ROWS), bf16),
            pltpu.VMEM((8, 4 * ROWS), f32),
            pltpu.VMEM((HD, 4 * ROWS), f32),
            pltpu.VMEM((4, 2, 2, 2 * ROWS, 2 * HD), bf16),
            pltpu.VMEM((4, 2, 2 * ROWS, 2 * HD), bf16),
            pltpu.VMEM((6, 2 * ROWS, 2 * HD), bf16),
            pltpu.VMEM((4, ROWS, 2 * HD), bf16),
            pltpu.VMEM((2, 4, ROWS // 2, HD), bf16),
            pltpu.VMEM((4, 2, ROWS // 2, HD), bf16),
            pltpu.VMEM((4, ROWS, 2 * HD), bf16),
            pltpu.SemaphoreType.DMA((count,)),
            pltpu.SemaphoreType.DMA((count,)),
            pltpu.SemaphoreType.DMA((10,)),
            pltpu.SemaphoreType.DMA((3,)),
        ]
        + sum_scratch(2 * given.shape[3])
        + weight_scratch(down_rows, width),
        compiler_params=pltpu.CompilerParams(
            collective_id=1, has_side_effects=True, vmem_limit_bytes=VMEM_LIMIT
        ),
        name="attention_backward",
    )(
        grad_heads, q_all, kv_all, o_all, lse, tops, weights, down_parts, given
    )


def last_kernel(
    x_ref, labels_ref, gains_ref, packed_ref, cos_ref, sin_ref, gains_two_ref, left_hbm, attn_hbm, mlp_hbm, g_mid_hbm,
    weight_hbm, out_left_hbm, g_low_hbm,
    input_hbm, layer_hbm, gains_out_ref, grad_qkv_ref, grad_out_ref,
    input_ref, layer_ref, attn, mlp, g_mid, weight, xhat, inverse, given, gains_part, gains_given, came, all_rows, y_send, y_recv, load_sems,
    qkv_left, qkv_right, *more,
):
    gain_scratch = more[: len(GAIN_SCRATCH)]
    gain_send, gain_recv = more[len(GAIN_SCRATCH) : len(GAIN_SCRATCH) + 2]
    qkv_scratch = more[len(GAIN_SCRATCH) + 2 : len(GAIN_SCRATCH) + 9]
    out_factors = more[len(GAIN_SCRATCH) + 9 : len(GAIN_SCRATCH) + 11]
    out_scratch = more[len(GAIN_SCRATCH) + 11 :]
    here = place()
    x, y, z, core = here
    loads = []
    for n, (src, dst) in enumerate(
        (
            (weight_hbm, weight),
            (left_hbm, qkv_left),
            (attn_hbm, attn),
            (mlp_hbm, mlp),
            (g_mid_hbm, g_mid),
        )
    ):
        loads.append(pltpu.make_async_copy(src, dst, load_sems.at[n]))
    loads[0].start()
    arrived = greet(
        [device(x, around(y, hop), z, core) for hop in HOPS]
        + [device(around(x, hop), y, z, core) for hop in HOPS]
        + [device(x, y, around(z, hop), core) for hop in HOPS]
        + [device(x, y, z, 1 - core)]
    )
    width = x_ref.shape[1]
    local = qkv_right.shape[1] // 3

    cosine, sine = cos_ref[...], sin_ref[...]
    for head in range(4):
        for part in range(3):
            grad = packed_ref[head, :, part * HD : (part + 1) * HD]
            if part < 2:
                grad = grad.astype(f32)
                scaled = grad * sine
                grad = (
                    grad * cosine
                    + jnp.concatenate([scaled[:, HD // 2 :], -scaled[:, : HD // 2]], axis=1)
                ).astype(bf16)
            start = part * local + head * HD
            qkv_right[0:ROWS, start : start + HD] = grad
    arrived()
    ring = weight_grad(here, grad_qkv_ref, qkv_scratch, (qkv_left, qkv_right))
    ring_out = weight_grad(
        here, grad_out_ref, out_scratch, out_factors, left=out_left_hbm, right=g_low_hbm
    )
    advance(ring)
    loads[0].wait()
    advance(ring_out)
    for load in loads[1:]:
        load.start()
    copies = Copies(y_send, y_recv)
    half_steps = width // WIDE // 2
    over_y = [
        sum_over_y(copies, here, given.at[half], came.at[half], all_rows.at[half])
        for half in range(2)
    ]

    def back_in(index, half):
        at = slab(index + half * half_steps, WIDE)
        part = sum(
            dot(qkv_right[pl.ds(0, ROWS), k * local : (k + 1) * local], weight[k, at, :], NT)
            for k in range(3)
        )
        given[half, :, :, slab(index, WIDE)] = part.astype(bf16).reshape(
            SIDE, ROWS // SIDE, WIDE
        )

    steps(half_steps, lambda index: back_in(index, 0))
    advance(over_y[0])
    loads[1].wait()
    advance(ring)
    steps(half_steps, lambda index: back_in(index, 1))
    advance(over_y[1])
    advance(ring, 2)
    advance(over_y[0])
    advance(ring, 2)
    advance(ring_out, 5)
    gains_part[...] = 0.25 * gains_two_ref[...]

    def norm(index):
        at = slab(index, NORM_ROWS)
        rows = x_ref[at, :].astype(f32)
        centred = rows - jnp.mean(rows, axis=-1, keepdims=True)
        scale = lax.rsqrt(jnp.mean(centred * centred, axis=-1, keepdims=True) + 1e-05)
        unit = centred * scale
        xhat[at, :] = unit
        inverse[at, :] = jnp.broadcast_to(scale, (NORM_ROWS, HD))
        labels = labels_ref[at, :1]
        product = summed_rows(given, index) * unit
        for mode in range(3):
            gains_part[mode : mode + 1, :] += jnp.sum(
                jnp.where(labels == mode, product, 0.0), axis=0, keepdims=True
            )

    norm_steps = ROWS // NORM_ROWS // 2
    steps(norm_steps, norm)
    advance(over_y[1])
    advance(over_y[0])
    advance(ring)
    steps(norm_steps, lambda index: norm(index + norm_steps))
    advance(over_y[1])
    advance(ring)
    for owner in range(32):
        gains_given[owner // 8, (owner // 2) % 4, owner % 2] = jnp.zeros((8, HD), f32)
        gains_given[owner // 8, (owner // 2) % 4, owner % 2, :, :64] = gains_part[
            :, owner * 64 : (owner + 1) * 64
        ]
    gain_copies = Copies(gain_send, gain_recv)
    over_all = sum_gains(gain_copies, here, gains_given, *gain_scratch, gains_out_ref)
    advance(over_all)
    advance(over_y[0])
    advance(over_y[1])
    advance(ring_out, 2)
    advance(ring)
    for load in loads[2:]:
        load.wait()

    def finish_layer(index):
        at = slab(index, NORM_ROWS)
        total = x_ref[at, :].astype(f32) + attn[at, :].astype(f32) + summed_rows(mlp, index)
        layer_ref[at, :] = total.astype(bf16)

    steps(ROWS // NORM_ROWS, finish_layer)
    keep = [pltpu.make_async_copy(layer_ref, layer_hbm, load_sems.at[5])]
    keep[0].start()
    advance(over_all)
    advance(ring)
    advance(over_all)
    advance(over_y[0])
    advance(ring_out, 2)
    advance(over_all)
    advance(over_y[1])

    def finish_input(index):
        at = slab(index, NORM_ROWS)
        unit = xhat[at, :]
        grad = summed_rows(all_rows, index) * gain_rows(labels_ref[at, :1], gains_ref, 0)
        mean = jnp.mean(grad, axis=-1, keepdims=True)
        along = jnp.mean(grad * unit, axis=-1, keepdims=True)
        input_ref[at, :] = g_mid[at, :] + inverse[at, :1] * (grad - mean - unit * along)

    for half in range(2):
        steps(norm_steps, lambda index: finish_input(index + half * norm_steps))
        at = pl.ds(half * (ROWS // 2), ROWS // 2)
        keep.append(
            pltpu.make_async_copy(input_ref.at[at], input_hbm.at[at], load_sems.at[6 + half])
        )
        keep[-1].start()
        advance(ring)
        advance(ring_out)
    advance(over_all)
    for copy in keep:
        copy.wait()
    copies.finish()
    gain_copies.finish()


def last(
    activations, labels, gains, packed, cosine, sine, gains_two, left, attn_sum, mlp_sum, g_mid, weight, out_left, g_low
):
    width = activations.shape[1]
    local = weight.shape[2]
    cols = 3 * local
    rows = width // 32
    whole = pl.BlockSpec(memory_space=pltpu.VMEM)
    anywhere = pl.BlockSpec(memory_space=pl.ANY)
    return pl.pallas_call(
        last_kernel,
        out_shape=[
            jax.ShapeDtypeStruct((ROWS, width), f32),
            jax.ShapeDtypeStruct((ROWS, width), bf16),
            jax.ShapeDtypeStruct((8, HD), f32),
            jax.ShapeDtypeStruct((3, rows, local), f32),
            jax.ShapeDtypeStruct((out_left.shape[2], width), f32),
        ],
        in_specs=[whole] * 7 + [anywhere] * 7,
        out_specs=[anywhere] * 2 + [whole] * 3,
        scratch_shapes=[
            pltpu.VMEM((ROWS, width), f32),
            pltpu.VMEM((ROWS, width), bf16),
            pltpu.VMEM(attn_sum.shape, bf16),
            pltpu.VMEM(mlp_sum.shape, bf16),
            pltpu.VMEM(g_mid.shape, f32),
            pltpu.VMEM(weight.shape, bf16),
            pltpu.VMEM((ROWS, width), f32),
            pltpu.VMEM((ROWS, HD), f32),
            pltpu.VMEM(mlp_sum.shape, bf16),
            pltpu.VMEM((8, width), f32),
            pltpu.VMEM((4, 4, 2, 8, HD), f32),
        ]
        + sum_scratch(width)
        + [pltpu.SemaphoreType.DMA((8,))]
        + factor_scratch(rows, cols)
        + [pltpu.VMEM(shape, f32) for shape in GAIN_SCRATCH]
        + [pltpu.SemaphoreType.DMA((10,)), pltpu.SemaphoreType.DMA((10,))]
        + weight_scratch(rows, cols)
        + factor_scratch(out_left.shape[2], width)
        + weight_scratch(out_left.shape[2], width),
        compiler_params=pltpu.CompilerParams(
            collective_id=3, has_side_effects=True, vmem_limit_bytes=VMEM_LIMIT
        ),
        name="last",
    )(
        activations,
        labels,
        gains,
        packed,
        cosine,
        sine,
        gains_two,
        left,
        attn_sum,
        mlp_sum,
        g_mid,
        weight,
        out_left,
        g_low,
    )


def finish_kernel(
    share_ref, layer_in, input_in, qkv_in, out_in, up_in, down_in,
    gains_ref, layer_out, input_out, qkv_out, out_out, up_out, down_out,
    layer, grad_input, qkv, out, up, down, load_sems, store_sems,
):
    ways = (
        (layer_in, layer, layer_out),
        (up_in, up, up_out),
        (qkv_in, qkv, qkv_out),
        (down_in, down, down_out),
        (out_in, out, out_out),
        (input_in, grad_input, input_out),
    )
    loads = [
        pltpu.make_async_copy(src, held, load_sems.at[n]) for n, (src, held, dst) in enumerate(ways)
    ]
    stores = [
        pltpu.make_async_copy(held, dst, store_sems.at[n]) for n, (src, held, dst) in enumerate(ways)
    ]
    for load in loads:
        load.start()
    gains_ref[...] = share_ref[: gains_ref.shape[0], : gains_ref.shape[1]]
    for load, store in zip(loads, stores):
        load.wait()
        store.start()
    for store in stores:
        store.wait()


def finish(modes, share, *arrays):
    whole = pl.BlockSpec(memory_space=pltpu.VMEM)
    anywhere = pl.BlockSpec(memory_space=pl.ANY)
    count = len(arrays)
    return pl.pallas_call(
        finish_kernel,
        out_shape=[jax.ShapeDtypeStruct((2 * modes, arrays[0].shape[1] // 32), f32)]
        + [jax.ShapeDtypeStruct(array.shape, array.dtype) for array in arrays],
        in_specs=[whole] + [anywhere] * count,
        out_specs=[whole] + [anywhere] * count,
        scratch_shapes=[pltpu.VMEM(array.shape, array.dtype) for array in arrays]
        + [pltpu.SemaphoreType.DMA((count,)), pltpu.SemaphoreType.DMA((count,))],
        name="finish",
    )(share, *arrays)


def per_device(
    activations,
    labels,
    position,
    norm_gains,
    qkv_weight,
    out_weight,
    up_weight,
    down_weight,
    cotangent,
):
    projections = qkv_weight.transpose(1, 0, 2)
    (
        q_all,
        kv_all,
        o_all,
        lse,
        out_left,
        attn_sum,
        grad_active,
        weights,
        tops,
        label_rows,
        cosine,
        sine,
        qkv_left,
        both_cotangents,
    ) = attention_forward(
        activations,
        labels.reshape(1, ROWS),
        position.reshape(1, ROWS),
        norm_gains,
        cotangent,
        projections,
        out_weight,
        down_weight,
    )
    g_mid, g_low, grad_heads, mlp_part, down_parts, gains_two, grad_up = middle(
        activations,
        attn_sum,
        label_rows,
        norm_gains,
        both_cotangents,
        out_weight,
        grad_active,
        up_weight,
        down_weight,
    )
    packed, grad_down, mlp_sum = attention_backward(
        grad_heads,
        q_all,
        kv_all,
        o_all,
        lse,
        tops,
        weights,
        down_parts,
        mlp_part,
    )
    grad_input, layer_out, share, grad_qkv, grad_out = last(
        activations,
        label_rows,
        norm_gains,
        packed,
        cosine,
        sine,
        gains_two,
        qkv_left,
        attn_sum,
        mlp_sum,
        g_mid,
        projections,
        out_left,
        g_low,
    )
    grad_gains, layer_out, grad_input, grad_qkv, grad_out, grad_up, grad_down = finish(
        norm_gains.shape[0] // 2,
        share,
        layer_out,
        grad_input,
        grad_qkv,
        grad_out,
        grad_up,
        grad_down,
    )
    return (
        layer_out,
        grad_input,
        grad_gains,
        grad_qkv.transpose(1, 0, 2),
        grad_out,
        grad_up,
        grad_down,
    )


def solution(mesh):
    return jax.shard_map(
        per_device,
        mesh=mesh,
        in_specs=(
            P("tok", None),
            P("tok"),
            P("tok"),
            P(),
            P(None, None, "head"),
            P("head", None),
            P(None, "head"),
            P("head", None),
            P("tok", None),
        ),
        out_specs=(
            P("tok", None),
            P("tok", None),
            P(None, "tok"),
            P("tok", None, "head"),
            P(("head", "tok"), None),
            P("tok", "head"),
            P(("head", "tok"), None),
        ),
        check_vma=False,
    )
```
